32 devices in a mesh: seq: 8 (over z, core), batch: 4 (over y, x).
Axes of the slice: x: 2, y: 2, z: 4, core: 2. Of those that a mesh axis runs over, the one named last changes fastest.
Arguments:
- tokens: bfloat16 [2, 8, 1024, 640], P(None, 'batch', 'seq'), may hold values from -6 to 6
- mask: int32 [2, 8, 1024], P(None, 'batch', 'seq'), may hold values from 0 to 1, as said below
- cotangent: bfloat16 [2, 8, 1024, 640], P(None, 'batch', 'seq'), may hold values from -6 to 6
- ln1_gain: float32 [640], replicated, may hold values from 0.1 to 1.9
- ln1_bias: float32 [640], replicated, may hold values from -1.75 to 1.75
- qkv_weight: bfloat16 [640, 1920], replicated, may hold values from -0.25 to 0.25
- q_bias: float32 [640], replicated, may hold values from -3 to 3
- v_bias: float32 [640], replicated, may hold values from -3 to 3
- out_weight: bfloat16 [640, 640], replicated, may hold values from -4 to 4
- out_bias: float32 [640], replicated, may hold values from -1.75 to 1.75
- ln2_gain: float32 [640], replicated, may hold values from 0.1 to 1.9
- ln2_bias: float32 [640], replicated, may hold values from -1.75 to 1.75
- up_weight: bfloat16 [640, 5120], replicated, may hold values from -0.25 to 0.25
- up_bias: float32 [5120], replicated, may hold values from -3 to 3
- down_weight: bfloat16 [5120, 640], replicated, may hold values from -0.078125 to 0.078125
- down_bias: float32 [640], replicated, may hold values from -1.75 to 1.75
Outputs:
- out: bfloat16 [2, 8, 1024, 640], P(None, 'batch', 'seq')
- grad_in: bfloat16 [2, 8, 1024, 640], P(None, 'batch', 'seq')
- ln1_gain_grad: float32 [640], replicated
- ln1_bias_grad: float32 [640], replicated
- qkv_weight_grad: float32 [640, 1920], P('seq', 'batch')
- q_bias_grad: float32 [640], replicated
- v_bias_grad: float32 [640], replicated
- out_weight_grad: float32 [640, 640], P('seq', 'batch')
- out_bias_grad: float32 [640], replicated
- ln2_gain_grad: float32 [640], replicated
- ln2_bias_grad: float32 [640], replicated
- up_weight_grad: float32 [640, 5120], P('seq', 'batch')
- up_bias_grad: float32 [5120], replicated
- down_weight_grad: float32 [5120, 640], P('seq', 'batch')
- down_bias_grad: float32 [640], replicated
The draws below stay inside these ranges and needn't reach their ends.
Inputs may be any that keep to these rules, and one draw needn't show every extreme that they name: `mask`: 1 marks a masked position; every sequence has one or more.
All inputs are finite; a program needn't handle non-finite values.
Results may differ from the reference program's by a relative error of at most 0.017.
Values may be sent and summed in bfloat16 or wider, within the bound.
No kernel may reach another device: no remote copies, remote signals or barrier semaphores. Data moves between devices by JAX's collectives and lax.ppermute only.
A program may use at most 192 MiB of HBM per device.

```python
import jax
import jax.numpy as jnp
from jax import lax

D = 640
HEADS = 20
FF = 5120
SEQ_LEN = 1024
MB = 2
SEQ_MB = 2
SEQS_B = 8
N_BATCH = 4


def draw_mask(key, part):
    key = jax.random.fold_in(key, 7)
    rate_key, roll_key = jax.random.split(key)
    rate_base = jax.random.randint(rate_key, (MB, SEQS_B, 1), 50, 200)
    position = jnp.arange(SEQ_LEN, dtype=jnp.int32)
    threshold = rate_base * (SEQ_LEN - 1 + 2 * position) // (SEQ_LEN - 1)
    rolled = jax.random.randint(roll_key, (MB, SEQS_B, SEQ_LEN), 0, 1000)
    chosen = jnp.where(rolled < threshold, 1, 0)
    return jnp.where(position == 0, 1, chosen).astype(jnp.int32)


def block_levels(own_key, shape, shards, smallest, high):
    level, own = 1.0, jax.random.fold_in(own_key, 6)
    for axis_at, shards_of in shards:
        draws = jnp.exp(jax.random.uniform(jax.random.fold_in(own, axis_at), (shards_of,), jnp.float32, smallest / len(shards), high / len(shards)))
        level = level * jnp.repeat(draws, shape[axis_at] // shards_of).reshape([-1 if axis == axis_at else 1 for axis in range(len(shape))])
    return level


def bell_draw(rng, dims, spread, most, shards=(), kind=jnp.bfloat16):
    array = jax.random.normal(rng, dims, jnp.float32) * spread
    if len(shards) > 0:
        array = block_levels(rng, dims, shards, -0.22, 0.18) * array
    return jnp.clip(array, min=-most, max=most).astype(kind)


def setup_inputs(seed: int = 0) -> dict:
    streams_of = jax.random.split(jax.random.key(seed), 17)
    return {
        "tokens": bell_draw(streams_of[0], (MB, SEQS_B, SEQ_LEN, D), 1.0, 6.0, ((1, 4), (2, 8))),
        "mask": draw_mask(jax.random.fold_in(streams_of[16], 71), 0),
        "cotangent": bell_draw(streams_of[2], (MB, SEQS_B, SEQ_LEN, D), 1.0, 6.0, ((1, 4), (2, 8))),
        "ln1_gain": jnp.clip(1.0 + 0.18 * jax.random.normal(streams_of[3], (D,), jnp.float32), 0.1, 1.9),
        "ln1_bias": bell_draw(streams_of[4], (D,), 0.3, 1.75, (), jnp.float32),
        "qkv_weight": bell_draw(streams_of[5], (D, 3 * D), D ** -0.5, 0.25),
        "q_bias": bell_draw(streams_of[6], (D,), 0.5, 3.0, (), jnp.float32),
        "v_bias": bell_draw(streams_of[7], (D,), 0.5, 3.0, (), jnp.float32),
        "out_weight": bell_draw(streams_of[8], (D, D), (max(D // 256, 1)) ** -0.5, 4.0),
        "out_bias": bell_draw(streams_of[9], (D,), 0.3, 1.75, (), jnp.float32),
        "ln2_gain": jnp.clip(1.0 + 0.18 * jax.random.normal(streams_of[10], (D,), jnp.float32), 0.1, 1.9),
        "ln2_bias": bell_draw(streams_of[11], (D,), 0.3, 1.75, (), jnp.float32),
        "up_weight": bell_draw(streams_of[12], (D, FF), D ** -0.5, 0.25),
        "up_bias": bell_draw(streams_of[13], (FF,), 0.5, 3.0, (), jnp.float32),
        "down_weight": bell_draw(streams_of[14], (FF, D), FF ** -0.5, 0.078125),
        "down_bias": bell_draw(streams_of[15], (D,), 0.3, 1.75, (), jnp.float32),
    }


@jax.custom_vjp
def low(v):
    return lax.optimization_barrier(v.astype(jnp.bfloat16)).astype(jnp.float32)

@jax.custom_vjp
def low_back(v):
    return v

def low_keep(v):
    return (low(v), None)

def low_pass(kept, grad):
    return (grad,)

def back_keep(v):
    return (v, None)

def back_low(kept, grad):
    return (low(grad),)
low.defvjp(low_keep, low_pass)
low_back.defvjp(back_keep, back_low)

def matmul_high(left, right):
    return jnp.dot(left, right, precision=lax.Precision.HIGHEST)

def layer_norm(rows_in, norm_gain, norm_shift):
    mean_val = lax.optimization_barrier(jnp.mean(rows_in, axis=-1, keepdims=True))
    centered = rows_in - mean_val
    variance = lax.optimization_barrier(jnp.mean(centered * centered, axis=-1, keepdims=True))
    return centered * lax.rsqrt(variance + 1e-05) * norm_gain + norm_shift

def head_attend(triple):
    queries, keys_all, values = triple
    score_scale = queries.shape[-1] ** (-0.5)
    scores = low_back(score_scale * jnp.einsum('gqd,gkd->gqk', queries, keys_all, precision=lax.Precision.HIGHEST))
    row_max = lax.optimization_barrier(jnp.max(scores, axis=-1, keepdims=True))
    exp_scores = jnp.exp(scores - row_max)
    probs = exp_scores / lax.optimization_barrier(jnp.sum(exp_scores, axis=-1, keepdims=True))
    return jnp.einsum('gqk,gkd->gqd', low(probs), values, precision=lax.Precision.HIGHEST)

def block_forward(tokens_f, params):
    ln1_gain, ln1_bias, qkv_w, q_b, v_b, out_w, out_b, ln2_gain, ln2_bias, up_w, up_b, down_w, down_b = params
    group_count, seq_len, width = tokens_f.shape
    head_dim = width // HEADS
    rows_in = tokens_f.reshape(-1, width)
    normed_first = low(layer_norm(rows_in, ln1_gain, ln1_bias))
    qkv_shift = jnp.concatenate([q_b, jnp.zeros_like(q_b), v_b])
    qkv_rows = low(low_back(matmul_high(normed_first, qkv_w) + qkv_shift))
    split_qkv = qkv_rows.reshape(group_count, seq_len, 3, HEADS, head_dim).transpose(2, 3, 0, 1, 4)
    attended = lax.map(jax.checkpoint(head_attend), (split_qkv[0], split_qkv[1], split_qkv[2]))
    attended = attended.transpose(1, 2, 0, 3).reshape(-1, width)
    attended = low(low_back(attended))
    mid = rows_in + low_back(matmul_high(attended, out_w) + out_b)
    second = low(layer_norm(mid, ln2_gain, ln2_bias))
    pre_act = low_back(matmul_high(second, up_w) + up_b)
    act_low = low(jax.nn.gelu(pre_act, approximate=False))
    result = mid + matmul_high(act_low, down_w) + down_b
    return result.reshape(group_count, seq_len, width)

def reference(tokens, mask, cotangent, ln1_gain, ln1_bias, qkv_weight, q_bias, v_bias, out_weight, out_bias, ln2_gain, ln2_bias, up_weight, up_bias, down_weight, down_bias):
    counts = lax.optimization_barrier(jnp.sum(mask, axis=2)).astype(jnp.float32)
    factor = SEQ_LEN / (4.0 * counts)
    grad_out = low(cotangent.astype(jnp.float32) * mask.astype(jnp.float32)[..., None] * factor[..., None, None])
    params = tuple((item.astype(jnp.float32) for item in (ln1_gain, ln1_bias, qkv_weight, q_bias, v_bias, out_weight, out_bias, ln2_gain, ln2_bias, up_weight, up_bias, down_weight, down_bias)))
    group_total = MB * N_BATCH
    token_groups = tokens.astype(jnp.float32).reshape(group_total, SEQ_MB, SEQ_LEN, D)
    grad_groups = grad_out.reshape(group_total, SEQ_MB, SEQ_LEN, D)

    def group_step(totals, group_pair):
        tokens_f, grad_f = group_pair
        result, pullback = jax.vjp(block_forward, tokens_f, params)
        grad_tokens, grad_params = pullback(grad_f)
        totals = jax.tree.map(jnp.add, totals, grad_params)
        return (totals, (result.astype(jnp.bfloat16), grad_tokens.astype(jnp.bfloat16)))
    zero_tree = jax.tree.map(jnp.zeros_like, params)
    totals, (results, grads_in) = lax.scan(group_step, zero_tree, (token_groups, grad_groups))
    out = results.reshape(MB, SEQS_B, SEQ_LEN, D)
    grad_in = grads_in.reshape(MB, SEQS_B, SEQ_LEN, D)
    return (out, grad_in, totals[0], totals[1], totals[2], totals[3], totals[4], totals[5], totals[6], totals[7], totals[8], totals[9], totals[10], totals[11], totals[12])
```

```python
from functools import partial

import jax
import jax.numpy as jnp
from jax import lax
from jax.experimental import pallas as pl
from jax.experimental.pallas import tpu as pltpu
from jax.sharding import PartitionSpec as P

HEADS = 20
EPS = 1e-05
LOG2E = 1.4426950408889634
ROWS = 256
F32 = jnp.float32
BF16 = jnp.bfloat16
LANES = 128


def dot(left, right):
    return jnp.dot(left, right, preferred_element_type=F32)


def dot_nt(left, right):
    return lax.dot_general(left, right, (((1,), (1,)), ((), ())), preferred_element_type=F32)


def norm_rows(rows_in):
    mean_val = jnp.mean(rows_in, axis=-1, keepdims=True)
    centered = rows_in - mean_val
    inv_std = lax.rsqrt(jnp.mean(centered * centered, axis=-1, keepdims=True) + EPS)
    return centered * inv_std, inv_std


def norm_back(scaled, normed, inv_std):
    inner = (
        scaled
        - jnp.mean(scaled, axis=-1, keepdims=True)
        - normed * jnp.mean(scaled * normed, axis=-1, keepdims=True)
    )
    return inner * inv_std


def params_of(mib):
    return pltpu.CompilerParams(vmem_limit_bytes=mib * 1024 * 1024)


def cost(flops, moved, trans=0):
    return pl.CostEstimate(flops=flops, bytes_accessed=moved, transcendentals=trans)


def sds(shape, dtype):
    return jax.ShapeDtypeStruct(shape, dtype)


def attend_forward(x_pieces, gain, shift, weight, bias, heads, head_dim):
    pieces = len(x_pieces)
    piece_rows, width = x_pieces[0].shape
    total = pieces * piece_rows
    wide = weight.shape[1] // 3
    tiles = wide // LANES
    per_tile = LANES // head_dim
    exp_scale = head_dim ** (-0.5) * LOG2E

    def body(*refs):
        x_refs = refs[:pieces]
        gain_ref, shift_ref, w_ref, bias_ref, qkv_ref, att_ref, lse_ref, keys, vals = refs[pieces:]
        for h in range(pieces):

            @pl.loop(0, piece_rows // ROWS)
            def _(i, h=h):
                at = pl.multiple_of(i * ROWS, ROWS)
                normed, _ = norm_rows(x_refs[h][pl.ds(at, ROWS), :].astype(F32))
                low = (normed * gain_ref[...] + shift_ref[...]).astype(BF16)
                out = (dot(low, w_ref[...]) + bias_ref[...]).astype(BF16)
                qkv_ref[pl.ds(h * piece_rows + at, ROWS), :] = out

        lse_ref[...] = jnp.zeros_like(lse_ref)
        lane = lax.broadcasted_iota(jnp.int32, (1, LANES), 1)
        row = lax.broadcasted_iota(jnp.int32, (LANES, 1), 0)
        vals[:, :, LANES:] = jnp.ones((per_tile, total, LANES), BF16)
        for t in range(tiles):
            live = min(per_tile, heads - t * per_tile)
            key_t = qkv_ref[:, wide + t * LANES : wide + (t + 1) * LANES].astype(F32).T
            val_f = qkv_ref[:, 2 * wide + t * LANES : 2 * wide + (t + 1) * LANES].astype(F32)
            for j in range(live):
                keys[j] = jnp.where(row // head_dim == j, key_t, 0.0).astype(BF16)
                vals[j, :, :LANES] = jnp.where(lane // head_dim == j, val_f, 0.0).astype(BF16)

            @pl.loop(0, total // ROWS)
            def _(i, t=t, live=live):
                at = pl.multiple_of(i * ROWS, ROWS)
                query = qkv_ref[pl.ds(at, ROWS), t * LANES : (t + 1) * LANES]
                acc = jnp.zeros((ROWS, LANES), F32)
                logs = lse_ref[pl.ds(at, ROWS), :]
                for j in range(live):
                    scores = dot(query, keys[j])
                    row_max = jnp.max(scores, axis=-1, keepdims=True) * exp_scale
                    expd = jnp.exp2(scores * exp_scale - row_max)
                    mixed = dot(expd.astype(BF16), vals[j])
                    den = mixed[:, LANES:]
                    acc = acc + mixed[:, :LANES] / den
                    logs = jnp.where(lane == t * per_tile + j, row_max + jnp.log2(den), logs)
                att_ref[pl.ds(at, ROWS), t * LANES : (t + 1) * LANES] = acc.astype(BF16)
                lse_ref[pl.ds(at, ROWS), :] = logs

    return pl.pallas_call(
        body,
        out_shape=(
            sds((total, 3 * wide), BF16),
            sds((total, wide), BF16),
            sds((total, LANES), F32),
        ),
        scratch_shapes=[
            pltpu.VMEM((per_tile, LANES, total), BF16),
            pltpu.VMEM((per_tile, total, 2 * LANES), BF16),
        ],
        compiler_params=params_of(48),
        cost_estimate=cost(
            2 * total * width * 3 * wide + 2 * heads * total * total * 256 * 2,
            8 * 1024 * 1024,
            heads * total * total,
        ),
        name="attend_forward",
    )(*x_pieces, gain, shift, weight, bias)


def gelu_parts(value):
    size = jnp.abs(value)
    near = 1.0 / (1.0 + (0.3275911 * 0.7071067811865476) * size)
    bell = jnp.exp2(value * value * (-0.5 * LOG2E))
    poly = near * (
        0.5 * 0.254829592
        + near
        * (
            0.5 * -0.284496736
            + near * (0.5 * 1.421413741 + near * (0.5 * -1.453152027 + near * (0.5 * 1.061405429)))
        )
    )
    tail = poly * bell
    area = jnp.where(value < 0.0, tail, 1.0 - tail)
    return value * area, area + value * bell * 0.3989422804014327


def feed_forward(
    x_pieces,
    att_pieces,
    grad_pieces,
    out_w,
    out_b,
    gain,
    shift,
    up,
    up_b,
    down,
    down_b,
    packed,
):
    pieces = len(x_pieces)
    piece_rows, width = x_pieces[0].shape
    total = pieces * piece_rows
    units = up.shape[1]
    step = 1280 if units % 1280 == 0 else units
    steps = units // step
    if packed is not None:
        blocks, quads = packed
        unit_block = units // blocks
        high = width // quads
        low_rows = width // blocks

    def body(*refs):
        x_refs, refs = refs[:pieces], refs[pieces:]
        att_refs, refs = refs[:pieces], refs[pieces:]
        grad_refs, refs = refs[:pieces], refs[pieces:]
        wo_refs, refs = refs[:pieces], refs[pieces:]
        ob_ref, gain_ref, shift_ref, up_ref, ub_ref, down_ref, db_ref = refs[:7]
        refs = refs[7:]
        mid_ref, own_ref, refs = refs[0], refs[1], refs[2:]
        send_refs, refs = refs[: pieces - 1], refs[pieces - 1 :]
        gs_ref, gsend_ref, ubg_ref, dw_ref = refs[:4]
        refs = refs[4:]
        if packed is None:
            dwd_ref, refs = refs[0], refs[1:]
        second, second_t, grad, grad_t, act, grad_pre, acc = refs
        k = pl.program_id(0)

        @pl.when(k == 0)
        def _():
            for h in range(pieces):

                @pl.loop(0, piece_rows // ROWS)
                def _(i, h=h):
                    at = pl.multiple_of(i * ROWS, ROWS)
                    dst = pl.ds(h * piece_rows + at, ROWS)
                    mid = x_refs[h][pl.ds(at, ROWS), :].astype(F32) + ob_ref[...]
                    for n in range(pieces):
                        src = pl.ds(((h - n) % pieces) * piece_rows + at, ROWS)
                        mid = mid + dot(att_refs[n][src, :], wo_refs[n][...])
                    mid_ref[dst, :] = mid
                    normed, _ = norm_rows(mid)
                    low = normed * gain_ref[...] + shift_ref[...]
                    second[dst, :] = low.astype(BF16)
                    second_t[:, dst] = low.T.astype(BF16)
                    grad_rows = grad_refs[h][pl.ds(at, ROWS), :]
                    grad[dst, :] = grad_rows
                    grad_t[:, dst] = grad_rows.astype(F32).T.astype(BF16)
                    acc[dst, :] = mid + db_ref[...] if h == 0 else jnp.zeros((ROWS, width), F32)
                    gs_ref[dst, :] = jnp.zeros((ROWS, width), F32)

        ubg_ref[...] = jnp.zeros_like(ubg_ref)

        @pl.loop(0, total // ROWS)
        def _(i):
            rows = pl.ds(pl.multiple_of(i * ROWS, ROWS), ROWS)
            pre = dot(second[rows, :], up_ref[...]) + ub_ref[...]
            value, slope = gelu_parts(pre)
            low_act = value.astype(BF16)
            act[rows, :] = low_act
            acc[rows, :] += dot(low_act, down_ref[...])
            grad_act = dot_nt(grad[rows, :], down_ref[...])
            low_grad = (grad_act * slope).astype(BF16)
            grad_pre[rows, :] = low_grad
            ubg_ref[0:1, :] += jnp.sum(low_grad.astype(F32), axis=0, keepdims=True)
            gs_ref[rows, :] += dot_nt(low_grad, up_ref[...])

        for i in range(step // 256):
            cols = slice(i * 256, (i + 1) * 256)
            up_grad = dot(second_t[...], grad_pre[:, cols]).astype(BF16)
            down_grad = dot(grad_t[...], act[:, cols]).astype(BF16)
            if packed is None:
                dw_ref[:, cols] = up_grad
                dwd_ref[:, cols] = down_grad
                continue
            start = i * 256
            while start < (i + 1) * 256:
                block = start // unit_block
                stop = min((i + 1) * 256, (block + 1) * unit_block)
                at = k * (step // unit_block) + block
                src = slice(start - i * 256, stop - i * 256)
                dst = slice(start - block * unit_block, stop - block * unit_block)
                for q in range(quads):
                    dw_ref[at, q, 0:high, dst] = up_grad[q * high : (q + 1) * high, src]
                for b in range(blocks):
                    dw_ref[b, at, high : high + low_rows, dst] = down_grad[
                        b * low_rows : (b + 1) * low_rows, src
                    ]
                start = stop

        @pl.when(k == steps - 1)
        def _():
            own_ref[...] = acc[0:piece_rows, :]
            for h in range(1, pieces):
                send_refs[h - 1][...] = acc[h * piece_rows : (h + 1) * piece_rows, :].astype(BF16)
            gsend_ref[...] = gs_ref[...].astype(BF16)

    def whole(shape):
        return pl.BlockSpec(shape, lambda k: (0,) * len(shape))

    if packed is None:
        grads = (sds((width, units), BF16),) * 2
        grad_specs = [pl.BlockSpec((width, step), lambda k: (0, k))] * 2
    else:
        shape = (blocks, quads, high + low_rows, unit_block)
        grads = (sds(shape, BF16),)
        grad_specs = [whole(shape)]
    wide = att_pieces[0].shape[1]
    row_spec = whole((1, width))
    return pl.pallas_call(
        body,
        grid=(steps,),
        in_specs=[whole((piece_rows, width))] * pieces
        + [whole((total, wide))] * pieces
        + [whole((piece_rows, width))] * pieces
        + [whole((wide, width))] * pieces
        + [
            row_spec,
            row_spec,
            row_spec,
            pl.BlockSpec((width, step), lambda k: (0, k)),
            pl.BlockSpec((1, step), lambda k: (0, k)),
            pl.BlockSpec((step, width), lambda k: (k, 0)),
            row_spec,
        ],
        out_specs=[whole((total, width)), whole((piece_rows, width))]
        + [whole((piece_rows, width))] * (pieces - 1)
        + [
            whole((total, width)),
            whole((total, width)),
            pl.BlockSpec((8, step), lambda k: (0, k)),
        ]
        + grad_specs,
        out_shape=[sds((total, width), F32), sds((piece_rows, width), F32)]
        + [sds((piece_rows, width), BF16)] * (pieces - 1)
        + [sds((total, width), F32), sds((total, width), BF16), sds((8, units), F32)]
        + list(grads),
        scratch_shapes=[
            pltpu.VMEM((total, width), BF16),
            pltpu.VMEM((width, total), BF16),
            pltpu.VMEM((total, width), BF16),
            pltpu.VMEM((width, total), BF16),
            pltpu.VMEM((total, step), BF16),
            pltpu.VMEM((total, step), BF16),
            pltpu.VMEM((total, width), F32),
        ],
        compiler_params=params_of(58),
        cost_estimate=cost(
            12 * total * width * units + 2 * total * width * width, 24 * 1024 * 1024, total * units
        ),
        name="feed_forward",
    )(
        *x_pieces,
        *att_pieces,
        *grad_pieces,
        *out_w,
        out_b,
        gain,
        shift,
        up,
        up_b,
        down,
        down_b,
    )


def mid_back(mid, grad_second, received, grad_pieces, gain, out_w, att):
    pieces = len(grad_pieces)
    piece_rows, width = grad_pieces[0].shape
    total = pieces * piece_rows
    wide = att.shape[1]

    def body(*refs):
        mid_ref, gs_ref, refs = refs[0], refs[1], refs[2:]
        recv_refs, refs = refs[: pieces - 1], refs[pieces - 1 :]
        go_refs, refs = refs[:pieces], refs[pieces:]
        gain_ref, wo_ref, att_ref, gm_ref, do_ref, dwo_ref, sums_ref, low_ref = refs
        sums_ref[...] = jnp.zeros_like(sums_ref)
        for h in range(pieces):

            @pl.loop(0, piece_rows // ROWS)
            def _(i, h=h):
                at = pl.multiple_of(i * ROWS, ROWS)
                rows = pl.ds(h * piece_rows + at, ROWS)
                normed, inv_std = norm_rows(mid_ref[rows, :])
                grad = gs_ref[rows, :]
                for n in range(1, pieces):
                    src = pl.ds(((h - n) % pieces) * piece_rows + at, ROWS)
                    grad = grad + recv_refs[n - 1][src, :].astype(F32)
                go = go_refs[h][pl.ds(at, ROWS), :].astype(F32)
                grad_mid = go + norm_back(grad * gain_ref[...], normed, inv_std)
                low = grad_mid.astype(BF16)
                low_ref[rows, :] = low
                do_ref[rows, :] = dot_nt(low, wo_ref[...]).astype(BF16)
                if h == 0:
                    gm_ref[rows, :] = grad_mid
                    for n, item in enumerate((grad * normed, grad, low.astype(F32), go)):
                        sums_ref[n : n + 1, :] += jnp.sum(item, axis=0, keepdims=True)

        dwo_ref[...] = dot(att_ref[...].astype(F32).T.astype(BF16), low_ref[...]).astype(BF16)

    return pl.pallas_call(
        body,
        out_shape=(
            sds((piece_rows, width), F32),
            sds((total, wide), BF16),
            sds((wide, width), BF16),
            sds((8, width), F32),
        ),
        scratch_shapes=[pltpu.VMEM((total, width), BF16)],
        compiler_params=params_of(40),
        cost_estimate=cost(4 * total * width * wide, 14 * 1024 * 1024),
        name="mid_back",
    )(mid, grad_second, *received, *grad_pieces, gain, out_w, att)


def attend_backward(qkv, grad_att, att, logs, heads, head_dim):
    total = qkv.shape[0]
    wide = att.shape[1]
    tiles = wide // LANES
    per_tile = LANES // head_dim
    scale = head_dim ** (-0.5)
    exp_scale = scale * LOG2E

    def body(
        qkv_ref, do_ref, att_ref, lse_ref, out_ref, km, vm, qm, dm, key_t, query_t, do_t, dq_t, lse_t, dot_t
    ):
        lane = lax.broadcasted_iota(jnp.int32, (1, LANES), 1)
        lse_t[...] = lse_ref[...].T
        for t in range(tiles):
            live = min(per_tile, heads - t * per_tile)
            cols = slice(t * LANES, (t + 1) * LANES)
            query = qkv_ref[:, cols].astype(F32)
            key = qkv_ref[:, wide + t * LANES : wide + (t + 1) * LANES].astype(F32)
            val = qkv_ref[:, 2 * wide + t * LANES : 2 * wide + (t + 1) * LANES].astype(F32)
            upstream = do_ref[:, cols].astype(F32)
            dot_t[...] = (upstream * att_ref[:, cols].astype(F32)).T
            query_t[...] = query.T.astype(BF16)
            do_t[...] = upstream.T.astype(BF16)
            key_t[...] = key.T.astype(BF16)
            for j in range(live):
                mine = lane // head_dim == j
                km[j] = jnp.where(mine, key, 0.0).astype(BF16)
                vm[j] = jnp.where(mine, val, 0.0).astype(BF16)
                qm[j] = jnp.where(mine, query, 0.0).astype(BF16)
                dm[j] = jnp.where(mine, upstream, 0.0).astype(BF16)
            dq_t[...] = jnp.zeros_like(dq_t)

            @pl.loop(0, total // ROWS)
            def _(i, t=t, live=live):
                at = pl.multiple_of(i * ROWS, ROWS)
                rows = pl.ds(at, ROWS)
                grad_key = jnp.zeros((ROWS, LANES), F32)
                grad_val = jnp.zeros((ROWS, LANES), F32)
                for j in range(live):
                    head = t * per_tile + j
                    own = slice(j * head_dim, (j + 1) * head_dim)
                    scores = dot(km[j, rows, :], query_t[...])
                    probs = jnp.exp2(scores * exp_scale - lse_t[head : head + 1, :])
                    grad_val = grad_val + dot(probs.astype(BF16), dm[j])
                    mean_grad = jnp.sum(dot_t[own, :], axis=0, keepdims=True)
                    grad_prob = dot(vm[j, rows, :], do_t[...])
                    grad_scores = (probs * (grad_prob - mean_grad)).astype(BF16)
                    grad_key = grad_key + dot(grad_scores, qm[j])
                    dq_t[own, :] += dot(key_t[own, rows], grad_scores)
                out_ref[rows, wide + t * LANES : wide + (t + 1) * LANES] = (
                    grad_key * scale
                ).astype(BF16)
                out_ref[rows, 2 * wide + t * LANES : 2 * wide + (t + 1) * LANES] = grad_val.astype(
                    BF16
                )

            out_ref[:, cols] = (dq_t[...].T * scale).astype(BF16)

    masked = pltpu.VMEM((per_tile, total, LANES), BF16)
    turned = pltpu.VMEM((LANES, total), BF16)
    turned_f = pltpu.VMEM((LANES, total), F32)
    return pl.pallas_call(
        body,
        out_shape=sds((total, 3 * wide), BF16),
        scratch_shapes=[masked] * 4 + [turned] * 3 + [turned_f] * 3,
        compiler_params=params_of(48),
        cost_estimate=cost(
            2 * heads * total * total * 256 * 5, 8 * 1024 * 1024, heads * total * total
        ),
        name="attend_backward",
    )(qkv, grad_att, att, logs)


def project_back(x_pieces, gain, shift, weight, grad_qkv, quads):
    pieces = len(x_pieces)
    piece_rows, width = x_pieces[0].shape
    total = pieces * piece_rows
    cols_all = weight.shape[1]
    chunk = width // (quads * pieces)

    def body(*refs):
        x_refs, refs = refs[:pieces], refs[pieces:]
        gain_ref, shift_ref, w_ref, dq_ref, own_ref = refs[:5]
        refs = refs[5:]
        send_refs, refs = refs[: pieces - 1], refs[pieces - 1 :]
        dw_ref, sums_ref, bias_ref, low_t = refs
        sums_ref[...] = jnp.zeros_like(sums_ref)
        bias_ref[...] = jnp.zeros_like(bias_ref)
        for h in range(pieces):

            @pl.loop(0, piece_rows // ROWS)
            def _(i, h=h):
                at = pl.multiple_of(i * ROWS, ROWS)
                src = pl.ds(at, ROWS)
                rows = pl.ds(h * piece_rows + at, ROWS)
                normed, _ = norm_rows(x_refs[h][src, :].astype(F32))
                low_t[:, rows] = (normed * gain_ref[...] + shift_ref[...]).T.astype(BF16)
                grad_rows = dq_ref[rows, :]
                grad = dot_nt(grad_rows, w_ref[...])
                if h == 0:
                    own_ref[src, :] = grad
                else:
                    send_refs[h - 1][src, :] = grad.astype(BF16)
                sums_ref[0:1, :] += jnp.sum(grad * normed, axis=0, keepdims=True)
                sums_ref[1:2, :] += jnp.sum(grad, axis=0, keepdims=True)
                bias_ref[0:1, :] += jnp.sum(grad_rows.astype(F32), axis=0, keepdims=True)

        for start in range(0, cols_all, 256):
            stop = min(start + 256, cols_all)
            part = dot(low_t[...], dq_ref[:, start:stop]).astype(BF16)
            for q in range(quads):
                for c in range(pieces):
                    at = (q * pieces + c) * chunk
                    dw_ref[c, q, :, start:stop] = part[at : at + chunk, :]

    return pl.pallas_call(
        body,
        out_shape=[sds((piece_rows, width), F32)]
        + [sds((piece_rows, width), BF16)] * (pieces - 1)
        + [
            sds((pieces, quads, chunk, cols_all), BF16),
            sds((8, width), F32),
            sds((8, cols_all), F32),
        ],
        scratch_shapes=[pltpu.VMEM((width, total), BF16)],
        compiler_params=params_of(40),
        cost_estimate=cost(4 * total * width * cols_all, 10 * 1024 * 1024),
        name="project_back",
    )(*x_pieces, gain, shift, weight, grad_qkv)


def finish_rows(x_own, gain, grad_mid, grad_own, received):
    rows, width = x_own.shape
    others = len(received)

    def body(*refs):
        x_ref, gain_ref, gm_ref, own_ref, refs = refs[0], refs[1], refs[2], refs[3], refs[4:]
        out_ref = refs[others]
        normed, inv_std = norm_rows(x_ref[...].astype(F32))
        grad = own_ref[...]
        for n in range(others):
            grad = grad + refs[n][...].astype(F32)
        out_ref[...] = (gm_ref[...] + norm_back(grad * gain_ref[...], normed, inv_std)).astype(BF16)

    tall = pl.BlockSpec((ROWS, width), lambda i: (i, 0))
    return pl.pallas_call(
        body,
        grid=(rows // ROWS,),
        in_specs=[tall, pl.BlockSpec((1, width), lambda i: (0, 0))] + [tall] * (2 + others),
        out_specs=tall,
        out_shape=sds((rows, width), BF16),
        compiler_params=params_of(32),
        cost_estimate=cost(20 * rows * width, 6 * 1024 * 1024),
        name="finish_rows",
    )(x_own, gain, grad_mid, grad_own, *received)


def on_device(
    tokens,
    mask,
    cotangent,
    ln1_gain,
    ln1_bias,
    qkv_weight,
    q_bias,
    v_bias,
    out_weight,
    out_bias,
    ln2_gain,
    ln2_bias,
    up_weight,
    up_bias,
    down_weight,
    down_bias,
):
    seq_size = lax.axis_size("seq")
    batch_size = lax.axis_size("batch")
    micro_count, seq_count, local_len, width = tokens.shape
    sequences = micro_count * seq_count
    group = seq_size // sequences
    units = up_weight.shape[1]
    head_dim = width // HEADS
    heads = HEADS // group
    real = heads * head_dim
    wide = -(-real // LANES) * LANES
    full_len = local_len * seq_size
    block_len = local_len // group
    rows = seq_size * block_len
    own_units = units // group
    part = lax.axis_index("seq") % group
    aligned = (
        seq_size == batch_size * group
        and group == 2
        and (seq_size // group) % group == 0
        and units % (batch_size * group * LANES) == 0
        and own_units % 1280 == 0
        and 1280 % (own_units // batch_size) == 0
    )

    def from_part(item, ahead):
        if ahead % group == 0:
            return item
        pairs = [
            (q * group + (c + ahead) % group, q * group + c)
            for q in range(sequences)
            for c in range(group)
        ]
        return lax.ppermute(item, "seq", pairs)

    def gather_parts(item):
        return [from_part(item, n) for n in range(group)]

    def row_of(item):
        return item.astype(F32)[None, :]

    x_own = lax.all_to_all(
        tokens.reshape(seq_size, block_len, width), "seq", 0, 0, tiled=True
    ).reshape(rows, width)
    x_pieces = gather_parts(x_own)

    count_rows = jnp.repeat(jnp.sum(mask, axis=2).reshape(sequences), group).astype(BF16)
    cot_low = jnp.where(mask[..., None] != 0, cotangent, jnp.zeros_like(cotangent))
    cot_send = jnp.concatenate(
        [
            cot_low.reshape(seq_size, block_len, width),
            jnp.broadcast_to(count_rows[:, None, None], (seq_size, 8, width)),
        ],
        axis=1,
    )
    cot_recv = lax.all_to_all(cot_send, "seq", 0, 0, tiled=True)
    counts = jnp.sum(cot_recv[:, block_len, 0].astype(F32))
    factor = full_len / (4.0 * counts)
    grad_own = (cot_recv[:, :block_len].astype(F32) * factor).astype(BF16).reshape(rows, width)
    grad_pieces = gather_parts(grad_own)

    def own_columns(matrix, blocks):
        split = matrix.reshape(matrix.shape[0], blocks, group, -1)
        return lax.dynamic_index_in_dim(split, part, 2, keepdims=False)

    def padded_heads(matrix):
        taken = own_columns(matrix, 3)
        taken = jnp.pad(taken, ((0, 0), (0, 0), (0, wide - real)))
        return taken.reshape(matrix.shape[0], 3 * wide)

    qkv_w = padded_heads(qkv_weight)
    qkv_b = padded_heads(jnp.concatenate([q_bias, jnp.zeros_like(q_bias), v_bias])[None, :])
    out_split = out_weight.reshape(group, real, width)
    out_w = [
        jnp.pad(
            lax.dynamic_index_in_dim(out_split, (part + n) % group, 0, keepdims=False),
            ((0, wide - real), (0, 0)),
        )
        for n in range(group)
    ]
    up_own = own_columns(up_weight, batch_size).reshape(width, own_units)
    up_b = own_columns(up_bias[None, :], batch_size).reshape(1, own_units)
    down_own = lax.dynamic_index_in_dim(
        down_weight.reshape(batch_size, group, -1, width), part, 1, keepdims=False
    ).reshape(own_units, width)

    qkv, att, logs = attend_forward(
        x_pieces, row_of(ln1_gain), row_of(ln1_bias), qkv_w, qkv_b, heads, head_dim
    )
    att_pieces = gather_parts(att)
    packed = (batch_size, sequences) if aligned else None
    found = feed_forward(
        x_pieces,
        att_pieces,
        grad_pieces,
        out_w,
        row_of(out_bias),
        row_of(ln2_gain),
        row_of(ln2_bias),
        up_own,
        up_b,
        down_own,
        row_of(down_bias),
        packed,
    )
    mid, result_own = found[0], found[1]
    result_send = found[2 : 1 + group]
    grad_second, second_send, up_sums = found[1 + group : 4 + group]
    ff_grads = found[4 + group :]

    second_recv = [from_part(second_send, n) for n in range(1, group)]
    for n in range(1, group):
        result_own = result_own + from_part(result_send[group - n - 1], n).astype(F32)
    result = lax.all_to_all(
        result_own.astype(BF16).reshape(seq_size, block_len, width), "seq", 0, 0, tiled=True
    ).reshape(tokens.shape)

    grad_mid, grad_att, out_grad, sums_mid = mid_back(
        mid, grad_second, second_recv, grad_pieces, row_of(ln2_gain), out_w[0], att
    )
    grad_qkv = attend_backward(qkv, grad_att, att, logs, heads, head_dim)
    found = project_back(
        x_pieces, row_of(ln1_gain), row_of(ln1_bias), qkv_w, grad_qkv, sequences
    )
    first_own, first_send = found[0], found[1:group]
    qkv_grad, sums_first, bias_sums = found[group:]
    first_recv = [from_part(first_send[group - n - 1], n) for n in range(1, group)]
    grad_rows = finish_rows(x_own, row_of(ln1_gain), grad_mid, first_own, first_recv)
    grad_in = lax.all_to_all(
        grad_rows.reshape(seq_size, block_len, width), "seq", 0, 0, tiled=True
    ).reshape(tokens.shape)

    def spread(item, blocks):
        split = item.reshape(blocks, 1, -1)
        empty = jnp.zeros((blocks, group, split.shape[2]), F32)
        return lax.dynamic_update_slice(empty, split, (0, part, 0)).reshape(-1)

    bias_sums = bias_sums[0].reshape(3, wide)[:, :real]
    small = jnp.concatenate(
        [
            sums_first[0],
            sums_first[1],
            spread(bias_sums[0], 1),
            spread(bias_sums[2], 1),
            sums_mid[2],
            sums_mid[0],
            sums_mid[1],
            spread(up_sums[0], batch_size),
            sums_mid[3],
        ]
    )
    columns = [
        [q * group + c for q in range(sequences)] for c in range(group)
    ]

    def add_up(item, axis):
        return jnp.sum(item.astype(F32), axis=axis)

    if aligned:
        chunk = width // seq_size
        unit_block = own_units // batch_size
        over_batch = lax.all_to_all(ff_grads[0], "batch", 0, 0, tiled=True)
        summed = add_up(over_batch, 0).astype(BF16)
        over_seq = lax.all_to_all(
            summed, "seq", 0, 0, axis_index_groups=columns, tiled=True
        )
        final = add_up(over_seq, 0)
        high = width // sequences
        up_rows = final[:high].reshape(group, chunk, unit_block)
        up_keep = lax.dynamic_index_in_dim(up_rows, part, 0, keepdims=False)
        up_send = lax.dynamic_index_in_dim(up_rows, (part + 1) % group, 0, keepdims=False)
        up_recv = from_part(up_send.astype(BF16), 1).astype(F32)
        up_grad = jnp.where(
            part == 0,
            jnp.concatenate([up_keep, up_recv], axis=1),
            jnp.concatenate([up_recv, up_keep], axis=1),
        )
        down_grad = final[high:].T
        keep = lax.dynamic_index_in_dim(qkv_grad, part, 0, keepdims=False)
        send = lax.dynamic_index_in_dim(qkv_grad, (part + 1) % group, 0, keepdims=False)
        recv = from_part(send, 1)

        def head_columns(item):
            return item.reshape(sequences, chunk, 3, wide)[..., :real]

        keep, recv = head_columns(keep), head_columns(recv)
        qkv_full = jnp.where(
            part == 0,
            jnp.concatenate([keep, recv], axis=3),
            jnp.concatenate([recv, keep], axis=3),
        ).reshape(sequences, chunk, batch_size, -1)
        out_rows = out_grad[:real].reshape(-1, group, chunk, width)
        out_keep = lax.dynamic_index_in_dim(out_rows, part, 1, keepdims=False)
        out_send = lax.dynamic_index_in_dim(out_rows, (part + 1) % group, 1, keepdims=False)
        out_recv = from_part(out_send, 1)
        out_full = jnp.where(
            part == 0,
            jnp.concatenate([out_keep, out_recv], axis=0),
            jnp.concatenate([out_recv, out_keep], axis=0),
        ).reshape(sequences, chunk, batch_size, -1)
        packed_grads = jnp.concatenate([qkv_full, out_full], axis=3).transpose(2, 0, 1, 3)
        lanes = packed_grads.shape[3]
        packed_grads = packed_grads.reshape(batch_size, sequences * chunk, lanes)

        def halves(item):
            filled = jnp.pad(item, (0, -item.shape[0] % lanes)).reshape(-1, lanes)
            first = filled.astype(BF16)
            return jnp.concatenate([first, (filled - first.astype(F32)).astype(BF16)], axis=0)

        small = small + from_part(small, 1)
        small_rows = halves(small)
        count = small_rows.shape[0]
        packed_grads = jnp.concatenate(
            [packed_grads, jnp.broadcast_to(small_rows[None], (batch_size, count, lanes))], axis=1
        )
        over_batch = lax.all_to_all(packed_grads, "batch", 0, 0, tiled=True)
        summed = add_up(over_batch, 0)
        body_rows = summed[: sequences * chunk].astype(BF16).reshape(sequences, chunk, lanes)
        small_mid = summed[sequences * chunk :]
        small_mid = small_mid[: count // 2] + small_mid[count // 2 :]
        small_rows = halves(small_mid.reshape(-1))
        packed_grads = jnp.concatenate(
            [body_rows, jnp.broadcast_to(small_rows[None], (sequences, count, lanes))], axis=1
        )
        over_seq = lax.all_to_all(packed_grads, "seq", 0, 0, axis_index_groups=columns, tiled=True)
        final = add_up(over_seq, 0)
        qkv_cols = qkv_weight.shape[1] // batch_size
        qkv_final = final[:chunk, :qkv_cols]
        out_final = final[:chunk, qkv_cols:]
        small_mid = final[chunk:]
        small = (small_mid[: count // 2] + small_mid[count // 2 :]).reshape(-1)
    else:

        def scattered(item):
            item = lax.psum_scatter(
                item.astype(BF16), "seq", scatter_dimension=0, tiled=True
            )
            return lax.psum_scatter(item, "batch", scatter_dimension=1, tiled=True).astype(F32)

        def spread_columns(item, blocks):
            split = item.reshape(item.shape[0], blocks, 1, -1)
            empty = jnp.zeros((item.shape[0], blocks, group, split.shape[3]), item.dtype)
            filled = lax.dynamic_update_slice(empty, split, (0, 0, part, 0))
            return filled.reshape(item.shape[0], -1)

        up_grad = scattered(spread_columns(ff_grads[0], batch_size))
        down_grad = scattered(spread_columns(ff_grads[1], batch_size).T)
        rows_full = qkv_grad.transpose(1, 0, 2, 3).reshape(width, 3, wide)[..., :real]
        qkv_final = scattered(spread_columns(rows_full.reshape(width, -1), 3))
        out_final = scattered(spread_columns(out_grad[:real].T, 1).T)
        small = lax.psum(small, ("seq", "batch"))

    edges = [width] * 7 + [units, width]
    pieces, start = [], 0
    for size in edges:
        pieces.append(small[start : start + size])
        start += size
    return (
        result,
        grad_in,
        pieces[0],
        pieces[1],
        qkv_final,
        pieces[2],
        pieces[3],
        out_final,
        pieces[4],
        pieces[5],
        pieces[6],
        up_grad,
        pieces[7],
        down_grad,
        pieces[8],
    )


def solution(mesh):
    rows = P(None, "batch", "seq", None)
    split = P("seq", "batch")
    in_specs = (rows, P(None, "batch", "seq"), rows) + (P(),) * 13
    out_specs = (
        rows,
        rows,
        P(),
        P(),
        split,
        P(),
        P(),
        split,
        P(),
        P(),
        P(),
        split,
        P(),
        split,
        P(),
    )
    return jax.shard_map(
        on_device, mesh=mesh, in_specs=in_specs, out_specs=out_specs, check_vma=False
    )
```

```python
import jax
import jax.numpy as jnp
from jax import lax
from jax.experimental import pallas as pl
from jax.experimental.pallas import tpu as pltpu
from jax.sharding import PartitionSpec as P

HEADS = 20
EPS = 1e-05
LOG2E = 1.4426950408889634
ROWS = 256
F32 = jnp.float32
BF16 = jnp.bfloat16
LANES = 128


def dot(left, right):
    return jnp.dot(left, right, preferred_element_type=F32)


def dot_nt(left, right):
    return lax.dot_general(left, right, (((1,), (1,)), ((), ())), preferred_element_type=F32)


def norm_rows(rows_in):
    mean_val = jnp.mean(rows_in, axis=-1, keepdims=True)
    centered = rows_in - mean_val
    inv_std = lax.rsqrt(jnp.mean(centered * centered, axis=-1, keepdims=True) + EPS)
    return centered * inv_std, inv_std


def norm_back(scaled, normed, inv_std):
    inner = (
        scaled
        - jnp.mean(scaled, axis=-1, keepdims=True)
        - normed * jnp.mean(scaled * normed, axis=-1, keepdims=True)
    )
    return inner * inv_std


def params_of(mib):
    return pltpu.CompilerParams(vmem_limit_bytes=mib * 1024 * 1024)


def cost(flops, moved, trans=0):
    return pl.CostEstimate(flops=flops, bytes_accessed=moved, transcendentals=trans)


def sds(shape, dtype):
    return jax.ShapeDtypeStruct(shape, dtype)


def place(group):
    spot = lax.axis_index("seq")
    return spot, lax.rem(spot, group), lax.div(spot, group)


def deal(item):
    count, rows, width = item.shape

    def body(in_ref, *out_refs):
        spot = lax.axis_index("seq")
        for d in range(count):
            out_refs[d][...] = in_ref[spot ^ d]

    return pl.pallas_call(
        body,
        out_shape=[sds((rows, width), item.dtype)] * count,
        compiler_params=params_of(16),
        cost_estimate=cost(0, 4 * count * rows * width),
        name="deal",
    )(item)


def collect(pieces):
    count = len(pieces)
    rows, width = pieces[0].shape

    def body(*refs):
        spot = lax.axis_index("seq")
        for d in range(count):
            refs[count][spot ^ d] = refs[d][...]

    return pl.pallas_call(
        body,
        out_shape=sds((count, rows, width), pieces[0].dtype),
        compiler_params=params_of(16),
        cost_estimate=cost(0, 4 * count * rows * width),
        name="collect",
    )(*pieces)


def swap(item, axis, size, distance):
    return lax.ppermute(item, axis, [(i, i ^ distance) for i in range(size)])


def trade(pieces):
    size = len(pieces)
    return [pieces[0]] + [swap(pieces[d], "seq", size, d) for d in range(1, size)]


def pick_weights(qkv_weight, qkv_bias, out_weight, group, real, wide):
    width = qkv_weight.shape[0]
    tiles = wide // LANES

    def body(w_ref, b_ref, o_ref, wo_ref, bo_ref, *out_refs):
        _, part, _ = place(group)
        wo_ref[...] = jnp.zeros_like(wo_ref)
        bo_ref[...] = jnp.zeros_like(bo_ref)
        for ref in out_refs:
            ref[...] = jnp.zeros_like(ref)
        for c in range(group):

            @pl.when(part == c)
            def _(c=c):
                for p in range(3):
                    for t in range(tiles):
                        some = min(LANES, real - t * LANES)
                        src = p * width + c * real + t * LANES
                        dst = (3 * t + p) * LANES
                        wo_ref[:, dst : dst + some] = w_ref[:, src : src + some]
                        bo_ref[:, dst : dst + some] = b_ref[:, src : src + some]
                for n in range(group):
                    src = (c + n) % group * real
                    out_refs[n][0:real, :] = o_ref[src : src + real, :]

    return pl.pallas_call(
        body,
        out_shape=[sds((width, 3 * wide), BF16), sds((1, 3 * wide), F32)]
        + [sds((wide, width), BF16)] * group,
        compiler_params=params_of(24),
        cost_estimate=cost(0, 8 * 1024 * 1024),
        name="pick_weights",
    )(qkv_weight, qkv_bias, out_weight)


def attend_forward(x_pieces, gain, shift, weight, bias, heads, head_dim):
    pieces = len(x_pieces)
    piece_rows, width = x_pieces[0].shape
    total = pieces * piece_rows
    wide = weight.shape[1] // 3
    tiles = wide // LANES
    per_tile = LANES // head_dim
    exp_scale = head_dim ** (-0.5) * LOG2E

    def body(*refs):
        x_refs = refs[:pieces]
        gain_ref, shift_ref, w_ref, bias_ref, qkv_ref, att_ref, lse_ref, keys, vals = refs[pieces:]
        for h in range(pieces):

            @pl.loop(0, piece_rows // ROWS)
            def _(i, h=h):
                at = pl.multiple_of(i * ROWS, ROWS)
                normed, _ = norm_rows(x_refs[h][pl.ds(at, ROWS), :].astype(F32))
                low = (normed * gain_ref[...] + shift_ref[...]).astype(BF16)
                out = (dot(low, w_ref[...]) + bias_ref[...]).astype(BF16)
                qkv_ref[pl.ds(h * piece_rows + at, ROWS), :] = out

        lse_ref[...] = jnp.zeros_like(lse_ref)
        lane = lax.broadcasted_iota(jnp.int32, (1, LANES), 1)
        row = lax.broadcasted_iota(jnp.int32, (LANES, 1), 0)
        vals[:, :, LANES:] = jnp.ones((per_tile, total, LANES), BF16)
        for t in range(tiles):
            live = min(per_tile, heads - t * per_tile)
            base = 3 * t * LANES
            key_t = qkv_ref[:, base + LANES : base + 2 * LANES].astype(F32).T
            val_f = qkv_ref[:, base + 2 * LANES : base + 3 * LANES].astype(F32)
            for j in range(live):
                keys[j] = jnp.where(row // head_dim == j, key_t, 0.0).astype(BF16)
                vals[j, :, :LANES] = jnp.where(lane // head_dim == j, val_f, 0.0).astype(BF16)

            @pl.loop(0, total // ROWS)
            def _(i, t=t, live=live, base=base):
                at = pl.multiple_of(i * ROWS, ROWS)
                query = qkv_ref[pl.ds(at, ROWS), base : base + LANES]
                acc = jnp.zeros((ROWS, LANES), F32)
                logs = lse_ref[pl.ds(at, ROWS), :]
                for j in range(live):
                    scores = dot(query, keys[j])
                    row_max = jnp.max(scores, axis=-1, keepdims=True) * exp_scale
                    expd = jnp.exp2(scores * exp_scale - row_max)
                    mixed = dot(expd.astype(BF16), vals[j])
                    den = mixed[:, LANES:]
                    acc = acc + mixed[:, :LANES] / den
                    logs = jnp.where(lane == t * per_tile + j, row_max + jnp.log2(den), logs)
                att_ref[pl.ds(at, ROWS), t * LANES : (t + 1) * LANES] = acc.astype(BF16)
                lse_ref[pl.ds(at, ROWS), :] = logs

    return pl.pallas_call(
        body,
        out_shape=(
            sds((total, 3 * wide), BF16),
            sds((total, wide), BF16),
            sds((total, LANES), F32),
        ),
        scratch_shapes=[
            pltpu.VMEM((per_tile, LANES, total), BF16),
            pltpu.VMEM((per_tile, total, 2 * LANES), BF16),
        ],
        compiler_params=params_of(48),
        cost_estimate=cost(
            2 * total * width * 3 * wide + 2 * heads * total * total * 256 * 2,
            8 * 1024 * 1024,
            heads * total * total,
        ),
        name="attend_forward",
    )(*x_pieces, gain, shift, weight, bias)


def gelu_parts(value):
    size = jnp.abs(value)
    near = 1.0 / (1.0 + (0.3275911 * 0.7071067811865476) * size)
    bell = jnp.exp2(value * value * (-0.5 * LOG2E))
    poly = near * (
        0.5 * 0.254829592
        + near
        * (
            0.5 * -0.284496736
            + near * (0.5 * 1.421413741 + near * (0.5 * -1.453152027 + near * (0.5 * 1.061405429)))
        )
    )
    tail = poly * bell
    area = jnp.where(value < 0.0, tail, 1.0 - tail)
    return value * area, area + value * bell * 0.3989422804014327


def feed_forward(
    x_pieces,
    att_pieces,
    grad_pieces,
    out_w,
    out_b,
    gain,
    shift,
    up,
    up_b,
    down,
    down_b,
    packed,
    units,
):
    pieces = len(x_pieces)
    piece_rows, width = x_pieces[0].shape
    total = pieces * piece_rows
    step = 1280 if units % 1280 == 0 else units
    steps = units // step
    if packed is not None:
        blocks, quads = packed
        unit_block = units // blocks
        high = width // quads
        parts = blocks
    else:
        unit_block = units
        parts = 1
    bias_width = up_b.shape[1]

    def body(*refs):
        x_refs, refs = refs[:pieces], refs[pieces:]
        att_refs, refs = refs[:pieces], refs[pieces:]
        grad_refs, refs = refs[:pieces], refs[pieces:]
        wo_refs, refs = refs[:pieces], refs[pieces:]
        ob_ref, gain_ref, shift_ref, up_hbm, ub_ref, down_hbm, db_ref = refs[:7]
        refs = refs[7:]
        mid_ref, own_ref, refs = refs[0], refs[1], refs[2:]
        send_refs, refs = refs[: pieces - 1], refs[pieces - 1 :]
        gs_ref, gsend_ref, ubg_ref = refs[:3]
        refs = refs[3:]
        if packed is None:
            dwu_ref, dwd_ref, refs = refs[0], refs[1], refs[2:]
        else:
            outs, refs = refs[:4], refs[4:]
            dwu_ref, dwd_ref, out_sem, refs = refs[0], refs[1], refs[2], refs[3:]
        second, second_t, grad, grad_t, act, grad_pre, acc, up_ref, down_ref, bias_ref, in_sem = refs
        spot = lax.axis_index("seq")
        part, quad, mine = lax.rem(spot, pieces), lax.div(spot, pieces), lax.axis_index("batch")
        loads = []
        for b in range(parts):
            src = 0
            if packed is not None:
                src = pl.multiple_of((b * pieces + part) * unit_block, unit_block)
            dst = pl.ds(b * unit_block, unit_block)
            loads.append(
                pltpu.make_async_copy(
                    up_hbm.at[:, pl.ds(src, unit_block)], up_ref.at[:, dst], in_sem.at[2 * b]
                )
            )
            loads.append(
                pltpu.make_async_copy(
                    down_hbm.at[pl.ds(src, unit_block), :], down_ref.at[dst, :], in_sem.at[2 * b + 1]
                )
            )
            bias_ref[0:1, dst] = ub_ref[:, pl.ds(src, unit_block)]
        for load in loads:
            load.start()
        ubg_ref[...] = jnp.zeros_like(ubg_ref)

        for h in range(pieces):

            @pl.loop(0, piece_rows // ROWS)
            def _(i, h=h):
                at = pl.multiple_of(i * ROWS, ROWS)
                dst = pl.ds(h * piece_rows + at, ROWS)
                mid = x_refs[h][pl.ds(at, ROWS), :].astype(F32) + ob_ref[...]
                for n in range(pieces):
                    src = pl.ds(((h - n) % pieces) * piece_rows + at, ROWS)
                    mid = mid + dot(att_refs[n][src, :], wo_refs[n][...])
                mid_ref[dst, :] = mid
                normed, _ = norm_rows(mid)
                low = normed * gain_ref[...] + shift_ref[...]
                second[dst, :] = low.astype(BF16)
                second_t[:, dst] = low.T.astype(BF16)
                grad_rows = grad_refs[h][pl.ds(at, ROWS), :]
                grad[dst, :] = grad_rows
                grad_t[:, dst] = grad_rows.astype(F32).T.astype(BF16)
                acc[dst, :] = mid + db_ref[...] if h == 0 else jnp.zeros((ROWS, width), F32)
                gs_ref[dst, :] = jnp.zeros((ROWS, width), F32)

        for load in loads:
            load.wait()

        @pl.loop(0, steps)
        def _(k):
            here = pl.ds(pl.multiple_of(k * step, step), step)

            @pl.loop(0, total // ROWS)
            def _(i):
                rows = pl.ds(pl.multiple_of(i * ROWS, ROWS), ROWS)
                pre = dot(second[rows, :], up_ref[:, here]) + bias_ref[0:1, here]
                value, slope = gelu_parts(pre)
                low_act = value.astype(BF16)
                act[rows, :] = low_act
                acc[rows, :] += dot(low_act, down_ref[here, :])
                grad_act = dot_nt(grad[rows, :], down_ref[here, :])
                low_grad = (grad_act * slope).astype(BF16)
                grad_pre[rows, :] = low_grad
                ubg_ref[0:1, here] += jnp.sum(low_grad.astype(F32), axis=0, keepdims=True)
                gs_ref[rows, :] += dot_nt(low_grad, up_ref[:, here])

            for i in range(step // 256):
                cols = slice(i * 256, (i + 1) * 256)
                up_grad = dot(second_t[...], grad_pre[:, cols]).astype(BF16)
                down_grad = dot(grad_t[...], act[:, cols]).astype(BF16)
                if packed is None:
                    spread = pl.ds(pl.multiple_of(k * step + i * 256, 256), 256)
                    dwu_ref[:, spread] = up_grad
                    dwd_ref[:, spread] = down_grad
                    continue
                start = i * 256
                while start < (i + 1) * 256:
                    block = start // unit_block
                    stop = min((i + 1) * 256, (block + 1) * unit_block)
                    at = k * (step // unit_block) + block
                    src = slice(start - i * 256, stop - i * 256)
                    dst = slice(start - block * unit_block, stop - block * unit_block)
                    for n in range(quads):
                        dwu_ref[at ^ mine, n ^ quad, :, dst] = up_grad[n * high : (n + 1) * high, src]
                    for n in range(blocks):
                        dwd_ref[n ^ mine, at ^ quad, :, dst] = down_grad[
                            n * high : (n + 1) * high, src
                        ]
                    start = stop

        stores = []
        if packed is not None:
            for n, (source, slot) in enumerate(
                ((dwu_ref, 0), (dwu_ref, 2), (dwu_ref, 1), (dwu_ref, 3))
            ):
                stores.append(
                    pltpu.make_async_copy(source.at[slot], outs[n // 2].at[n % 2], out_sem.at[n])
                )
            for n, (source, slot) in enumerate(
                ((dwd_ref, 0), (dwd_ref, 1), (dwd_ref, 2), (dwd_ref, 3))
            ):
                stores.append(
                    pltpu.make_async_copy(
                        source.at[slot], outs[2 + n // 2].at[n % 2], out_sem.at[4 + n]
                    )
                )
            for store in stores:
                store.start()
        own_ref[...] = acc[0:piece_rows, :]
        for h in range(1, pieces):
            send_refs[h - 1][...] = acc[h * piece_rows : (h + 1) * piece_rows, :].astype(BF16)
        gsend_ref[...] = gs_ref[...].astype(BF16)
        for store in stores:
            store.wait()

    vmem = pl.BlockSpec(memory_space=pltpu.VMEM)
    hbm = pl.BlockSpec(memory_space=pl.ANY)
    extra = []
    if packed is None:
        grads = [sds((width, units), BF16)] * 2
        grad_specs = [vmem] * 2
    else:
        grads = [sds((2, quads, high, unit_block), BF16)] * 4
        grad_specs = [hbm] * 4
        extra = [pltpu.VMEM((blocks, quads, high, unit_block), BF16)] * 2
        extra.append(pltpu.SemaphoreType.DMA((8,)))
    return pl.pallas_call(
        body,
        in_specs=[vmem] * (4 * pieces) + [vmem, vmem, vmem, hbm, vmem, hbm, vmem],
        out_specs=[vmem] * (4 + pieces) + grad_specs,
        out_shape=[sds((total, width), F32), sds((piece_rows, width), F32)]
        + [sds((piece_rows, width), BF16)] * (pieces - 1)
        + [sds((total, width), F32), sds((total, width), BF16), sds((8, units), F32)]
        + grads,
        scratch_shapes=extra
        + [
            pltpu.VMEM((total, width), BF16),
            pltpu.VMEM((width, total), BF16),
            pltpu.VMEM((total, width), BF16),
            pltpu.VMEM((width, total), BF16),
            pltpu.VMEM((total, step), BF16),
            pltpu.VMEM((total, step), BF16),
            pltpu.VMEM((total, width), F32),
            pltpu.VMEM((width, units), BF16),
            pltpu.VMEM((units, width), BF16),
            pltpu.VMEM((8, units), F32),
            pltpu.SemaphoreType.DMA((2 * parts,)),
        ],
        compiler_params=params_of(56),
        cost_estimate=cost(
            12 * total * width * units + 2 * total * width * width, 24 * 1024 * 1024, total * units
        ),
        name="feed_forward",
    )(
        *x_pieces,
        *att_pieces,
        *grad_pieces,
        *out_w,
        out_b,
        gain,
        shift,
        up,
        up_b,
        down,
        down_b,
    )


def mid_back(mid, grad_second, received, grad_pieces, gain, out_w, att, chunk):
    pieces = len(grad_pieces)
    piece_rows, width = grad_pieces[0].shape
    total = pieces * piece_rows
    wide = att.shape[1]

    def body(*refs):
        mid_ref, gs_ref, refs = refs[0], refs[1], refs[2:]
        recv_refs, refs = refs[: pieces - 1], refs[pieces - 1 :]
        go_refs, refs = refs[:pieces], refs[pieces:]
        gain_ref, wo_ref, att_ref, gm_ref, do_ref, sums_ref, refs = *refs[:6], refs[6:]
        dwo_refs, low_ref = refs[:-1], refs[-1]
        sums_ref[...] = jnp.zeros_like(sums_ref)
        for h in range(pieces):

            @pl.loop(0, piece_rows // ROWS)
            def _(i, h=h):
                at = pl.multiple_of(i * ROWS, ROWS)
                rows = pl.ds(h * piece_rows + at, ROWS)
                normed, inv_std = norm_rows(mid_ref[rows, :])
                grad = gs_ref[rows, :]
                for n in range(1, pieces):
                    src = pl.ds(((h - n) % pieces) * piece_rows + at, ROWS)
                    grad = grad + recv_refs[n - 1][src, :].astype(F32)
                go = go_refs[h][pl.ds(at, ROWS), :].astype(F32)
                grad_mid = go + norm_back(grad * gain_ref[...], normed, inv_std)
                low = grad_mid.astype(BF16)
                low_ref[rows, :] = low
                do_ref[rows, :] = dot_nt(low, wo_ref[...]).astype(BF16)
                if h == 0:
                    gm_ref[rows, :] = grad_mid
                    for n, item in enumerate((grad * normed, grad, low.astype(F32), go)):
                        sums_ref[n : n + 1, :] += jnp.sum(item, axis=0, keepdims=True)

        grad_out_w = dot(att_ref[...].astype(F32).T.astype(BF16), low_ref[...]).astype(BF16)
        if chunk == 0:
            dwo_refs[0][...] = grad_out_w
            return
        _, part, _ = place(pieces)
        for c in range(pieces):

            @pl.when(part == c)
            def _(c=c):
                for n in range(dwo_refs[0].shape[0]):
                    for e in range(pieces):
                        at = (n * pieces + (c + e) % pieces) * chunk
                        dwo_refs[e][n] = grad_out_w[at : at + chunk, :]

    if chunk == 0:
        grads = [sds((wide, width), BF16)]
    else:
        grads = [sds((width // (pieces * pieces * chunk), chunk, width), BF16)] * pieces
    return pl.pallas_call(
        body,
        out_shape=[
            sds((piece_rows, width), F32),
            sds((total, wide), BF16),
            sds((8, width), F32),
        ]
        + grads,
        scratch_shapes=[pltpu.VMEM((total, width), BF16)],
        compiler_params=params_of(40),
        cost_estimate=cost(4 * total * width * wide, 14 * 1024 * 1024),
        name="mid_back",
    )(mid, grad_second, *received, *grad_pieces, gain, out_w, att)


def attend_backward(qkv, grad_att, att, logs, tile, heads, head_dim):
    total = qkv.shape[0]
    per_tile = LANES // head_dim
    live = min(per_tile, heads - tile * per_tile)
    scale = head_dim ** (-0.5)
    exp_scale = scale * LOG2E

    def body(
        qkv_ref, do_ref, att_ref, lse_ref, out_ref, km, vm, qm, dm, key_t, query_t, do_t, dq_t, lse_t, dot_t
    ):
        lane = lax.broadcasted_iota(jnp.int32, (1, LANES), 1)
        lse_t[...] = lse_ref[...].T
        query = qkv_ref[:, 0:LANES].astype(F32)
        key = qkv_ref[:, LANES : 2 * LANES].astype(F32)
        val = qkv_ref[:, 2 * LANES : 3 * LANES].astype(F32)
        upstream = do_ref[...].astype(F32)
        dot_t[...] = (upstream * att_ref[...].astype(F32)).T
        query_t[...] = query.T.astype(BF16)
        do_t[...] = upstream.T.astype(BF16)
        key_t[...] = key.T.astype(BF16)
        for j in range(live):
            mine = lane // head_dim == j
            km[j] = jnp.where(mine, key, 0.0).astype(BF16)
            vm[j] = jnp.where(mine, val, 0.0).astype(BF16)
            qm[j] = jnp.where(mine, query, 0.0).astype(BF16)
            dm[j] = jnp.where(mine, upstream, 0.0).astype(BF16)
        dq_t[...] = jnp.zeros_like(dq_t)

        @pl.loop(0, total // ROWS)
        def _(i):
            rows = pl.ds(pl.multiple_of(i * ROWS, ROWS), ROWS)
            grad_key = jnp.zeros((ROWS, LANES), F32)
            grad_val = jnp.zeros((ROWS, LANES), F32)
            for j in range(live):
                head = tile * per_tile + j
                own = slice(j * head_dim, (j + 1) * head_dim)
                scores = dot(km[j, rows, :], query_t[...])
                probs = jnp.exp2(scores * exp_scale - lse_t[head : head + 1, :])
                grad_val = grad_val + dot(probs.astype(BF16), dm[j])
                mean_grad = jnp.sum(dot_t[own, :], axis=0, keepdims=True)
                grad_prob = dot(vm[j, rows, :], do_t[...])
                grad_scores = (probs * (grad_prob - mean_grad)).astype(BF16)
                grad_key = grad_key + dot(grad_scores, qm[j])
                dq_t[own, :] += dot(key_t[own, rows], grad_scores)
            out_ref[rows, LANES : 2 * LANES] = (grad_key * scale).astype(BF16)
            out_ref[rows, 2 * LANES : 3 * LANES] = grad_val.astype(BF16)

        out_ref[:, 0:LANES] = (dq_t[...].T * scale).astype(BF16)

    masked = pltpu.VMEM((live, total, LANES), BF16)
    turned = pltpu.VMEM((LANES, total), BF16)
    turned_f = pltpu.VMEM((LANES, total), F32)
    return pl.pallas_call(
        body,
        grid=(1,),
        in_specs=[
            pl.BlockSpec((total, 3 * LANES), lambda i: (0, tile)),
            pl.BlockSpec((total, LANES), lambda i: (0, tile)),
            pl.BlockSpec((total, LANES), lambda i: (0, tile)),
            pl.BlockSpec((total, LANES), lambda i: (0, 0)),
        ],
        out_specs=pl.BlockSpec((total, 3 * LANES), lambda i: (0, 0)),
        out_shape=sds((total, 3 * LANES), BF16),
        scratch_shapes=[masked] * 4 + [turned] * 3 + [turned_f] * 3,
        compiler_params=params_of(40),
        cost_estimate=cost(
            2 * live * total * total * 256 * 5, 3 * 1024 * 1024, live * total * total
        ),
        name="attend_backward",
    )(qkv, grad_att, att, logs)


def project_back(x_pieces, gain, shift, weight, grad_tiles, quads, packed):
    pieces = len(x_pieces)
    piece_rows, width = x_pieces[0].shape
    total = pieces * piece_rows
    cols_all = weight.shape[1]
    tiles = len(grad_tiles)
    tile_cols = cols_all // tiles
    chunk = width // (quads * pieces)

    def body(*refs):
        x_refs, refs = refs[:pieces], refs[pieces:]
        gain_ref, shift_ref, w_ref, refs = refs[0], refs[1], refs[2], refs[3:]
        dq_refs, refs = refs[:tiles], refs[tiles:]
        own_ref, refs = refs[0], refs[1:]
        send_refs, refs = refs[: pieces - 1], refs[pieces - 1 :]
        sums_ref, bias_ref, refs = refs[0], refs[1], refs[2:]
        dw_refs, low_t, part_ref = refs[:-2], refs[-2], refs[-1]
        _, part, quad = place(pieces)
        sums_ref[...] = jnp.zeros_like(sums_ref)
        bias_ref[...] = jnp.zeros_like(bias_ref)
        for h in range(pieces):

            @pl.loop(0, piece_rows // ROWS)
            def _(i, h=h):
                at = pl.multiple_of(i * ROWS, ROWS)
                src = pl.ds(at, ROWS)
                rows = pl.ds(h * piece_rows + at, ROWS)
                normed, _ = norm_rows(x_refs[h][src, :].astype(F32))
                low_t[:, rows] = (normed * gain_ref[...] + shift_ref[...]).T.astype(BF16)
                grad = jnp.zeros((ROWS, width), F32)
                for t in range(tiles):
                    grad_rows = dq_refs[t][rows, :]
                    cols = slice(t * tile_cols, (t + 1) * tile_cols)
                    grad = grad + dot_nt(grad_rows, w_ref[:, cols])
                    bias_ref[0:1, cols] += jnp.sum(grad_rows.astype(F32), axis=0, keepdims=True)
                if h == 0:
                    own_ref[src, :] = grad
                else:
                    send_refs[h - 1][src, :] = grad.astype(BF16)
                sums_ref[0:1, :] += jnp.sum(grad * normed, axis=0, keepdims=True)
                sums_ref[1:2, :] += jnp.sum(grad, axis=0, keepdims=True)

        for t in range(tiles):
            cols = slice(t * tile_cols, (t + 1) * tile_cols)
            part_ref[...] = dot(low_t[...], dq_refs[t][...]).astype(BF16)
            if not packed:
                dw_refs[0][:, cols] = part_ref[...]
                continue
            for c in range(pieces):

                @pl.when(part == c)
                def _(c=c, cols=cols):
                    for q in range(quads):
                        for e in range(pieces):
                            at = (q * pieces + (c + e) % pieces) * chunk
                            dw_refs[e][q ^ quad, :, cols] = part_ref[at : at + chunk, :]

    if packed:
        grads = [sds((quads, chunk, cols_all), BF16)] * pieces
    else:
        grads = [sds((width, cols_all), BF16)]
    return pl.pallas_call(
        body,
        out_shape=[sds((piece_rows, width), F32)]
        + [sds((piece_rows, width), BF16)] * (pieces - 1)
        + [sds((8, width), F32), sds((8, cols_all), F32)]
        + grads,
        scratch_shapes=[pltpu.VMEM((width, total), BF16), pltpu.VMEM((width, tile_cols), BF16)],
        compiler_params=params_of(40),
        cost_estimate=cost(4 * total * width * cols_all, 10 * 1024 * 1024),
        name="project_back",
    )(*x_pieces, gain, shift, weight, *grad_tiles)


def finish_rows(x_own, gain, grad_mid, grad_own, received, count):
    rows, width = x_own.shape
    others = len(received)
    piece = rows // count
    per_step = ROWS // piece

    def body(*refs):
        x_ref, gain_ref, gm_ref, own_ref, refs = refs[0], refs[1], refs[2], refs[3], refs[4:]
        recv_refs, out_refs = refs[:others], refs[others:]
        for n in range(rows // ROWS):
            at = slice(n * ROWS, (n + 1) * ROWS)
            normed, inv_std = norm_rows(x_ref[at, :].astype(F32))
            grad = own_ref[at, :]
            for ref in recv_refs:
                grad = grad + ref[at, :].astype(F32)
            done = gm_ref[at, :] + norm_back(grad * gain_ref[...], normed, inv_std)
            for e in range(per_step):
                out_refs[n * per_step + e][...] = done[e * piece : (e + 1) * piece, :].astype(BF16)

    return pl.pallas_call(
        body,
        out_shape=[sds((piece, width), BF16)] * count,
        compiler_params=params_of(32),
        cost_estimate=cost(20 * rows * width, 6 * 1024 * 1024),
        name="finish_rows",
    )(x_own, gain, grad_mid, grad_own, *received)


def finish_result(own, received, count):
    rows, width = own.shape
    others = len(received)
    piece = rows // count

    def body(*refs):
        out_refs = refs[1 + others :]
        for n in range(count):
            at = slice(n * piece, (n + 1) * piece)
            total = refs[0][at, :]
            for ref in refs[1 : 1 + others]:
                total = total + ref[at, :].astype(F32)
            out_refs[n][...] = total.astype(BF16)

    return pl.pallas_call(
        body,
        out_shape=[sds((piece, width), BF16)] * count,
        compiler_params=params_of(16),
        cost_estimate=cost(2 * rows * width, 3 * 1024 * 1024),
        name="finish_result",
    )(own, *received)


def pack_attention(qkv_keep, qkv_recv, out_keep, out_recv, real, blocks):
    quads, chunk, cols_all = qkv_keep.shape
    wide = cols_all // 3
    tiles = wide // LANES
    width = out_keep.shape[2]
    qkv_lanes = 6 * real // blocks
    out_lanes = width // blocks
    lanes = qkv_lanes + out_lanes
    halves = quads // 2

    def body(qk_ref, qr_ref, ok_ref, or_ref, *out_refs):
        _, part, quad = place(2)
        mine = lax.axis_index("batch")
        slots = out_refs[4]

        def heads_of(rows, p):
            return [
                rows[:, (3 * t + p) * LANES : (3 * t + p) * LANES + min(LANES, real - t * LANES)]
                for t in range(tiles)
            ]

        for c in range(2):

            @pl.when(part == c)
            def _(c=c):
                for q in range(quads):
                    pair = (qk_ref[q], qr_ref[q])
                    if c == 1:
                        pair = pair[::-1]
                    parts = []
                    for p in range(3):
                        parts += heads_of(pair[0], p) + heads_of(pair[1], p)
                    row = jnp.concatenate(parts, axis=1)
                    for b in range(blocks):
                        slots[b ^ mine, q, :, 0:qkv_lanes] = row[
                            :, b * qkv_lanes : (b + 1) * qkv_lanes
                        ]
                for e, ref in enumerate((ok_ref, or_ref)):
                    for n in range(halves):
                        q = ((c + e) % 2) * halves + n
                        for b in range(blocks):
                            slots[b ^ mine, q ^ quad, :, qkv_lanes:lanes] = ref[
                                n, :, b * out_lanes : (b + 1) * out_lanes
                            ]

        for n, order in enumerate(((0, 2), (1, 3), (0, 1), (2, 3))):
            some = slice(0, halves) if n < 2 else slice(halves, quads)
            for e in range(2):
                out_refs[n][e] = slots[order[e], some]

    return pl.pallas_call(
        body,
        out_shape=[sds((2, halves, chunk, lanes), BF16)] * 4,
        scratch_shapes=[pltpu.VMEM((blocks, quads, chunk, lanes), BF16)],
        compiler_params=params_of(24),
        cost_estimate=cost(0, 4 * 1024 * 1024),
        name="pack_attention",
    )(qkv_keep, qkv_recv, out_keep, out_recv)


def sum_first(keeps, received):
    count = len(keeps)
    shape = keeps[0].shape[1:]

    def body(*refs):
        for n in range(count):
            for e in range(2):
                total = refs[n][e].astype(F32) + refs[count + n][e].astype(F32)
                refs[2 * count + 2 * n + e][...] = total.astype(BF16)

    return pl.pallas_call(
        body,
        out_shape=[sds(shape, BF16)] * (2 * count),
        compiler_params=params_of(32),
        cost_estimate=cost(0, 6 * count * keeps[0].size),
        name="sum_first",
    )(*keeps, *received)


def sum_second(keeps, received, joined):
    first, rows, width = keeps[0].shape
    quads = first if joined else 2 * first

    def body(ka, kb, ra, rb, *out_refs):
        for d in range(quads):
            if joined:
                for e, (keep, recv) in enumerate(((ka, ra), (kb, rb))):
                    total = keep[d].astype(F32) + recv[d].astype(F32)
                    out_refs[d][e] = total.astype(BF16)
            else:
                keep, recv = ((ka, ra), (kb, rb))[d // first]
                total = keep[d % first].astype(F32) + recv[d % first].astype(F32)
                out_refs[d][...] = total.astype(BF16)

    shape = (2, rows, width) if joined else (rows, width)
    return pl.pallas_call(
        body,
        out_shape=[sds(shape, BF16)] * quads,
        compiler_params=params_of(32),
        cost_estimate=cost(0, 12 * keeps[0].size),
        name="sum_second",
    )(*keeps, *received)


def over_batch(keeps, sends, size):
    first = sum_first(
        keeps, [swap(sends[0], "batch", size, 1), swap(sends[1], "batch", size, 2)]
    )
    return [first[0], first[2]], [swap(first[1], "batch", size, 2), swap(first[3], "batch", size, 1)]


def over_quads(pieces, group):
    return [
        piece if d == 0 else swap(piece, "seq", len(pieces) * group, d * group)
        for d, piece in enumerate(pieces)
    ]


def final_units(pieces, chunk):
    _, high, unit_block = pieces[0].shape
    count = len(pieces)

    def body(*refs):
        _, part, _ = place(2)
        keep_ref, send_ref, down_ref = refs[count:]
        up = refs[0][0].astype(F32)
        down = refs[0][1].astype(F32)
        for ref in refs[1:count]:
            up = up + ref[0].astype(F32)
            down = down + ref[1].astype(F32)
        down_ref[...] = down.T
        for c in range(2):

            @pl.when(part == c)
            def _(c=c):
                keep_ref[...] = up[c * chunk : (c + 1) * chunk, :]
                send_ref[...] = up[(1 - c) * chunk : (2 - c) * chunk, :].astype(BF16)

    return pl.pallas_call(
        body,
        out_shape=[
            sds((chunk, unit_block), F32),
            sds((chunk, unit_block), BF16),
            sds((unit_block, high), F32),
        ],
        compiler_params=params_of(24),
        cost_estimate=cost(0, 4 * 1024 * 1024),
        name="final_units",
    )(*pieces)


def final_join(keep, recv):
    chunk, unit_block = keep.shape

    def body(keep_ref, recv_ref, out_ref):
        _, part, _ = place(2)
        for c in range(2):

            @pl.when(part == c)
            def _(c=c):
                out_ref[:, c * unit_block : (c + 1) * unit_block] = keep_ref[...]
                out_ref[:, (1 - c) * unit_block : (2 - c) * unit_block] = recv_ref[...].astype(F32)

    return pl.pallas_call(
        body,
        out_shape=sds((chunk, 2 * unit_block), F32),
        compiler_params=params_of(16),
        cost_estimate=cost(0, 1024 * 1024),
        name="final_join",
    )(keep, recv)


def final_attention(pieces, qkv_lanes):
    chunk, lanes = pieces[0].shape
    count = len(pieces)

    def body(*refs):
        total = refs[0][...].astype(F32)
        for ref in refs[1:count]:
            total = total + ref[...].astype(F32)
        refs[count][...] = total[:, :qkv_lanes]
        refs[count + 1][...] = total[:, qkv_lanes:]

    return pl.pallas_call(
        body,
        out_shape=[sds((chunk, qkv_lanes), F32), sds((chunk, lanes - qkv_lanes), F32)],
        compiler_params=params_of(16),
        cost_estimate=cost(0, 1024 * 1024),
        name="final_attention",
    )(*pieces)


def on_device(
    tokens,
    mask,
    cotangent,
    ln1_gain,
    ln1_bias,
    qkv_weight,
    q_bias,
    v_bias,
    out_weight,
    out_bias,
    ln2_gain,
    ln2_bias,
    up_weight,
    up_bias,
    down_weight,
    down_bias,
):
    seq_size = lax.axis_size("seq")
    batch_size = lax.axis_size("batch")
    micro_count, seq_count, local_len, width = tokens.shape
    sequences = micro_count * seq_count
    group = seq_size // sequences
    units = up_weight.shape[1]
    head_dim = width // HEADS
    heads = HEADS // group
    real = heads * head_dim
    wide = -(-real // LANES) * LANES
    full_len = local_len * seq_size
    block_len = local_len // group
    rows = seq_size * block_len
    own_units = units // group
    part = lax.axis_index("seq") % group
    aligned = (
        seq_size == batch_size * group
        and group == 2
        and batch_size == 4
        and (seq_size // group) % group == 0
        and units % (batch_size * group * LANES) == 0
        and own_units % 1280 == 0
        and 1280 % (own_units // batch_size) == 0
    )

    def from_part(item, ahead):
        if ahead % group == 0:
            return item
        pairs = [
            (q * group + (c + ahead) % group, q * group + c)
            for q in range(sequences)
            for c in range(group)
        ]
        return lax.ppermute(item, "seq", pairs)

    def gather_parts(item):
        return [from_part(item, n) for n in range(group)]

    def row_of(item):
        return item.astype(F32)[None, :]

    def blocks_of(item):
        return item.reshape(seq_size, block_len, width)

    x_own = jnp.concatenate(trade(deal(blocks_of(tokens))), axis=0)
    x_pieces = gather_parts(x_own)

    count_rows = jnp.repeat(jnp.sum(mask, axis=2).reshape(sequences), group).astype(BF16)
    cot_low = jnp.where(mask[..., None] != 0, cotangent, jnp.zeros_like(cotangent))
    cot_send = jnp.concatenate(
        [blocks_of(cot_low), jnp.broadcast_to(count_rows[:, None, None], (seq_size, 16, width))],
        axis=1,
    )
    cot_recv = trade(deal(cot_send))
    counts = sum(item[block_len, 0].astype(F32) for item in cot_recv)
    factor = full_len / (4.0 * counts)
    grad_own = jnp.concatenate([item[:block_len] for item in cot_recv], axis=0)
    grad_own = (grad_own.astype(F32) * factor).astype(BF16)
    grad_pieces = gather_parts(grad_own)

    qkv_w, qkv_b, *out_w = pick_weights(
        qkv_weight,
        jnp.concatenate([q_bias, jnp.zeros_like(q_bias), v_bias])[None, :],
        out_weight,
        group,
        real,
        wide,
    )
    if aligned:
        up_own, up_b, down_own = up_weight, up_bias[None, :], down_weight
    else:

        def own_columns(matrix, blocks):
            split = matrix.reshape(matrix.shape[0], blocks, group, -1)
            return lax.dynamic_index_in_dim(split, part, 2, keepdims=False)

        up_own = own_columns(up_weight, batch_size).reshape(width, own_units)
        up_b = own_columns(up_bias[None, :], batch_size).reshape(1, own_units)
        down_own = lax.dynamic_index_in_dim(
            down_weight.reshape(batch_size, group, -1, width), part, 1, keepdims=False
        ).reshape(own_units, width)

    qkv, att, logs = attend_forward(
        x_pieces, row_of(ln1_gain), row_of(ln1_bias), qkv_w, qkv_b, heads, head_dim
    )
    att_pieces = gather_parts(att)
    found = feed_forward(
        x_pieces,
        att_pieces,
        grad_pieces,
        out_w,
        row_of(out_bias),
        row_of(ln2_gain),
        row_of(ln2_bias),
        up_own,
        up_b,
        down_own,
        row_of(down_bias),
        (batch_size, sequences) if aligned else None,
        own_units,
    )
    mid, result_own = found[0], found[1]
    result_send = found[2 : 1 + group]
    grad_second, second_send, up_sums = found[1 + group : 4 + group]
    ff_grads = found[4 + group :]

    second_recv = [from_part(second_send, n) for n in range(1, group)]
    result_recv = [from_part(result_send[group - n - 1], n) for n in range(1, group)]
    result = collect(trade(finish_result(result_own, result_recv, seq_size))).reshape(tokens.shape)

    chunk = width // seq_size
    grad_mid, grad_att, sums_mid, *out_grad = mid_back(
        mid,
        grad_second,
        second_recv,
        grad_pieces,
        row_of(ln2_gain),
        out_w[0],
        att,
        chunk if aligned else 0,
    )
    grad_tiles = [
        attend_backward(qkv, grad_att, att, logs, t, heads, head_dim) for t in range(wide // LANES)
    ]
    found = project_back(
        x_pieces, row_of(ln1_gain), row_of(ln1_bias), qkv_w, grad_tiles, sequences, aligned
    )
    first_own, first_send = found[0], found[1:group]
    sums_first, bias_sums, *qkv_grad = found[group:]
    first_recv = [from_part(first_send[group - n - 1], n) for n in range(1, group)]
    grad_in = collect(
        trade(finish_rows(x_own, row_of(ln1_gain), grad_mid, first_own, first_recv, seq_size))
    ).reshape(tokens.shape)

    def spread(item, blocks):
        split = item.reshape(blocks, 1, -1)
        empty = jnp.zeros((blocks, group, split.shape[2]), F32)
        return lax.dynamic_update_slice(empty, split, (0, part, 0)).reshape(-1)

    bias_sums = bias_sums[0].reshape(wide // LANES, 3, LANES).transpose(1, 0, 2)
    bias_sums = bias_sums.reshape(3, wide)[:, :real]
    small = jnp.concatenate(
        [
            sums_first[0],
            sums_first[1],
            spread(bias_sums[0], 1),
            spread(bias_sums[2], 1),
            sums_mid[2],
            sums_mid[0],
            sums_mid[1],
            spread(up_sums[0], batch_size),
            sums_mid[3],
        ]
    )

    if aligned:
        keeps, received = over_batch(
            [ff_grads[0], ff_grads[2]], [ff_grads[1], ff_grads[3]], batch_size
        )
        up_keep, up_send, down_grad = final_units(
            over_quads(sum_second(keeps, received, True), group), chunk
        )
        up_grad = final_join(up_keep, from_part(up_send, 1))
        packed = pack_attention(
            qkv_grad[0],
            from_part(qkv_grad[1], 1),
            out_grad[0],
            from_part(out_grad[1], 1),
            real,
            batch_size,
        )
        keeps, received = over_batch([packed[0], packed[2]], [packed[1], packed[3]], batch_size)
        qkv_final, out_final = final_attention(
            over_quads(sum_second(keeps, received, False), group),
            qkv_weight.shape[1] // batch_size,
        )
        for axis, size in (("seq", seq_size), ("batch", batch_size)):
            distance = 1
            while distance < size:
                small = small + swap(small, axis, size, distance)
                distance *= 2
    else:

        def scattered(item):
            item = lax.psum_scatter(item.astype(BF16), "seq", scatter_dimension=0, tiled=True)
            return lax.psum_scatter(item, "batch", scatter_dimension=1, tiled=True).astype(F32)

        def spread_columns(item, blocks):
            split = item.reshape(item.shape[0], blocks, 1, -1)
            empty = jnp.zeros((item.shape[0], blocks, group, split.shape[3]), item.dtype)
            filled = lax.dynamic_update_slice(empty, split, (0, 0, part, 0))
            return filled.reshape(item.shape[0], -1)

        up_grad = scattered(spread_columns(ff_grads[0], batch_size))
        down_grad = scattered(spread_columns(ff_grads[1], batch_size).T)
        rows_full = qkv_grad[0].reshape(width, wide // LANES, 3, LANES).transpose(0, 2, 1, 3)
        rows_full = rows_full.reshape(width, 3, wide)[..., :real]
        qkv_final = scattered(spread_columns(rows_full.reshape(width, -1), 3))
        out_final = scattered(spread_columns(out_grad[0][:real].T, 1).T)
        small = lax.psum(small, ("seq", "batch"))

    edges = [width] * 7 + [units, width]
    pieces, start = [], 0
    for size in edges:
        pieces.append(small[start : start + size])
        start += size
    return (
        result,
        grad_in,
        pieces[0],
        pieces[1],
        qkv_final,
        pieces[2],
        pieces[3],
        out_final,
        pieces[4],
        pieces[5],
        pieces[6],
        up_grad,
        pieces[7],
        down_grad,
        pieces[8],
    )


def solution(mesh):
    rows = P(None, "batch", "seq", None)
    split = P("seq", "batch")
    in_specs = (rows, P(None, "batch", "seq"), rows) + (P(),) * 13
    out_specs = (
        rows,
        rows,
        P(),
        P(),
        split,
        P(),
        P(),
        split,
        P(),
        P(),
        P(),
        split,
        P(),
        split,
        P(),
    )
    return jax.shard_map(
        on_device, mesh=mesh, in_specs=in_specs, out_specs=out_specs, check_vma=False
    )
```

```python
import jax
import jax.numpy as jnp
from jax import lax
from jax.experimental import pallas as pl
from jax.experimental.pallas import tpu as pltpu
from jax.sharding import PartitionSpec as P

HEADS = 20
EPS = 1e-05
LOG2E = 1.4426950408889634
ROWS = 256
F32 = jnp.float32
BF16 = jnp.bfloat16
LANES = 128


def dot(left, right):
    return jnp.dot(left, right, preferred_element_type=F32)


def dot_nt(left, right):
    return lax.dot_general(left, right, (((1,), (1,)), ((), ())), preferred_element_type=F32)


def norm_rows(rows_in):
    mean_val = jnp.mean(rows_in, axis=-1, keepdims=True)
    centered = rows_in - mean_val
    inv_std = lax.rsqrt(jnp.mean(centered * centered, axis=-1, keepdims=True) + EPS)
    return centered * inv_std, inv_std


def norm_back(scaled, normed, inv_std):
    inner = (
        scaled
        - jnp.mean(scaled, axis=-1, keepdims=True)
        - normed * jnp.mean(scaled * normed, axis=-1, keepdims=True)
    )
    return inner * inv_std


def params_of(mib):
    return pltpu.CompilerParams(vmem_limit_bytes=mib * 1024 * 1024)


def cost(flops, moved, trans=0):
    return pl.CostEstimate(flops=flops, bytes_accessed=moved, transcendentals=trans)


def sds(shape, dtype):
    return jax.ShapeDtypeStruct(shape, dtype)


VMEM = pl.BlockSpec(memory_space=pltpu.VMEM)
HBM = pl.BlockSpec(memory_space=pl.ANY)


def run(body, operands, after=(), in_specs=None, out_specs=None, vmem=32, **more):
    count, extra = len(operands), len(after)

    def inner(*refs):
        body(*refs[:count], *refs[count + extra :])

    specs = [VMEM] * count if in_specs is None else list(in_specs)
    shapes = more["out_shape"]
    if out_specs is None:
        out_specs = [VMEM] * len(shapes) if isinstance(shapes, (list, tuple)) else VMEM
    return pl.pallas_call(
        inner,
        in_specs=specs + [HBM] * extra,
        out_specs=out_specs,
        compiler_params=params_of(vmem),
        **more,
    )(*operands, *after)


def place(group):
    spot = lax.axis_index("seq")
    return spot, lax.rem(spot, group), lax.div(spot, group)


def deal(item, group, after=()):
    count, rows, width = item.shape

    def body(in_ref, *out_refs):
        _, _, quad = place(group)
        for d in range(count):
            out_refs[d][...] = in_ref[quad ^ d]

    return run(
        body,
        [item],
        after,
        out_shape=[sds((rows, width), item.dtype)] * count,
        vmem=16,
        cost_estimate=cost(0, 4 * count * rows * width),
        name="deal",
    )


def collect(pieces, group):
    count = len(pieces)
    rows, width = pieces[0].shape

    def body(*refs):
        _, _, quad = place(group)
        for d in range(count):
            refs[count][quad ^ d] = refs[d][...]

    return run(
        body,
        pieces,
        out_shape=sds((count, rows, width), pieces[0].dtype),
        vmem=16,
        cost_estimate=cost(0, 4 * count * rows * width),
        name="collect",
    )


def stack(pieces, after):
    count = len(pieces)

    def body(*refs):
        for d in range(count):
            refs[count][d] = refs[d][...]

    return run(
        body,
        pieces,
        after,
        out_shape=sds((count,) + pieces[0].shape, pieces[0].dtype),
        vmem=16,
        cost_estimate=cost(0, 4 * count * pieces[0].size),
        name="stack",
    )


def swap(item, axis, size, distance):
    return lax.ppermute(item, axis, [(i, i ^ distance) for i in range(size)])


def over_quads(pieces, group):
    return [
        piece if d == 0 else swap(piece, "seq", len(pieces) * group, d * group)
        for d, piece in enumerate(pieces)
    ]


def pick_weights(qkv_weight, qkv_bias, out_weight, group, real, wide):
    width = qkv_weight.shape[0]
    tiles = wide // LANES

    def body(w_ref, b_ref, o_ref, wo_ref, bo_ref, *out_refs):
        _, part, _ = place(group)
        wo_ref[...] = jnp.zeros_like(wo_ref)
        bo_ref[...] = jnp.zeros_like(bo_ref)
        for ref in out_refs:
            ref[...] = jnp.zeros_like(ref)
        for c in range(group):

            @pl.when(part == c)
            def _(c=c):
                for p in range(3):
                    for t in range(tiles):
                        some = min(LANES, real - t * LANES)
                        src = p * width + c * real + t * LANES
                        dst = (3 * t + p) * LANES
                        wo_ref[:, dst : dst + some] = w_ref[:, src : src + some]
                        bo_ref[:, dst : dst + some] = b_ref[:, src : src + some]
                for n in range(group):
                    src = (c + n) % group * real
                    out_refs[n][0:real, :] = o_ref[src : src + real, :]

    return pl.pallas_call(
        body,
        out_shape=[sds((width, 3 * wide), BF16), sds((1, 3 * wide), F32)]
        + [sds((wide, width), BF16)] * group,
        compiler_params=params_of(24),
        cost_estimate=cost(0, 8 * 1024 * 1024),
        name="pick_weights",
    )(qkv_weight, qkv_bias, out_weight)


def attend_tiles(query_at, keys_at, vals_at, att_ref, lse_ref, keys, vals, tiles, heads, head_dim):
    per_tile = LANES // head_dim
    total = att_ref.shape[0]
    exp_scale = head_dim ** (-0.5) * LOG2E
    lane = lax.broadcasted_iota(jnp.int32, (1, LANES), 1)
    row = lax.broadcasted_iota(jnp.int32, (LANES, 1), 0)
    lse_ref[...] = jnp.zeros_like(lse_ref)
    vals[:, :, LANES:] = jnp.ones((per_tile, total, LANES), BF16)
    for n, t in enumerate(tiles):
        live = min(per_tile, heads - t * per_tile)
        key_t = keys_at(n).astype(F32).T
        val_f = vals_at(n).astype(F32)
        for j in range(live):
            keys[j] = jnp.where(row // head_dim == j, key_t, 0.0).astype(BF16)
            vals[j, :, :LANES] = jnp.where(lane // head_dim == j, val_f, 0.0).astype(BF16)

        @pl.loop(0, total // ROWS)
        def _(i, n=n, live=live):
            rows = pl.ds(pl.multiple_of(i * ROWS, ROWS), ROWS)
            query = query_at(n, rows)
            acc = jnp.zeros((ROWS, LANES), F32)
            logs = lse_ref[rows, :]
            scores = dot(query, keys[0])
            for j in range(live):
                ahead = dot(query, keys[j + 1]) if j + 1 < live else None
                row_max = jnp.max(scores, axis=-1, keepdims=True) * exp_scale
                expd = jnp.exp2(scores * exp_scale - row_max).astype(BF16)
                mixed = dot(expd, vals[j])
                den = mixed[:, LANES:]
                acc = acc + mixed[:, :LANES] / den
                logs = jnp.where(lane == n * per_tile + j, row_max + jnp.log2(den), logs)
                scores = ahead
            att_ref[rows, n * LANES : (n + 1) * LANES] = acc.astype(BF16)
            lse_ref[rows, :] = logs


def attend_scratch(total, head_dim):
    per_tile = LANES // head_dim
    return [
        pltpu.VMEM((per_tile, LANES, total), BF16),
        pltpu.VMEM((per_tile, total, 2 * LANES), BF16),
    ]


def attend_first(x_pieces, gain, shift, weight, bias, tiles, heads, head_dim):
    count = len(x_pieces)
    piece_rows, width = x_pieces[0].shape
    total = count * piece_rows
    cols_all = weight.shape[1]

    def body(*refs):
        x_refs = refs[:count]
        gain_ref, shift_ref, w_ref, bias_ref = refs[count : count + 4]
        x_ref, qkv_ref, att_ref, lse_ref, keys, vals = refs[count + 4 :]
        for n in range(count):
            x_ref[n * piece_rows : (n + 1) * piece_rows, :] = x_refs[n][...]

        @pl.loop(0, total // ROWS)
        def _(i):
            rows = pl.ds(pl.multiple_of(i * ROWS, ROWS), ROWS)
            normed, _ = norm_rows(x_ref[rows, :].astype(F32))
            low = (normed * gain_ref[...] + shift_ref[...]).astype(BF16)
            qkv_ref[rows, :] = (dot(low, w_ref[...]) + bias_ref[...]).astype(BF16)

        def columns(at):
            return slice(at * LANES, (at + 1) * LANES)

        attend_tiles(
            lambda n, rows: qkv_ref[rows, columns(3 * n)],
            lambda n: qkv_ref[:, columns(3 * n + 1)],
            lambda n: qkv_ref[:, columns(3 * n + 2)],
            att_ref,
            lse_ref,
            keys,
            vals,
            range(tiles),
            heads,
            head_dim,
        )

    return run(
        body,
        [*x_pieces, gain, shift, weight, bias],
        out_shape=[
            sds((total, width), BF16),
            sds((total, cols_all), BF16),
            sds((total, tiles * LANES), BF16),
            sds((total, LANES), F32),
        ],
        scratch_shapes=attend_scratch(total, head_dim),
        vmem=40,
        cost_estimate=cost(
            2 * total * width * cols_all + 4 * heads * total * total * 256,
            8 * 1024 * 1024,
            heads * total * total,
        ),
        name="attend_first",
    )


def attend_last(qkv, tile, heads, head_dim, after):
    total = qkv.shape[0]

    def body(qkv_ref, att_ref, lse_ref, keys, vals):
        attend_tiles(
            lambda n, rows: qkv_ref[rows, 0:LANES],
            lambda n: qkv_ref[:, LANES : 2 * LANES],
            lambda n: qkv_ref[:, 2 * LANES : 3 * LANES],
            att_ref,
            lse_ref,
            keys,
            vals,
            [tile],
            heads,
            head_dim,
        )

    live = heads - tile * (LANES // head_dim)
    return run(
        body,
        [qkv],
        after,
        grid=(1,),
        in_specs=[pl.BlockSpec((total, 3 * LANES), lambda i: (0, tile))],
        out_specs=[pl.BlockSpec((total, LANES), lambda i: (0, 0))] * 2,
        out_shape=[sds((total, LANES), BF16), sds((total, LANES), F32)],
        scratch_shapes=attend_scratch(total, head_dim),
        vmem=24,
        cost_estimate=cost(4 * live * total * total * 256, 2 * 1024 * 1024, live * total * total),
        name="attend_last",
    )


def gelu_parts(value):
    size = jnp.abs(value)
    near = pl.reciprocal(1.0 + (0.3275911 * 0.7071067811865476) * size, approx=True)
    bell = jnp.exp2(value * value * (-0.5 * LOG2E))
    poly = near * (
        0.5 * 0.254829592
        + near
        * (
            0.5 * -0.284496736
            + near * (0.5 * 1.421413741 + near * (0.5 * -1.453152027 + near * (0.5 * 1.061405429)))
        )
    )
    tail = poly * bell
    area = jnp.where(value < 0.0, tail, 1.0 - tail)
    return value * area, area + value * bell * 0.3989422804014327


def feed_forward(
    rows_all,
    att_first,
    att_last,
    cot_pieces,
    out_w,
    out_b,
    gain,
    shift,
    up,
    up_b,
    down,
    down_b,
    packed,
    units,
):
    pieces = len(att_first)
    total, width = rows_all.shape
    piece_rows = total // pieces
    count = len(cot_pieces)
    cot_rows = total // count
    split = att_first[0].shape[1]
    step = 1280 if units % 1280 == 0 else units
    steps = units // step
    chunks = total // ROWS
    if packed is not None:
        blocks, quads = packed
        unit_block = units // blocks
        high = width // quads
        half = high // 2
        parts = blocks
    else:
        unit_block = units
        parts = 1

    def body(*refs):
        x_ref, refs = refs[0], refs[1:]
        att_refs, refs = refs[: 2 * pieces], refs[2 * pieces :]
        cot_refs, refs = refs[:count], refs[count:]
        wo_refs, refs = refs[:pieces], refs[pieces:]
        ob_ref, gain_ref, shift_ref, up_hbm, ub_ref, down_hbm, db_ref = refs[:7]
        refs = refs[7:]
        mid_ref, grad, own_ref, refs = refs[0], refs[1], refs[2], refs[3:]
        send_refs, refs = refs[: pieces - 1], refs[pieces - 1 :]
        gs_ref, gsend_ref, ubg_ref = refs[:3]
        refs = refs[3:]
        if packed is None:
            dwu_ref, dwd_ref, refs = refs[0], refs[1], refs[2:]
        else:
            outs, refs = refs[:8], refs[8:]
            dwu_ref, dwd_ref, out_sem, refs = refs[0], refs[1], refs[2], refs[3:]
        second, second_t, grad_t, acts, grad_pres, acc, up_ref, down_ref, bias_ref, in_sem = refs
        spot, part, quad = place(pieces)
        mine = lax.axis_index("batch")
        loads = []
        for b in range(parts):
            src = 0
            if packed is not None:
                src = pl.multiple_of((b * pieces + part) * unit_block, unit_block)
            dst = pl.ds(b * unit_block, unit_block)
            loads.append(
                pltpu.make_async_copy(
                    up_hbm.at[:, pl.ds(src, unit_block)], up_ref.at[:, dst], in_sem.at[2 * b]
                )
            )
            loads.append(
                pltpu.make_async_copy(
                    down_hbm.at[pl.ds(src, unit_block), :], down_ref.at[dst, :], in_sem.at[2 * b + 1]
                )
            )
            bias_ref[0:1, dst] = ub_ref[:, pl.ds(src, unit_block)]
        for load in loads:
            load.start()
        ubg_ref[...] = jnp.zeros_like(ubg_ref)

        masked = jnp.zeros((1, width), F32)
        for ref in cot_refs:
            masked = masked + ref[cot_rows : cot_rows + 1, :].astype(F32)
        factor = total / (4.0 * masked)
        for n in range(count):
            scaled = cot_refs[n][0:cot_rows, :].astype(F32) * factor
            dst = slice(n * cot_rows, (n + 1) * cot_rows)
            grad[dst, :] = scaled.astype(BF16)

        for h in range(pieces):

            @pl.loop(0, piece_rows // ROWS)
            def _(i, h=h):
                at = pl.multiple_of(i * ROWS, ROWS)
                dst = pl.ds(h * piece_rows + at, ROWS)
                mid = x_ref[dst, :].astype(F32) + ob_ref[...]
                for n in range(pieces):
                    src = pl.ds(((h - n) % pieces) * piece_rows + at, ROWS)
                    mid = mid + dot(att_refs[2 * n][src, :], wo_refs[n][0:split, :])
                    mid = mid + dot(att_refs[2 * n + 1][src, :], wo_refs[n][split:, :])
                mid_ref[dst, :] = mid
                normed, _ = norm_rows(mid)
                low = normed * gain_ref[...] + shift_ref[...]
                second[dst, :] = low.astype(BF16)
                second_t[:, dst] = low.T.astype(BF16)
                grad_t[:, dst] = grad[dst, :].astype(F32).T.astype(BF16)
                acc[dst, :] = mid + db_ref[...] if h == 0 else jnp.zeros((ROWS, width), F32)
                gs_ref[dst, :] = jnp.zeros((ROWS, width), F32)

        for load in loads:
            load.wait()

        def enter(k, i):
            rows = slice(i * ROWS, (i + 1) * ROWS)
            here = slice(k * step, (k + 1) * step)
            pre = dot(second[rows, :], up_ref[:, here]) + bias_ref[0:1, here]
            return pre, dot_nt(grad[rows, :], down_ref[here, :])

        def leave(k, i, pre, grad_act):
            rows = slice(i * ROWS, (i + 1) * ROWS)
            here = slice(k * step, (k + 1) * step)
            value, slope = gelu_parts(pre)
            low_act = value.astype(BF16)
            low_grad = (grad_act * slope).astype(BF16)
            acts[k % 2, rows, :] = low_act
            grad_pres[k % 2, rows, :] = low_grad
            ubg_ref[0:1, here] += jnp.sum(low_grad.astype(F32), axis=0, keepdims=True)
            acc[rows, :] += dot(low_act, down_ref[here, :])
            gs_ref[rows, :] += dot_nt(low_grad, up_ref[:, here])

        def weights(k, i):
            cols = slice(i * 256, (i + 1) * 256)
            up_grad = dot(second_t[...], grad_pres[k % 2, :, cols]).astype(BF16)
            down_grad = dot(grad_t[...], acts[k % 2, :, cols]).astype(BF16)
            if packed is None:
                spread = slice(k * step + i * 256, k * step + (i + 1) * 256)
                dwu_ref[:, spread] = up_grad
                dwd_ref[:, spread] = down_grad
                return
            start = i * 256
            while start < (i + 1) * 256:
                block = start // unit_block
                stop = min((i + 1) * 256, (block + 1) * unit_block)
                at = k * (step // unit_block) + block
                src = slice(start - i * 256, stop - i * 256)
                dst = slice(start - block * unit_block, stop - block * unit_block)
                for n in range(quads):
                    dwu_ref[at ^ mine, n ^ quad, :, dst] = up_grad[n * high : (n + 1) * high, src]
                for n in range(blocks):
                    dwd_ref[n ^ mine, at ^ quad, :, dst] = down_grad[n * high : (n + 1) * high, src]
                start = stop

        stages = [(k, i) for k in range(steps) for i in range(chunks)]
        todo = []
        ready = enter(*stages[0])
        for n, (k, i) in enumerate(stages):
            ahead = enter(*stages[n + 1]) if n + 1 < len(stages) else None
            leave(k, i, *ready)
            ready = ahead
            for _ in range(-(-(step // 256) // chunks)):
                if todo:
                    weights(*todo.pop(0))
            if i == chunks - 1:
                for item in todo:
                    weights(*item)
                todo = [(k, j) for j in range(step // 256)]
        for item in todo:
            weights(*item)

        stores = []
        if packed is not None:
            order = ((dwu_ref, (0, 2)), (dwu_ref, (1, 3)), (dwd_ref, (0, 1)), (dwd_ref, (2, 3)))
            for e in range(2):
                some = pl.ds(e * half, half)
                for m, (source, slots) in enumerate(order):
                    for n in range(2):
                        stores.append(
                            pltpu.make_async_copy(
                                source.at[slots[n], :, some, :],
                                outs[4 * e + m].at[n],
                                out_sem.at[8 * e + 2 * m + n],
                            )
                        )
            for store in stores:
                store.start()
        own_ref[...] = acc[0:piece_rows, :]
        for h in range(1, pieces):
            send_refs[h - 1][...] = acc[h * piece_rows : (h + 1) * piece_rows, :].astype(BF16)
        gsend_ref[...] = gs_ref[...].astype(BF16)
        for store in stores:
            store.wait()

    extra = []
    if packed is None:
        grads = [sds((width, units), BF16)] * 2
        grad_specs = [VMEM] * 2
    else:
        grads = [sds((2, quads, half, unit_block), BF16)] * 8
        grad_specs = [HBM] * 8
        extra = [pltpu.VMEM((blocks, quads, high, unit_block), BF16)] * 2
        extra.append(pltpu.SemaphoreType.DMA((16,)))
    att_all = [item for pair in zip(att_first, att_last) for item in pair]
    return run(
        body,
        [
            rows_all,
            *att_all,
            *cot_pieces,
            *out_w,
            out_b,
            gain,
            shift,
            up,
            up_b,
            down,
            down_b,
        ],
        in_specs=[VMEM] * (1 + 3 * pieces + count) + [VMEM, VMEM, VMEM, HBM, VMEM, HBM, VMEM],
        out_specs=[VMEM] * (5 + pieces) + grad_specs,
        out_shape=[
            sds((total, width), F32),
            sds((total, width), BF16),
            sds((piece_rows, width), F32),
        ]
        + [sds((piece_rows, width), BF16)] * (pieces - 1)
        + [sds((total, width), F32), sds((total, width), BF16), sds((8, units), F32)]
        + grads,
        scratch_shapes=extra
        + [
            pltpu.VMEM((total, width), BF16),
            pltpu.VMEM((width, total), BF16),
            pltpu.VMEM((width, total), BF16),
            pltpu.VMEM((2, total, step), BF16),
            pltpu.VMEM((2, total, step), BF16),
            pltpu.VMEM((total, width), F32),
            pltpu.VMEM((width, units), BF16),
            pltpu.VMEM((units, width), BF16),
            pltpu.VMEM((8, units), F32),
            pltpu.SemaphoreType.DMA((2 * parts,)),
        ],
        vmem=54,
        cost_estimate=cost(
            12 * total * width * units + 2 * total * width * width, 24 * 1024 * 1024, total * units
        ),
        name="feed_forward",
    )


def mid_back(mid, grad_second, received, grad_rows, gain, out_w, att_first, att_last, chunk):
    pieces = 1 + len(received)
    total, width = mid.shape
    piece_rows = total // pieces
    split = att_first.shape[1]
    wide = split + att_last.shape[1]

    def body(*refs):
        mid_ref, gs_ref, refs = refs[0], refs[1], refs[2:]
        recv_refs, refs = refs[: pieces - 1], refs[pieces - 1 :]
        go_ref, gain_ref, wo_ref, att_ref, last_ref = refs[:5]
        gm_ref, do_ref, sums_ref, *dwo_refs, low_ref = refs[5:]
        sums_ref[...] = jnp.zeros_like(sums_ref)
        for h in range(pieces):

            @pl.loop(0, piece_rows // ROWS)
            def _(i, h=h):
                at = pl.multiple_of(i * ROWS, ROWS)
                rows = pl.ds(h * piece_rows + at, ROWS)
                normed, inv_std = norm_rows(mid_ref[rows, :])
                grad = gs_ref[rows, :]
                for n in range(1, pieces):
                    src = pl.ds(((h - n) % pieces) * piece_rows + at, ROWS)
                    grad = grad + recv_refs[n - 1][src, :].astype(F32)
                go = go_ref[rows, :].astype(F32)
                grad_mid = go + norm_back(grad * gain_ref[...], normed, inv_std)
                low = grad_mid.astype(BF16)
                low_ref[rows, :] = low
                do_ref[rows, :] = dot_nt(low, wo_ref[...]).astype(BF16)
                if h == 0:
                    gm_ref[rows, :] = grad_mid
                    for n, item in enumerate((grad * normed, grad, low.astype(F32), go)):
                        sums_ref[n : n + 1, :] += jnp.sum(item, axis=0, keepdims=True)

        grad_out_w = jnp.concatenate(
            [
                dot(ref[...].astype(F32).T.astype(BF16), low_ref[...]).astype(BF16)
                for ref in (att_ref, last_ref)
            ],
            axis=0,
        )
        if chunk == 0:
            dwo_refs[0][...] = grad_out_w
            return
        _, part, _ = place(pieces)
        for c in range(pieces):

            @pl.when(part == c)
            def _(c=c):
                for n in range(dwo_refs[0].shape[0]):
                    for e in range(pieces):
                        at = (n * pieces + (c + e) % pieces) * chunk
                        dwo_refs[e][n] = grad_out_w[at : at + chunk, :]

    if chunk == 0:
        grads = [sds((wide, width), BF16)]
    else:
        grads = [sds((width // (pieces * pieces * chunk), chunk, width), BF16)] * pieces
    return run(
        body,
        [mid, grad_second, *received, grad_rows, gain, out_w, att_first, att_last],
        out_shape=[
            sds((piece_rows, width), F32),
            sds((total, wide), BF16),
            sds((8, width), F32),
        ]
        + grads,
        scratch_shapes=[pltpu.VMEM((total, width), BF16)],
        vmem=32,
        cost_estimate=cost(4 * total * width * wide, 14 * 1024 * 1024),
        name="mid_back",
    )


def attend_backward(qkv, grad_att, att, att_tile, logs, lane_first, tile, heads, head_dim, after=()):
    total = qkv.shape[0]
    per_tile = LANES // head_dim
    live = min(per_tile, heads - tile * per_tile)
    scale = head_dim ** (-0.5)
    exp_scale = scale * LOG2E

    def body(
        qkv_ref, do_ref, att_ref, lse_ref, out_ref, km, vm, qm, dm, key_t, query_t, do_t, dq_t, lse_t, mean_t
    ):
        lane = lax.broadcasted_iota(jnp.int32, (1, LANES), 1)
        lse_t[...] = lse_ref[...].T
        query = qkv_ref[:, 0:LANES].astype(F32)
        key = qkv_ref[:, LANES : 2 * LANES].astype(F32)
        val = qkv_ref[:, 2 * LANES : 3 * LANES].astype(F32)
        upstream = do_ref[...].astype(F32)
        both_t = (upstream * att_ref[...].astype(F32)).T
        for j in range(live):
            mean_t[j : j + 1, :] = jnp.sum(
                both_t[j * head_dim : (j + 1) * head_dim, :], axis=0, keepdims=True
            )
        query_t[...] = query.T.astype(BF16)
        do_t[...] = upstream.T.astype(BF16)
        key_t[...] = key.T.astype(BF16)
        for j in range(live):
            mine = lane // head_dim == j
            km[j] = jnp.where(mine, key, 0.0).astype(BF16)
            vm[j] = jnp.where(mine, val, 0.0).astype(BF16)
            qm[j] = jnp.where(mine, query, 0.0).astype(BF16)
            dm[j] = jnp.where(mine, upstream, 0.0).astype(BF16)
        dq_t[...] = jnp.zeros_like(dq_t)

        @pl.loop(0, total // ROWS)
        def _(i):
            rows = pl.ds(pl.multiple_of(i * ROWS, ROWS), ROWS)
            grad_key = jnp.zeros((ROWS, LANES), F32)
            grad_val = jnp.zeros((ROWS, LANES), F32)

            def enter(j):
                return dot(km[j, rows, :], query_t[...]), dot(vm[j, rows, :], do_t[...])

            ready = enter(0)
            for j in range(live):
                ahead = enter(j + 1) if j + 1 < live else None
                scores, grad_prob = ready
                head = lane_first + j
                own = slice(j * head_dim, (j + 1) * head_dim)
                probs = jnp.exp2(scores * exp_scale - lse_t[head : head + 1, :])
                grad_scores = (probs * (grad_prob - mean_t[j : j + 1, :])).astype(BF16)
                grad_val = grad_val + dot(probs.astype(BF16), dm[j])
                grad_key = grad_key + dot(grad_scores, qm[j])
                dq_t[own, :] += dot(key_t[own, rows], grad_scores)
                ready = ahead
            out_ref[rows, LANES : 2 * LANES] = (grad_key * scale).astype(BF16)
            out_ref[rows, 2 * LANES : 3 * LANES] = grad_val.astype(BF16)

        out_ref[:, 0:LANES] = (dq_t[...].T * scale).astype(BF16)

    masked = pltpu.VMEM((live, total, LANES), BF16)
    turned = pltpu.VMEM((LANES, total), BF16)
    turned_f = pltpu.VMEM((LANES, total), F32)
    return run(
        body,
        [qkv, grad_att, att, logs],
        after,
        grid=(1,),
        in_specs=[
            pl.BlockSpec((total, 3 * LANES), lambda i: (0, tile)),
            pl.BlockSpec((total, LANES), lambda i: (0, tile)),
            pl.BlockSpec((total, LANES), lambda i: (0, att_tile)),
            pl.BlockSpec((total, LANES), lambda i: (0, 0)),
        ],
        out_specs=pl.BlockSpec((total, 3 * LANES), lambda i: (0, 0)),
        out_shape=sds((total, 3 * LANES), BF16),
        scratch_shapes=[masked] * 4
        + [turned] * 3
        + [turned_f] * 2
        + [pltpu.VMEM((8, total), F32)],
        vmem=32,
        cost_estimate=cost(
            2 * live * total * total * 256 * 5, 3 * 1024 * 1024, live * total * total
        ),
        name="attend_backward",
    )


def project_back(rows_all, gain, shift, weight, grad_tiles, sums_mid, up_sums, pieces, quads, packed, real, after):
    total, width = rows_all.shape
    piece_rows = total // pieces
    cols_all = weight.shape[1]
    tiles = len(grad_tiles)
    tile_cols = cols_all // tiles
    chunk = width // (quads * pieces)

    def body(*refs):
        x_ref, gain_ref, shift_ref, w_ref, mid_ref, ups_ref, refs = *refs[:6], refs[6:]
        dq_refs, refs = refs[:tiles], refs[tiles:]
        own_ref, refs = refs[0], refs[1:]
        send_refs, refs = refs[: pieces - 1], refs[pieces - 1 :]
        sums_ref, bias_ref, *dw_refs, low_t, part_ref = refs
        _, part, quad = place(pieces)
        sums_ref[...] = jnp.zeros_like(sums_ref)
        bias_ref[...] = jnp.zeros_like(bias_ref)
        for h in range(pieces):

            @pl.loop(0, piece_rows // ROWS)
            def _(i, h=h):
                at = pl.multiple_of(i * ROWS, ROWS)
                src = pl.ds(at, ROWS)
                rows = pl.ds(h * piece_rows + at, ROWS)
                normed, _ = norm_rows(x_ref[rows, :].astype(F32))
                low_t[:, rows] = (normed * gain_ref[...] + shift_ref[...]).T.astype(BF16)
                grad = jnp.zeros((ROWS, width), F32)
                for t in range(tiles):
                    grad_rows = dq_refs[t][rows, :]
                    cols = slice(t * tile_cols, (t + 1) * tile_cols)
                    grad = grad + dot_nt(grad_rows, w_ref[:, cols])
                    bias_ref[0:1, cols] += jnp.sum(grad_rows.astype(F32), axis=0, keepdims=True)
                if h == 0:
                    own_ref[src, :] = grad
                else:
                    send_refs[h - 1][src, :] = grad.astype(BF16)
                sums_ref[0:1, :] += jnp.sum(grad * normed, axis=0, keepdims=True)
                sums_ref[1:2, :] += jnp.sum(grad, axis=0, keepdims=True)

        for t in range(tiles):
            cols = slice(t * tile_cols, (t + 1) * tile_cols)
            part_ref[...] = dot(low_t[...], dq_refs[t][...]).astype(BF16)
            if not packed:
                dw_refs[0][:, cols] = part_ref[...]
                continue
            for c in range(pieces):

                @pl.when(part == c)
                def _(c=c, cols=cols):
                    for q in range(quads):
                        for e in range(pieces):
                            at = (q * pieces + (c + e) % pieces) * chunk
                            dw_refs[e][q ^ quad, :, cols] = part_ref[at : at + chunk, :]

        if not packed:
            return
        for row, src in ((4, 2), (5, 0), (6, 1), (15, 3)):
            sums_ref[row : row + 1, :] = mid_ref[src : src + 1, :]
        for c in range(pieces):

            @pl.when(part == c)
            def _(c=c):
                for row, p in ((2, 0), (3, 2)):
                    mine = jnp.concatenate(
                        [
                            bias_ref[0:1, (3 * t + p) * LANES :][:, : min(LANES, real - t * LANES)]
                            for t in range(tiles)
                        ],
                        axis=1,
                    )
                    sums_ref[row : row + 1, c * real : (c + 1) * real] = mine
                for n in range(quads):
                    row = 7 + n * pieces + c
                    sums_ref[row : row + 1, :] = ups_ref[0:1, n * width : (n + 1) * width]

    if packed:
        grads = [sds((quads, chunk, cols_all), BF16)] * pieces
    else:
        grads = [sds((width, cols_all), BF16)]
    return run(
        body,
        [rows_all, gain, shift, weight, sums_mid, up_sums, *grad_tiles],
        after,
        out_shape=[sds((piece_rows, width), F32)]
        + [sds((piece_rows, width), BF16)] * (pieces - 1)
        + [sds((16, width), F32), sds((8, cols_all), F32)]
        + grads,
        scratch_shapes=[pltpu.VMEM((width, total), BF16), pltpu.VMEM((width, tile_cols), BF16)],
        vmem=32,
        cost_estimate=cost(4 * total * width * cols_all, 10 * 1024 * 1024),
        name="project_back",
    )


def finish_rows(rows_all, gain, grad_mid, grad_own, received, count):
    rows, width = grad_mid.shape
    others = len(received)
    piece = rows // count
    per_step = ROWS // piece

    def body(*refs):
        x_ref, gain_ref, gm_ref, own_ref, refs = refs[0], refs[1], refs[2], refs[3], refs[4:]
        recv_refs, out_refs = refs[:others], refs[others:]
        for n in range(rows // ROWS):
            at = slice(n * ROWS, (n + 1) * ROWS)
            normed, inv_std = norm_rows(x_ref[at, :].astype(F32))
            grad = own_ref[at, :]
            for ref in recv_refs:
                grad = grad + ref[at, :].astype(F32)
            done = gm_ref[at, :] + norm_back(grad * gain_ref[...], normed, inv_std)
            for e in range(per_step):
                out_refs[n * per_step + e][...] = done[e * piece : (e + 1) * piece, :].astype(BF16)

    return run(
        body,
        [rows_all, gain, grad_mid, grad_own, *received],
        out_shape=[sds((piece, width), BF16)] * count,
        vmem=24,
        cost_estimate=cost(20 * rows * width, 6 * 1024 * 1024),
        name="finish_rows",
    )


def finish_result(own, received, count):
    rows, width = own.shape
    others = len(received)
    piece = rows // count

    def body(*refs):
        out_refs = refs[1 + others :]
        for n in range(count):
            at = slice(n * piece, (n + 1) * piece)
            total = refs[0][at, :]
            for ref in refs[1 : 1 + others]:
                total = total + ref[at, :].astype(F32)
            out_refs[n][...] = total.astype(BF16)

    return run(
        body,
        [own, *received],
        out_shape=[sds((piece, width), BF16)] * count,
        vmem=16,
        cost_estimate=cost(2 * rows * width, 3 * 1024 * 1024),
        name="finish_result",
    )


def two_parts(item):
    first = item.astype(BF16)
    return first, (item - first.astype(F32)).astype(BF16)


def pack_attention(qkv_keep, qkv_recv, out_keep, out_recv, small, small_recv, real, blocks):
    quads, chunk, cols_all = qkv_keep.shape
    wide = cols_all // 3
    tiles = wide // LANES
    width = out_keep.shape[2]
    qkv_lanes = 6 * real // blocks
    out_lanes = width // blocks
    lanes = qkv_lanes + out_lanes
    halves = quads // 2
    slot = halves * chunk
    small_rows = small.shape[0]

    def body(qk_ref, qr_ref, ok_ref, or_ref, small_ref, srecv_ref, *out_refs):
        _, part, quad = place(2)
        mine = lax.axis_index("batch")
        slots = out_refs[4]

        def heads_of(rows, p):
            return [
                rows[:, (3 * t + p) * LANES : (3 * t + p) * LANES + min(LANES, real - t * LANES)]
                for t in range(tiles)
            ]

        for c in range(2):

            @pl.when(part == c)
            def _(c=c):
                for q in range(quads):
                    pair = (qk_ref[q], qr_ref[q])
                    if c == 1:
                        pair = pair[::-1]
                    parts = []
                    for p in range(3):
                        parts += heads_of(pair[0], p) + heads_of(pair[1], p)
                    row = jnp.concatenate(parts, axis=1)
                    for b in range(blocks):
                        slots[b ^ mine, q, :, 0:qkv_lanes] = row[
                            :, b * qkv_lanes : (b + 1) * qkv_lanes
                        ]
                for e, ref in enumerate((ok_ref, or_ref)):
                    for n in range(halves):
                        q = ((c + e) % 2) * halves + n
                        for b in range(blocks):
                            slots[b ^ mine, q ^ quad, :, qkv_lanes:lanes] = ref[
                                n, :, b * out_lanes : (b + 1) * out_lanes
                            ]

        for n, order in enumerate(((0, 2), (1, 3), (0, 1), (2, 3))):
            for e in range(2):
                for f in range(halves):
                    at = e * slot + f * chunk
                    src = f if n < 2 else halves + f
                    out_refs[n][at : at + chunk, :] = slots[order[e], src]
        parts = two_parts(small_ref[...] + srecv_ref[...])
        for n in range(2):
            for e in range(2):
                at = 2 * slot + e * small_rows
                out_refs[n][at : at + small_rows, :] = parts[e]

    first = sds((2 * slot + 2 * small_rows, lanes), BF16)
    other = sds((2 * slot, lanes), BF16)
    return run(
        body,
        [qkv_keep, qkv_recv, out_keep, out_recv, small, small_recv],
        out_shape=[first, first, other, other],
        scratch_shapes=[pltpu.VMEM((blocks, quads, chunk, lanes), BF16)],
        vmem=24,
        cost_estimate=cost(0, 4 * 1024 * 1024),
        name="pack_attention",
    )


def sum_first(keeps, received, after=()):
    count = len(keeps)
    shape = keeps[0].shape[1:]

    def body(*refs):
        for n in range(count):
            for e in range(2):
                total = refs[n][e].astype(F32) + refs[count + n][e].astype(F32)
                refs[2 * count + 2 * n + e][...] = total.astype(BF16)

    return run(
        body,
        [*keeps, *received],
        after,
        out_shape=[sds(shape, BF16)] * (2 * count),
        vmem=24,
        cost_estimate=cost(0, 6 * count * keeps[0].size),
        name="sum_first",
    )


def sum_second(keeps, received, after=()):
    quads, rows, width = keeps[0].shape

    def body(ka, kb, ra, rb, *out_refs):
        for d in range(quads):
            for e, (keep, recv) in enumerate(((ka, ra), (kb, rb))):
                total = keep[d].astype(F32) + recv[d].astype(F32)
                out_refs[d][e] = total.astype(BF16)

    return run(
        body,
        [*keeps, *received],
        after,
        out_shape=[sds((2, rows, width), BF16)] * quads,
        vmem=24,
        cost_estimate=cost(0, 12 * keeps[0].size),
        name="sum_second",
    )


def small_sum(refs, rows, count):
    total = None
    for ref in refs:
        for e in range(2):
            item = ref[rows + e * count : rows + (e + 1) * count, :].astype(F32)
            total = item if total is None else total + item
    return total


def sum_first_attention(keeps, received, slot, small_rows):
    lanes = keeps[0].shape[1]

    def body(ka, kb, ra, rb, stay_a, pass_a, stay_b, pass_b):
        parts = two_parts(small_sum((ka, ra), 2 * slot, small_rows))
        for keep, recv, stay, on in ((ka, ra, stay_a, pass_a), (kb, rb, stay_b, pass_b)):
            for e, ref in enumerate((stay, on)):
                at = slice(e * slot, (e + 1) * slot)
                ref[0:slot, :] = (keep[at, :].astype(F32) + recv[at, :].astype(F32)).astype(BF16)
        for ref in (stay_a, pass_a):
            for e in range(2):
                ref[slot + e * small_rows : slot + (e + 1) * small_rows, :] = parts[e]

    first = sds((slot + 2 * small_rows, lanes), BF16)
    other = sds((slot, lanes), BF16)
    return run(
        body,
        [*keeps, *received],
        out_shape=[first, first, other, other],
        vmem=16,
        cost_estimate=cost(0, 3 * 1024 * 1024),
        name="sum_first_attention",
    )


def sum_second_attention(keeps, received, chunk, quads, small_rows):
    lanes = keeps[0].shape[1]
    halves = quads // 2
    slot = halves * chunk

    def body(ka, kb, ra, rb, *out_refs):
        parts = two_parts(small_sum((ka, ra), slot, small_rows))
        for d in range(quads):
            keep, recv = ((ka, ra), (kb, rb))[d // halves]
            at = slice(d % halves * chunk, (d % halves + 1) * chunk)
            total = keep[at, :].astype(F32) + recv[at, :].astype(F32)
            out_refs[d][0:chunk, :] = total.astype(BF16)
            for e in range(2):
                at = chunk + e * small_rows
                out_refs[d][at : at + small_rows, :] = parts[e]

    return run(
        body,
        [*keeps, *received],
        out_shape=[sds((chunk + 2 * small_rows, lanes), BF16)] * quads,
        vmem=16,
        cost_estimate=cost(0, 2 * 1024 * 1024),
        name="sum_second_attention",
    )


def final_attention(pieces, chunk, qkv_lanes, small_rows):
    lanes = pieces[0].shape[1]
    count = len(pieces)

    def body(*refs):
        total = refs[0][0:chunk, :].astype(F32)
        for ref in refs[1:count]:
            total = total + ref[0:chunk, :].astype(F32)
        refs[count][...] = total[:, :qkv_lanes]
        refs[count + 1][...] = total[:, qkv_lanes:]
        refs[count + 2][...] = small_sum(refs[:count], chunk, small_rows)

    return run(
        body,
        pieces,
        out_shape=[
            sds((chunk, qkv_lanes), F32),
            sds((chunk, lanes - qkv_lanes), F32),
            sds((small_rows, lanes), F32),
        ],
        vmem=16,
        cost_estimate=cost(0, 1024 * 1024),
        name="final_attention",
    )


def final_units(first, second):
    _, half, unit_block = first[0].shape
    count = len(first)

    def body(*refs):
        _, part, _ = place(2)
        keep_ref, send_ref, down_ref = refs[2 * count :]
        for h in range(2):
            pieces = refs[h * count : (h + 1) * count]
            up, down = pieces[0][0].astype(F32), pieces[0][1].astype(F32)
            for ref in pieces[1:]:
                up = up + ref[0].astype(F32)
                down = down + ref[1].astype(F32)
            down_ref[:, h * half : (h + 1) * half] = down.T

            @pl.when(part == h)
            def _(up=up):
                keep_ref[...] = up

            @pl.when(part != h)
            def _(up=up):
                send_ref[...] = up.astype(BF16)

    return run(
        body,
        [*first, *second],
        out_shape=[
            sds((half, unit_block), F32),
            sds((half, unit_block), BF16),
            sds((unit_block, 2 * half), F32),
        ],
        vmem=24,
        cost_estimate=cost(0, 4 * 1024 * 1024),
        name="final_units",
    )


def final_join(keep, recv):
    chunk, unit_block = keep.shape

    def body(keep_ref, recv_ref, out_ref):
        _, part, _ = place(2)
        for c in range(2):

            @pl.when(part == c)
            def _(c=c):
                out_ref[:, c * unit_block : (c + 1) * unit_block] = keep_ref[...]
                out_ref[:, (1 - c) * unit_block : (2 - c) * unit_block] = recv_ref[...].astype(F32)

    return run(
        body,
        [keep, recv],
        out_shape=sds((chunk, 2 * unit_block), F32),
        vmem=16,
        cost_estimate=cost(0, 1024 * 1024),
        name="final_join",
    )


def on_device(
    tokens,
    mask,
    cotangent,
    ln1_gain,
    ln1_bias,
    qkv_weight,
    q_bias,
    v_bias,
    out_weight,
    out_bias,
    ln2_gain,
    ln2_bias,
    up_weight,
    up_bias,
    down_weight,
    down_bias,
):
    seq_size = lax.axis_size("seq")
    batch_size = lax.axis_size("batch")
    micro_count, seq_count, local_len, width = tokens.shape
    sequences = micro_count * seq_count
    group = seq_size // sequences
    units = up_weight.shape[1]
    head_dim = width // HEADS
    heads = HEADS // group
    real = heads * head_dim
    wide = -(-real // LANES) * LANES
    full_len = local_len * seq_size
    block_len = local_len // group
    rows = seq_size * block_len
    own_units = units // group
    part = lax.axis_index("seq") % group
    aligned = (
        seq_size == batch_size * group
        and group == 2
        and batch_size == 4
        and wide == 3 * LANES
        and (seq_size // group) % group == 0
        and units % (batch_size * group * LANES) == 0
        and own_units % 1280 == 0
        and 1280 % (own_units // batch_size) == 0
    )

    def from_part(item, ahead):
        if ahead % group == 0:
            return item
        pairs = [
            (q * group + (c + ahead) % group, q * group + c)
            for q in range(sequences)
            for c in range(group)
        ]
        return lax.ppermute(item, "seq", pairs)

    def gather_parts(item):
        return [from_part(item, n) for n in range(group)]

    def row_of(item):
        return item.astype(F32)[None, :]

    def blocks_of(item):
        return item.reshape(sequences, local_len, width)

    x_own = over_quads(deal(blocks_of(tokens), group), group)
    x_pieces = [from_part(item, n) for n in range(group) for item in x_own]

    count_rows = jnp.sum(mask, axis=2).reshape(sequences).astype(BF16)
    cot_low = jnp.where(mask[..., None] != 0, cotangent, jnp.zeros_like(cotangent))
    cot_send = jnp.concatenate(
        [blocks_of(cot_low), jnp.broadcast_to(count_rows[:, None, None], (sequences, 16, width))],
        axis=1,
    )
    cot_own = over_quads(deal(cot_send, group, x_own[1:]), group)

    qkv_w, qkv_b, *out_w = pick_weights(
        qkv_weight,
        jnp.concatenate([q_bias, jnp.zeros_like(q_bias), v_bias])[None, :],
        out_weight,
        group,
        real,
        wide,
    )
    if aligned:
        up_own, up_b, down_own = up_weight, up_bias[None, :], down_weight
    else:

        def own_columns(matrix, blocks):
            split = matrix.reshape(matrix.shape[0], blocks, group, -1)
            return lax.dynamic_index_in_dim(split, part, 2, keepdims=False)

        up_own = own_columns(up_weight, batch_size).reshape(width, own_units)
        up_b = own_columns(up_bias[None, :], batch_size).reshape(1, own_units)
        down_own = lax.dynamic_index_in_dim(
            down_weight.reshape(batch_size, group, -1, width), part, 1, keepdims=False
        ).reshape(own_units, width)

    tiles = wide // LANES
    x_all, qkv, att_first, logs_first = attend_first(
        x_pieces, row_of(ln1_gain), row_of(ln1_bias), qkv_w, qkv_b, tiles - 1, heads, head_dim
    )
    cot_stack = stack(cot_own, [logs_first])
    att_last, logs_last = attend_last(qkv, tiles - 1, heads, head_dim, [cot_stack])
    cot_pieces = cot_own + [
        item[d]
        for item in gather_parts(cot_stack)[1:]
        for d in range(sequences)
    ]
    found = feed_forward(
        x_all,
        gather_parts(att_first),
        gather_parts(att_last),
        cot_pieces,
        out_w,
        row_of(out_bias),
        row_of(ln2_gain),
        row_of(ln2_bias),
        up_own,
        up_b,
        down_own,
        row_of(down_bias),
        (batch_size, sequences) if aligned else None,
        own_units,
    )
    mid, grad_rows, result_own = found[0], found[1], found[2]
    result_send = found[3 : 2 + group]
    grad_second, second_send, up_sums = found[2 + group : 5 + group]
    ff_grads = found[5 + group :]

    second_recv = [from_part(second_send, n) for n in range(1, group)]
    if aligned:
        first_swaps = [
            swap(ff_grads[4 * e + 1 + 2 * m], "batch", batch_size, 1 + m)
            for e in range(2)
            for m in range(2)
        ]
    result_recv = [from_part(result_send[group - n - 1], n) for n in range(1, group)]
    result = collect(
        over_quads(finish_result(result_own, result_recv, sequences), group), group
    ).reshape(tokens.shape)

    chunk = width // seq_size
    grad_mid, grad_att, sums_mid, *out_grad = mid_back(
        mid,
        grad_second,
        second_recv,
        grad_rows,
        row_of(ln2_gain),
        out_w[0],
        att_first,
        att_last,
        chunk if aligned else 0,
    )

    def tile_back(t, after):
        last = t == tiles - 1
        return attend_backward(
            qkv,
            grad_att,
            att_last if last else att_first,
            0 if last else t,
            logs_last if last else logs_first,
            0 if last else t * (LANES // head_dim),
            t,
            heads,
            head_dim,
            after,
        )

    def begin_sum(e, after):
        stay_a, pass_a, stay_b, pass_b = sum_first(
            [ff_grads[4 * e], ff_grads[4 * e + 2]], first_swaps[2 * e : 2 * e + 2], after
        )
        moved = [swap(pass_a, "batch", batch_size, 2), swap(pass_b, "batch", batch_size, 1)]
        return [stay_a, stay_b], moved

    after = []
    grad_tiles = []
    waiting = []
    for t in range(tiles):
        grad_tiles.append(tile_back(t, after))
        after = []
        if aligned and t in (0, 2):
            waiting.append(begin_sum(t // 2, [grad_tiles[-1]]))
            after = waiting[-1][0][:1]
    if aligned:
        summed = sum_second(*waiting[0], after)
        after = summed[:1]
        unit_first = over_quads(summed, group)
    found = project_back(
        x_all,
        row_of(ln1_gain),
        row_of(ln1_bias),
        qkv_w,
        grad_tiles,
        sums_mid,
        up_sums,
        group,
        sequences,
        aligned,
        real,
        after,
    )
    first_own, first_send = found[0], found[1:group]
    small, bias_sums, *qkv_grad = found[group:]
    first_recv = [from_part(first_send[group - n - 1], n) for n in range(1, group)]
    grad_in = collect(
        over_quads(
            finish_rows(x_all, row_of(ln1_gain), grad_mid, first_own, first_recv, sequences), group
        ),
        group,
    ).reshape(tokens.shape)

    if aligned:
        small_rows = small.shape[0]
        packed = pack_attention(
            qkv_grad[0],
            from_part(qkv_grad[1], 1),
            out_grad[0],
            from_part(out_grad[1], 1),
            small,
            from_part(small, 1),
            real,
            batch_size,
        )
        stay_a, pass_a, stay_b, pass_b = sum_first_attention(
            [packed[0], packed[2]],
            [swap(packed[1], "batch", batch_size, 1), swap(packed[3], "batch", batch_size, 2)],
            sequences // 2 * chunk,
            small_rows,
        )
        summed = sum_second_attention(
            [stay_a, stay_b],
            [swap(pass_a, "batch", batch_size, 2), swap(pass_b, "batch", batch_size, 1)],
            chunk,
            sequences,
            small_rows,
        )
        unit_second = over_quads(sum_second(*waiting[1], [packed[0]]), group)
        up_keep, up_send, down_grad = final_units(unit_first, unit_second)
        up_grad = final_join(up_keep, from_part(up_send, 1))
        qkv_final, out_final, small = final_attention(
            over_quads(summed, group), chunk, qkv_weight.shape[1] // batch_size, small_rows
        )
        small = small.reshape(-1)
    else:

        def spread(item, blocks):
            split = item.reshape(blocks, 1, -1)
            empty = jnp.zeros((blocks, group, split.shape[2]), F32)
            return lax.dynamic_update_slice(empty, split, (0, part, 0)).reshape(-1)

        bias_sums = bias_sums[0].reshape(tiles, 3, LANES).transpose(1, 0, 2)
        bias_sums = bias_sums.reshape(3, wide)[:, :real]
        small = jnp.concatenate(
            [
                small[0],
                small[1],
                spread(bias_sums[0], 1),
                spread(bias_sums[2], 1),
                sums_mid[2],
                sums_mid[0],
                sums_mid[1],
                spread(up_sums[0], batch_size),
                sums_mid[3],
            ]
        )

        def scattered(item):
            item = lax.psum_scatter(item.astype(BF16), "seq", scatter_dimension=0, tiled=True)
            return lax.psum_scatter(item, "batch", scatter_dimension=1, tiled=True).astype(F32)

        def spread_columns(item, blocks):
            split = item.reshape(item.shape[0], blocks, 1, -1)
            empty = jnp.zeros((item.shape[0], blocks, group, split.shape[3]), item.dtype)
            filled = lax.dynamic_update_slice(empty, split, (0, 0, part, 0))
            return filled.reshape(item.shape[0], -1)

        up_grad = scattered(spread_columns(ff_grads[0], batch_size))
        down_grad = scattered(spread_columns(ff_grads[1], batch_size).T)
        rows_full = qkv_grad[0].reshape(width, tiles, 3, LANES).transpose(0, 2, 1, 3)
        rows_full = rows_full.reshape(width, 3, wide)[..., :real]
        qkv_final = scattered(spread_columns(rows_full.reshape(width, -1), 3))
        out_final = scattered(spread_columns(out_grad[0][:real].T, 1).T)
        small = lax.psum(small, ("seq", "batch"))

    edges = [width] * 7 + [units, width]
    pieces, start = [], 0
    for size in edges:
        pieces.append(small[start : start + size])
        start += size
    return (
        result,
        grad_in,
        pieces[0],
        pieces[1],
        qkv_final,
        pieces[2],
        pieces[3],
        out_final,
        pieces[4],
        pieces[5],
        pieces[6],
        up_grad,
        pieces[7],
        down_grad,
        pieces[8],
    )


def solution(mesh):
    rows = P(None, "batch", "seq", None)
    split = P("seq", "batch")
    in_specs = (rows, P(None, "batch", "seq"), rows) + (P(),) * 13
    out_specs = (
        rows,
        rows,
        P(),
        P(),
        split,
        P(),
        P(),
        split,
        P(),
        P(),
        P(),
        split,
        P(),
        split,
        P(),
    )
    return jax.shard_map(
        on_device, mesh=mesh, in_specs=in_specs, out_specs=out_specs, check_vma=False
    )
```

```python
import jax
import jax.numpy as jnp
from jax import lax
from jax.experimental import pallas as pl
from jax.experimental.pallas import tpu as pltpu
from jax.sharding import PartitionSpec as P

HEADS = 20
EPS = 1e-05
LOG2E = 1.4426950408889634
ROWS = 256
F32 = jnp.float32
BF16 = jnp.bfloat16
LANES = 128


def dot(left, right):
    return jnp.dot(left, right, preferred_element_type=F32)


def dot_nt(left, right):
    return lax.dot_general(left, right, (((1,), (1,)), ((), ())), preferred_element_type=F32)


def norm_rows(rows_in):
    mean_val = jnp.mean(rows_in, axis=-1, keepdims=True)
    centered = rows_in - mean_val
    inv_std = lax.rsqrt(jnp.mean(centered * centered, axis=-1, keepdims=True) + EPS)
    return centered * inv_std, inv_std


def norm_back(scaled, normed, inv_std):
    inner = (
        scaled
        - jnp.mean(scaled, axis=-1, keepdims=True)
        - normed * jnp.mean(scaled * normed, axis=-1, keepdims=True)
    )
    return inner * inv_std


def params_of(mib):
    return pltpu.CompilerParams(vmem_limit_bytes=mib * 1024 * 1024)


def cost(flops, moved, trans=0):
    return pl.CostEstimate(flops=flops // 64, bytes_accessed=moved // 64, transcendentals=trans // 64)


def sds(shape, dtype):
    return jax.ShapeDtypeStruct(shape, dtype)


VMEM = pl.BlockSpec(memory_space=pltpu.VMEM)
HBM = pl.BlockSpec(memory_space=pl.ANY)


def run(body, operands, after=(), in_specs=None, out_specs=None, vmem=32, **more):
    count, extra = len(operands), len(after)

    def inner(*refs):
        body(*refs[:count], *refs[count + extra :])

    specs = [VMEM] * count if in_specs is None else list(in_specs)
    shapes = more["out_shape"]
    if out_specs is None:
        out_specs = [VMEM] * len(shapes) if isinstance(shapes, (list, tuple)) else VMEM
    return pl.pallas_call(
        inner,
        in_specs=specs + [HBM] * extra,
        out_specs=out_specs,
        compiler_params=params_of(vmem),
        **more,
    )(*operands, *after)


def place(group):
    spot = lax.axis_index("seq")
    return spot, lax.rem(spot, group), lax.div(spot, group)


def deal(item, group, after=()):
    count, rows, width = item.shape

    def body(in_ref, *out_refs):
        _, _, quad = place(group)
        for d in range(count):
            out_refs[d][...] = in_ref[quad ^ d]

    return run(
        body,
        [item],
        after,
        out_shape=[sds((rows, width), item.dtype)] * count,
        vmem=16,
        cost_estimate=cost(0, 4 * count * rows * width),
        name="deal",
    )


def collect(pieces, group, after=()):
    count = len(pieces)
    rows, width = pieces[0].shape

    def body(*refs):
        _, _, quad = place(group)
        for d in range(count):
            refs[count][quad ^ d] = refs[d][...]

    return run(
        body,
        pieces,
        after,
        out_shape=sds((count, rows, width), pieces[0].dtype),
        vmem=16,
        cost_estimate=cost(0, 4 * count * rows * width),
        name="collect",
    )


def stack(pieces, after):
    count = len(pieces)

    def body(*refs):
        for d in range(count):
            refs[count][d] = refs[d][...]

    return run(
        body,
        pieces,
        after,
        out_shape=sds((count,) + pieces[0].shape, pieces[0].dtype),
        vmem=16,
        cost_estimate=cost(0, 4 * count * pieces[0].size),
        name="stack",
    )


def swap(item, axis, size, distance):
    return lax.ppermute(item, axis, [(i, i ^ distance) for i in range(size)])


def over_quads(pieces, group):
    return [
        piece if d == 0 else swap(piece, "seq", len(pieces) * group, d * group)
        for d, piece in enumerate(pieces)
    ]


def pick_weights(qkv_weight, qkv_bias, out_weight, group, real, wide):
    width = qkv_weight.shape[0]
    tiles = wide // LANES

    def body(w_ref, b_ref, o_ref, wo_ref, bo_ref, *out_refs):
        _, part, _ = place(group)
        wo_ref[...] = jnp.zeros_like(wo_ref)
        bo_ref[...] = jnp.zeros_like(bo_ref)
        for ref in out_refs:
            ref[...] = jnp.zeros_like(ref)
        for c in range(group):

            @pl.when(part == c)
            def _(c=c):
                for p in range(3):
                    for t in range(tiles):
                        some = min(LANES, real - t * LANES)
                        src = p * width + c * real + t * LANES
                        dst = (3 * t + p) * LANES
                        wo_ref[:, dst : dst + some] = w_ref[:, src : src + some]
                        bo_ref[:, dst : dst + some] = b_ref[:, src : src + some]
                for n in range(group):
                    src = (c + n) % group * real
                    out_refs[n][0:real, :] = o_ref[src : src + real, :]

    return pl.pallas_call(
        body,
        out_shape=[sds((width, 3 * wide), BF16), sds((1, 3 * wide), F32)]
        + [sds((wide, width), BF16)] * group,
        compiler_params=params_of(24),
        cost_estimate=cost(0, 8 * 1024 * 1024),
        name="pick_weights",
    )(qkv_weight, qkv_bias, out_weight)


def by_pairs(live, visit):
    size = 2 if live % 2 == 0 else 1

    @pl.loop(0, live // size)
    def _(i):
        visit([i * size + e for e in range(size)])


def attend_tiles(query_at, keys_at, vals_at, att_ref, lse_ref, keys, vals, acc, tiles, heads, head_dim):
    per_tile = LANES // head_dim
    total = att_ref.shape[0]
    exp_scale = head_dim ** (-0.5) * LOG2E
    lane = lax.broadcasted_iota(jnp.int32, (1, LANES), 1)
    row = lax.broadcasted_iota(jnp.int32, (LANES, 1), 0)
    lse_ref[...] = jnp.zeros_like(lse_ref)
    vals[:, :, LANES:] = jnp.ones((per_tile, total, LANES), BF16)
    for n, t in enumerate(tiles):
        live = min(per_tile, heads - t * per_tile)
        key_t = keys_at(n).astype(F32).T
        val_f = vals_at(n).astype(F32)
        for j in range(live):
            keys[j] = jnp.where(row // head_dim == j, key_t, 0.0).astype(BF16)
            vals[j, :, :LANES] = jnp.where(lane // head_dim == j, val_f, 0.0).astype(BF16)
        acc[...] = jnp.zeros_like(acc)

        def visit(some, n=n):
            scores = [dot(query_at(n), keys[j]) for j in some]
            for item, j in zip(scores, some):
                row_max = jnp.max(item, axis=-1, keepdims=True) * exp_scale
                expd = jnp.exp2(item * exp_scale - row_max).astype(BF16)
                mixed = dot(expd, vals[j])
                den = mixed[:, LANES:]
                acc[...] += mixed[:, :LANES] / den
                lse_ref[...] = jnp.where(
                    lane == n * per_tile + j, row_max + jnp.log2(den), lse_ref[...]
                )

        by_pairs(live, visit)
        att_ref[:, n * LANES : (n + 1) * LANES] = acc[...].astype(BF16)


def attend_scratch(total, head_dim):
    per_tile = LANES // head_dim
    return [
        pltpu.VMEM((per_tile, LANES, total), BF16),
        pltpu.VMEM((per_tile, total, 2 * LANES), BF16),
        pltpu.VMEM((total, LANES), F32),
    ]


def attend_first(x_pieces, gain, shift, weight, bias, tiles, heads, head_dim):
    count = len(x_pieces)
    piece_rows, width = x_pieces[0].shape
    total = count * piece_rows
    cols_all = weight.shape[1]

    def body(*refs):
        x_refs = refs[:count]
        gain_ref, shift_ref, w_ref, bias_ref = refs[count : count + 4]
        x_ref, qkv_ref, att_ref, lse_ref, keys, vals, acc = refs[count + 4 :]
        for n in range(count):
            x_ref[n * piece_rows : (n + 1) * piece_rows, :] = x_refs[n][...]

        @pl.loop(0, total // ROWS)
        def _(i):
            rows = pl.ds(pl.multiple_of(i * ROWS, ROWS), ROWS)
            normed, _ = norm_rows(x_ref[rows, :].astype(F32))
            low = (normed * gain_ref[...] + shift_ref[...]).astype(BF16)
            qkv_ref[rows, :] = (dot(low, w_ref[...]) + bias_ref[...]).astype(BF16)

        def columns(at):
            return slice(at * LANES, (at + 1) * LANES)

        attend_tiles(
            lambda n: qkv_ref[:, columns(3 * n)],
            lambda n: qkv_ref[:, columns(3 * n + 1)],
            lambda n: qkv_ref[:, columns(3 * n + 2)],
            att_ref,
            lse_ref,
            keys,
            vals,
            acc,
            range(tiles),
            heads,
            head_dim,
        )

    return run(
        body,
        [*x_pieces, gain, shift, weight, bias],
        out_shape=[
            sds((total, width), BF16),
            sds((total, cols_all), BF16),
            sds((total, tiles * LANES), BF16),
            sds((total, LANES), F32),
        ],
        scratch_shapes=attend_scratch(total, head_dim),
        vmem=48,
        cost_estimate=cost(
            2 * total * width * cols_all + 4 * heads * total * total * 256,
            8 * 1024 * 1024,
            heads * total * total,
        ),
        name="attend_first",
    )


def attend_last(qkv, tile, heads, head_dim, after):
    total = qkv.shape[0]

    def body(qkv_ref, att_ref, lse_ref, keys, vals, acc):
        attend_tiles(
            lambda n: qkv_ref[:, 0:LANES],
            lambda n: qkv_ref[:, LANES : 2 * LANES],
            lambda n: qkv_ref[:, 2 * LANES : 3 * LANES],
            att_ref,
            lse_ref,
            keys,
            vals,
            acc,
            [tile],
            heads,
            head_dim,
        )

    live = heads - tile * (LANES // head_dim)
    return run(
        body,
        [qkv],
        after,
        grid=(1,),
        in_specs=[pl.BlockSpec((total, 3 * LANES), lambda i: (0, tile))],
        out_specs=[pl.BlockSpec((total, LANES), lambda i: (0, 0))] * 2,
        out_shape=[sds((total, LANES), BF16), sds((total, LANES), F32)],
        scratch_shapes=attend_scratch(total, head_dim),
        vmem=40,
        cost_estimate=cost(4 * live * total * total * 256, 2 * 1024 * 1024, live * total * total),
        name="attend_last",
    )


def gelu_parts(value):
    size = jnp.abs(value)
    near = pl.reciprocal(1.0 + (0.3275911 * 0.7071067811865476) * size, approx=True)
    bell = jnp.exp2(value * value * (-0.5 * LOG2E))
    poly = near * (
        0.5 * 0.254829592
        + near
        * (
            0.5 * -0.284496736
            + near * (0.5 * 1.421413741 + near * (0.5 * -1.453152027 + near * (0.5 * 1.061405429)))
        )
    )
    tail = poly * bell
    area = jnp.where(value < 0.0, tail, 1.0 - tail)
    return value * area, area + value * bell * 0.3989422804014327


class Units:
    def __init__(self, block, blocks, start, size, stride, quads, high):
        self.block, self.blocks, self.start, self.size = block, blocks, start, size
        self.stride, self.quads, self.high = stride, quads, high
        self.count = blocks * size
        self.chunk = 512 if self.count % 512 == 0 else 256
        self.packed = quads is not None

    def loads(self, part, hbm_up, hbm_down, hbm_bias, up_ref, down_ref, bias_ref, sem):
        copies = []
        for b in range(self.blocks):
            src = self.start
            if self.packed:
                src = pl.multiple_of((b * self.stride + part) * self.block, LANES) + self.start
            src = pl.ds(src, self.size)
            dst = pl.ds(b * self.size, self.size)
            copies.append(
                pltpu.make_async_copy(hbm_up.at[:, src], up_ref.at[:, dst], sem.at[2 * b])
            )
            copies.append(
                pltpu.make_async_copy(hbm_down.at[src, :], down_ref.at[dst, :], sem.at[2 * b + 1])
            )
            bias_ref[0:1, dst] = hbm_bias[:, src]
        return copies

    def grad_shapes(self, width):
        if self.packed:
            return [sds((2, self.quads, self.high, self.size), BF16)] * 4
        return [sds((width, self.count), BF16)] * 2

    def scratch(self, total, width):
        grads = (self.blocks, self.quads, self.high, self.size) if self.packed else (8, LANES)
        return [
            pltpu.VMEM(grads, BF16),
            pltpu.VMEM(grads, BF16),
            pltpu.SemaphoreType.DMA((8,)),
            pltpu.VMEM((width, self.count), BF16),
            pltpu.VMEM((self.count, width), BF16),
            pltpu.VMEM((8, self.count), F32),
            pltpu.SemaphoreType.DMA((2 * self.blocks,)),
        ]

    def compute(self, part, second, second_t, grad, grad_t, acc, gs, ubg, scratch, outs):
        up_slots, down_slots, out_sem, up_ref, down_ref, bias_ref, _ = scratch
        if not self.packed:
            up_slots, down_slots = outs
        quad = lax.div(lax.axis_index("seq"), self.stride)
        mine = lax.axis_index("batch")

        def enter(n):
            here = slice(n * self.chunk, (n + 1) * self.chunk)
            pre = dot(second[...], up_ref[:, here]) + bias_ref[0:1, here]
            return pre, dot_nt(grad[...], down_ref[here, :])

        def weights(n, act, grad_pre):
            up_grad = dot(second_t[...], grad_pre).astype(BF16)
            down_grad = dot(grad_t[...], act).astype(BF16)
            first, last = n * self.chunk, (n + 1) * self.chunk
            if not self.packed:
                up_slots[:, first:last] = up_grad
                down_slots[:, first:last] = down_grad
                return
            at = first
            while at < last:
                block = at // self.size
                stop = min(last, (block + 1) * self.size)
                src = slice(at - first, stop - first)
                dst = slice(at - block * self.size, stop - block * self.size)
                for m in range(self.blocks):
                    rows = slice(m * self.high, (m + 1) * self.high)
                    up_slots[block ^ mine, m ^ quad, :, dst] = up_grad[rows, src]
                    down_slots[m ^ mine, block ^ quad, :, dst] = down_grad[rows, src]
                at = stop

        ready = enter(0)
        chunks = self.count // self.chunk
        for n in range(chunks):
            ahead = enter(n + 1) if n + 1 < chunks else None
            here = slice(n * self.chunk, (n + 1) * self.chunk)
            pre, grad_act = ready
            value, slope = gelu_parts(pre)
            act = value.astype(BF16)
            grad_pre = (grad_act * slope).astype(BF16)
            ubg[0:1, here] = jnp.sum(grad_pre.astype(F32), axis=0, keepdims=True)
            acc[...] += dot(act, down_ref[here, :])
            gs[...] += dot_nt(grad_pre, up_ref[:, here])
            weights(n, act, grad_pre)
            ready = ahead
        stores = []
        if self.packed:
            order = ((up_slots, (0, 2)), (up_slots, (1, 3)), (down_slots, (0, 1)), (down_slots, (2, 3)))
            for m, (source, slots) in enumerate(order):
                for n in range(2):
                    stores.append(
                        pltpu.make_async_copy(
                            source.at[slots[n]], outs[m].at[n], out_sem.at[2 * m + n]
                        )
                    )
        return stores


def feed_first(
    rows_all, att_first, att_last, cot_pieces, out_w, out_b, gain, shift, up, up_b, down, down_b, units
):
    pieces = len(att_first)
    total, width = rows_all.shape
    piece_rows = total // pieces
    count = len(cot_pieces)
    cot_rows = total // count
    split = att_first[0].shape[1]
    grads = units.grad_shapes(width)

    def body(*refs):
        x_ref, refs = refs[0], refs[1:]
        att_refs, refs = refs[: 2 * pieces], refs[2 * pieces :]
        cot_refs, refs = refs[:count], refs[count:]
        wo_refs, refs = refs[:pieces], refs[pieces:]
        ob_ref, gain_ref, shift_ref, up_hbm, ub_ref, down_hbm, db_ref = refs[:7]
        mid_ref, second, second_t, grad, grad_t, acc, gs, ubg = refs[7:15]
        outs, scratch = refs[15 : 15 + len(grads)], refs[15 + len(grads) :]
        _, part, _ = place(pieces)
        loads = units.loads(part, up_hbm, down_hbm, ub_ref, *scratch[3:])
        for load in loads:
            load.start()
        ubg[...] = jnp.zeros_like(ubg)
        masked = jnp.zeros((1, width), F32)
        for ref in cot_refs:
            masked = masked + ref[cot_rows : cot_rows + 1, :].astype(F32)
        factor = total / (4.0 * masked)
        for n in range(count):
            scaled = cot_refs[n][0:cot_rows, :].astype(F32) * factor
            dst = slice(n * cot_rows, (n + 1) * cot_rows)
            grad[dst, :] = scaled.astype(BF16)

        for h in range(pieces):

            @pl.loop(0, piece_rows // ROWS)
            def _(i, h=h):
                at = pl.multiple_of(i * ROWS, ROWS)
                dst = pl.ds(h * piece_rows + at, ROWS)
                mid = x_ref[dst, :].astype(F32) + ob_ref[...]
                for n in range(pieces):
                    src = pl.ds(((h - n) % pieces) * piece_rows + at, ROWS)
                    mid = mid + dot(att_refs[2 * n][src, :], wo_refs[n][0:split, :])
                    mid = mid + dot(att_refs[2 * n + 1][src, :], wo_refs[n][split:, :])
                mid_ref[dst, :] = mid
                normed, _ = norm_rows(mid)
                low = normed * gain_ref[...] + shift_ref[...]
                second[dst, :] = low.astype(BF16)
                second_t[:, dst] = low.T.astype(BF16)
                grad_t[:, dst] = grad[dst, :].astype(F32).T.astype(BF16)
                acc[dst, :] = mid + db_ref[...] if h == 0 else jnp.zeros((ROWS, width), F32)
                gs[dst, :] = jnp.zeros((ROWS, width), F32)

        for load in loads:
            load.wait()
        stores = units.compute(
            part, second, second_t, grad, grad_t, acc, gs, ubg, scratch, outs
        )
        for store in stores:
            store.start()
        for store in stores:
            store.wait()

    att_all = [item for pair in zip(att_first, att_last) for item in pair]
    turned = sds((width, total), BF16)
    flat = sds((total, width), BF16)
    wide = sds((total, width), F32)
    return run(
        body,
        [rows_all, *att_all, *cot_pieces, *out_w, out_b, gain, shift, up, up_b, down, down_b],
        in_specs=[VMEM] * (1 + 3 * pieces + count) + [VMEM, VMEM, VMEM, HBM, VMEM, HBM, VMEM],
        out_specs=[VMEM] * 8 + [HBM if units.packed else VMEM] * len(grads),
        out_shape=[wide, flat, turned, flat, turned, wide, wide, sds((8, units.count), F32)] + grads,
        scratch_shapes=units.scratch(total, width),
        vmem=50,
        cost_estimate=cost(12 * total * width * units.count, 24 * 1024 * 1024, total * units.count),
        name="feed_first",
    )


def feed_second(second, second_t, grad, grad_t, acc_first, gs_first, up, up_b, down, units, pieces, after):
    total, width = second.shape
    piece_rows = total // pieces
    grads = units.grad_shapes(width)

    def body(*refs):
        second, second_t, grad, grad_t, acc_in, gs_in, up_hbm, ub_ref, down_hbm = refs[:9]
        own_ref, gs, gsend_ref, ubg, refs = refs[9], refs[10], refs[11], refs[12], refs[13:]
        send_refs, refs = refs[: pieces - 1], refs[pieces - 1 :]
        outs, acc, scratch = refs[: len(grads)], refs[len(grads)], refs[len(grads) + 1 :]
        _, part, _ = place(pieces)
        loads = units.loads(part, up_hbm, down_hbm, ub_ref, *scratch[3:])
        for load in loads:
            load.start()
        ubg[...] = jnp.zeros_like(ubg)
        acc[...] = acc_in[...]
        gs[...] = gs_in[...]
        for load in loads:
            load.wait()
        stores = units.compute(
            part, second, second_t, grad, grad_t, acc, gs, ubg, scratch, outs
        )
        for store in stores:
            store.start()
        own_ref[...] = acc[0:piece_rows, :]
        for h in range(1, pieces):
            send_refs[h - 1][...] = acc[h * piece_rows : (h + 1) * piece_rows, :].astype(BF16)
        gsend_ref[...] = gs[...].astype(BF16)
        for store in stores:
            store.wait()

    return run(
        body,
        [second, second_t, grad, grad_t, acc_first, gs_first, up, up_b, down],
        after,
        in_specs=[VMEM] * 6 + [HBM, VMEM, HBM],
        out_specs=[VMEM] * (3 + pieces) + [HBM if units.packed else VMEM] * len(grads),
        out_shape=[
            sds((piece_rows, width), F32),
            sds((total, width), F32),
            sds((total, width), BF16),
            sds((8, units.count), F32),
        ]
        + [sds((piece_rows, width), BF16)] * (pieces - 1)
        + grads,
        scratch_shapes=[pltpu.VMEM((total, width), F32)] + units.scratch(total, width),
        vmem=50,
        cost_estimate=cost(12 * total * width * units.count, 24 * 1024 * 1024, total * units.count),
        name="feed_second",
    )


def mid_back(mid, grad_second, received, grad_rows, gain, out_w, att_first, att_last, chunk):
    pieces = 1 + len(received)
    total, width = mid.shape
    piece_rows = total // pieces
    split = att_first.shape[1]
    wide = split + att_last.shape[1]

    def body(*refs):
        mid_ref, gs_ref, refs = refs[0], refs[1], refs[2:]
        recv_refs, refs = refs[: pieces - 1], refs[pieces - 1 :]
        go_ref, gain_ref, wo_ref, att_ref, last_ref = refs[:5]
        gm_ref, do_ref, sums_ref, *dwo_refs, low_ref = refs[5:]
        sums_ref[...] = jnp.zeros_like(sums_ref)
        for h in range(pieces):

            @pl.loop(0, piece_rows // ROWS)
            def _(i, h=h):
                at = pl.multiple_of(i * ROWS, ROWS)
                rows = pl.ds(h * piece_rows + at, ROWS)
                normed, inv_std = norm_rows(mid_ref[rows, :])
                grad = gs_ref[rows, :]
                for n in range(1, pieces):
                    src = pl.ds(((h - n) % pieces) * piece_rows + at, ROWS)
                    grad = grad + recv_refs[n - 1][src, :].astype(F32)
                go = go_ref[rows, :].astype(F32)
                grad_mid = go + norm_back(grad * gain_ref[...], normed, inv_std)
                low = grad_mid.astype(BF16)
                low_ref[rows, :] = low
                do_ref[rows, :] = dot_nt(low, wo_ref[...]).astype(BF16)
                if h == 0:
                    gm_ref[rows, :] = grad_mid
                    for n, item in enumerate((grad * normed, grad, low.astype(F32), go)):
                        sums_ref[n : n + 1, :] += jnp.sum(item, axis=0, keepdims=True)

        grad_out_w = jnp.concatenate(
            [
                dot(ref[...].astype(F32).T.astype(BF16), low_ref[...]).astype(BF16)
                for ref in (att_ref, last_ref)
            ],
            axis=0,
        )
        if chunk == 0:
            dwo_refs[0][...] = grad_out_w
            return
        _, part, _ = place(pieces)
        for c in range(pieces):

            @pl.when(part == c)
            def _(c=c):
                for n in range(dwo_refs[0].shape[0]):
                    for e in range(pieces):
                        at = (n * pieces + (c + e) % pieces) * chunk
                        dwo_refs[e][n] = grad_out_w[at : at + chunk, :]

    if chunk == 0:
        grads = [sds((wide, width), BF16)]
    else:
        grads = [sds((width // (pieces * pieces * chunk), chunk, width), BF16)] * pieces
    return run(
        body,
        [mid, grad_second, *received, grad_rows, gain, out_w, att_first, att_last],
        out_shape=[
            sds((piece_rows, width), F32),
            sds((total, wide), BF16),
            sds((8, width), F32),
        ]
        + grads,
        scratch_shapes=[pltpu.VMEM((total, width), BF16)],
        vmem=32,
        cost_estimate=cost(4 * total * width * wide, 14 * 1024 * 1024),
        name="mid_back",
    )


def attend_backward(qkv, grad_att, att, att_tile, logs, lane_first, tile, heads, head_dim, after=()):
    total = qkv.shape[0]
    per_tile = LANES // head_dim
    live = min(per_tile, heads - tile * per_tile)
    scale = head_dim ** (-0.5)
    exp_scale = scale * LOG2E

    def body(qkv_ref, do_ref, att_ref, lse_ref, out_ref, *scratch):
        km, vm, qm, dm, key_t, query_t, do_t, dq_t, lse_t, mean_t, grad_key, grad_val = scratch
        lane = lax.broadcasted_iota(jnp.int32, (1, LANES), 1)
        lse_t[...] = lse_ref[...].T
        query = qkv_ref[:, 0:LANES].astype(F32)
        key = qkv_ref[:, LANES : 2 * LANES].astype(F32)
        val = qkv_ref[:, 2 * LANES : 3 * LANES].astype(F32)
        upstream = do_ref[...].astype(F32)
        both_t = (upstream * att_ref[...].astype(F32)).T
        for j in range(live):
            mean_t[j : j + 1, :] = jnp.sum(
                both_t[j * head_dim : (j + 1) * head_dim, :], axis=0, keepdims=True
            )
        query_t[...] = query.T.astype(BF16)
        do_t[...] = upstream.T.astype(BF16)
        key_t[...] = key.T.astype(BF16)
        for j in range(live):
            mine = lane // head_dim == j
            km[j] = jnp.where(mine, key, 0.0).astype(BF16)
            vm[j] = jnp.where(mine, val, 0.0).astype(BF16)
            qm[j] = jnp.where(mine, query, 0.0).astype(BF16)
            dm[j] = jnp.where(mine, upstream, 0.0).astype(BF16)
        grad_key[...] = jnp.zeros_like(grad_key)
        grad_val[...] = jnp.zeros_like(grad_val)
        if live * head_dim < LANES:
            dq_t[...] = jnp.zeros_like(dq_t)

        def visit(some):
            ready = [(dot(km[j], query_t[...]), dot(vm[j], do_t[...])) for j in some]
            for (scores, grad_prob), j in zip(ready, some):
                own = pl.ds(pl.multiple_of(j * head_dim, head_dim), head_dim)
                probs = jnp.exp2(scores * exp_scale - lse_t[pl.ds(lane_first + j, 1), :])
                grad_scores = (probs * (grad_prob - mean_t[pl.ds(j, 1), :])).astype(BF16)
                grad_val[...] += dot(probs.astype(BF16), dm[j])
                grad_key[...] += dot(grad_scores, qm[j])
                dq_t[own, :] = dot(key_t[own, :], grad_scores)

        by_pairs(live, visit)
        out_ref[:, 0:LANES] = (dq_t[...].T * scale).astype(BF16)
        out_ref[:, LANES : 2 * LANES] = (grad_key[...] * scale).astype(BF16)
        out_ref[:, 2 * LANES : 3 * LANES] = grad_val[...].astype(BF16)

    masked = pltpu.VMEM((live, total, LANES), BF16)
    turned = pltpu.VMEM((LANES, total), BF16)
    turned_f = pltpu.VMEM((LANES, total), F32)
    return run(
        body,
        [qkv, grad_att, att, logs],
        after,
        grid=(1,),
        in_specs=[
            pl.BlockSpec((total, 3 * LANES), lambda i: (0, tile)),
            pl.BlockSpec((total, LANES), lambda i: (0, tile)),
            pl.BlockSpec((total, LANES), lambda i: (0, att_tile)),
            pl.BlockSpec((total, LANES), lambda i: (0, 0)),
        ],
        out_specs=pl.BlockSpec((total, 3 * LANES), lambda i: (0, 0)),
        out_shape=sds((total, 3 * LANES), BF16),
        scratch_shapes=[masked] * 4
        + [turned] * 3
        + [turned_f] * 2
        + [pltpu.VMEM((8, total), F32)]
        + [pltpu.VMEM((total, LANES), F32)] * 2,
        vmem=50,
        cost_estimate=cost(
            2 * live * total * total * 256 * 5, 3 * 1024 * 1024, live * total * total
        ),
        name="attend_backward",
    )


def project_back(
    rows_all, gain, shift, weight, grad_tiles, sums_mid, up_sums, pieces, quads, packed, real, after
):
    total, width = rows_all.shape
    piece_rows = total // pieces
    cols_all = weight.shape[1]
    tiles = len(grad_tiles)
    tile_cols = cols_all // tiles
    chunk = width // (quads * pieces)

    def body(*refs):
        x_ref, gain_ref, shift_ref, w_ref, mid_ref, *ups_refs = refs[:7]
        refs = refs[7:]
        dq_refs, refs = refs[:tiles], refs[tiles:]
        own_ref, refs = refs[0], refs[1:]
        send_refs, refs = refs[: pieces - 1], refs[pieces - 1 :]
        sums_ref, bias_ref, *dw_refs, low_t, part_ref = refs
        _, part, quad = place(pieces)
        sums_ref[...] = jnp.zeros_like(sums_ref)
        bias_ref[...] = jnp.zeros_like(bias_ref)
        for h in range(pieces):

            @pl.loop(0, piece_rows // ROWS)
            def _(i, h=h):
                at = pl.multiple_of(i * ROWS, ROWS)
                src = pl.ds(at, ROWS)
                rows = pl.ds(h * piece_rows + at, ROWS)
                normed, _ = norm_rows(x_ref[rows, :].astype(F32))
                low_t[:, rows] = (normed * gain_ref[...] + shift_ref[...]).T.astype(BF16)
                grad = jnp.zeros((ROWS, width), F32)
                for t in range(tiles):
                    grad_rows = dq_refs[t][rows, :]
                    cols = slice(t * tile_cols, (t + 1) * tile_cols)
                    grad = grad + dot_nt(grad_rows, w_ref[:, cols])
                    bias_ref[0:1, cols] += jnp.sum(grad_rows.astype(F32), axis=0, keepdims=True)
                if h == 0:
                    own_ref[src, :] = grad
                else:
                    send_refs[h - 1][src, :] = grad.astype(BF16)
                sums_ref[0:1, :] += jnp.sum(grad * normed, axis=0, keepdims=True)
                sums_ref[1:2, :] += jnp.sum(grad, axis=0, keepdims=True)

        for t in range(tiles):
            cols = slice(t * tile_cols, (t + 1) * tile_cols)
            part_ref[...] = dot(low_t[...], dq_refs[t][...]).astype(BF16)
            if not packed:
                dw_refs[0][:, cols] = part_ref[...]
                continue
            for c in range(pieces):

                @pl.when(part == c)
                def _(c=c, cols=cols):
                    for q in range(quads):
                        for e in range(pieces):
                            at = (q * pieces + (c + e) % pieces) * chunk
                            dw_refs[e][q ^ quad, :, cols] = part_ref[at : at + chunk, :]

        if not packed:
            return
        for row, src in ((4, 2), (5, 0), (6, 1), (15, 3)):
            sums_ref[row : row + 1, :] = mid_ref[src : src + 1, :]
        for c in range(pieces):

            @pl.when(part == c)
            def _(c=c):
                for row, p in ((2, 0), (3, 2)):
                    mine = jnp.concatenate(
                        [
                            bias_ref[0:1, (3 * t + p) * LANES :][:, : min(LANES, real - t * LANES)]
                            for t in range(tiles)
                        ],
                        axis=1,
                    )
                    sums_ref[row : row + 1, c * real : (c + 1) * real] = mine
                for n in range(quads):
                    row = 7 + n * pieces + c
                    start = 0
                    for ref in ups_refs:
                        size = ref.shape[1] // quads
                        here = ref[0:1, n * size : (n + 1) * size]
                        sums_ref[row : row + 1, start : start + size] = here
                        start += size

    if packed:
        grads = [sds((quads, chunk, cols_all), BF16)] * pieces
    else:
        grads = [sds((width, cols_all), BF16)]
    return run(
        body,
        [rows_all, gain, shift, weight, sums_mid, *up_sums, *grad_tiles],
        after,
        out_shape=[sds((piece_rows, width), F32)]
        + [sds((piece_rows, width), BF16)] * (pieces - 1)
        + [sds((16, width), F32), sds((8, cols_all), F32)]
        + grads,
        scratch_shapes=[pltpu.VMEM((width, total), BF16), pltpu.VMEM((width, tile_cols), BF16)],
        vmem=32,
        cost_estimate=cost(4 * total * width * cols_all, 10 * 1024 * 1024),
        name="project_back",
    )


def finish_rows(rows_all, gain, grad_mid, grad_own, received, count, after):
    rows, width = grad_mid.shape
    others = len(received)
    piece = rows // count
    per_step = ROWS // piece

    def body(*refs):
        x_ref, gain_ref, gm_ref, own_ref, refs = refs[0], refs[1], refs[2], refs[3], refs[4:]
        recv_refs, out_refs = refs[:others], refs[others:]
        for n in range(rows // ROWS):
            at = slice(n * ROWS, (n + 1) * ROWS)
            normed, inv_std = norm_rows(x_ref[at, :].astype(F32))
            grad = own_ref[at, :]
            for ref in recv_refs:
                grad = grad + ref[at, :].astype(F32)
            done = gm_ref[at, :] + norm_back(grad * gain_ref[...], normed, inv_std)
            for e in range(per_step):
                out_refs[n * per_step + e][...] = done[e * piece : (e + 1) * piece, :].astype(BF16)

    return run(
        body,
        [rows_all, gain, grad_mid, grad_own, *received],
        after,
        out_shape=[sds((piece, width), BF16)] * count,
        vmem=24,
        cost_estimate=cost(20 * rows * width, 6 * 1024 * 1024),
        name="finish_rows",
    )


def finish_result(own, received, count):
    rows, width = own.shape
    others = len(received)
    piece = rows // count

    def body(*refs):
        out_refs = refs[1 + others :]
        for n in range(count):
            at = slice(n * piece, (n + 1) * piece)
            total = refs[0][at, :]
            for ref in refs[1 : 1 + others]:
                total = total + ref[at, :].astype(F32)
            out_refs[n][...] = total.astype(BF16)

    return run(
        body,
        [own, *received],
        out_shape=[sds((piece, width), BF16)] * count,
        vmem=16,
        cost_estimate=cost(2 * rows * width, 3 * 1024 * 1024),
        name="finish_result",
    )


def two_parts(item):
    first = item.astype(BF16)
    return first, (item - first.astype(F32)).astype(BF16)


def pack_attention(qkv_keep, qkv_recv, out_keep, out_recv, small, small_recv, real, blocks):
    quads, chunk, cols_all = qkv_keep.shape
    wide = cols_all // 3
    tiles = wide // LANES
    width = out_keep.shape[2]
    qkv_lanes = 6 * real // blocks
    out_lanes = width // blocks
    lanes = qkv_lanes + out_lanes
    halves = quads // 2
    slot = halves * chunk
    small_rows = small.shape[0]

    def body(qk_ref, qr_ref, ok_ref, or_ref, small_ref, srecv_ref, *out_refs):
        _, part, quad = place(2)
        mine = lax.axis_index("batch")
        slots = out_refs[4]

        def heads_of(rows, p):
            return [
                rows[:, (3 * t + p) * LANES : (3 * t + p) * LANES + min(LANES, real - t * LANES)]
                for t in range(tiles)
            ]

        for c in range(2):

            @pl.when(part == c)
            def _(c=c):
                for q in range(quads):
                    pair = (qk_ref[q], qr_ref[q])
                    if c == 1:
                        pair = pair[::-1]
                    parts = []
                    for p in range(3):
                        parts += heads_of(pair[0], p) + heads_of(pair[1], p)
                    row = jnp.concatenate(parts, axis=1)
                    for b in range(blocks):
                        slots[b ^ mine, q, :, 0:qkv_lanes] = row[
                            :, b * qkv_lanes : (b + 1) * qkv_lanes
                        ]
                for e, ref in enumerate((ok_ref, or_ref)):
                    for n in range(halves):
                        q = ((c + e) % 2) * halves + n
                        for b in range(blocks):
                            slots[b ^ mine, q ^ quad, :, qkv_lanes:lanes] = ref[
                                n, :, b * out_lanes : (b + 1) * out_lanes
                            ]

        for n, order in enumerate(((0, 2), (1, 3), (0, 1), (2, 3))):
            for e in range(2):
                for f in range(halves):
                    at = e * slot + f * chunk
                    src = f if n < 2 else halves + f
                    out_refs[n][at : at + chunk, :] = slots[order[e], src]
        parts = two_parts(small_ref[...] + srecv_ref[...])
        for n in range(2):
            for e in range(2):
                at = 2 * slot + e * small_rows
                out_refs[n][at : at + small_rows, :] = parts[e]

    first = sds((2 * slot + 2 * small_rows, lanes), BF16)
    other = sds((2 * slot, lanes), BF16)
    return run(
        body,
        [qkv_keep, qkv_recv, out_keep, out_recv, small, small_recv],
        out_shape=[first, first, other, other],
        scratch_shapes=[pltpu.VMEM((blocks, quads, chunk, lanes), BF16)],
        vmem=24,
        cost_estimate=cost(0, 4 * 1024 * 1024),
        name="pack_attention",
    )


def sum_first(keeps, received, after=()):
    count = len(keeps)
    shape = keeps[0].shape[1:]

    def body(*refs):
        for n in range(count):
            for e in range(2):
                total = refs[n][e].astype(F32) + refs[count + n][e].astype(F32)
                refs[2 * count + 2 * n + e][...] = total.astype(BF16)

    return run(
        body,
        [*keeps, *received],
        after,
        out_shape=[sds(shape, BF16)] * (2 * count),
        vmem=24,
        cost_estimate=cost(0, 6 * count * keeps[0].size),
        name="sum_first",
    )


def sum_second(keeps, received, after=()):
    quads, rows, width = keeps[0].shape

    def body(ka, kb, ra, rb, *out_refs):
        for d in range(quads):
            for e, (keep, recv) in enumerate(((ka, ra), (kb, rb))):
                total = keep[d].astype(F32) + recv[d].astype(F32)
                out_refs[d][e] = total.astype(BF16)

    return run(
        body,
        [*keeps, *received],
        after,
        out_shape=[sds((2, rows, width), BF16)] * quads,
        vmem=24,
        cost_estimate=cost(0, 12 * keeps[0].size),
        name="sum_second",
    )


def small_sum(refs, rows, count):
    total = None
    for ref in refs:
        for e in range(2):
            item = ref[rows + e * count : rows + (e + 1) * count, :].astype(F32)
            total = item if total is None else total + item
    return total


def sum_first_attention(keeps, received, slot, small_rows, after):
    lanes = keeps[0].shape[1]

    def body(ka, kb, ra, rb, stay_a, pass_a, stay_b, pass_b):
        parts = two_parts(small_sum((ka, ra), 2 * slot, small_rows))
        for keep, recv, stay, on in ((ka, ra, stay_a, pass_a), (kb, rb, stay_b, pass_b)):
            for e, ref in enumerate((stay, on)):
                at = slice(e * slot, (e + 1) * slot)
                ref[0:slot, :] = (keep[at, :].astype(F32) + recv[at, :].astype(F32)).astype(BF16)
        for ref in (stay_a, pass_a):
            for e in range(2):
                ref[slot + e * small_rows : slot + (e + 1) * small_rows, :] = parts[e]

    first = sds((slot + 2 * small_rows, lanes), BF16)
    other = sds((slot, lanes), BF16)
    return run(
        body,
        [*keeps, *received],
        after,
        out_shape=[first, first, other, other],
        vmem=16,
        cost_estimate=cost(0, 3 * 1024 * 1024),
        name="sum_first_attention",
    )


def sum_second_attention(keeps, received, chunk, quads, small_rows):
    lanes = keeps[0].shape[1]
    halves = quads // 2
    slot = halves * chunk

    def body(ka, kb, ra, rb, *out_refs):
        parts = two_parts(small_sum((ka, ra), slot, small_rows))
        for d in range(quads):
            keep, recv = ((ka, ra), (kb, rb))[d // halves]
            at = slice(d % halves * chunk, (d % halves + 1) * chunk)
            total = keep[at, :].astype(F32) + recv[at, :].astype(F32)
            out_refs[d][0:chunk, :] = total.astype(BF16)
            for e in range(2):
                at = chunk + e * small_rows
                out_refs[d][at : at + small_rows, :] = parts[e]

    return run(
        body,
        [*keeps, *received],
        out_shape=[sds((chunk + 2 * small_rows, lanes), BF16)] * quads,
        vmem=16,
        cost_estimate=cost(0, 2 * 1024 * 1024),
        name="sum_second_attention",
    )


def final_attention(pieces, chunk, qkv_lanes, small_rows):
    lanes = pieces[0].shape[1]
    count = len(pieces)

    def body(*refs):
        total = refs[0][0:chunk, :].astype(F32)
        for ref in refs[1:count]:
            total = total + ref[0:chunk, :].astype(F32)
        refs[count][...] = total[:, :qkv_lanes]
        refs[count + 1][...] = total[:, qkv_lanes:]
        refs[count + 2][...] = small_sum(refs[:count], chunk, small_rows)

    return run(
        body,
        pieces,
        out_shape=[
            sds((chunk, qkv_lanes), F32),
            sds((chunk, lanes - qkv_lanes), F32),
            sds((small_rows, lanes), F32),
        ],
        vmem=16,
        cost_estimate=cost(0, 1024 * 1024),
        name="final_attention",
    )


def final_units(first, second, after):
    high = first[0].shape[1]
    sizes = [first[0].shape[2], second[0].shape[2]]
    unit_block = sum(sizes)
    count = len(first)
    half = high // 2

    def body(*refs):
        _, part, _ = place(2)
        keep_ref, send_ref, down_ref = refs[2 * count :]
        for h in range(2):
            pieces = refs[h * count : (h + 1) * count]
            up, down = pieces[0][0].astype(F32), pieces[0][1].astype(F32)
            for ref in pieces[1:]:
                up = up + ref[0].astype(F32)
                down = down + ref[1].astype(F32)
            here = slice(h * sizes[0], h * sizes[0] + sizes[h])
            down_ref[here, :] = down.T
            for c in range(2):

                @pl.when(part == c)
                def _(up=up, here=here, c=c):
                    keep_ref[:, here] = up[c * half : (c + 1) * half, :]
                    send_ref[:, here] = up[(1 - c) * half : (2 - c) * half, :].astype(BF16)

    return run(
        body,
        [*first, *second],
        after,
        out_shape=[
            sds((half, unit_block), F32),
            sds((half, unit_block), BF16),
            sds((unit_block, high), F32),
        ],
        vmem=24,
        cost_estimate=cost(0, 4 * 1024 * 1024),
        name="final_units",
    )


def final_join(keep, recv):
    chunk, unit_block = keep.shape

    def body(keep_ref, recv_ref, out_ref):
        _, part, _ = place(2)
        for c in range(2):

            @pl.when(part == c)
            def _(c=c):
                out_ref[:, c * unit_block : (c + 1) * unit_block] = keep_ref[...]
                out_ref[:, (1 - c) * unit_block : (2 - c) * unit_block] = recv_ref[...].astype(F32)

    return run(
        body,
        [keep, recv],
        out_shape=sds((chunk, 2 * unit_block), F32),
        vmem=16,
        cost_estimate=cost(0, 1024 * 1024),
        name="final_join",
    )


def on_device(
    tokens,
    mask,
    cotangent,
    ln1_gain,
    ln1_bias,
    qkv_weight,
    q_bias,
    v_bias,
    out_weight,
    out_bias,
    ln2_gain,
    ln2_bias,
    up_weight,
    up_bias,
    down_weight,
    down_bias,
):
    seq_size = lax.axis_size("seq")
    batch_size = lax.axis_size("batch")
    micro_count, seq_count, local_len, width = tokens.shape
    sequences = micro_count * seq_count
    group = seq_size // sequences
    units = up_weight.shape[1]
    head_dim = width // HEADS
    heads = HEADS // group
    real = heads * head_dim
    wide = -(-real // LANES) * LANES
    full_len = local_len * seq_size
    block_len = local_len // group
    rows = seq_size * block_len
    own_units = units // group
    part = lax.axis_index("seq") % group
    aligned = (
        seq_size == batch_size * group
        and group == 2
        and batch_size == 4
        and wide == 3 * LANES
        and (seq_size // group) % group == 0
        and units % (batch_size * group * LANES) == 0
        and own_units // batch_size == width
    )

    def from_part(item, ahead):
        if ahead % group == 0:
            return item
        pairs = [
            (q * group + (c + ahead) % group, q * group + c)
            for q in range(sequences)
            for c in range(group)
        ]
        return lax.ppermute(item, "seq", pairs)

    def gather_parts(item):
        return [from_part(item, n) for n in range(group)]

    def row_of(item):
        return item.astype(F32)[None, :]

    def blocks_of(item):
        return item.reshape(sequences, local_len, width)

    x_own = over_quads(deal(blocks_of(tokens), group), group)
    x_pieces = [from_part(item, n) for n in range(group) for item in x_own]

    count_rows = jnp.sum(mask, axis=2).reshape(sequences).astype(BF16)
    cot_low = jnp.where(mask[..., None] != 0, cotangent, jnp.zeros_like(cotangent))
    cot_send = jnp.concatenate(
        [blocks_of(cot_low), jnp.broadcast_to(count_rows[:, None, None], (sequences, 16, width))],
        axis=1,
    )
    cot_own = over_quads(deal(cot_send, group, x_own[1:]), group)

    qkv_w, qkv_b, *out_w = pick_weights(
        qkv_weight,
        jnp.concatenate([q_bias, jnp.zeros_like(q_bias), v_bias])[None, :],
        out_weight,
        group,
        real,
        wide,
    )
    if aligned:
        up_own, up_b, down_own = up_weight, up_bias[None, :], down_weight
    else:

        def own_columns(matrix, blocks):
            split = matrix.reshape(matrix.shape[0], blocks, group, -1)
            return lax.dynamic_index_in_dim(split, part, 2, keepdims=False)

        up_own = own_columns(up_weight, batch_size).reshape(width, own_units)
        up_b = own_columns(up_bias[None, :], batch_size).reshape(1, own_units)
        down_own = lax.dynamic_index_in_dim(
            down_weight.reshape(batch_size, group, -1, width), part, 1, keepdims=False
        ).reshape(own_units, width)

    tiles = wide // LANES
    x_all, qkv, att_first, logs_first = attend_first(
        x_pieces, row_of(ln1_gain), row_of(ln1_bias), qkv_w, qkv_b, tiles - 1, heads, head_dim
    )
    cot_stack = stack(cot_own, [logs_first])
    att_last, logs_last = attend_last(qkv, tiles - 1, heads, head_dim, [cot_stack])
    cot_pieces = cot_own + [
        item[d]
        for item in gather_parts(cot_stack)[1:]
        for d in range(sequences)
    ]
    blocks = batch_size if aligned else 1
    unit_block = own_units // blocks
    size = unit_block * 3 // 5
    shape = (group, sequences if aligned else None, width // sequences)
    calls = [
        Units(unit_block, blocks, 0, size, *shape),
        Units(unit_block, blocks, size, unit_block - size, *shape),
    ]
    mid, second, second_t, grad_rows, grad_t, acc, grad_second, *found = feed_first(
        x_all,
        gather_parts(att_first),
        gather_parts(att_last),
        cot_pieces,
        out_w,
        row_of(out_bias),
        row_of(ln2_gain),
        row_of(ln2_bias),
        up_own,
        up_b,
        down_own,
        row_of(down_bias),
        calls[0],
    )
    up_sums, ff_grads = [found[0]], [found[1:]]
    result_own, grad_second, second_send, *found = feed_second(
        second,
        second_t,
        grad_rows,
        grad_t,
        acc,
        grad_second,
        up_own,
        up_b,
        down_own,
        calls[1],
        group,
        [],
    )
    up_sums.append(found[0])
    result_send = found[1:group]
    ff_grads.append(found[group:])

    second_recv = [from_part(second_send, n) for n in range(1, group)]
    if aligned:
        first_swaps = [
            [swap(item[1], "batch", batch_size, 1), swap(item[3], "batch", batch_size, 2)]
            for item in ff_grads
        ]
    result_recv = [from_part(result_send[group - n - 1], n) for n in range(1, group)]
    result_parts = finish_result(result_own, result_recv, sequences)
    result_moved = over_quads(result_parts, group)

    chunk = width // seq_size
    grad_mid, grad_att, sums_mid, *out_grad = mid_back(
        mid,
        grad_second,
        second_recv,
        grad_rows,
        row_of(ln2_gain),
        out_w[0],
        att_first,
        att_last,
        chunk if aligned else 0,
    )

    def tile_back(t, after):
        last = t == tiles - 1
        return attend_backward(
            qkv,
            grad_att,
            att_last if last else att_first,
            0 if last else t,
            logs_last if last else logs_first,
            0 if last else t * (LANES // head_dim),
            t,
            heads,
            head_dim,
            after,
        )

    def begin_sum(e, after):
        stay_a, pass_a, stay_b, pass_b = sum_first(
            [ff_grads[e][0], ff_grads[e][2]], first_swaps[e], after
        )
        moved = [swap(pass_a, "batch", batch_size, 2), swap(pass_b, "batch", batch_size, 1)]
        return [stay_a, stay_b], moved

    after = [result_parts[0]]
    grad_tiles = []
    if aligned:
        waiting = begin_sum(0, [grad_mid])
        after = after + waiting[0][:1]
    grad_tiles.append(tile_back(0, after))
    grad_tiles.append(tile_back(1, result_moved[1:]))
    after = []
    if aligned:
        summed = sum_second(*waiting, [grad_tiles[1]])
        unit_first = over_quads(summed, group)
        waiting = begin_sum(1, [grad_tiles[1]])
        after = [summed[0], waiting[0][0]]
    for t in range(2, tiles):
        grad_tiles.append(tile_back(t, after))
    if aligned:
        summed = sum_second(*waiting, [grad_tiles[2]])
        unit_second = over_quads(summed, group)
        after = summed[:1]
    found = project_back(
        x_all,
        row_of(ln1_gain),
        row_of(ln1_bias),
        qkv_w,
        grad_tiles,
        sums_mid,
        up_sums,
        group,
        sequences,
        aligned,
        real,
        after,
    )
    first_own, first_send = found[0], found[1:group]
    small, bias_sums, *qkv_grad = found[group:]
    first_recv = [from_part(first_send[group - n - 1], n) for n in range(1, group)]
    after = []
    if aligned:
        small_rows = small.shape[0]
        packed = pack_attention(
            qkv_grad[0],
            from_part(qkv_grad[1], 1),
            out_grad[0],
            from_part(out_grad[1], 1),
            small,
            from_part(small, 1),
            real,
            batch_size,
        )
        after = packed[:1]
    row_parts = finish_rows(
        x_all, row_of(ln1_gain), grad_mid, first_own, first_recv, sequences, after
    )
    row_moved = over_quads(row_parts, group)
    if aligned:
        stay_a, pass_a, stay_b, pass_b = sum_first_attention(
            [packed[0], packed[2]],
            [swap(packed[1], "batch", batch_size, 1), swap(packed[3], "batch", batch_size, 2)],
            sequences // 2 * chunk,
            small_rows,
            row_parts[:1],
        )
        summed = sum_second_attention(
            [stay_a, stay_b],
            [swap(pass_a, "batch", batch_size, 2), swap(pass_b, "batch", batch_size, 1)],
            chunk,
            sequences,
            small_rows,
        )
        after = summed[:1]
        up_keep, up_send, down_grad = final_units(unit_first, unit_second, after)
        up_grad = final_join(up_keep, from_part(up_send, 1))
        qkv_final, out_final, small = final_attention(
            over_quads(summed, group), chunk, qkv_weight.shape[1] // batch_size, small_rows
        )
        small = small.reshape(-1)
    result = collect(result_moved, group, after).reshape(tokens.shape)
    grad_in = collect(row_moved, group, after).reshape(tokens.shape)
    if not aligned:

        def spread(item, blocks):
            split = item.reshape(blocks, 1, -1)
            empty = jnp.zeros((blocks, group, split.shape[2]), F32)
            return lax.dynamic_update_slice(empty, split, (0, part, 0)).reshape(-1)

        bias_sums = bias_sums[0].reshape(tiles, 3, LANES).transpose(1, 0, 2)
        bias_sums = bias_sums.reshape(3, wide)[:, :real]
        small = jnp.concatenate(
            [
                small[0],
                small[1],
                spread(bias_sums[0], 1),
                spread(bias_sums[2], 1),
                sums_mid[2],
                sums_mid[0],
                sums_mid[1],
                spread(jnp.concatenate([item[0] for item in up_sums]), batch_size),
                sums_mid[3],
            ]
        )

        def scattered(item):
            item = lax.psum_scatter(item.astype(BF16), "seq", scatter_dimension=0, tiled=True)
            return lax.psum_scatter(item, "batch", scatter_dimension=1, tiled=True).astype(F32)

        def spread_columns(item, blocks):
            split = item.reshape(item.shape[0], blocks, 1, -1)
            empty = jnp.zeros((item.shape[0], blocks, group, split.shape[3]), item.dtype)
            filled = lax.dynamic_update_slice(empty, split, (0, 0, part, 0))
            return filled.reshape(item.shape[0], -1)

        up_full, down_full = [
            jnp.concatenate([item[e] for item in ff_grads], axis=1) for e in range(2)
        ]
        up_grad = scattered(spread_columns(up_full, batch_size))
        down_grad = scattered(spread_columns(down_full, batch_size).T)
        rows_full = qkv_grad[0].reshape(width, tiles, 3, LANES).transpose(0, 2, 1, 3)
        rows_full = rows_full.reshape(width, 3, wide)[..., :real]
        qkv_final = scattered(spread_columns(rows_full.reshape(width, -1), 3))
        out_final = scattered(spread_columns(out_grad[0][:real].T, 1).T)
        small = lax.psum(small, ("seq", "batch"))

    edges = [width] * 7 + [units, width]
    pieces, start = [], 0
    for size in edges:
        pieces.append(small[start : start + size])
        start += size
    return (
        result,
        grad_in,
        pieces[0],
        pieces[1],
        qkv_final,
        pieces[2],
        pieces[3],
        out_final,
        pieces[4],
        pieces[5],
        pieces[6],
        up_grad,
        pieces[7],
        down_grad,
        pieces[8],
    )


def solution(mesh):
    rows = P(None, "batch", "seq", None)
    split = P("seq", "batch")
    in_specs = (rows, P(None, "batch", "seq"), rows) + (P(),) * 13
    out_specs = (
        rows,
        rows,
        P(),
        P(),
        split,
        P(),
        P(),
        split,
        P(),
        P(),
        P(),
        split,
        P(),
        split,
        P(),
    )
    return jax.shard_map(
        on_device, mesh=mesh, in_specs=in_specs, out_specs=out_specs, check_vma=False
    )
```

```python
import jax
import jax.numpy as jnp
from jax import lax
from jax.experimental import pallas as pl
from jax.experimental.pallas import tpu as pltpu
from jax.sharding import PartitionSpec as P

HEADS = 20
EPS = 1e-05
LOG2E = 1.4426950408889634
ROWS = 256
F32 = jnp.float32
BF16 = jnp.bfloat16
LANES = 128


def dot(left, right):
    return jnp.dot(left, right, preferred_element_type=F32)


def dot_nt(left, right):
    return lax.dot_general(left, right, (((1,), (1,)), ((), ())), preferred_element_type=F32)


def norm_rows(rows_in):
    mean_val = jnp.mean(rows_in, axis=-1, keepdims=True)
    centered = rows_in - mean_val
    inv_std = lax.rsqrt(jnp.mean(centered * centered, axis=-1, keepdims=True) + EPS)
    return centered * inv_std, inv_std


def norm_back(scaled, normed, inv_std):
    inner = (
        scaled
        - jnp.mean(scaled, axis=-1, keepdims=True)
        - normed * jnp.mean(scaled * normed, axis=-1, keepdims=True)
    )
    return inner * inv_std


def params_of(mib):
    return pltpu.CompilerParams(vmem_limit_bytes=mib * 1024 * 1024)


def cost(flops, moved, trans=0, part=1):
    return pl.CostEstimate(
        flops=flops // part, bytes_accessed=moved // part, transcendentals=trans // part
    )


def sds(shape, dtype):
    return jax.ShapeDtypeStruct(shape, dtype)


VMEM = pl.BlockSpec(memory_space=pltpu.VMEM)
HBM = pl.BlockSpec(memory_space=pl.ANY)


def run(body, operands, after=(), in_specs=None, out_specs=None, vmem=32, **more):
    count, extra = len(operands), len(after)

    def inner(*refs):
        body(*refs[:count], *refs[count + extra :])

    specs = [VMEM] * count if in_specs is None else list(in_specs)
    shapes = more["out_shape"]
    if out_specs is None:
        out_specs = [VMEM] * len(shapes) if isinstance(shapes, (list, tuple)) else VMEM
    return pl.pallas_call(
        inner,
        in_specs=specs + [HBM] * extra,
        out_specs=out_specs,
        compiler_params=params_of(vmem),
        **more,
    )(*operands, *after)


def place(group):
    spot = lax.axis_index("seq")
    return spot, lax.rem(spot, group), lax.div(spot, group)


def deal(item, group, after=()):
    count, rows, width = item.shape

    def body(in_ref, *out_refs):
        _, _, quad = place(group)
        for d in range(count):
            out_refs[d][...] = in_ref[quad ^ d]

    return run(
        body,
        [item],
        after,
        out_shape=[sds((rows, width), item.dtype)] * count,
        vmem=16,
        cost_estimate=cost(0, 4 * count * rows * width),
        name="deal",
    )


def collect(pieces, group, after=()):
    count = len(pieces)
    rows, width = pieces[0].shape

    def body(*refs):
        _, _, quad = place(group)
        for d in range(count):
            refs[count][quad ^ d] = refs[d][...]

    return run(
        body,
        pieces,
        after,
        out_shape=sds((count, rows, width), pieces[0].dtype),
        vmem=16,
        cost_estimate=cost(0, 4 * count * rows * width),
        name="collect",
    )


def stack(pieces, after):
    count = len(pieces)

    def body(*refs):
        for d in range(count):
            refs[count][d] = refs[d][...]

    return run(
        body,
        pieces,
        after,
        out_shape=sds((count,) + pieces[0].shape, pieces[0].dtype),
        vmem=16,
        cost_estimate=cost(0, 4 * count * pieces[0].size),
        name="stack",
    )


def swap(item, axis, size, distance):
    return lax.ppermute(item, axis, [(i, i ^ distance) for i in range(size)])


def over_quads(pieces, group):
    return [
        piece if d == 0 else swap(piece, "seq", len(pieces) * group, d * group)
        for d, piece in enumerate(pieces)
    ]


def pick_weights(qkv_weight, qkv_bias, out_weight, group, real, wide):
    width = qkv_weight.shape[0]
    tiles = wide // LANES

    def body(w_ref, b_ref, o_ref, wo_ref, bo_ref, *out_refs):
        _, part, _ = place(group)
        wo_ref[...] = jnp.zeros_like(wo_ref)
        bo_ref[...] = jnp.zeros_like(bo_ref)
        for ref in out_refs:
            ref[...] = jnp.zeros_like(ref)
        for c in range(group):

            @pl.when(part == c)
            def _(c=c):
                for p in range(3):
                    for t in range(tiles):
                        some = min(LANES, real - t * LANES)
                        src = p * width + c * real + t * LANES
                        dst = (3 * t + p) * LANES
                        wo_ref[:, dst : dst + some] = w_ref[:, src : src + some]
                        bo_ref[:, dst : dst + some] = b_ref[:, src : src + some]
                for n in range(group):
                    src = (c + n) % group * real
                    out_refs[n][0:real, :] = o_ref[src : src + real, :]

    return pl.pallas_call(
        body,
        out_shape=[sds((width, 3 * wide), BF16), sds((1, 3 * wide), F32)]
        + [sds((wide, width), BF16)] * group,
        compiler_params=params_of(24),
        cost_estimate=cost(0, 8 * 1024 * 1024),
        name="pick_weights",
    )(qkv_weight, qkv_bias, out_weight)


def by_pairs(live, visit):
    size = 2 if live % 2 == 0 else 1

    @pl.loop(0, live // size)
    def _(i):
        visit([i * size + e for e in range(size)])


def attend_tiles(query_at, keys_at, vals_at, att_ref, lse_ref, keys, vals, acc, tiles, heads, head_dim):
    per_tile = LANES // head_dim
    total = att_ref.shape[0]
    exp_scale = head_dim ** (-0.5) * LOG2E
    lane = lax.broadcasted_iota(jnp.int32, (1, LANES), 1)
    row = lax.broadcasted_iota(jnp.int32, (LANES, 1), 0)
    lse_ref[...] = jnp.zeros_like(lse_ref)
    vals[:, :, LANES:] = jnp.ones((per_tile, total, LANES), BF16)
    for n, t in enumerate(tiles):
        live = min(per_tile, heads - t * per_tile)
        key_t = keys_at(n).astype(F32).T
        val_f = vals_at(n).astype(F32)
        for j in range(live):
            keys[j] = jnp.where(row // head_dim == j, key_t, 0.0).astype(BF16)
            vals[j, :, :LANES] = jnp.where(lane // head_dim == j, val_f, 0.0).astype(BF16)
        acc[...] = jnp.zeros_like(acc)

        def visit(some, n=n):
            scores = [dot(query_at(n), keys[j]) for j in some]
            for item, j in zip(scores, some):
                row_max = jnp.max(item, axis=-1, keepdims=True) * exp_scale
                expd = jnp.exp2(item * exp_scale - row_max).astype(BF16)
                mixed = dot(expd, vals[j])
                den = mixed[:, LANES:]
                acc[...] += mixed[:, :LANES] / den
                lse_ref[...] = jnp.where(
                    lane == n * per_tile + j, row_max + jnp.log2(den), lse_ref[...]
                )

        by_pairs(live, visit)
        att_ref[:, n * LANES : (n + 1) * LANES] = acc[...].astype(BF16)


def attend_scratch(total, head_dim):
    per_tile = LANES // head_dim
    return [
        pltpu.VMEM((per_tile, LANES, total), BF16),
        pltpu.VMEM((per_tile, total, 2 * LANES), BF16),
        pltpu.VMEM((total, LANES), F32),
    ]


def attend_first(x_pieces, gain, shift, weight, bias, tiles, heads, head_dim):
    count = len(x_pieces)
    piece_rows, width = x_pieces[0].shape
    total = count * piece_rows
    cols_all = weight.shape[1]

    def body(*refs):
        x_refs = refs[:count]
        gain_ref, shift_ref, w_ref, bias_ref = refs[count : count + 4]
        x_ref, qkv_ref, att_ref, lse_ref, keys, vals, acc = refs[count + 4 :]
        for n in range(count):
            x_ref[n * piece_rows : (n + 1) * piece_rows, :] = x_refs[n][...]

        @pl.loop(0, total // ROWS)
        def _(i):
            rows = pl.ds(pl.multiple_of(i * ROWS, ROWS), ROWS)
            normed, _ = norm_rows(x_ref[rows, :].astype(F32))
            low = (normed * gain_ref[...] + shift_ref[...]).astype(BF16)
            qkv_ref[rows, :] = (dot(low, w_ref[...]) + bias_ref[...]).astype(BF16)

        def columns(at):
            return slice(at * LANES, (at + 1) * LANES)

        attend_tiles(
            lambda n: qkv_ref[:, columns(3 * n)],
            lambda n: qkv_ref[:, columns(3 * n + 1)],
            lambda n: qkv_ref[:, columns(3 * n + 2)],
            att_ref,
            lse_ref,
            keys,
            vals,
            acc,
            range(tiles),
            heads,
            head_dim,
        )

    return run(
        body,
        [*x_pieces, gain, shift, weight, bias],
        out_shape=[
            sds((total, width), BF16),
            sds((total, cols_all), BF16),
            sds((total, tiles * LANES), BF16),
            sds((total, LANES), F32),
        ],
        scratch_shapes=attend_scratch(total, head_dim),
        vmem=48,
        cost_estimate=cost(
            2 * total * width * cols_all + 4 * heads * total * total * 256,
            8 * 1024 * 1024,
            heads * total * total,
        ),
        name="attend_first",
    )


def attend_last(qkv, tile, heads, head_dim, after):
    total = qkv.shape[0]

    def body(qkv_ref, att_ref, lse_ref, keys, vals, acc):
        attend_tiles(
            lambda n: qkv_ref[:, 0:LANES],
            lambda n: qkv_ref[:, LANES : 2 * LANES],
            lambda n: qkv_ref[:, 2 * LANES : 3 * LANES],
            att_ref,
            lse_ref,
            keys,
            vals,
            acc,
            [tile],
            heads,
            head_dim,
        )

    live = heads - tile * (LANES // head_dim)
    return run(
        body,
        [qkv],
        after,
        grid=(1,),
        in_specs=[pl.BlockSpec((total, 3 * LANES), lambda i: (0, tile))],
        out_specs=[pl.BlockSpec((total, LANES), lambda i: (0, 0))] * 2,
        out_shape=[sds((total, LANES), BF16), sds((total, LANES), F32)],
        scratch_shapes=attend_scratch(total, head_dim),
        vmem=40,
        cost_estimate=cost(4 * live * total * total * 256, 2 * 1024 * 1024, live * total * total),
        name="attend_last",
    )


def gelu_parts(value):
    size = jnp.abs(value)
    near = pl.reciprocal(1.0 + (0.3275911 * 0.7071067811865476) * size, approx=True)
    bell = jnp.exp2(value * value * (-0.5 * LOG2E))
    poly = near * (
        0.5 * 0.254829592
        + near
        * (
            0.5 * -0.284496736
            + near * (0.5 * 1.421413741 + near * (0.5 * -1.453152027 + near * (0.5 * 1.061405429)))
        )
    )
    tail = poly * bell
    area = jnp.where(value < 0.0, tail, 1.0 - tail)
    return value * area, area + value * bell * 0.3989422804014327


class Units:
    def __init__(self, block, blocks, start, size, stride, quads, high):
        self.block, self.blocks, self.start, self.size = block, blocks, start, size
        self.stride, self.quads, self.high = stride, quads, high
        self.count = blocks * size
        self.chunk = 512 if self.count % 512 == 0 else 256
        self.packed = quads is not None

    def loads(self, part, hbm_up, hbm_down, hbm_bias, up_ref, down_ref, bias_ref, sem):
        copies = []
        for b in range(self.blocks):
            src = self.start
            if self.packed:
                src = pl.multiple_of((b * self.stride + part) * self.block, LANES) + self.start
            src = pl.ds(src, self.size)
            dst = pl.ds(b * self.size, self.size)
            copies.append(
                pltpu.make_async_copy(hbm_up.at[:, src], up_ref.at[:, dst], sem.at[2 * b])
            )
            copies.append(
                pltpu.make_async_copy(hbm_down.at[src, :], down_ref.at[dst, :], sem.at[2 * b + 1])
            )
            bias_ref[0:1, dst] = hbm_bias[:, src]
        return copies

    def grad_shapes(self, width):
        if self.packed:
            return [sds((2, self.quads, self.high, self.size), BF16)] * 4
        return [sds((width, self.count), BF16)] * 2

    def scratch(self, total, width):
        grads = (self.blocks, self.quads, self.high, self.size) if self.packed else (8, LANES)
        return [
            pltpu.VMEM(grads, BF16),
            pltpu.VMEM(grads, BF16),
            pltpu.SemaphoreType.DMA((8,)),
            pltpu.VMEM((total, self.count), BF16),
            pltpu.VMEM((total, self.count), BF16),
            pltpu.VMEM((width, self.count), BF16),
            pltpu.VMEM((self.count, width), BF16),
            pltpu.VMEM((8, self.count), F32),
            pltpu.SemaphoreType.DMA((2 * self.blocks,)),
        ]

    def compute(self, part, second, second_t, grad, grad_t, acc, gs, ubg, scratch, outs):
        up_slots, down_slots, out_sem, acts, grad_pres, up_ref, down_ref, bias_ref, _ = scratch
        if not self.packed:
            up_slots, down_slots = outs
        quad = lax.div(lax.axis_index("seq"), self.stride)
        mine = lax.axis_index("batch")

        def enter(i):
            rows = slice(i * ROWS, (i + 1) * ROWS)
            pre = dot(second[rows, :], up_ref[...]) + bias_ref[0:1, :]
            return pre, dot_nt(grad[rows, :], down_ref[...])

        def weights(n):
            first, last = n * self.chunk, (n + 1) * self.chunk
            up_grad = dot(second_t[...], grad_pres[:, first:last]).astype(BF16)
            down_grad = dot(grad_t[...], acts[:, first:last]).astype(BF16)
            if not self.packed:
                up_slots[:, first:last] = up_grad
                down_slots[:, first:last] = down_grad
                return
            at = first
            while at < last:
                block = at // self.size
                stop = min(last, (block + 1) * self.size)
                src = slice(at - first, stop - first)
                dst = slice(at - block * self.size, stop - block * self.size)
                for m in range(self.blocks):
                    rows = slice(m * self.high, (m + 1) * self.high)
                    up_slots[block ^ mine, m ^ quad, :, dst] = up_grad[rows, src]
                    down_slots[m ^ mine, block ^ quad, :, dst] = down_grad[rows, src]
                at = stop

        ready = enter(0)
        chunks = second.shape[0] // ROWS
        for i in range(chunks):
            ahead = enter(i + 1) if i + 1 < chunks else None
            rows = slice(i * ROWS, (i + 1) * ROWS)
            pre, grad_act = ready
            value, slope = gelu_parts(pre)
            act = value.astype(BF16)
            grad_pre = (grad_act * slope).astype(BF16)
            acts[rows, :] = act
            grad_pres[rows, :] = grad_pre
            ubg[0:1, :] += jnp.sum(grad_pre.astype(F32), axis=0, keepdims=True)
            acc[rows, :] += dot(act, down_ref[...])
            gs[rows, :] += dot_nt(grad_pre, up_ref[...])
            ready = ahead
        for n in range(self.count // self.chunk):
            weights(n)
        stores = []
        if self.packed:
            order = ((up_slots, (0, 2)), (up_slots, (1, 3)), (down_slots, (0, 1)), (down_slots, (2, 3)))
            for m, (source, slots) in enumerate(order):
                for n in range(2):
                    stores.append(
                        pltpu.make_async_copy(
                            source.at[slots[n]], outs[m].at[n], out_sem.at[2 * m + n]
                        )
                    )
        return stores


def feed_first(
    rows_all, att_first, att_last, cot_pieces, out_w, out_b, gain, shift, up, up_b, down, down_b, units
):
    pieces = len(att_first)
    total, width = rows_all.shape
    piece_rows = total // pieces
    count = len(cot_pieces)
    cot_rows = total // count
    split = att_first[0].shape[1]
    grads = units.grad_shapes(width)

    def body(*refs):
        x_ref, refs = refs[0], refs[1:]
        att_refs, refs = refs[: 2 * pieces], refs[2 * pieces :]
        cot_refs, refs = refs[:count], refs[count:]
        wo_refs, refs = refs[:pieces], refs[pieces:]
        ob_ref, gain_ref, shift_ref, up_hbm, ub_ref, down_hbm, db_ref = refs[:7]
        mid_ref, second, second_t, grad, grad_t, acc, gs, ubg = refs[7:15]
        outs, scratch = refs[15 : 15 + len(grads)], refs[15 + len(grads) :]
        _, part, _ = place(pieces)
        loads = units.loads(part, up_hbm, down_hbm, ub_ref, *scratch[5:])
        for load in loads:
            load.start()
        ubg[...] = jnp.zeros_like(ubg)
        masked = jnp.zeros((1, width), F32)
        for ref in cot_refs:
            masked = masked + ref[cot_rows : cot_rows + 1, :].astype(F32)
        factor = total / (4.0 * masked)
        for n in range(count):
            scaled = cot_refs[n][0:cot_rows, :].astype(F32) * factor
            dst = slice(n * cot_rows, (n + 1) * cot_rows)
            grad[dst, :] = scaled.astype(BF16)

        for h in range(pieces):

            @pl.loop(0, piece_rows // ROWS)
            def _(i, h=h):
                at = pl.multiple_of(i * ROWS, ROWS)
                dst = pl.ds(h * piece_rows + at, ROWS)
                mid = x_ref[dst, :].astype(F32) + ob_ref[...]
                for n in range(pieces):
                    src = pl.ds(((h - n) % pieces) * piece_rows + at, ROWS)
                    mid = mid + dot(att_refs[2 * n][src, :], wo_refs[n][0:split, :])
                    mid = mid + dot(att_refs[2 * n + 1][src, :], wo_refs[n][split:, :])
                mid_ref[dst, :] = mid
                normed, _ = norm_rows(mid)
                low = normed * gain_ref[...] + shift_ref[...]
                second[dst, :] = low.astype(BF16)
                second_t[:, dst] = low.T.astype(BF16)
                grad_t[:, dst] = grad[dst, :].astype(F32).T.astype(BF16)
                acc[dst, :] = mid + db_ref[...] if h == 0 else jnp.zeros((ROWS, width), F32)
                gs[dst, :] = jnp.zeros((ROWS, width), F32)

        for load in loads:
            load.wait()
        stores = units.compute(
            part, second, second_t, grad, grad_t, acc, gs, ubg, scratch, outs
        )
        for store in stores:
            store.start()
        for store in stores:
            store.wait()

    att_all = [item for pair in zip(att_first, att_last) for item in pair]
    turned = sds((width, total), BF16)
    flat = sds((total, width), BF16)
    wide = sds((total, width), F32)
    return run(
        body,
        [rows_all, *att_all, *cot_pieces, *out_w, out_b, gain, shift, up, up_b, down, down_b],
        in_specs=[VMEM] * (1 + 3 * pieces + count) + [VMEM, VMEM, VMEM, HBM, VMEM, HBM, VMEM],
        out_specs=[VMEM] * 8 + [HBM if units.packed else VMEM] * len(grads),
        out_shape=[wide, flat, turned, flat, turned, wide, wide, sds((8, units.count), F32)] + grads,
        scratch_shapes=units.scratch(total, width),
        vmem=46,
        cost_estimate=cost(12 * total * width * units.count, 24 * 1024 * 1024, total * units.count),
        name="feed_first",
    )


def feed_second(second, second_t, grad, grad_t, acc_first, gs_first, up, up_b, down, units, pieces, after):
    total, width = second.shape
    piece_rows = total // pieces
    grads = units.grad_shapes(width)

    def body(*refs):
        second, second_t, grad, grad_t, acc_in, gs_in, up_hbm, ub_ref, down_hbm = refs[:9]
        own_ref, gs, ubg, refs = refs[9], refs[10], refs[11], refs[12:]
        send_refs, refs = refs[: pieces - 1], refs[pieces - 1 :]
        outs, acc, scratch = refs[: len(grads)], refs[len(grads)], refs[len(grads) + 1 :]
        _, part, _ = place(pieces)
        loads = units.loads(part, up_hbm, down_hbm, ub_ref, *scratch[5:])
        for load in loads:
            load.start()
        ubg[...] = jnp.zeros_like(ubg)
        acc[...] = acc_in[...]
        gs[...] = gs_in[...]
        for load in loads:
            load.wait()
        stores = units.compute(
            part, second, second_t, grad, grad_t, acc, gs, ubg, scratch, outs
        )
        for store in stores:
            store.start()
        own_ref[...] = acc[0:piece_rows, :]
        for h in range(1, pieces):
            send_refs[h - 1][...] = acc[h * piece_rows : (h + 1) * piece_rows, :].astype(BF16)
        for store in stores:
            store.wait()

    return run(
        body,
        [second, second_t, grad, grad_t, acc_first, gs_first, up, up_b, down],
        after,
        in_specs=[VMEM] * 6 + [HBM, VMEM, HBM],
        out_specs=[VMEM] * (2 + pieces) + [HBM if units.packed else VMEM] * len(grads),
        out_shape=[
            sds((piece_rows, width), F32),
            sds((total, width), F32),
            sds((8, units.count), F32),
        ]
        + [sds((piece_rows, width), BF16)] * (pieces - 1)
        + grads,
        scratch_shapes=[pltpu.VMEM((total, width), F32)] + units.scratch(total, width),
        vmem=48,
        cost_estimate=cost(12 * total * width * units.count, 24 * 1024 * 1024, total * units.count),
        name="feed_second",
    )


def mid_back(mid, grad_second, received, grad_rows, gain, out_w, att_first, att_last, chunk):
    pieces = 1 + len(received)
    total, width = mid.shape
    piece_rows = total // pieces
    split = att_first.shape[1]
    wide = split + att_last.shape[1]

    def body(*refs):
        mid_ref, gs_ref, refs = refs[0], refs[1], refs[2:]
        recv_refs, refs = refs[: pieces - 1], refs[pieces - 1 :]
        go_ref, gain_ref, wo_ref, att_ref, last_ref = refs[:5]
        gm_ref, do_ref, sums_ref, *dwo_refs, low_ref = refs[5:]
        sums_ref[...] = jnp.zeros_like(sums_ref)
        for h in range(pieces):

            @pl.loop(0, piece_rows // ROWS)
            def _(i, h=h):
                at = pl.multiple_of(i * ROWS, ROWS)
                rows = pl.ds(h * piece_rows + at, ROWS)
                normed, inv_std = norm_rows(mid_ref[rows, :])
                grad = gs_ref[rows, :]
                for n in range(1, pieces):
                    src = pl.ds(((h - n) % pieces) * piece_rows + at, ROWS)
                    grad = grad + recv_refs[n - 1][src, :].astype(F32)
                go = go_ref[rows, :].astype(F32)
                grad_mid = go + norm_back(grad * gain_ref[...], normed, inv_std)
                low = grad_mid.astype(BF16)
                low_ref[rows, :] = low
                do_ref[rows, :] = dot_nt(low, wo_ref[...]).astype(BF16)
                if h == 0:
                    gm_ref[rows, :] = grad_mid
                    for n, item in enumerate((grad * normed, grad, low.astype(F32), go)):
                        sums_ref[n : n + 1, :] += jnp.sum(item, axis=0, keepdims=True)

        grad_out_w = jnp.concatenate(
            [
                dot(ref[...].astype(F32).T.astype(BF16), low_ref[...]).astype(BF16)
                for ref in (att_ref, last_ref)
            ],
            axis=0,
        )
        if chunk == 0:
            dwo_refs[0][...] = grad_out_w
            return
        _, part, _ = place(pieces)
        for c in range(pieces):

            @pl.when(part == c)
            def _(c=c):
                for n in range(dwo_refs[0].shape[0]):
                    for e in range(pieces):
                        at = (n * pieces + (c + e) % pieces) * chunk
                        dwo_refs[e][n] = grad_out_w[at : at + chunk, :]

    if chunk == 0:
        grads = [sds((wide, width), BF16)]
    else:
        grads = [sds((width // (pieces * pieces * chunk), chunk, width), BF16)] * pieces
    return run(
        body,
        [mid, grad_second, *received, grad_rows, gain, out_w, att_first, att_last],
        out_shape=[
            sds((piece_rows, width), F32),
            sds((total, wide), BF16),
            sds((8, width), F32),
        ]
        + grads,
        scratch_shapes=[pltpu.VMEM((total, width), BF16)],
        vmem=32,
        cost_estimate=cost(4 * total * width * wide, 14 * 1024 * 1024),
        name="mid_back",
    )


def attend_backward(qkv, grad_att, att, att_tile, logs, lane_first, tile, heads, head_dim, after=()):
    total = qkv.shape[0]
    per_tile = LANES // head_dim
    live = min(per_tile, heads - tile * per_tile)
    scale = head_dim ** (-0.5)
    exp_scale = scale * LOG2E

    def body(qkv_ref, do_ref, att_ref, lse_ref, out_ref, *scratch):
        km, vm, qm, dm, key_t, query_t, do_t, dq_t, lse_t, mean_t, grad_key, grad_val = scratch
        lane = lax.broadcasted_iota(jnp.int32, (1, LANES), 1)
        lse_t[...] = lse_ref[...].T
        query = qkv_ref[:, 0:LANES].astype(F32)
        key = qkv_ref[:, LANES : 2 * LANES].astype(F32)
        val = qkv_ref[:, 2 * LANES : 3 * LANES].astype(F32)
        upstream = do_ref[...].astype(F32)
        both_t = (upstream * att_ref[...].astype(F32)).T
        for j in range(live):
            mean_t[j : j + 1, :] = jnp.sum(
                both_t[j * head_dim : (j + 1) * head_dim, :], axis=0, keepdims=True
            )
        query_t[...] = query.T.astype(BF16)
        do_t[...] = upstream.T.astype(BF16)
        key_t[...] = key.T.astype(BF16)
        for j in range(live):
            mine = lane // head_dim == j
            km[j] = jnp.where(mine, key, 0.0).astype(BF16)
            vm[j] = jnp.where(mine, val, 0.0).astype(BF16)
            qm[j] = jnp.where(mine, query, 0.0).astype(BF16)
            dm[j] = jnp.where(mine, upstream, 0.0).astype(BF16)
        grad_key[...] = jnp.zeros_like(grad_key)
        grad_val[...] = jnp.zeros_like(grad_val)
        if live * head_dim < LANES:
            dq_t[...] = jnp.zeros_like(dq_t)

        def visit(some):
            ready = [(dot(km[j], query_t[...]), dot(vm[j], do_t[...])) for j in some]
            for (scores, grad_prob), j in zip(ready, some):
                own = pl.ds(pl.multiple_of(j * head_dim, head_dim), head_dim)
                probs = jnp.exp2(scores * exp_scale - lse_t[pl.ds(lane_first + j, 1), :])
                grad_scores = (probs * (grad_prob - mean_t[pl.ds(j, 1), :])).astype(BF16)
                grad_val[...] += dot(probs.astype(BF16), dm[j])
                grad_key[...] += dot(grad_scores, qm[j])
                dq_t[own, :] = dot(key_t[own, :], grad_scores)

        by_pairs(live, visit)
        out_ref[:, 0:LANES] = (dq_t[...].T * scale).astype(BF16)
        out_ref[:, LANES : 2 * LANES] = (grad_key[...] * scale).astype(BF16)
        out_ref[:, 2 * LANES : 3 * LANES] = grad_val[...].astype(BF16)

    masked = pltpu.VMEM((live, total, LANES), BF16)
    turned = pltpu.VMEM((LANES, total), BF16)
    turned_f = pltpu.VMEM((LANES, total), F32)
    return run(
        body,
        [qkv, grad_att, att, logs],
        after,
        grid=(1,),
        in_specs=[
            pl.BlockSpec((total, 3 * LANES), lambda i: (0, tile)),
            pl.BlockSpec((total, LANES), lambda i: (0, tile)),
            pl.BlockSpec((total, LANES), lambda i: (0, att_tile)),
            pl.BlockSpec((total, LANES), lambda i: (0, 0)),
        ],
        out_specs=pl.BlockSpec((total, 3 * LANES), lambda i: (0, 0)),
        out_shape=sds((total, 3 * LANES), BF16),
        scratch_shapes=[masked] * 4
        + [turned] * 3
        + [turned_f] * 2
        + [pltpu.VMEM((8, total), F32)]
        + [pltpu.VMEM((total, LANES), F32)] * 2,
        vmem=50,
        cost_estimate=cost(
            2 * live * total * total * 256 * 5, 3 * 1024 * 1024, live * total * total
        ),
        name="attend_backward",
    )


def project_back(
    rows_all, gain, shift, weight, grad_tiles, sums_mid, up_sums, pieces, quads, packed, real, after
):
    total, width = rows_all.shape
    piece_rows = total // pieces
    cols_all = weight.shape[1]
    tiles = len(grad_tiles)
    tile_cols = cols_all // tiles
    chunk = width // (quads * pieces)

    def body(*refs):
        x_ref, gain_ref, shift_ref, w_ref, mid_ref, *ups_refs = refs[:7]
        refs = refs[7:]
        dq_refs, refs = refs[:tiles], refs[tiles:]
        own_ref, refs = refs[0], refs[1:]
        send_refs, refs = refs[: pieces - 1], refs[pieces - 1 :]
        sums_ref, bias_ref, *dw_refs, low_t, part_ref = refs
        _, part, quad = place(pieces)
        sums_ref[...] = jnp.zeros_like(sums_ref)
        bias_ref[...] = jnp.zeros_like(bias_ref)
        for h in range(pieces):

            @pl.loop(0, piece_rows // ROWS)
            def _(i, h=h):
                at = pl.multiple_of(i * ROWS, ROWS)
                src = pl.ds(at, ROWS)
                rows = pl.ds(h * piece_rows + at, ROWS)
                normed, _ = norm_rows(x_ref[rows, :].astype(F32))
                low_t[:, rows] = (normed * gain_ref[...] + shift_ref[...]).T.astype(BF16)
                grad = jnp.zeros((ROWS, width), F32)
                for t in range(tiles):
                    grad_rows = dq_refs[t][rows, :]
                    cols = slice(t * tile_cols, (t + 1) * tile_cols)
                    grad = grad + dot_nt(grad_rows, w_ref[:, cols])
                    bias_ref[0:1, cols] += jnp.sum(grad_rows.astype(F32), axis=0, keepdims=True)
                if h == 0:
                    own_ref[src, :] = grad
                else:
                    send_refs[h - 1][src, :] = grad.astype(BF16)
                sums_ref[0:1, :] += jnp.sum(grad * normed, axis=0, keepdims=True)
                sums_ref[1:2, :] += jnp.sum(grad, axis=0, keepdims=True)

        for t in range(tiles):
            cols = slice(t * tile_cols, (t + 1) * tile_cols)
            part_ref[...] = dot(low_t[...], dq_refs[t][...]).astype(BF16)
            if not packed:
                dw_refs[0][:, cols] = part_ref[...]
                continue
            for c in range(pieces):

                @pl.when(part == c)
                def _(c=c, cols=cols):
                    for q in range(quads):
                        for e in range(pieces):
                            at = (q * pieces + (c + e) % pieces) * chunk
                            dw_refs[e][q ^ quad, :, cols] = part_ref[at : at + chunk, :]

        if not packed:
            return
        for row, src in ((4, 2), (5, 0), (6, 1), (15, 3)):
            sums_ref[row : row + 1, :] = mid_ref[src : src + 1, :]
        for c in range(pieces):

            @pl.when(part == c)
            def _(c=c):
                for row, p in ((2, 0), (3, 2)):
                    mine = jnp.concatenate(
                        [
                            bias_ref[0:1, (3 * t + p) * LANES :][:, : min(LANES, real - t * LANES)]
                            for t in range(tiles)
                        ],
                        axis=1,
                    )
                    sums_ref[row : row + 1, c * real : (c + 1) * real] = mine
                for n in range(quads):
                    row = 7 + n * pieces + c
                    start = 0
                    for ref in ups_refs:
                        size = ref.shape[1] // quads
                        here = ref[0:1, n * size : (n + 1) * size]
                        sums_ref[row : row + 1, start : start + size] = here
                        start += size

    if packed:
        grads = [sds((quads, chunk, cols_all), BF16)] * pieces
    else:
        grads = [sds((width, cols_all), BF16)]
    return run(
        body,
        [rows_all, gain, shift, weight, sums_mid, *up_sums, *grad_tiles],
        after,
        out_shape=[sds((piece_rows, width), F32)]
        + [sds((piece_rows, width), BF16)] * (pieces - 1)
        + [sds((16, width), F32), sds((8, cols_all), F32)]
        + grads,
        scratch_shapes=[pltpu.VMEM((width, total), BF16), pltpu.VMEM((width, tile_cols), BF16)],
        vmem=32,
        cost_estimate=cost(4 * total * width * cols_all, 10 * 1024 * 1024),
        name="project_back",
    )


def finish_rows(rows_all, gain, grad_mid, grad_own, received, count, after):
    rows, width = grad_mid.shape
    others = len(received)
    piece = rows // count
    per_step = ROWS // piece

    def body(*refs):
        x_ref, gain_ref, gm_ref, own_ref, refs = refs[0], refs[1], refs[2], refs[3], refs[4:]
        recv_refs, out_refs = refs[:others], refs[others:]
        for n in range(rows // ROWS):
            at = slice(n * ROWS, (n + 1) * ROWS)
            normed, inv_std = norm_rows(x_ref[at, :].astype(F32))
            grad = own_ref[at, :]
            for ref in recv_refs:
                grad = grad + ref[at, :].astype(F32)
            done = gm_ref[at, :] + norm_back(grad * gain_ref[...], normed, inv_std)
            for e in range(per_step):
                out_refs[n * per_step + e][...] = done[e * piece : (e + 1) * piece, :].astype(BF16)

    return run(
        body,
        [rows_all, gain, grad_mid, grad_own, *received],
        after,
        out_shape=[sds((piece, width), BF16)] * count,
        vmem=24,
        cost_estimate=cost(20 * rows * width, 6 * 1024 * 1024),
        name="finish_rows",
    )


def finish_result(own, received, count):
    rows, width = own.shape
    others = len(received)
    piece = rows // count

    def body(*refs):
        out_refs = refs[1 + others :]
        for n in range(count):
            at = slice(n * piece, (n + 1) * piece)
            total = refs[0][at, :]
            for ref in refs[1 : 1 + others]:
                total = total + ref[at, :].astype(F32)
            out_refs[n % 2][n // 2] = total.astype(BF16)

    return run(
        body,
        [own, *received],
        out_shape=[sds((count // 2, piece, width), BF16)] * 2,
        vmem=16,
        cost_estimate=cost(2 * rows * width, 3 * 1024 * 1024),
        name="finish_result",
    )


def pass_on(keep, received, after):
    def body(keep_ref, recv_ref, out_ref):
        out_ref[0] = keep_ref[1]
        out_ref[1] = recv_ref[1]

    return run(
        body,
        [keep, received],
        after,
        out_shape=sds(keep.shape, keep.dtype),
        vmem=16,
        cost_estimate=cost(0, 4 * keep.size),
        name="pass_on",
    )


def collect_halves(keep, near, far, group, after):
    _, rows, width = keep.shape

    def body(keep_ref, near_ref, far_ref, out_ref):
        _, _, quad = place(group)
        out_ref[quad] = keep_ref[0]
        out_ref[quad ^ 1] = near_ref[0]
        out_ref[quad ^ 2] = far_ref[0]
        out_ref[quad ^ 3] = far_ref[1]

    return run(
        body,
        [keep, near, far],
        after,
        out_shape=sds((4, rows, width), keep.dtype),
        vmem=16,
        cost_estimate=cost(0, 16 * rows * width),
        name="collect_halves",
    )


def two_parts(item):
    first = item.astype(BF16)
    return first, (item - first.astype(F32)).astype(BF16)


def pack_attention(qkv_keep, qkv_recv, out_keep, out_recv, small, small_recv, real, blocks):
    quads, chunk, cols_all = qkv_keep.shape
    wide = cols_all // 3
    tiles = wide // LANES
    width = out_keep.shape[2]
    qkv_lanes = 6 * real // blocks
    out_lanes = width // blocks
    lanes = qkv_lanes + out_lanes
    halves = quads // 2
    slot = halves * chunk
    small_rows = small.shape[0]

    def body(qk_ref, qr_ref, ok_ref, or_ref, small_ref, srecv_ref, *out_refs):
        _, part, quad = place(2)
        mine = lax.axis_index("batch")
        slots = out_refs[4]

        def heads_of(rows, p):
            return [
                rows[:, (3 * t + p) * LANES : (3 * t + p) * LANES + min(LANES, real - t * LANES)]
                for t in range(tiles)
            ]

        for c in range(2):

            @pl.when(part == c)
            def _(c=c):
                for q in range(quads):
                    pair = (qk_ref[q], qr_ref[q])
                    if c == 1:
                        pair = pair[::-1]
                    parts = []
                    for p in range(3):
                        parts += heads_of(pair[0], p) + heads_of(pair[1], p)
                    row = jnp.concatenate(parts, axis=1)
                    for b in range(blocks):
                        slots[b ^ mine, q, :, 0:qkv_lanes] = row[
                            :, b * qkv_lanes : (b + 1) * qkv_lanes
                        ]
                for e, ref in enumerate((ok_ref, or_ref)):
                    for n in range(halves):
                        q = ((c + e) % 2) * halves + n
                        for b in range(blocks):
                            slots[b ^ mine, q ^ quad, :, qkv_lanes:lanes] = ref[
                                n, :, b * out_lanes : (b + 1) * out_lanes
                            ]

        for n, order in enumerate(((0, 2), (1, 3), (0, 1), (2, 3))):
            for e in range(2):
                for f in range(halves):
                    at = e * slot + f * chunk
                    src = f if n < 2 else halves + f
                    out_refs[n][at : at + chunk, :] = slots[order[e], src]
        parts = two_parts(small_ref[...] + srecv_ref[...])
        for n in range(2):
            for e in range(2):
                at = 2 * slot + e * small_rows
                out_refs[n][at : at + small_rows, :] = parts[e]

    first = sds((2 * slot + 2 * small_rows, lanes), BF16)
    other = sds((2 * slot, lanes), BF16)
    return run(
        body,
        [qkv_keep, qkv_recv, out_keep, out_recv, small, small_recv],
        out_shape=[first, first, other, other],
        scratch_shapes=[pltpu.VMEM((blocks, quads, chunk, lanes), BF16)],
        vmem=24,
        cost_estimate=cost(0, 4 * 1024 * 1024),
        name="pack_attention",
    )


def sum_first(keeps, received, after=(), lower=None):
    count = len(keeps)
    shape = keeps[0].shape[1:]
    extra = [] if lower is None else [lower]

    def body(*refs):
        outs = refs[2 * count + len(extra) :]
        for n in range(count):
            for e in range(2):
                total = refs[n][e].astype(F32) + refs[count + n][e].astype(F32)
                outs[2 * n + e][...] = total.astype(BF16)
        if extra:
            outs[-1][...] = refs[2 * count][...].astype(BF16)

    return run(
        body,
        [*keeps, *received, *extra],
        after,
        out_shape=[sds(shape, BF16)] * (2 * count) + [sds(item.shape, BF16) for item in extra],
        vmem=32,
        cost_estimate=cost(0, 6 * count * keeps[0].size),
        name="sum_first",
    )


def sum_second(keeps, received, after=()):
    quads, rows, width = keeps[0].shape

    def body(ka, kb, ra, rb, keep_ref, send_ref):
        for d in range(quads):
            ref = send_ref if d % 2 else keep_ref
            for e, (keep, recv) in enumerate(((ka, ra), (kb, rb))):
                total = keep[d].astype(F32) + recv[d].astype(F32)
                ref[d // 2, e] = total.astype(BF16)

    return run(
        body,
        [*keeps, *received],
        after,
        out_shape=[sds((quads // 2, 2, rows, width), BF16)] * 2,
        vmem=24,
        cost_estimate=cost(0, 12 * keeps[0].size),
        name="sum_second",
    )


def sum_third(keep, received, after=()):
    def body(keep_ref, recv_ref, stay_ref, pass_ref):
        for ref, e in ((stay_ref, 0), (pass_ref, 1)):
            ref[...] = (keep_ref[e].astype(F32) + recv_ref[e].astype(F32)).astype(BF16)

    return run(
        body,
        [keep, received],
        after,
        out_shape=[sds(keep.shape[1:], BF16)] * 2,
        vmem=16,
        cost_estimate=cost(0, 6 * keep.size),
        name="sum_third",
    )


def small_sum(refs, rows, count):
    total = None
    for ref in refs:
        for e in range(2):
            item = ref[rows + e * count : rows + (e + 1) * count, :].astype(F32)
            total = item if total is None else total + item
    return total


def sum_first_attention(keeps, received, slot, small_rows, after):
    lanes = keeps[0].shape[1]

    def body(ka, kb, ra, rb, stay_a, pass_a, stay_b, pass_b):
        parts = two_parts(small_sum((ka, ra), 2 * slot, small_rows))
        for keep, recv, stay, on in ((ka, ra, stay_a, pass_a), (kb, rb, stay_b, pass_b)):
            for e, ref in enumerate((stay, on)):
                at = slice(e * slot, (e + 1) * slot)
                ref[0:slot, :] = (keep[at, :].astype(F32) + recv[at, :].astype(F32)).astype(BF16)
        for ref in (stay_a, pass_a):
            for e in range(2):
                ref[slot + e * small_rows : slot + (e + 1) * small_rows, :] = parts[e]

    first = sds((slot + 2 * small_rows, lanes), BF16)
    other = sds((slot, lanes), BF16)
    return run(
        body,
        [*keeps, *received],
        after,
        out_shape=[first, first, other, other],
        vmem=16,
        cost_estimate=cost(0, 3 * 1024 * 1024),
        name="sum_first_attention",
    )


def sum_second_attention(keeps, received, chunk, quads, small_rows):
    lanes = keeps[0].shape[1]
    halves = quads // 2
    slot = halves * chunk

    def body(ka, kb, ra, rb, *out_refs):
        parts = two_parts(small_sum((ka, ra), slot, small_rows))
        for d in range(quads):
            keep, recv = ((ka, ra), (kb, rb))[d // halves]
            at = slice(d % halves * chunk, (d % halves + 1) * chunk)
            total = keep[at, :].astype(F32) + recv[at, :].astype(F32)
            out_refs[d][0:chunk, :] = total.astype(BF16)
            for e in range(2):
                at = chunk + e * small_rows
                out_refs[d][at : at + small_rows, :] = parts[e]

    return run(
        body,
        [*keeps, *received],
        out_shape=[sds((chunk + 2 * small_rows, lanes), BF16)] * quads,
        vmem=16,
        cost_estimate=cost(0, 2 * 1024 * 1024),
        name="sum_second_attention",
    )


def final_attention(pieces, chunk, qkv_lanes, small_rows):
    lanes = pieces[0].shape[1]
    count = len(pieces)

    def body(*refs):
        total = refs[0][0:chunk, :].astype(F32)
        for ref in refs[1:count]:
            total = total + ref[0:chunk, :].astype(F32)
        refs[count][...] = total[:, :qkv_lanes]
        refs[count + 1][...] = total[:, qkv_lanes:]
        refs[count + 2][...] = small_sum(refs[:count], chunk, small_rows)

    return run(
        body,
        pieces,
        out_shape=[
            sds((chunk, qkv_lanes), F32),
            sds((chunk, lanes - qkv_lanes), F32),
            sds((small_rows, lanes), F32),
        ],
        vmem=16,
        cost_estimate=cost(0, 1024 * 1024),
        name="final_attention",
    )


def final_units(first, second, after):
    high = first[0].shape[1]
    sizes = [first[0].shape[2], second[0].shape[2]]
    unit_block = sum(sizes)
    count = len(first)
    half = high // 2

    def body(*refs):
        _, part, _ = place(2)
        keep_ref, send_ref, down_ref = refs[2 * count :]
        for h in range(2):
            pieces = refs[h * count : (h + 1) * count]
            up, down = pieces[0][0].astype(F32), pieces[0][1].astype(F32)
            for ref in pieces[1:]:
                up = up + ref[0].astype(F32)
                down = down + ref[1].astype(F32)
            here = slice(h * sizes[0], h * sizes[0] + sizes[h])
            down_ref[here, :] = down.T
            for c in range(2):

                @pl.when(part == c)
                def _(up=up, here=here, c=c):
                    keep_ref[:, here] = up[c * half : (c + 1) * half, :]
                    send_ref[:, here] = up[(1 - c) * half : (2 - c) * half, :].astype(BF16)

    return run(
        body,
        [*first, *second],
        after,
        out_shape=[
            sds((half, unit_block), F32),
            sds((half, unit_block), BF16),
            sds((unit_block, high), F32),
        ],
        vmem=24,
        cost_estimate=cost(0, 4 * 1024 * 1024),
        name="final_units",
    )


def final_join(keep, recv):
    chunk, unit_block = keep.shape

    def body(keep_ref, recv_ref, out_ref):
        _, part, _ = place(2)
        for c in range(2):

            @pl.when(part == c)
            def _(c=c):
                out_ref[:, c * unit_block : (c + 1) * unit_block] = keep_ref[...]
                out_ref[:, (1 - c) * unit_block : (2 - c) * unit_block] = recv_ref[...].astype(F32)

    return run(
        body,
        [keep, recv],
        out_shape=sds((chunk, 2 * unit_block), F32),
        vmem=16,
        cost_estimate=cost(0, 1024 * 1024),
        name="final_join",
    )


def on_device(
    tokens,
    mask,
    cotangent,
    ln1_gain,
    ln1_bias,
    qkv_weight,
    q_bias,
    v_bias,
    out_weight,
    out_bias,
    ln2_gain,
    ln2_bias,
    up_weight,
    up_bias,
    down_weight,
    down_bias,
):
    seq_size = lax.axis_size("seq")
    batch_size = lax.axis_size("batch")
    micro_count, seq_count, local_len, width = tokens.shape
    sequences = micro_count * seq_count
    group = seq_size // sequences
    units = up_weight.shape[1]
    head_dim = width // HEADS
    heads = HEADS // group
    real = heads * head_dim
    wide = -(-real // LANES) * LANES
    full_len = local_len * seq_size
    block_len = local_len // group
    rows = seq_size * block_len
    own_units = units // group
    part = lax.axis_index("seq") % group
    aligned = (
        seq_size == batch_size * group
        and group == 2
        and batch_size == 4
        and wide == 3 * LANES
        and (seq_size // group) % group == 0
        and units % (batch_size * group * LANES) == 0
        and own_units // batch_size == width
    )

    def from_part(item, ahead):
        if ahead % group == 0:
            return item
        pairs = [
            (q * group + (c + ahead) % group, q * group + c)
            for q in range(sequences)
            for c in range(group)
        ]
        return lax.ppermute(item, "seq", pairs)

    def gather_parts(item):
        return [from_part(item, n) for n in range(group)]

    def row_of(item):
        return item.astype(F32)[None, :]

    def blocks_of(item):
        return item.reshape(sequences, local_len, width)

    x_own = over_quads(deal(blocks_of(tokens), group), group)
    x_pieces = [from_part(item, n) for n in range(group) for item in x_own]

    count_rows = jnp.sum(mask, axis=2).reshape(sequences).astype(BF16)
    cot_low = jnp.where(mask[..., None] != 0, cotangent, jnp.zeros_like(cotangent))
    cot_send = jnp.concatenate(
        [blocks_of(cot_low), jnp.broadcast_to(count_rows[:, None, None], (sequences, 16, width))],
        axis=1,
    )
    cot_own = over_quads(deal(cot_send, group, x_pieces[sequences:]), group)

    qkv_w, qkv_b, *out_w = pick_weights(
        qkv_weight,
        jnp.concatenate([q_bias, jnp.zeros_like(q_bias), v_bias])[None, :],
        out_weight,
        group,
        real,
        wide,
    )
    if aligned:
        up_own, up_b, down_own = up_weight, up_bias[None, :], down_weight
    else:

        def own_columns(matrix, blocks):
            split = matrix.reshape(matrix.shape[0], blocks, group, -1)
            return lax.dynamic_index_in_dim(split, part, 2, keepdims=False)

        up_own = own_columns(up_weight, batch_size).reshape(width, own_units)
        up_b = own_columns(up_bias[None, :], batch_size).reshape(1, own_units)
        down_own = lax.dynamic_index_in_dim(
            down_weight.reshape(batch_size, group, -1, width), part, 1, keepdims=False
        ).reshape(own_units, width)

    tiles = wide // LANES
    x_all, qkv, att_first, logs_first = attend_first(
        x_pieces, row_of(ln1_gain), row_of(ln1_bias), qkv_w, qkv_b, tiles - 1, heads, head_dim
    )
    cot_stack = stack(cot_own, [logs_first])
    att_last, logs_last = attend_last(qkv, tiles - 1, heads, head_dim, [cot_stack])
    cot_pieces = cot_own + [
        item[d]
        for item in gather_parts(cot_stack)[1:]
        for d in range(sequences)
    ]
    blocks = batch_size if aligned else 1
    unit_block = own_units // blocks
    size = unit_block * 2 // 5
    shape = (group, sequences if aligned else None, width // sequences)
    calls = [
        Units(unit_block, blocks, 0, size, *shape),
        Units(unit_block, blocks, size, unit_block - size, *shape),
    ]
    mid, second, second_t, grad_rows, grad_t, acc, grad_second, *found = feed_first(
        x_all,
        gather_parts(att_first),
        gather_parts(att_last),
        cot_pieces,
        out_w,
        row_of(out_bias),
        row_of(ln2_gain),
        row_of(ln2_bias),
        up_own,
        up_b,
        down_own,
        row_of(down_bias),
        calls[0],
    )
    up_sums, ff_grads = [found[0]], [found[1:]]
    result_own, grad_second, *found = feed_second(
        second,
        second_t,
        grad_rows,
        grad_t,
        acc,
        grad_second,
        up_own,
        up_b,
        down_own,
        calls[1],
        group,
        [],
    )
    up_sums.append(found[0])
    result_send = found[1:group]
    ff_grads.append(found[group:])

    if aligned:
        first_swaps = [
            [swap(item[1], "batch", batch_size, 1), swap(item[3], "batch", batch_size, 2)]
            for item in ff_grads
        ]

        def begin_sum(e, after, lower=None):
            stay_a, pass_a, stay_b, pass_b, *low = sum_first(
                [ff_grads[e][0], ff_grads[e][2]], first_swaps[e], after, lower
            )
            moved = [swap(pass_a, "batch", batch_size, 2), swap(pass_b, "batch", batch_size, 1)]
            return [[stay_a, stay_b], moved], low

        waiting, (second_send,) = begin_sum(0, [], grad_second)
    else:
        second_send = grad_second.astype(BF16)
    second_recv = [from_part(second_send, n) for n in range(1, group)]
    result_recv = [from_part(result_send[group - n - 1], n) for n in range(1, group)]
    result_keep, result_pass = finish_result(result_own, result_recv, sequences)

    def quad_swap(item, distance):
        return swap(item, "seq", seq_size, distance * group)

    result_near = quad_swap(result_pass, 1)

    chunk = width // seq_size
    grad_mid, grad_att, sums_mid, *out_grad = mid_back(
        mid,
        grad_second,
        second_recv,
        grad_rows,
        row_of(ln2_gain),
        out_w[0],
        att_first,
        att_last,
        chunk if aligned else 0,
    )

    def tile_back(t, after):
        last = t == tiles - 1
        return attend_backward(
            qkv,
            grad_att,
            att_last if last else att_first,
            0 if last else t,
            logs_last if last else logs_first,
            0 if last else t * (LANES // head_dim),
            t,
            heads,
            head_dim,
            after,
        )

    grad_tiles = [None] * tiles
    grad_tiles[-1] = tile_back(tiles - 1, [result_keep])
    result_pass = pass_on(result_keep, result_near, grad_tiles[-1:])
    result_far = quad_swap(result_pass, 2)
    after = [result_pass]
    if aligned:
        keep, send = sum_second(*waiting, [grad_tiles[-1]])
        moved = quad_swap(send, 1)
        out_recv = from_part(out_grad[1], 1)
        after = [keep, result_pass]
    grad_tiles[0] = tile_back(0, after)
    after = [result_far]
    if aligned:
        waiting, _ = begin_sum(1, [grad_tiles[0]])
        unit_first = list(sum_third(keep, moved, [grad_tiles[0]]))
        unit_first[1] = quad_swap(unit_first[1], 2)
        after = waiting[0][:1] + unit_first[:1]
    for t in range(1, tiles - 1):
        grad_tiles[t] = tile_back(t, after)
    after = [result_far]
    if aligned:
        keep, send = sum_second(*waiting, [grad_tiles[-2]])
        moved = quad_swap(send, 1)
        after = [keep, unit_first[1], result_far, out_recv]
    found = project_back(
        x_all,
        row_of(ln1_gain),
        row_of(ln1_bias),
        qkv_w,
        grad_tiles,
        sums_mid,
        up_sums,
        group,
        sequences,
        aligned,
        real,
        after,
    )
    first_own, first_send = found[0], found[1:group]
    small, bias_sums, *qkv_grad = found[group:]
    first_recv = [from_part(first_send[group - n - 1], n) for n in range(1, group)]
    after = []
    if aligned:
        small_rows = small.shape[0]
        packed = pack_attention(
            qkv_grad[0],
            from_part(qkv_grad[1], 1),
            out_grad[0],
            out_recv,
            small,
            from_part(small, 1),
            real,
            batch_size,
        )
        unit_second = list(sum_third(keep, moved, packed[:1]))
        unit_second[1] = quad_swap(unit_second[1], 2)
        after = unit_second[:1]
    row_parts = finish_rows(
        x_all, row_of(ln1_gain), grad_mid, first_own, first_recv, sequences, after
    )
    row_moved = over_quads(row_parts, group)
    if aligned:
        stay_a, pass_a, stay_b, pass_b = sum_first_attention(
            [packed[0], packed[2]],
            [swap(packed[1], "batch", batch_size, 1), swap(packed[3], "batch", batch_size, 2)],
            sequences // 2 * chunk,
            small_rows,
            row_parts[:1],
        )
        summed = sum_second_attention(
            [stay_a, stay_b],
            [swap(pass_a, "batch", batch_size, 2), swap(pass_b, "batch", batch_size, 1)],
            chunk,
            sequences,
            small_rows,
        )
        after = summed[:1]
        up_keep, up_send, down_grad = final_units(unit_first, unit_second, after)
        up_grad = final_join(up_keep, from_part(up_send, 1))
        qkv_final, out_final, small = final_attention(
            over_quads(summed, group), chunk, qkv_weight.shape[1] // batch_size, small_rows
        )
        small = small.reshape(-1)
    result = collect_halves(result_keep, result_near, result_far, group, after)
    result = result.reshape(tokens.shape)
    grad_in = collect(row_moved, group, after).reshape(tokens.shape)
    if not aligned:

        def spread(item, blocks):
            split = item.reshape(blocks, 1, -1)
            empty = jnp.zeros((blocks, group, split.shape[2]), F32)
            return lax.dynamic_update_slice(empty, split, (0, part, 0)).reshape(-1)

        bias_sums = bias_sums[0].reshape(tiles, 3, LANES).transpose(1, 0, 2)
        bias_sums = bias_sums.reshape(3, wide)[:, :real]
        small = jnp.concatenate(
            [
                small[0],
                small[1],
                spread(bias_sums[0], 1),
                spread(bias_sums[2], 1),
                sums_mid[2],
                sums_mid[0],
                sums_mid[1],
                spread(jnp.concatenate([item[0] for item in up_sums]), batch_size),
                sums_mid[3],
            ]
        )

        def scattered(item):
            item = lax.psum_scatter(item.astype(BF16), "seq", scatter_dimension=0, tiled=True)
            return lax.psum_scatter(item, "batch", scatter_dimension=1, tiled=True).astype(F32)

        def spread_columns(item, blocks):
            split = item.reshape(item.shape[0], blocks, 1, -1)
            empty = jnp.zeros((item.shape[0], blocks, group, split.shape[3]), item.dtype)
            filled = lax.dynamic_update_slice(empty, split, (0, 0, part, 0))
            return filled.reshape(item.shape[0], -1)

        up_full, down_full = [
            jnp.concatenate([item[e] for item in ff_grads], axis=1) for e in range(2)
        ]
        up_grad = scattered(spread_columns(up_full, batch_size))
        down_grad = scattered(spread_columns(down_full, batch_size).T)
        rows_full = qkv_grad[0].reshape(width, tiles, 3, LANES).transpose(0, 2, 1, 3)
        rows_full = rows_full.reshape(width, 3, wide)[..., :real]
        qkv_final = scattered(spread_columns(rows_full.reshape(width, -1), 3))
        out_final = scattered(spread_columns(out_grad[0][:real].T, 1).T)
        small = lax.psum(small, ("seq", "batch"))

    edges = [width] * 7 + [units, width]
    pieces, start = [], 0
    for size in edges:
        pieces.append(small[start : start + size])
        start += size
    return (
        result,
        grad_in,
        pieces[0],
        pieces[1],
        qkv_final,
        pieces[2],
        pieces[3],
        out_final,
        pieces[4],
        pieces[5],
        pieces[6],
        up_grad,
        pieces[7],
        down_grad,
        pieces[8],
    )


def solution(mesh):
    rows = P(None, "batch", "seq", None)
    split = P("seq", "batch")
    in_specs = (rows, P(None, "batch", "seq"), rows) + (P(),) * 13
    out_specs = (
        rows,
        rows,
        P(),
        P(),
        split,
        P(),
        P(),
        split,
        P(),
        P(),
        P(),
        split,
        P(),
        split,
        P(),
    )
    return jax.shard_map(
        on_device, mesh=mesh, in_specs=in_specs, out_specs=out_specs, check_vma=False
    )
```

```python
import jax
import jax.numpy as jnp
from jax import lax
from jax.experimental import pallas as pl
from jax.experimental.pallas import tpu as pltpu
from jax.sharding import PartitionSpec as P

HEADS = 20
EPS = 1e-05
LOG2E = 1.4426950408889634
ROWS = 256
F32 = jnp.float32
BF16 = jnp.bfloat16
LANES = 128


def dot(left, right):
    return jnp.dot(left, right, preferred_element_type=F32)


def dot_nt(left, right):
    return lax.dot_general(left, right, (((1,), (1,)), ((), ())), preferred_element_type=F32)


def norm_rows(rows_in):
    mean_val = jnp.mean(rows_in, axis=-1, keepdims=True)
    centered = rows_in - mean_val
    inv_std = lax.rsqrt(jnp.mean(centered * centered, axis=-1, keepdims=True) + EPS)
    return centered * inv_std, inv_std


def norm_back(scaled, normed, inv_std):
    inner = (
        scaled
        - jnp.mean(scaled, axis=-1, keepdims=True)
        - normed * jnp.mean(scaled * normed, axis=-1, keepdims=True)
    )
    return inner * inv_std


def params_of(mib):
    return pltpu.CompilerParams(vmem_limit_bytes=mib * 1024 * 1024)


def cost(flops, moved, trans=0, part=1):
    return pl.CostEstimate(
        flops=flops // part, bytes_accessed=moved // part, transcendentals=trans // part
    )


def sds(shape, dtype):
    return jax.ShapeDtypeStruct(shape, dtype)


VMEM = pl.BlockSpec(memory_space=pltpu.VMEM)
HBM = pl.BlockSpec(memory_space=pl.ANY)


def run(body, operands, after=(), in_specs=None, out_specs=None, vmem=32, **more):
    count, extra = len(operands), len(after)

    def inner(*refs):
        body(*refs[:count], *refs[count + extra :])

    specs = [VMEM] * count if in_specs is None else list(in_specs)
    shapes = more["out_shape"]
    if out_specs is None:
        out_specs = [VMEM] * len(shapes) if isinstance(shapes, (list, tuple)) else VMEM
    return pl.pallas_call(
        inner,
        in_specs=specs + [HBM] * extra,
        out_specs=out_specs,
        compiler_params=params_of(vmem),
        **more,
    )(*operands, *after)


def gate(items, after):
    def body(*refs):
        del refs

    return pl.pallas_call(
        body,
        in_specs=[HBM] * (len(items) + len(after)),
        out_specs=[HBM] * len(items),
        out_shape=[sds(item.shape, item.dtype) for item in items],
        input_output_aliases={n: n for n in range(len(items))},
        cost_estimate=cost(0, 0),
        name="gate",
    )(*items, *after)


def place(group):
    spot = lax.axis_index("seq")
    return spot, lax.rem(spot, group), lax.div(spot, group)


def deal(item, group, after=()):
    count, rows, width = item.shape

    def body(in_ref, *out_refs):
        _, _, quad = place(group)
        for d in range(count):
            out_refs[d][...] = in_ref[quad ^ d]

    return run(
        body,
        [item],
        after,
        out_shape=[sds((rows, width), item.dtype)] * count,
        vmem=16,
        cost_estimate=cost(0, 4 * count * rows * width),
        name="deal",
    )


def collect(pieces, group, after=()):
    count = len(pieces)
    rows, width = pieces[0].shape

    def body(*refs):
        _, _, quad = place(group)
        for d in range(count):
            refs[count][quad ^ d] = refs[d][...]

    return run(
        body,
        pieces,
        after,
        out_shape=sds((count, rows, width), pieces[0].dtype),
        vmem=16,
        cost_estimate=cost(0, 4 * count * rows * width),
        name="collect",
    )


def stack(pieces, after):
    count = len(pieces)

    def body(*refs):
        for d in range(count):
            refs[count][d] = refs[d][...]

    return run(
        body,
        pieces,
        after,
        out_shape=sds((count,) + pieces[0].shape, pieces[0].dtype),
        vmem=16,
        cost_estimate=cost(0, 4 * count * pieces[0].size),
        name="stack",
    )


def swap(item, axis, size, distance):
    return lax.ppermute(item, axis, [(i, i ^ distance) for i in range(size)])


def over_quads(pieces, group):
    return [
        piece if d == 0 else swap(piece, "seq", len(pieces) * group, d * group)
        for d, piece in enumerate(pieces)
    ]


def pick_weights(qkv_weight, qkv_bias, out_weight, group, real, wide):
    width = qkv_weight.shape[0]
    tiles = wide // LANES

    def body(w_ref, b_ref, o_ref, wo_ref, bo_ref, *out_refs):
        _, part, _ = place(group)
        wo_ref[...] = jnp.zeros_like(wo_ref)
        bo_ref[...] = jnp.zeros_like(bo_ref)
        for ref in out_refs:
            ref[...] = jnp.zeros_like(ref)
        for c in range(group):

            @pl.when(part == c)
            def _(c=c):
                for p in range(3):
                    for t in range(tiles):
                        some = min(LANES, real - t * LANES)
                        src = p * width + c * real + t * LANES
                        dst = (3 * t + p) * LANES
                        wo_ref[:, dst : dst + some] = w_ref[:, src : src + some]
                        bo_ref[:, dst : dst + some] = b_ref[:, src : src + some]
                for n in range(group):
                    src = (c + n) % group * real
                    out_refs[n][0:real, :] = o_ref[src : src + real, :]

    return pl.pallas_call(
        body,
        out_shape=[sds((width, 3 * wide), BF16), sds((1, 3 * wide), F32)]
        + [sds((wide, width), BF16)] * group,
        compiler_params=params_of(24),
        cost_estimate=cost(0, 8 * 1024 * 1024),
        name="pick_weights",
    )(qkv_weight, qkv_bias, out_weight)


def by_pairs(live, visit):
    size = 2 if live % 2 == 0 else 1

    @pl.loop(0, live // size)
    def _(i):
        visit([i * size + e for e in range(size)])


def attend_tiles(query_at, keys_at, vals_at, att_ref, lse_ref, keys, vals, acc, tiles, heads, head_dim):
    per_tile = LANES // head_dim
    total = att_ref.shape[0]
    exp_scale = head_dim ** (-0.5) * LOG2E
    lane = lax.broadcasted_iota(jnp.int32, (1, LANES), 1)
    row = lax.broadcasted_iota(jnp.int32, (LANES, 1), 0)
    lse_ref[...] = jnp.zeros_like(lse_ref)
    vals[:, :, LANES:] = jnp.ones((per_tile, total, LANES), BF16)
    for n, t in enumerate(tiles):
        live = min(per_tile, heads - t * per_tile)
        key_t = keys_at(n).astype(F32).T
        val_f = vals_at(n).astype(F32)
        for j in range(live):
            keys[j] = jnp.where(row // head_dim == j, key_t, 0.0).astype(BF16)
            vals[j, :, :LANES] = jnp.where(lane // head_dim == j, val_f, 0.0).astype(BF16)
        acc[...] = jnp.zeros_like(acc)

        def visit(some, n=n):
            scores = [dot(query_at(n), keys[j]) for j in some]
            for item, j in zip(scores, some):
                row_max = jnp.max(item, axis=-1, keepdims=True) * exp_scale
                expd = jnp.exp2(item * exp_scale - row_max).astype(BF16)
                mixed = dot(expd, vals[j])
                den = mixed[:, LANES:]
                acc[...] += mixed[:, :LANES] / den
                lse_ref[...] = jnp.where(
                    lane == n * per_tile + j, row_max + jnp.log2(den), lse_ref[...]
                )

        by_pairs(live, visit)
        att_ref[:, n * LANES : (n + 1) * LANES] = acc[...].astype(BF16)


def attend_scratch(total, head_dim):
    per_tile = LANES // head_dim
    return [
        pltpu.VMEM((per_tile, LANES, total), BF16),
        pltpu.VMEM((per_tile, total, 2 * LANES), BF16),
        pltpu.VMEM((total, LANES), F32),
    ]


def attend_first(x_pieces, gain, shift, weight, bias, tiles, heads, head_dim):
    count = len(x_pieces)
    piece_rows, width = x_pieces[0].shape
    total = count * piece_rows
    cols_all = weight.shape[1]

    def body(*refs):
        x_refs = refs[:count]
        gain_ref, shift_ref, w_ref, bias_ref = refs[count : count + 4]
        x_ref, qkv_ref, att_ref, lse_ref, keys, vals, acc = refs[count + 4 :]
        for n in range(count):
            x_ref[n * piece_rows : (n + 1) * piece_rows, :] = x_refs[n][...]

        @pl.loop(0, total // ROWS)
        def _(i):
            rows = pl.ds(pl.multiple_of(i * ROWS, ROWS), ROWS)
            normed, _ = norm_rows(x_ref[rows, :].astype(F32))
            low = (normed * gain_ref[...] + shift_ref[...]).astype(BF16)
            qkv_ref[rows, :] = (dot(low, w_ref[...]) + bias_ref[...]).astype(BF16)

        def columns(at):
            return slice(at * LANES, (at + 1) * LANES)

        attend_tiles(
            lambda n: qkv_ref[:, columns(3 * n)],
            lambda n: qkv_ref[:, columns(3 * n + 1)],
            lambda n: qkv_ref[:, columns(3 * n + 2)],
            att_ref,
            lse_ref,
            keys,
            vals,
            acc,
            range(tiles),
            heads,
            head_dim,
        )

    return run(
        body,
        [*x_pieces, gain, shift, weight, bias],
        out_shape=[
            sds((total, width), BF16),
            sds((total, cols_all), BF16),
            sds((total, tiles * LANES), BF16),
            sds((total, LANES), F32),
        ],
        scratch_shapes=attend_scratch(total, head_dim),
        vmem=30,
        cost_estimate=cost(
            2 * total * width * cols_all + 4 * heads * total * total * 256,
            8 * 1024 * 1024,
            heads * total * total,
        ),
        name="attend_first",
    )


def attend_last(qkv, tile, heads, head_dim, after):
    total = qkv.shape[0]

    def body(qkv_ref, att_ref, lse_ref, keys, vals, acc):
        attend_tiles(
            lambda n: qkv_ref[:, 0:LANES],
            lambda n: qkv_ref[:, LANES : 2 * LANES],
            lambda n: qkv_ref[:, 2 * LANES : 3 * LANES],
            att_ref,
            lse_ref,
            keys,
            vals,
            acc,
            [tile],
            heads,
            head_dim,
        )

    live = heads - tile * (LANES // head_dim)
    return run(
        body,
        [qkv],
        after,
        grid=(1,),
        in_specs=[pl.BlockSpec((total, 3 * LANES), lambda i: (0, tile))],
        out_specs=[pl.BlockSpec((total, LANES), lambda i: (0, 0))] * 2,
        out_shape=[sds((total, LANES), BF16), sds((total, LANES), F32)],
        scratch_shapes=attend_scratch(total, head_dim),
        vmem=26,
        cost_estimate=cost(4 * live * total * total * 256, 2 * 1024 * 1024, live * total * total),
        name="attend_last",
    )


def gelu_parts(value):
    size = jnp.abs(value)
    near = pl.reciprocal(1.0 + (0.3275911 * 0.7071067811865476) * size, approx=True)
    bell = jnp.exp2(value * value * (-0.5 * LOG2E))
    poly = near * (
        0.5 * 0.254829592
        + near
        * (
            0.5 * -0.284496736
            + near * (0.5 * 1.421413741 + near * (0.5 * -1.453152027 + near * (0.5 * 1.061405429)))
        )
    )
    tail = poly * bell
    area = jnp.where(value < 0.0, tail, 1.0 - tail)
    return value * area, area + value * bell * 0.3989422804014327


class Units:
    def __init__(self, block, blocks, start, size, stride, quads, high):
        self.block, self.blocks, self.start, self.size = block, blocks, start, size
        self.stride, self.quads, self.high = stride, quads, high
        self.count = blocks * size
        self.chunk = 512 if self.count % 512 == 0 else 256
        self.packed = quads is not None

    def loads(self, part, hbm_up, hbm_down, hbm_bias, up_ref, down_ref, bias_ref, sem):
        copies = []
        for b in range(self.blocks):
            src = self.start
            if self.packed:
                src = pl.multiple_of((b * self.stride + part) * self.block, LANES) + self.start
            src = pl.ds(src, self.size)
            dst = pl.ds(b * self.size, self.size)
            copies.append(
                pltpu.make_async_copy(hbm_up.at[:, src], up_ref.at[:, dst], sem.at[2 * b])
            )
            copies.append(
                pltpu.make_async_copy(hbm_down.at[src, :], down_ref.at[dst, :], sem.at[2 * b + 1])
            )
            bias_ref[0:1, dst] = hbm_bias[:, src]
        return copies

    def grad_shapes(self, width):
        if self.packed:
            return [sds((2, self.quads, self.high, self.size), BF16)] * 4
        return [sds((width, self.count), BF16)] * 2

    def scratch(self, total, width):
        grads = (self.blocks, self.quads, self.high, self.size) if self.packed else (8, LANES)
        return [
            pltpu.VMEM(grads, BF16),
            pltpu.VMEM(grads, BF16),
            pltpu.SemaphoreType.DMA((8,)),
            pltpu.VMEM((total, self.count), BF16),
            pltpu.VMEM((total, self.count), BF16),
            pltpu.VMEM((width, self.count), BF16),
            pltpu.VMEM((self.count, width), BF16),
            pltpu.VMEM((8, self.count), F32),
            pltpu.SemaphoreType.DMA((2 * self.blocks,)),
        ]

    def compute(self, part, second, second_t, grad, grad_t, acc, gs, ubg, scratch, outs):
        up_slots, down_slots, out_sem, acts, grad_pres, up_ref, down_ref, bias_ref, _ = scratch
        if not self.packed:
            up_slots, down_slots = outs
        quad = lax.div(lax.axis_index("seq"), self.stride)
        mine = lax.axis_index("batch")

        def enter(i):
            rows = slice(i * ROWS, (i + 1) * ROWS)
            pre = dot(second[rows, :], up_ref[...]) + bias_ref[0:1, :]
            return pre, dot_nt(grad[rows, :], down_ref[...])

        def weights(n):
            first, last = n * self.chunk, (n + 1) * self.chunk
            up_grad = dot(second_t[...], grad_pres[:, first:last]).astype(BF16)
            down_grad = dot(grad_t[...], acts[:, first:last]).astype(BF16)
            if not self.packed:
                up_slots[:, first:last] = up_grad
                down_slots[:, first:last] = down_grad
                return
            at = first
            while at < last:
                block = at // self.size
                stop = min(last, (block + 1) * self.size)
                src = slice(at - first, stop - first)
                dst = slice(at - block * self.size, stop - block * self.size)
                for m in range(self.blocks):
                    rows = slice(m * self.high, (m + 1) * self.high)
                    up_slots[block ^ mine, m ^ quad, :, dst] = up_grad[rows, src]
                    down_slots[m ^ mine, block ^ quad, :, dst] = down_grad[rows, src]
                at = stop

        ready = enter(0)
        chunks = second.shape[0] // ROWS
        for i in range(chunks):
            ahead = enter(i + 1) if i + 1 < chunks else None
            rows = slice(i * ROWS, (i + 1) * ROWS)
            pre, grad_act = ready
            value, slope = gelu_parts(pre)
            act = value.astype(BF16)
            grad_pre = (grad_act * slope).astype(BF16)
            acts[rows, :] = act
            grad_pres[rows, :] = grad_pre
            ubg[0:1, :] += jnp.sum(grad_pre.astype(F32), axis=0, keepdims=True)
            acc[rows, :] += dot(act, down_ref[...])
            gs[rows, :] += dot_nt(grad_pre, up_ref[...])
            ready = ahead
        for n in range(self.count // self.chunk):
            weights(n)
        stores = []
        if self.packed:
            order = ((up_slots, (0, 2)), (up_slots, (1, 3)), (down_slots, (0, 1)), (down_slots, (2, 3)))
            for m, (source, slots) in enumerate(order):
                for n in range(2):
                    stores.append(
                        pltpu.make_async_copy(
                            source.at[slots[n]], outs[m].at[n], out_sem.at[2 * m + n]
                        )
                    )
        return stores


def feed_first(
    rows_all, att_first, att_last, cot_pieces, out_w, out_b, gain, shift, up, up_b, down, down_b, units
):
    pieces = len(att_first)
    total, width = rows_all.shape
    piece_rows = total // pieces
    count = len(cot_pieces)
    cot_rows = total // count
    split = att_first[0].shape[1]
    grads = units.grad_shapes(width)

    def body(*refs):
        x_ref, refs = refs[0], refs[1:]
        att_refs, refs = refs[: 2 * pieces], refs[2 * pieces :]
        cot_refs, refs = refs[:count], refs[count:]
        wo_refs, refs = refs[:pieces], refs[pieces:]
        ob_ref, gain_ref, shift_ref, up_hbm, ub_ref, down_hbm, db_ref = refs[:7]
        mid_ref, second, second_t, grad, grad_t, acc, gs, ubg = refs[7:15]
        outs, scratch = refs[15 : 15 + len(grads)], refs[15 + len(grads) :]
        _, part, _ = place(pieces)
        loads = units.loads(part, up_hbm, down_hbm, ub_ref, *scratch[5:])
        for load in loads:
            load.start()
        ubg[...] = jnp.zeros_like(ubg)
        masked = jnp.zeros((1, width), F32)
        for ref in cot_refs:
            masked = masked + ref[cot_rows : cot_rows + 1, :].astype(F32)
        factor = total / (4.0 * masked)
        for n in range(count):
            scaled = cot_refs[n][0:cot_rows, :].astype(F32) * factor
            dst = slice(n * cot_rows, (n + 1) * cot_rows)
            grad[dst, :] = scaled.astype(BF16)

        for h in range(pieces):

            @pl.loop(0, piece_rows // ROWS)
            def _(i, h=h):
                at = pl.multiple_of(i * ROWS, ROWS)
                dst = pl.ds(h * piece_rows + at, ROWS)
                mid = x_ref[dst, :].astype(F32) + ob_ref[...]
                for n in range(pieces):
                    src = pl.ds(((h - n) % pieces) * piece_rows + at, ROWS)
                    mid = mid + dot(att_refs[2 * n][src, :], wo_refs[n][0:split, :])
                    mid = mid + dot(att_refs[2 * n + 1][src, :], wo_refs[n][split:, :])
                mid_ref[dst, :] = mid
                normed, _ = norm_rows(mid)
                low = normed * gain_ref[...] + shift_ref[...]
                second[dst, :] = low.astype(BF16)
                second_t[:, dst] = low.T.astype(BF16)
                grad_t[:, dst] = grad[dst, :].astype(F32).T.astype(BF16)
                acc[dst, :] = mid + db_ref[...] if h == 0 else jnp.zeros((ROWS, width), F32)
                gs[dst, :] = jnp.zeros((ROWS, width), F32)

        for load in loads:
            load.wait()
        stores = units.compute(
            part, second, second_t, grad, grad_t, acc, gs, ubg, scratch, outs
        )
        for store in stores:
            store.start()
        for store in stores:
            store.wait()

    att_all = [item for pair in zip(att_first, att_last) for item in pair]
    turned = sds((width, total), BF16)
    flat = sds((total, width), BF16)
    wide = sds((total, width), F32)
    return run(
        body,
        [rows_all, *att_all, *cot_pieces, *out_w, out_b, gain, shift, up, up_b, down, down_b],
        in_specs=[VMEM] * (1 + 3 * pieces + count) + [VMEM, VMEM, VMEM, HBM, VMEM, HBM, VMEM],
        out_specs=[VMEM] * 8 + [HBM if units.packed else VMEM] * len(grads),
        out_shape=[wide, flat, turned, flat, turned, wide, wide, sds((8, units.count), F32)] + grads,
        scratch_shapes=units.scratch(total, width),
        vmem=24,
        cost_estimate=cost(12 * total * width * units.count, 24 * 1024 * 1024, total * units.count),
        name="feed_first",
    )


def feed_second(second, second_t, grad, grad_t, acc_first, gs_first, up, up_b, down, units, pieces, after):
    total, width = second.shape
    piece_rows = total // pieces
    grads = units.grad_shapes(width)

    def body(*refs):
        second, second_t, grad, grad_t, acc_in, gs_in, up_hbm, ub_ref, down_hbm = refs[:9]
        own_ref, low_ref, ubg, refs = refs[9], refs[10], refs[11], refs[12:]
        send_refs, refs = refs[: pieces - 1], refs[pieces - 1 :]
        outs, (acc, gs), scratch = refs[: len(grads)], refs[len(grads) :][:2], refs[len(grads) + 2 :]
        _, part, _ = place(pieces)
        loads = units.loads(part, up_hbm, down_hbm, ub_ref, *scratch[5:])
        for load in loads:
            load.start()
        ubg[...] = jnp.zeros_like(ubg)
        acc[...] = acc_in[...]
        gs[...] = gs_in[...]
        for load in loads:
            load.wait()
        stores = units.compute(
            part, second, second_t, grad, grad_t, acc, gs, ubg, scratch, outs
        )
        for store in stores:
            store.start()
        low_ref[...] = gs[...].astype(BF16)
        own_ref[...] = acc[0:piece_rows, :]
        for h in range(1, pieces):
            send_refs[h - 1][...] = acc[h * piece_rows : (h + 1) * piece_rows, :].astype(BF16)
        for store in stores:
            store.wait()

    return run(
        body,
        [second, second_t, grad, grad_t, acc_first, gs_first, up, up_b, down],
        after,
        in_specs=[VMEM] * 6 + [HBM, VMEM, HBM],
        out_specs=[VMEM] * (2 + pieces) + [HBM if units.packed else VMEM] * len(grads),
        out_shape=[
            sds((piece_rows, width), F32),
            sds((total, width), BF16),
            sds((8, units.count), F32),
        ]
        + [sds((piece_rows, width), BF16)] * (pieces - 1)
        + grads,
        scratch_shapes=[pltpu.VMEM((total, width), F32)] * 2 + units.scratch(total, width),
        vmem=34,
        cost_estimate=cost(12 * total * width * units.count, 24 * 1024 * 1024, total * units.count),
        name="feed_second",
    )


def mid_back(mid, grad_second, received, grad_rows, gain, out_w, att_first, att_last, chunk):
    pieces = 1 + len(received)
    total, width = mid.shape
    piece_rows = total // pieces
    split = att_first.shape[1]
    wide = split + att_last.shape[1]

    def body(*refs):
        mid_ref, gs_ref, refs = refs[0], refs[1], refs[2:]
        recv_refs, refs = refs[: pieces - 1], refs[pieces - 1 :]
        go_ref, gain_ref, wo_ref, att_ref, last_ref = refs[:5]
        gm_ref, do_ref, sums_ref, *dwo_refs, low_ref = refs[5:]
        sums_ref[...] = jnp.zeros_like(sums_ref)
        for h in range(pieces):

            @pl.loop(0, piece_rows // ROWS)
            def _(i, h=h):
                at = pl.multiple_of(i * ROWS, ROWS)
                rows = pl.ds(h * piece_rows + at, ROWS)
                normed, inv_std = norm_rows(mid_ref[rows, :])
                grad = gs_ref[rows, :].astype(F32)
                for n in range(1, pieces):
                    src = pl.ds(((h - n) % pieces) * piece_rows + at, ROWS)
                    grad = grad + recv_refs[n - 1][src, :].astype(F32)
                go = go_ref[rows, :].astype(F32)
                grad_mid = go + norm_back(grad * gain_ref[...], normed, inv_std)
                low = grad_mid.astype(BF16)
                low_ref[rows, :] = low
                do_ref[rows, :] = dot_nt(low, wo_ref[...]).astype(BF16)
                if h == 0:
                    gm_ref[rows, :] = grad_mid
                    for n, item in enumerate((grad * normed, grad, low.astype(F32), go)):
                        sums_ref[n : n + 1, :] += jnp.sum(item, axis=0, keepdims=True)

        grad_out_w = jnp.concatenate(
            [
                dot(ref[...].astype(F32).T.astype(BF16), low_ref[...]).astype(BF16)
                for ref in (att_ref, last_ref)
            ],
            axis=0,
        )
        if chunk == 0:
            dwo_refs[0][...] = grad_out_w
            return
        _, part, _ = place(pieces)
        for c in range(pieces):

            @pl.when(part == c)
            def _(c=c):
                for n in range(dwo_refs[0].shape[0]):
                    for e in range(pieces):
                        at = (n * pieces + (c + e) % pieces) * chunk
                        dwo_refs[e][n] = grad_out_w[at : at + chunk, :]

    if chunk == 0:
        grads = [sds((wide, width), BF16)]
    else:
        grads = [sds((width // (pieces * pieces * chunk), chunk, width), BF16)] * pieces
    return run(
        body,
        [mid, grad_second, *received, grad_rows, gain, out_w, att_first, att_last],
        out_shape=[
            sds((piece_rows, width), F32),
            sds((total, wide), BF16),
            sds((8, width), F32),
        ]
        + grads,
        scratch_shapes=[pltpu.VMEM((total, width), BF16)],
        vmem=20,
        cost_estimate=cost(4 * total * width * wide, 14 * 1024 * 1024),
        name="mid_back",
    )


def attend_backward(
    qkv, grad_att, att, att_tile, logs, lane_first, tile, heads, head_dim, after=(), part=1
):
    total = qkv.shape[0]
    per_tile = LANES // head_dim
    live = min(per_tile, heads - tile * per_tile)
    scale = head_dim ** (-0.5)
    exp_scale = scale * LOG2E

    def body(qkv_ref, do_ref, att_ref, lse_ref, out_ref, *scratch):
        km, vm, qm, dm, key_t, query_t, do_t, dq_t, lse_t, mean_t = scratch
        lane = lax.broadcasted_iota(jnp.int32, (1, LANES), 1)
        lse_t[...] = lse_ref[...].T
        query = qkv_ref[:, 0:LANES].astype(F32)
        key = qkv_ref[:, LANES : 2 * LANES].astype(F32)
        val = qkv_ref[:, 2 * LANES : 3 * LANES].astype(F32)
        upstream = do_ref[...].astype(F32)
        both_t = (upstream * att_ref[...].astype(F32)).T
        for j in range(live):
            mean_t[j : j + 1, :] = jnp.sum(
                both_t[j * head_dim : (j + 1) * head_dim, :], axis=0, keepdims=True
            )
        query_t[...] = query.T.astype(BF16)
        do_t[...] = upstream.T.astype(BF16)
        key_t[...] = key.T.astype(BF16)
        for j in range(live):
            mine = lane // head_dim == j
            km[j] = jnp.where(mine, key, 0.0).astype(BF16)
            vm[j] = jnp.where(mine, val, 0.0).astype(BF16)
            qm[j] = jnp.where(mine, query, 0.0).astype(BF16)
            dm[j] = jnp.where(mine, upstream, 0.0).astype(BF16)
        dq_t[...] = jnp.zeros_like(dq_t)

        @pl.loop(0, total // ROWS)
        def _(i):
            rows = pl.ds(pl.multiple_of(i * ROWS, ROWS), ROWS)
            grad_key = jnp.zeros((ROWS, LANES), F32)
            grad_val = jnp.zeros((ROWS, LANES), F32)

            def enter(j):
                return dot(km[j, rows, :], query_t[...]), dot(vm[j, rows, :], do_t[...])

            ready = enter(0)
            for j in range(live):
                ahead = enter(j + 1) if j + 1 < live else None
                scores, grad_prob = ready
                head = lane_first + j
                own = slice(j * head_dim, (j + 1) * head_dim)
                probs = jnp.exp2(scores * exp_scale - lse_t[head : head + 1, :])
                grad_scores = (probs * (grad_prob - mean_t[j : j + 1, :])).astype(BF16)
                grad_val = grad_val + dot(probs.astype(BF16), dm[j])
                grad_key = grad_key + dot(grad_scores, qm[j])
                dq_t[own, :] += dot(key_t[own, rows], grad_scores)
                ready = ahead
            out_ref[rows, LANES : 2 * LANES] = (grad_key * scale).astype(BF16)
            out_ref[rows, 2 * LANES : 3 * LANES] = grad_val.astype(BF16)

        out_ref[:, 0:LANES] = (dq_t[...].T * scale).astype(BF16)

    masked = pltpu.VMEM((live, total, LANES), BF16)
    turned = pltpu.VMEM((LANES, total), BF16)
    turned_f = pltpu.VMEM((LANES, total), F32)
    return run(
        body,
        [qkv, grad_att, att, logs],
        after,
        grid=(1,),
        in_specs=[
            pl.BlockSpec((total, 3 * LANES), lambda i: (0, tile)),
            pl.BlockSpec((total, LANES), lambda i: (0, tile)),
            pl.BlockSpec((total, LANES), lambda i: (0, att_tile)),
            pl.BlockSpec((total, LANES), lambda i: (0, 0)),
        ],
        out_specs=pl.BlockSpec((total, 3 * LANES), lambda i: (0, 0)),
        out_shape=sds((total, 3 * LANES), BF16),
        scratch_shapes=[masked] * 4
        + [turned] * 3
        + [turned_f] * 2
        + [pltpu.VMEM((8, total), F32)],
        vmem=22,
        cost_estimate=cost(
            2 * live * total * total * 256 * 5, 3 * 1024 * 1024, live * total * total, part
        ),
        name="attend_backward",
    )


def project_weights(rows_all, gain, shift, grad_tiles, pieces, quads, packed, after):
    total, width = rows_all.shape
    tiles = len(grad_tiles)
    tile_cols = grad_tiles[0].shape[1]
    cols_all = tiles * tile_cols
    chunk = width // (quads * pieces)

    def body(*refs):
        x_ref, gain_ref, shift_ref, refs = refs[0], refs[1], refs[2], refs[3:]
        dq_refs, (*dw_refs, low_t, part_ref) = refs[:tiles], refs[tiles:]
        _, part, quad = place(pieces)

        @pl.loop(0, total // ROWS)
        def _(i):
            rows = pl.ds(pl.multiple_of(i * ROWS, ROWS), ROWS)
            normed, _ = norm_rows(x_ref[rows, :].astype(F32))
            low_t[:, rows] = (normed * gain_ref[...] + shift_ref[...]).T.astype(BF16)

        for t in range(tiles):
            cols = slice(t * tile_cols, (t + 1) * tile_cols)
            part_ref[...] = dot(low_t[...], dq_refs[t][...]).astype(BF16)
            if not packed:
                dw_refs[0][:, cols] = part_ref[...]
                continue
            for c in range(pieces):

                @pl.when(part == c)
                def _(c=c, cols=cols):
                    for q in range(quads):
                        for e in range(pieces):
                            at = (q * pieces + (c + e) % pieces) * chunk
                            dw_refs[e][q ^ quad, :, cols] = part_ref[at : at + chunk, :]

    if packed:
        grads = [sds((quads, chunk, cols_all), BF16)] * pieces
    else:
        grads = [sds((width, cols_all), BF16)]
    return run(
        body,
        [rows_all, gain, shift, *grad_tiles],
        after,
        out_shape=grads,
        scratch_shapes=[pltpu.VMEM((width, total), BF16), pltpu.VMEM((width, tile_cols), BF16)],
        vmem=14,
        cost_estimate=cost(2 * total * width * cols_all, 6 * 1024 * 1024, 0, 64),
        name="project_weights",
    )


def project_rows(
    rows_all, weight, grad_tiles, sums_mid, up_sums, pieces, quads, packed, real, after
):
    total, width = rows_all.shape
    piece_rows = total // pieces
    cols_all = weight.shape[1]
    tiles = len(grad_tiles)
    tile_cols = cols_all // tiles

    def body(*refs):
        x_ref, w_ref, mid_ref, refs = *refs[:3], refs[3:]
        ups_refs, refs = refs[: len(up_sums)], refs[len(up_sums) :]
        dq_refs, refs = refs[:tiles], refs[tiles:]
        own_ref, refs = refs[0], refs[1:]
        send_refs, (sums_ref, bias_ref) = refs[: pieces - 1], refs[pieces - 1 :]
        _, part, _ = place(pieces)
        sums_ref[...] = jnp.zeros_like(sums_ref)
        bias_ref[...] = jnp.zeros_like(bias_ref)
        for h in range(pieces):

            @pl.loop(0, piece_rows // ROWS)
            def _(i, h=h):
                at = pl.multiple_of(i * ROWS, ROWS)
                src = pl.ds(at, ROWS)
                rows = pl.ds(h * piece_rows + at, ROWS)
                normed, _ = norm_rows(x_ref[rows, :].astype(F32))
                grad = jnp.zeros((ROWS, width), F32)
                for t in range(tiles):
                    grad_rows = dq_refs[t][rows, :]
                    cols = slice(t * tile_cols, (t + 1) * tile_cols)
                    grad = grad + dot_nt(grad_rows, w_ref[:, cols])
                    bias_ref[0:1, cols] += jnp.sum(grad_rows.astype(F32), axis=0, keepdims=True)
                if h == 0:
                    own_ref[src, :] = grad
                else:
                    send_refs[h - 1][src, :] = grad.astype(BF16)
                sums_ref[0:1, :] += jnp.sum(grad * normed, axis=0, keepdims=True)
                sums_ref[1:2, :] += jnp.sum(grad, axis=0, keepdims=True)

        if not packed:
            return
        for row, src in ((4, 2), (5, 0), (6, 1), (15, 3)):
            sums_ref[row : row + 1, :] = mid_ref[src : src + 1, :]
        for c in range(pieces):

            @pl.when(part == c)
            def _(c=c):
                for row, p in ((2, 0), (3, 2)):
                    mine = jnp.concatenate(
                        [
                            bias_ref[0:1, (3 * t + p) * LANES :][:, : min(LANES, real - t * LANES)]
                            for t in range(tiles)
                        ],
                        axis=1,
                    )
                    sums_ref[row : row + 1, c * real : (c + 1) * real] = mine
                for n in range(quads):
                    row = 7 + n * pieces + c
                    start = 0
                    for ref in ups_refs:
                        size = ref.shape[1] // quads
                        here = ref[0:1, n * size : (n + 1) * size]
                        sums_ref[row : row + 1, start : start + size] = here
                        start += size

    return run(
        body,
        [rows_all, weight, sums_mid, *up_sums, *grad_tiles],
        after,
        out_shape=[sds((piece_rows, width), F32)]
        + [sds((piece_rows, width), BF16)] * (pieces - 1)
        + [sds((16, width), F32), sds((8, cols_all), F32)],
        vmem=16,
        cost_estimate=cost(2 * total * width * cols_all, 8 * 1024 * 1024, 0, 64),
        name="project_rows",
    )


def finish_rows(rows_all, gain, grad_mid, grad_own, received, count, after):
    rows, width = grad_mid.shape
    others = len(received)
    piece = rows // count
    per_step = ROWS // piece

    def body(*refs):
        x_ref, gain_ref, gm_ref, own_ref, refs = refs[0], refs[1], refs[2], refs[3], refs[4:]
        recv_refs, out_refs = refs[:others], refs[others:]
        for n in range(rows // ROWS):
            at = slice(n * ROWS, (n + 1) * ROWS)
            normed, inv_std = norm_rows(x_ref[at, :].astype(F32))
            grad = own_ref[at, :]
            for ref in recv_refs:
                grad = grad + ref[at, :].astype(F32)
            done = gm_ref[at, :] + norm_back(grad * gain_ref[...], normed, inv_std)
            for e in range(per_step):
                out_refs[n * per_step + e][...] = done[e * piece : (e + 1) * piece, :].astype(BF16)

    return run(
        body,
        [rows_all, gain, grad_mid, grad_own, *received],
        after,
        out_shape=[sds((piece, width), BF16)] * count,
        vmem=24,
        cost_estimate=cost(20 * rows * width, 6 * 1024 * 1024),
        name="finish_rows",
    )


def finish_result(own, received, count):
    rows, width = own.shape
    others = len(received)
    piece = rows // count

    def body(*refs):
        out_refs = refs[1 + others :]
        for n in range(count):
            at = slice(n * piece, (n + 1) * piece)
            total = refs[0][at, :]
            for ref in refs[1 : 1 + others]:
                total = total + ref[at, :].astype(F32)
            out_refs[n % 2][n // 2] = total.astype(BF16)

    return run(
        body,
        [own, *received],
        out_shape=[sds((count // 2, piece, width), BF16)] * 2,
        vmem=16,
        cost_estimate=cost(2 * rows * width, 3 * 1024 * 1024),
        name="finish_result",
    )


def pass_on(keep, received, after):
    def body(keep_ref, recv_ref, out_ref):
        out_ref[0] = keep_ref[1]
        out_ref[1] = recv_ref[1]

    return run(
        body,
        [keep, received],
        after,
        out_shape=sds(keep.shape, keep.dtype),
        vmem=16,
        cost_estimate=cost(0, 4 * keep.size),
        name="pass_on",
    )


def collect_halves(keep, near, far, group, after):
    _, rows, width = keep.shape

    def body(keep_ref, near_ref, far_ref, out_ref):
        _, _, quad = place(group)
        out_ref[quad] = keep_ref[0]
        out_ref[quad ^ 1] = near_ref[0]
        out_ref[quad ^ 2] = far_ref[0]
        out_ref[quad ^ 3] = far_ref[1]

    return run(
        body,
        [keep, near, far],
        after,
        out_shape=sds((4, rows, width), keep.dtype),
        vmem=16,
        cost_estimate=cost(0, 16 * rows * width),
        name="collect_halves",
    )


def two_parts(item):
    first = item.astype(BF16)
    return first, (item - first.astype(F32)).astype(BF16)


def pack_attention(
    qkv_keep, qkv_recv, out_keep, out_recv, small, small_recv, real, blocks, after
):
    quads, chunk, cols_all = qkv_keep.shape
    wide = cols_all // 3
    tiles = wide // LANES
    width = out_keep.shape[2]
    qkv_lanes = 6 * real // blocks
    out_lanes = width // blocks
    lanes = qkv_lanes + out_lanes
    halves = quads // 2
    slot = halves * chunk
    small_rows = small.shape[0]

    def body(qk_ref, qr_ref, ok_ref, or_ref, small_ref, srecv_ref, *out_refs):
        _, part, quad = place(2)
        mine = lax.axis_index("batch")
        slots = out_refs[4]

        def heads_of(rows, p):
            return [
                rows[:, (3 * t + p) * LANES : (3 * t + p) * LANES + min(LANES, real - t * LANES)]
                for t in range(tiles)
            ]

        for c in range(2):

            @pl.when(part == c)
            def _(c=c):
                for q in range(quads):
                    pair = (qk_ref[q], qr_ref[q])
                    if c == 1:
                        pair = pair[::-1]
                    parts = []
                    for p in range(3):
                        parts += heads_of(pair[0], p) + heads_of(pair[1], p)
                    row = jnp.concatenate(parts, axis=1)
                    for b in range(blocks):
                        slots[b ^ mine, q, :, 0:qkv_lanes] = row[
                            :, b * qkv_lanes : (b + 1) * qkv_lanes
                        ]
                for e, ref in enumerate((ok_ref, or_ref)):
                    for n in range(halves):
                        q = ((c + e) % 2) * halves + n
                        for b in range(blocks):
                            slots[b ^ mine, q ^ quad, :, qkv_lanes:lanes] = ref[
                                n, :, b * out_lanes : (b + 1) * out_lanes
                            ]

        for n, order in enumerate(((0, 2), (1, 3), (0, 1), (2, 3))):
            for e in range(2):
                for f in range(halves):
                    at = e * slot + f * chunk
                    src = f if n < 2 else halves + f
                    out_refs[n][at : at + chunk, :] = slots[order[e], src]
        parts = two_parts(small_ref[...] + srecv_ref[...])
        for n in range(2):
            for e in range(2):
                at = 2 * slot + e * small_rows
                out_refs[n][at : at + small_rows, :] = parts[e]

    first = sds((2 * slot + 2 * small_rows, lanes), BF16)
    other = sds((2 * slot, lanes), BF16)
    return run(
        body,
        [qkv_keep, qkv_recv, out_keep, out_recv, small, small_recv],
        after,
        out_shape=[first, first, other, other],
        scratch_shapes=[pltpu.VMEM((blocks, quads, chunk, lanes), BF16)],
        vmem=24,
        cost_estimate=cost(0, 4 * 1024 * 1024),
        name="pack_attention",
    )


def sum_first(keeps, received, after=()):
    count = len(keeps)
    shape = keeps[0].shape[1:]

    def body(*refs):
        for n in range(count):
            for e in range(2):
                total = refs[n][e].astype(F32) + refs[count + n][e].astype(F32)
                refs[2 * count + 2 * n + e][...] = total.astype(BF16)

    return run(
        body,
        [*keeps, *received],
        after,
        out_shape=[sds(shape, BF16)] * (2 * count),
        vmem=24,
        cost_estimate=cost(0, 6 * count * keeps[0].size),
        name="sum_first",
    )


def sum_second(keeps, received, after=()):
    quads, rows, width = keeps[0].shape

    def body(ka, kb, ra, rb, keep_ref, send_ref):
        for d in range(quads):
            ref = send_ref if d % 2 else keep_ref
            for e, (keep, recv) in enumerate(((ka, ra), (kb, rb))):
                total = keep[d].astype(F32) + recv[d].astype(F32)
                ref[d // 2, e] = total.astype(BF16)

    return run(
        body,
        [*keeps, *received],
        after,
        out_shape=[sds((quads // 2, 2, rows, width), BF16)] * 2,
        vmem=24,
        cost_estimate=cost(0, 12 * keeps[0].size),
        name="sum_second",
    )


def sum_third(keep, received, after=()):
    def body(keep_ref, recv_ref, stay_ref, pass_ref):
        for ref, e in ((stay_ref, 0), (pass_ref, 1)):
            ref[...] = (keep_ref[e].astype(F32) + recv_ref[e].astype(F32)).astype(BF16)

    return run(
        body,
        [keep, received],
        after,
        out_shape=[sds(keep.shape[1:], BF16)] * 2,
        vmem=16,
        cost_estimate=cost(0, 6 * keep.size),
        name="sum_third",
    )


def small_sum(refs, rows, count):
    total = None
    for ref in refs:
        for e in range(2):
            item = ref[rows + e * count : rows + (e + 1) * count, :].astype(F32)
            total = item if total is None else total + item
    return total


def sum_first_attention(keeps, received, slot, small_rows, after):
    lanes = keeps[0].shape[1]

    def body(ka, kb, ra, rb, stay_a, pass_a, stay_b, pass_b):
        parts = two_parts(small_sum((ka, ra), 2 * slot, small_rows))
        for keep, recv, stay, on in ((ka, ra, stay_a, pass_a), (kb, rb, stay_b, pass_b)):
            for e, ref in enumerate((stay, on)):
                at = slice(e * slot, (e + 1) * slot)
                ref[0:slot, :] = (keep[at, :].astype(F32) + recv[at, :].astype(F32)).astype(BF16)
        for ref in (stay_a, pass_a):
            for e in range(2):
                ref[slot + e * small_rows : slot + (e + 1) * small_rows, :] = parts[e]

    first = sds((slot + 2 * small_rows, lanes), BF16)
    other = sds((slot, lanes), BF16)
    return run(
        body,
        [*keeps, *received],
        after,
        out_shape=[first, first, other, other],
        vmem=16,
        cost_estimate=cost(0, 3 * 1024 * 1024),
        name="sum_first_attention",
    )


def sum_second_attention(keeps, received, chunk, quads, small_rows, after):
    lanes = keeps[0].shape[1]
    halves = quads // 2
    slot = halves * chunk

    def body(ka, kb, ra, rb, *out_refs):
        parts = two_parts(small_sum((ka, ra), slot, small_rows))
        for d in range(quads):
            keep, recv = ((ka, ra), (kb, rb))[d // halves]
            at = slice(d % halves * chunk, (d % halves + 1) * chunk)
            total = keep[at, :].astype(F32) + recv[at, :].astype(F32)
            out_refs[d][0:chunk, :] = total.astype(BF16)
            for e in range(2):
                at = chunk + e * small_rows
                out_refs[d][at : at + small_rows, :] = parts[e]

    return run(
        body,
        [*keeps, *received],
        after,
        out_shape=[sds((chunk + 2 * small_rows, lanes), BF16)] * quads,
        vmem=16,
        cost_estimate=cost(0, 2 * 1024 * 1024),
        name="sum_second_attention",
    )


def final_attention(pieces, chunk, qkv_lanes, small_rows):
    lanes = pieces[0].shape[1]
    count = len(pieces)

    def body(*refs):
        total = refs[0][0:chunk, :].astype(F32)
        for ref in refs[1:count]:
            total = total + ref[0:chunk, :].astype(F32)
        refs[count][...] = total[:, :qkv_lanes]
        refs[count + 1][...] = total[:, qkv_lanes:]
        refs[count + 2][...] = small_sum(refs[:count], chunk, small_rows)

    return run(
        body,
        pieces,
        out_shape=[
            sds((chunk, qkv_lanes), F32),
            sds((chunk, lanes - qkv_lanes), F32),
            sds((small_rows, lanes), F32),
        ],
        vmem=16,
        cost_estimate=cost(0, 1024 * 1024),
        name="final_attention",
    )


def final_units(first, second, after):
    high = first[0].shape[1]
    sizes = [first[0].shape[2], second[0].shape[2]]
    unit_block = sum(sizes)
    count = len(first)
    half = high // 2

    def body(*refs):
        _, part, _ = place(2)
        keep_ref, send_ref, down_ref = refs[2 * count :]
        for h in range(2):
            pieces = refs[h * count : (h + 1) * count]
            up, down = pieces[0][0].astype(F32), pieces[0][1].astype(F32)
            for ref in pieces[1:]:
                up = up + ref[0].astype(F32)
                down = down + ref[1].astype(F32)
            here = slice(h * sizes[0], h * sizes[0] + sizes[h])
            down_ref[here, :] = down.T
            for c in range(2):

                @pl.when(part == c)
                def _(up=up, here=here, c=c):
                    keep_ref[:, here] = up[c * half : (c + 1) * half, :]
                    send_ref[:, here] = up[(1 - c) * half : (2 - c) * half, :].astype(BF16)

    return run(
        body,
        [*first, *second],
        after,
        out_shape=[
            sds((half, unit_block), F32),
            sds((half, unit_block), BF16),
            sds((unit_block, high), F32),
        ],
        vmem=24,
        cost_estimate=cost(0, 4 * 1024 * 1024),
        name="final_units",
    )


def final_join(keep, recv):
    chunk, unit_block = keep.shape

    def body(keep_ref, recv_ref, out_ref):
        _, part, _ = place(2)
        for c in range(2):

            @pl.when(part == c)
            def _(c=c):
                out_ref[:, c * unit_block : (c + 1) * unit_block] = keep_ref[...]
                out_ref[:, (1 - c) * unit_block : (2 - c) * unit_block] = recv_ref[...].astype(F32)

    return run(
        body,
        [keep, recv],
        out_shape=sds((chunk, 2 * unit_block), F32),
        vmem=16,
        cost_estimate=cost(0, 1024 * 1024),
        name="final_join",
    )


def on_device(
    tokens,
    mask,
    cotangent,
    ln1_gain,
    ln1_bias,
    qkv_weight,
    q_bias,
    v_bias,
    out_weight,
    out_bias,
    ln2_gain,
    ln2_bias,
    up_weight,
    up_bias,
    down_weight,
    down_bias,
):
    seq_size = lax.axis_size("seq")
    batch_size = lax.axis_size("batch")
    micro_count, seq_count, local_len, width = tokens.shape
    sequences = micro_count * seq_count
    group = seq_size // sequences
    units = up_weight.shape[1]
    head_dim = width // HEADS
    heads = HEADS // group
    real = heads * head_dim
    wide = -(-real // LANES) * LANES
    full_len = local_len * seq_size
    block_len = local_len // group
    rows = seq_size * block_len
    own_units = units // group
    part = lax.axis_index("seq") % group
    aligned = (
        seq_size == batch_size * group
        and group == 2
        and batch_size == 4
        and wide == 3 * LANES
        and (seq_size // group) % group == 0
        and units % (batch_size * group * LANES) == 0
        and own_units // batch_size == width
    )

    def from_part(item, ahead):
        if ahead % group == 0:
            return item
        pairs = [
            (q * group + (c + ahead) % group, q * group + c)
            for q in range(sequences)
            for c in range(group)
        ]
        return lax.ppermute(item, "seq", pairs)

    def gather_parts(item):
        return [from_part(item, n) for n in range(group)]

    def row_of(item):
        return item.astype(F32)[None, :]

    def blocks_of(item):
        return item.reshape(sequences, local_len, width)

    x_own = over_quads(deal(blocks_of(tokens), group), group)
    x_pieces = [from_part(item, n) for n in range(group) for item in x_own]

    count_rows = jnp.sum(mask, axis=2).reshape(sequences).astype(BF16)
    cot_low = jnp.where(mask[..., None] != 0, cotangent, jnp.zeros_like(cotangent))
    cot_send = jnp.concatenate(
        [blocks_of(cot_low), jnp.broadcast_to(count_rows[:, None, None], (sequences, 16, width))],
        axis=1,
    )
    cot_own = over_quads(deal(cot_send, group, x_pieces[sequences:]), group)

    qkv_w, qkv_b, *out_w = pick_weights(
        qkv_weight,
        jnp.concatenate([q_bias, jnp.zeros_like(q_bias), v_bias])[None, :],
        out_weight,
        group,
        real,
        wide,
    )
    if aligned:
        up_own, up_b, down_own = up_weight, up_bias[None, :], down_weight
    else:

        def own_columns(matrix, blocks):
            split = matrix.reshape(matrix.shape[0], blocks, group, -1)
            return lax.dynamic_index_in_dim(split, part, 2, keepdims=False)

        up_own = own_columns(up_weight, batch_size).reshape(width, own_units)
        up_b = own_columns(up_bias[None, :], batch_size).reshape(1, own_units)
        down_own = lax.dynamic_index_in_dim(
            down_weight.reshape(batch_size, group, -1, width), part, 1, keepdims=False
        ).reshape(own_units, width)

    tiles = wide // LANES
    x_all, qkv, att_first, logs_first = attend_first(
        x_pieces, row_of(ln1_gain), row_of(ln1_bias), qkv_w, qkv_b, tiles - 1, heads, head_dim
    )
    cot_stack = stack(cot_own, [logs_first])
    att_last, logs_last = attend_last(qkv, tiles - 1, heads, head_dim, [cot_stack])
    cot_pieces = cot_own + [
        item[d]
        for item in gather_parts(cot_stack)[1:]
        for d in range(sequences)
    ]
    blocks = batch_size if aligned else 1
    unit_block = own_units // blocks
    size = unit_block * 2 // 5
    shape = (group, sequences if aligned else None, width // sequences)
    calls = [
        Units(unit_block, blocks, 0, size, *shape),
        Units(unit_block, blocks, size, unit_block - size, *shape),
    ]
    mid, second, second_t, grad_rows, grad_t, acc, grad_second, *found = feed_first(
        x_all,
        gather_parts(att_first),
        gather_parts(att_last),
        cot_pieces,
        out_w,
        row_of(out_bias),
        row_of(ln2_gain),
        row_of(ln2_bias),
        up_own,
        up_b,
        down_own,
        row_of(down_bias),
        calls[0],
    )
    up_sums, ff_grads = [found[0]], [found[1:]]
    result_own, grad_second, *found = feed_second(
        second,
        second_t,
        grad_rows,
        grad_t,
        acc,
        grad_second,
        up_own,
        up_b,
        down_own,
        calls[1],
        group,
        [],
    )
    up_sums.append(found[0])
    result_send = found[1:group]
    ff_grads.append(found[group:])

    def begin_sum(e, sends, after):
        moved = [swap(sends[0], "batch", batch_size, 1), swap(sends[1], "batch", batch_size, 2)]
        stay_a, pass_a, stay_b, pass_b = sum_first(
            [ff_grads[e][0], ff_grads[e][2]], moved, after
        )
        moved = [swap(pass_a, "batch", batch_size, 2), swap(pass_b, "batch", batch_size, 1)]
        return [stay_a, stay_b], moved

    if aligned:
        waiting = begin_sum(0, [ff_grads[0][1], ff_grads[0][3]], [])
        (grad_second,) = gate([grad_second], waiting[0][:1])
    second_send = grad_second
    second_recv = [from_part(second_send, n) for n in range(1, group)]
    result_recv = [from_part(result_send[group - n - 1], n) for n in range(1, group)]
    result_keep, result_pass = finish_result(result_own, result_recv, sequences)

    def quad_swap(item, distance):
        return swap(item, "seq", seq_size, distance * group)

    result_near = quad_swap(result_pass, 1)

    chunk = width // seq_size
    grad_mid, grad_att, sums_mid, *out_grad = mid_back(
        mid,
        grad_second,
        second_recv,
        grad_rows,
        row_of(ln2_gain),
        out_w[0],
        att_first,
        att_last,
        chunk if aligned else 0,
    )

    def tile_back(t, after, cost_part=1):
        last = t == tiles - 1
        return attend_backward(
            qkv,
            grad_att,
            att_last if last else att_first,
            0 if last else t,
            logs_last if last else logs_first,
            0 if last else t * (LANES // head_dim),
            t,
            heads,
            head_dim,
            after,
            cost_part,
        )

    grad_tiles = [None] * tiles
    grad_tiles[-1] = tile_back(tiles - 1, [result_keep], 64)
    result_pass = pass_on(result_keep, result_near, grad_tiles[-1:])
    result_far = quad_swap(result_pass, 2)
    after = [result_pass]
    if aligned:
        keep, send = sum_second(*waiting, [grad_tiles[-1]])
        moved = quad_swap(send, 1)
        sends = gate([ff_grads[1][1], ff_grads[1][3]], [keep])
        after = [keep, result_pass]
    grad_tiles[0] = tile_back(0, after, 64)
    after = [result_far]
    if aligned:
        unit_first = list(sum_third(keep, moved, [grad_tiles[0]]))
        unit_first[1] = quad_swap(unit_first[1], 2)
        after = unit_first[:1]
    for t in range(1, tiles - 1):
        grad_tiles[t] = tile_back(t, after)
    after = [result_far]
    if aligned:
        out_recv = from_part(out_grad[1], 1)
        waiting = begin_sum(1, sends, [grad_tiles[-2]])
        after = [waiting[0][0], unit_first[1], result_far, out_recv]
    qkv_grad = project_weights(
        x_all, row_of(ln1_gain), row_of(ln1_bias), grad_tiles, group, sequences, aligned, after
    )
    first_own, *found = project_rows(
        x_all,
        qkv_w,
        grad_tiles,
        sums_mid,
        up_sums,
        group,
        sequences,
        aligned,
        real,
        qkv_grad[:1],
    )
    first_send, (small, bias_sums) = found[: group - 1], found[group - 1 :]
    first_recv = [from_part(first_send[group - n - 1], n) for n in range(1, group)]
    row_parts = finish_rows(
        x_all, row_of(ln1_gain), grad_mid, first_own, first_recv, sequences, [first_own]
    )
    row_moved = over_quads(row_parts, group)

    after = []
    if aligned:
        small_rows = small.shape[0]
        packed = pack_attention(
            qkv_grad[0],
            from_part(qkv_grad[1], 1),
            out_grad[0],
            out_recv,
            small,
            from_part(small, 1),
            real,
            batch_size,
            [],
        )
        keep, send = sum_second(*waiting, packed[:1])
        unit_second = list(sum_third(keep, quad_swap(send, 1), packed[:1]))
        unit_second[1] = quad_swap(unit_second[1], 2)
        stay_a, pass_a, stay_b, pass_b = sum_first_attention(
            [packed[0], packed[2]],
            [swap(packed[1], "batch", batch_size, 1), swap(packed[3], "batch", batch_size, 2)],
            sequences // 2 * chunk,
            small_rows,
            [keep],
        )
        summed = sum_second_attention(
            [stay_a, stay_b],
            [swap(pass_a, "batch", batch_size, 2), swap(pass_b, "batch", batch_size, 1)],
            chunk,
            sequences,
            small_rows,
            row_moved[1:],
        )
        after = summed[:1]
        up_keep, up_send, down_grad = final_units(unit_first, unit_second, after)
        up_grad = final_join(up_keep, from_part(up_send, 1))
        qkv_final, out_final, small = final_attention(
            over_quads(summed, group), chunk, qkv_weight.shape[1] // batch_size, small_rows
        )
        small = small.reshape(-1)
    result = collect_halves(result_keep, result_near, result_far, group, after)
    result = result.reshape(tokens.shape)
    grad_in = collect(row_moved, group, after).reshape(tokens.shape)
    if not aligned:

        def spread(item, blocks):
            split = item.reshape(blocks, 1, -1)
            empty = jnp.zeros((blocks, group, split.shape[2]), F32)
            return lax.dynamic_update_slice(empty, split, (0, part, 0)).reshape(-1)

        bias_sums = bias_sums[0].reshape(tiles, 3, LANES).transpose(1, 0, 2)
        bias_sums = bias_sums.reshape(3, wide)[:, :real]
        small = jnp.concatenate(
            [
                small[0],
                small[1],
                spread(bias_sums[0], 1),
                spread(bias_sums[2], 1),
                sums_mid[2],
                sums_mid[0],
                sums_mid[1],
                spread(jnp.concatenate([item[0] for item in up_sums]), batch_size),
                sums_mid[3],
            ]
        )

        def scattered(item):
            item = lax.psum_scatter(item.astype(BF16), "seq", scatter_dimension=0, tiled=True)
            return lax.psum_scatter(item, "batch", scatter_dimension=1, tiled=True).astype(F32)

        def spread_columns(item, blocks):
            split = item.reshape(item.shape[0], blocks, 1, -1)
            empty = jnp.zeros((item.shape[0], blocks, group, split.shape[3]), item.dtype)
            filled = lax.dynamic_update_slice(empty, split, (0, 0, part, 0))
            return filled.reshape(item.shape[0], -1)

        up_full, down_full = [
            jnp.concatenate([item[e] for item in ff_grads], axis=1) for e in range(2)
        ]
        up_grad = scattered(spread_columns(up_full, batch_size))
        down_grad = scattered(spread_columns(down_full, batch_size).T)
        rows_full = qkv_grad[0].reshape(width, tiles, 3, LANES).transpose(0, 2, 1, 3)
        rows_full = rows_full.reshape(width, 3, wide)[..., :real]
        qkv_final = scattered(spread_columns(rows_full.reshape(width, -1), 3))
        out_final = scattered(spread_columns(out_grad[0][:real].T, 1).T)
        small = lax.psum(small, ("seq", "batch"))

    edges = [width] * 7 + [units, width]
    pieces, start = [], 0
    for size in edges:
        pieces.append(small[start : start + size])
        start += size
    return (
        result,
        grad_in,
        pieces[0],
        pieces[1],
        qkv_final,
        pieces[2],
        pieces[3],
        out_final,
        pieces[4],
        pieces[5],
        pieces[6],
        up_grad,
        pieces[7],
        down_grad,
        pieces[8],
    )


def solution(mesh):
    rows = P(None, "batch", "seq", None)
    split = P("seq", "batch")
    in_specs = (rows, P(None, "batch", "seq"), rows) + (P(),) * 13
    out_specs = (
        rows,
        rows,
        P(),
        P(),
        split,
        P(),
        P(),
        split,
        P(),
        P(),
        P(),
        split,
        P(),
        split,
        P(),
    )
    return jax.shard_map(
        on_device, mesh=mesh, in_specs=in_specs, out_specs=out_specs, check_vma=False
    )
```

```python
import jax
import jax.numpy as jnp
from jax import lax
from jax.experimental import pallas as pl
from jax.experimental.pallas import tpu as pltpu
from jax.sharding import PartitionSpec as P

HEADS = 20
EPS = 1e-05
LOG2E = 1.4426950408889634
ROWS = 256
F32 = jnp.float32
BF16 = jnp.bfloat16
LANES = 128


def dot(left, right):
    return jnp.dot(left, right, preferred_element_type=F32)


def dot_nt(left, right):
    return lax.dot_general(left, right, (((1,), (1,)), ((), ())), preferred_element_type=F32)


def norm_rows(rows_in):
    mean_val = jnp.mean(rows_in, axis=-1, keepdims=True)
    centered = rows_in - mean_val
    inv_std = lax.rsqrt(jnp.mean(centered * centered, axis=-1, keepdims=True) + EPS)
    return centered * inv_std, inv_std


def norm_back(scaled, normed, inv_std):
    inner = (
        scaled
        - jnp.mean(scaled, axis=-1, keepdims=True)
        - normed * jnp.mean(scaled * normed, axis=-1, keepdims=True)
    )
    return inner * inv_std


def params_of(mib):
    return pltpu.CompilerParams(vmem_limit_bytes=mib * 1024 * 1024)


def cost(flops, moved, trans=0, part=1):
    return pl.CostEstimate(
        flops=flops // part, bytes_accessed=moved // part, transcendentals=trans // part
    )


def sds(shape, dtype):
    return jax.ShapeDtypeStruct(shape, dtype)


VMEM = pl.BlockSpec(memory_space=pltpu.VMEM)
ANY = pl.BlockSpec(memory_space=pl.ANY)
HBM = pl.BlockSpec(memory_space=pltpu.HBM)


def run(body, operands, after=(), in_specs=None, out_specs=None, vmem=32, **more):
    count, extra = len(operands), len(after)

    def inner(*refs):
        body(*refs[:count], *refs[count + extra :])

    specs = [VMEM] * count if in_specs is None else list(in_specs)
    shapes = more["out_shape"]
    if out_specs is None:
        out_specs = [VMEM] * len(shapes) if isinstance(shapes, (list, tuple)) else VMEM
    return pl.pallas_call(
        inner,
        in_specs=specs + [ANY] * extra,
        out_specs=out_specs,
        compiler_params=params_of(vmem),
        **more,
    )(*operands, *after)


def gate(items, after):
    def body(*refs):
        del refs

    return pl.pallas_call(
        body,
        in_specs=[ANY] * (len(items) + len(after)),
        out_specs=[ANY] * len(items),
        out_shape=[sds(item.shape, item.dtype) for item in items],
        input_output_aliases={n: n for n in range(len(items))},
        cost_estimate=cost(0, 0),
        name="gate",
    )(*items, *after)


def place(group):
    spot = lax.axis_index("seq")
    return spot, lax.rem(spot, group), lax.div(spot, group)


def deal(item, group, after=()):
    count, rows, width = item.shape

    def body(in_ref, *out_refs):
        _, _, quad = place(group)
        for d in range(count):
            out_refs[d][...] = in_ref[quad ^ d]

    return run(
        body,
        [item],
        after,
        out_shape=[sds((rows, width), item.dtype)] * count,
        vmem=16,
        cost_estimate=cost(0, 4 * count * rows * width),
        name="deal",
    )


def stack(pieces, after):
    count = len(pieces)

    def body(*refs):
        for d in range(count):
            refs[count][d] = refs[d][...]

    return run(
        body,
        pieces,
        after,
        out_shape=sds((count,) + pieces[0].shape, pieces[0].dtype),
        vmem=16,
        cost_estimate=cost(0, 4 * count * pieces[0].size),
        name="stack",
    )


def swap(item, axis, size, distance):
    return lax.ppermute(item, axis, [(i, i ^ distance) for i in range(size)])


def over_quads(pieces, group):
    return [
        piece if d == 0 else swap(piece, "seq", len(pieces) * group, d * group)
        for d, piece in enumerate(pieces)
    ]


def pick_weights(qkv_weight, qkv_bias, out_weight, group, real, wide):
    width = qkv_weight.shape[0]
    tiles = wide // LANES

    def body(w_ref, b_ref, o_ref, wo_ref, bo_ref, *out_refs):
        _, part, _ = place(group)
        wo_ref[...] = jnp.zeros_like(wo_ref)
        bo_ref[...] = jnp.zeros_like(bo_ref)
        for ref in out_refs:
            ref[...] = jnp.zeros_like(ref)
        for c in range(group):

            @pl.when(part == c)
            def _(c=c):
                for p in range(3):
                    for t in range(tiles):
                        some = min(LANES, real - t * LANES)
                        src = p * width + c * real + t * LANES
                        dst = (3 * t + p) * LANES
                        wo_ref[:, dst : dst + some] = w_ref[:, src : src + some]
                        bo_ref[:, dst : dst + some] = b_ref[:, src : src + some]
                for n in range(group):
                    src = (c + n) % group * real
                    out_refs[n][0:real, :] = o_ref[src : src + real, :]

    return pl.pallas_call(
        body,
        out_shape=[sds((width, 3 * wide), BF16), sds((1, 3 * wide), F32)]
        + [sds((wide, width), BF16)] * group,
        compiler_params=params_of(24),
        cost_estimate=cost(0, 8 * 1024 * 1024),
        name="pick_weights",
    )(qkv_weight, qkv_bias, out_weight)


def by_pairs(live, visit):
    size = 2 if live % 2 == 0 else 1

    @pl.loop(0, live // size)
    def _(i):
        visit([i * size + e for e in range(size)])


def attend_tiles(query_at, keys_at, vals_at, att_ref, lse_ref, keys, vals, acc, tiles, heads, head_dim):
    per_tile = LANES // head_dim
    total = att_ref.shape[0]
    exp_scale = head_dim ** (-0.5) * LOG2E
    lane = lax.broadcasted_iota(jnp.int32, (1, LANES), 1)
    row = lax.broadcasted_iota(jnp.int32, (LANES, 1), 0)
    lse_ref[...] = jnp.zeros_like(lse_ref)
    vals[:, :, LANES:] = jnp.ones((per_tile, total, LANES), BF16)
    for n, t in enumerate(tiles):
        live = min(per_tile, heads - t * per_tile)
        key_t = keys_at(n).astype(F32).T
        val_f = vals_at(n).astype(F32)
        for j in range(live):
            keys[j] = jnp.where(row // head_dim == j, key_t, 0.0).astype(BF16)
            vals[j, :, :LANES] = jnp.where(lane // head_dim == j, val_f, 0.0).astype(BF16)
        acc[...] = jnp.zeros_like(acc)

        def visit(some, n=n):
            scores = [dot(query_at(n), keys[j]) for j in some]
            for item, j in zip(scores, some):
                row_max = jnp.max(item, axis=-1, keepdims=True) * exp_scale
                expd = jnp.exp2(item * exp_scale - row_max).astype(BF16)
                mixed = dot(expd, vals[j])
                den = mixed[:, LANES:]
                acc[...] += mixed[:, :LANES] / den
                lse_ref[...] = jnp.where(
                    lane == n * per_tile + j, row_max + jnp.log2(den), lse_ref[...]
                )

        by_pairs(live, visit)
        att_ref[:, n * LANES : (n + 1) * LANES] = acc[...].astype(BF16)


def attend_scratch(total, head_dim):
    per_tile = LANES // head_dim
    return [
        pltpu.VMEM((per_tile, LANES, total), BF16),
        pltpu.VMEM((per_tile, total, 2 * LANES), BF16),
        pltpu.VMEM((total, LANES), F32),
    ]


def attend_first(x_pieces, gain, shift, weight, bias, tiles, heads, head_dim):
    count = len(x_pieces)
    piece_rows, width = x_pieces[0].shape
    total = count * piece_rows
    cols_all = weight.shape[1]

    def body(*refs):
        x_refs = refs[:count]
        gain_ref, shift_ref, w_ref, bias_ref = refs[count : count + 4]
        x_ref, qkv_ref, att_ref, lse_ref, keys, vals, acc = refs[count + 4 :]
        for n in range(count):
            x_ref[n * piece_rows : (n + 1) * piece_rows, :] = x_refs[n][...]

        @pl.loop(0, total // ROWS)
        def _(i):
            rows = pl.ds(pl.multiple_of(i * ROWS, ROWS), ROWS)
            normed, _ = norm_rows(x_ref[rows, :].astype(F32))
            low = (normed * gain_ref[...] + shift_ref[...]).astype(BF16)
            qkv_ref[rows, :] = (dot(low, w_ref[...]) + bias_ref[...]).astype(BF16)

        def columns(at):
            return slice(at * LANES, (at + 1) * LANES)

        attend_tiles(
            lambda n: qkv_ref[:, columns(3 * n)],
            lambda n: qkv_ref[:, columns(3 * n + 1)],
            lambda n: qkv_ref[:, columns(3 * n + 2)],
            att_ref,
            lse_ref,
            keys,
            vals,
            acc,
            range(tiles),
            heads,
            head_dim,
        )

    return run(
        body,
        [*x_pieces, gain, shift, weight, bias],
        out_shape=[
            sds((total, width), BF16),
            sds((total, cols_all), BF16),
            sds((total, tiles * LANES), BF16),
            sds((total, LANES), F32),
        ],
        scratch_shapes=attend_scratch(total, head_dim),
        vmem=30,
        cost_estimate=cost(
            2 * total * width * cols_all + 4 * heads * total * total * 256,
            8 * 1024 * 1024,
            heads * total * total,
        ),
        name="attend_first",
    )


def attend_last(qkv, tile, heads, head_dim, after):
    total = qkv.shape[0]

    def body(qkv_ref, att_ref, lse_ref, keys, vals, acc):
        attend_tiles(
            lambda n: qkv_ref[:, 0:LANES],
            lambda n: qkv_ref[:, LANES : 2 * LANES],
            lambda n: qkv_ref[:, 2 * LANES : 3 * LANES],
            att_ref,
            lse_ref,
            keys,
            vals,
            acc,
            [tile],
            heads,
            head_dim,
        )

    live = heads - tile * (LANES // head_dim)
    return run(
        body,
        [qkv],
        after,
        grid=(1,),
        in_specs=[pl.BlockSpec((total, 3 * LANES), lambda i: (0, tile))],
        out_specs=[pl.BlockSpec((total, LANES), lambda i: (0, 0))] * 2,
        out_shape=[sds((total, LANES), BF16), sds((total, LANES), F32)],
        scratch_shapes=attend_scratch(total, head_dim),
        vmem=26,
        cost_estimate=cost(4 * live * total * total * 256, 2 * 1024 * 1024, live * total * total),
        name="attend_last",
    )


def gelu_parts(value):
    size = jnp.abs(value)
    near = pl.reciprocal(1.0 + (0.3275911 * 0.7071067811865476) * size, approx=True)
    bell = jnp.exp2(value * value * (-0.5 * LOG2E))
    poly = near * (
        0.5 * 0.254829592
        + near
        * (
            0.5 * -0.284496736
            + near * (0.5 * 1.421413741 + near * (0.5 * -1.453152027 + near * (0.5 * 1.061405429)))
        )
    )
    tail = poly * bell
    area = jnp.where(value < 0.0, tail, 1.0 - tail)
    return value * area, area + value * bell * 0.3989422804014327


class Units:
    def __init__(self, block, blocks, start, size, stride, quads, high):
        self.block, self.blocks, self.start, self.size = block, blocks, start, size
        self.stride, self.quads, self.high = stride, quads, high
        self.count = blocks * size
        self.chunk = 512 if self.count % 512 == 0 else 256
        self.packed = quads is not None

    def loads(self, part, hbm_up, hbm_down, hbm_bias, up_ref, down_ref, bias_ref, sem):
        copies = []
        for b in range(self.blocks):
            src = self.start
            if self.packed:
                src = pl.multiple_of((b * self.stride + part) * self.block, LANES) + self.start
            src = pl.ds(src, self.size)
            dst = pl.ds(b * self.size, self.size)
            copies.append(
                pltpu.make_async_copy(hbm_up.at[:, src], up_ref.at[:, dst], sem.at[2 * b])
            )
            copies.append(
                pltpu.make_async_copy(hbm_down.at[src, :], down_ref.at[dst, :], sem.at[2 * b + 1])
            )
            bias_ref[0:1, dst] = hbm_bias[:, src]
        return copies

    def grad_shapes(self, width):
        if self.packed:
            return [sds((2, self.quads, self.high, self.size), BF16)] * 4
        return [sds((width, self.count), BF16)] * 2

    def scratch(self, total, width):
        grads = (self.blocks, self.quads, self.high, self.size) if self.packed else (8, LANES)
        return [
            pltpu.VMEM(grads, BF16),
            pltpu.VMEM(grads, BF16),
            pltpu.SemaphoreType.DMA((8,)),
            pltpu.VMEM((total, self.count), BF16),
            pltpu.VMEM((total, self.count), BF16),
            pltpu.VMEM((width, self.count), BF16),
            pltpu.VMEM((self.count, width), BF16),
            pltpu.VMEM((8, self.count), F32),
            pltpu.SemaphoreType.DMA((2 * self.blocks,)),
        ]

    def compute(self, part, second, second_t, grad, grad_t, acc, gs, ubg, scratch, outs):
        up_slots, down_slots, out_sem, acts, grad_pres, up_ref, down_ref, bias_ref, _ = scratch
        if not self.packed:
            up_slots, down_slots = outs
        quad = lax.div(lax.axis_index("seq"), self.stride)
        mine = lax.axis_index("batch")

        def enter(i):
            rows = slice(i * ROWS, (i + 1) * ROWS)
            pre = dot(second[rows, :], up_ref[...]) + bias_ref[0:1, :]
            return pre, dot_nt(grad[rows, :], down_ref[...])

        def weights(n):
            first, last = n * self.chunk, (n + 1) * self.chunk
            up_grad = dot(second_t[...], grad_pres[:, first:last]).astype(BF16)
            down_grad = dot(grad_t[...], acts[:, first:last]).astype(BF16)
            if not self.packed:
                up_slots[:, first:last] = up_grad
                down_slots[:, first:last] = down_grad
                return
            at = first
            while at < last:
                block = at // self.size
                stop = min(last, (block + 1) * self.size)
                src = slice(at - first, stop - first)
                dst = slice(at - block * self.size, stop - block * self.size)
                for m in range(self.blocks):
                    rows = slice(m * self.high, (m + 1) * self.high)
                    up_slots[block ^ mine, m ^ quad, :, dst] = up_grad[rows, src]
                    down_slots[m ^ mine, block ^ quad, :, dst] = down_grad[rows, src]
                at = stop

        ready = enter(0)
        chunks = second.shape[0] // ROWS
        for i in range(chunks):
            ahead = enter(i + 1) if i + 1 < chunks else None
            rows = slice(i * ROWS, (i + 1) * ROWS)
            pre, grad_act = ready
            value, slope = gelu_parts(pre)
            act = value.astype(BF16)
            grad_pre = (grad_act * slope).astype(BF16)
            acts[rows, :] = act
            grad_pres[rows, :] = grad_pre
            ubg[0:1, :] += jnp.sum(grad_pre.astype(F32), axis=0, keepdims=True)
            acc[rows, :] += dot(act, down_ref[...])
            gs[rows, :] += dot_nt(grad_pre, up_ref[...])
            ready = ahead
        for n in range(self.count // self.chunk):
            weights(n)
        stores = []
        if self.packed:
            order = ((up_slots, (0, 2)), (up_slots, (1, 3)), (down_slots, (0, 1)), (down_slots, (2, 3)))
            for m, (source, slots) in enumerate(order):
                for n in range(2):
                    stores.append(
                        pltpu.make_async_copy(
                            source.at[slots[n]], outs[m].at[n], out_sem.at[2 * m + n]
                        )
                    )
        return stores


def feed_first(
    rows_all, att_first, att_last, cot_pieces, out_w, out_b, gain, shift, up, up_b, down, down_b, units
):
    pieces = len(att_first)
    total, width = rows_all.shape
    piece_rows = total // pieces
    count = len(cot_pieces)
    cot_rows = total // count
    split = att_first[0].shape[1]
    grads = units.grad_shapes(width)

    def body(*refs):
        x_ref, refs = refs[0], refs[1:]
        att_refs, refs = refs[: 2 * pieces], refs[2 * pieces :]
        cot_refs, refs = refs[:count], refs[count:]
        wo_refs, refs = refs[:pieces], refs[pieces:]
        ob_ref, gain_ref, shift_ref, up_hbm, ub_ref, down_hbm, db_ref = refs[:7]
        mid_ref, second, second_t, grad, grad_t, own_ref, low_ref, ubg, refs = *refs[7:15], refs[15:]
        send_refs, refs = refs[: pieces - 1], refs[pieces - 1 :]
        outs, (acc, gs), scratch = refs[: len(grads)], refs[len(grads) :][:2], refs[len(grads) + 2 :]
        _, part, _ = place(pieces)
        loads = units.loads(part, up_hbm, down_hbm, ub_ref, *scratch[5:])
        for load in loads:
            load.start()
        ubg[...] = jnp.zeros_like(ubg)
        masked = jnp.zeros((1, width), F32)
        for ref in cot_refs:
            masked = masked + ref[cot_rows : cot_rows + 1, :].astype(F32)
        factor = total / (4.0 * masked)
        for n in range(count):
            scaled = cot_refs[n][0:cot_rows, :].astype(F32) * factor
            dst = slice(n * cot_rows, (n + 1) * cot_rows)
            grad[dst, :] = scaled.astype(BF16)

        for h in range(pieces):

            @pl.loop(0, piece_rows // ROWS)
            def _(i, h=h):
                at = pl.multiple_of(i * ROWS, ROWS)
                dst = pl.ds(h * piece_rows + at, ROWS)
                mid = x_ref[dst, :].astype(F32) + ob_ref[...]
                for n in range(pieces):
                    src = pl.ds(((h - n) % pieces) * piece_rows + at, ROWS)
                    mid = mid + dot(att_refs[2 * n][src, :], wo_refs[n][0:split, :])
                    mid = mid + dot(att_refs[2 * n + 1][src, :], wo_refs[n][split:, :])
                mid_ref[dst, :] = mid
                normed, _ = norm_rows(mid)
                low = normed * gain_ref[...] + shift_ref[...]
                second[dst, :] = low.astype(BF16)
                second_t[:, dst] = low.T.astype(BF16)
                grad_t[:, dst] = grad[dst, :].astype(F32).T.astype(BF16)
                acc[dst, :] = mid + db_ref[...] if h == 0 else jnp.zeros((ROWS, width), F32)
                gs[dst, :] = jnp.zeros((ROWS, width), F32)

        for load in loads:
            load.wait()
        stores = units.compute(
            part, second, second_t, grad, grad_t, acc, gs, ubg, scratch, outs
        )
        for store in stores:
            store.start()
        own_ref[...] = acc[0:piece_rows, :]
        low_ref[...] = gs[...].astype(BF16)
        for h in range(1, pieces):
            send_refs[h - 1][...] = acc[h * piece_rows : (h + 1) * piece_rows, :].astype(BF16)
        for store in stores:
            store.wait()

    att_all = [item for pair in zip(att_first, att_last) for item in pair]
    turned = sds((width, total), BF16)
    flat = sds((total, width), BF16)
    wide = sds((total, width), F32)
    half = sds((piece_rows, width), F32)
    return run(
        body,
        [rows_all, *att_all, *cot_pieces, *out_w, out_b, gain, shift, up, up_b, down, down_b],
        in_specs=[VMEM] * (1 + 3 * pieces + count) + [VMEM, VMEM, VMEM, HBM, VMEM, HBM, VMEM],
        out_specs=[VMEM] * (7 + pieces) + [HBM if units.packed else VMEM] * len(grads),
        out_shape=[wide, flat, turned, flat, turned, half, flat, sds((8, units.count), F32)]
        + [sds((piece_rows, width), BF16)] * (pieces - 1)
        + grads,
        scratch_shapes=[pltpu.VMEM((total, width), F32)] * 2 + units.scratch(total, width),
        vmem=24,
        cost_estimate=cost(12 * total * width * units.count, 24 * 1024 * 1024, total * units.count),
        name="feed_first",
    )


def feed_second(second, second_t, grad, grad_t, own_first, low_first, sends, up, up_b, down, units):
    pieces = 1 + len(sends)
    total, width = second.shape
    piece_rows = total // pieces
    grads = units.grad_shapes(width)

    def body(*refs):
        second, second_t, grad, grad_t, own_in, low_in, up_hbm, ub_ref, down_hbm, refs = (
            *refs[:9],
            refs[9:],
        )
        send_ins, refs = refs[: pieces - 1], refs[pieces - 1 :]
        own_ref, low_ref, ubg, refs = refs[0], refs[1], refs[2], refs[3:]
        send_refs, refs = refs[: pieces - 1], refs[pieces - 1 :]
        outs, (acc, gs), scratch = refs[: len(grads)], refs[len(grads) :][:2], refs[len(grads) + 2 :]
        _, part, _ = place(pieces)
        loads = units.loads(part, up_hbm, down_hbm, ub_ref, *scratch[5:])
        for load in loads:
            load.start()
        ubg[...] = jnp.zeros_like(ubg)
        acc[...] = jnp.zeros_like(acc)
        gs[...] = jnp.zeros_like(gs)
        for load in loads:
            load.wait()
        stores = units.compute(
            part, second, second_t, grad, grad_t, acc, gs, ubg, scratch, outs
        )
        for store in stores:
            store.start()
        low_ref[...] = (gs[...] + low_in[...].astype(F32)).astype(BF16)
        own_ref[...] = acc[0:piece_rows, :] + own_in[...]
        for h in range(1, pieces):
            item = acc[h * piece_rows : (h + 1) * piece_rows, :] + send_ins[h - 1][...].astype(F32)
            send_refs[h - 1][...] = item.astype(BF16)
        for store in stores:
            store.wait()

    return run(
        body,
        [second, second_t, grad, grad_t, own_first, low_first, up, up_b, down, *sends],
        in_specs=[VMEM] * 6 + [HBM, VMEM, HBM] + [VMEM] * (pieces - 1),
        out_specs=[VMEM] * (2 + pieces) + [HBM if units.packed else VMEM] * len(grads),
        out_shape=[
            sds((piece_rows, width), F32),
            sds((total, width), BF16),
            sds((8, units.count), F32),
        ]
        + [sds((piece_rows, width), BF16)] * (pieces - 1)
        + grads,
        scratch_shapes=[pltpu.VMEM((total, width), F32)] * 2 + units.scratch(total, width),
        vmem=34,
        cost_estimate=cost(12 * total * width * units.count, 24 * 1024 * 1024, total * units.count),
        name="feed_second",
    )


def mid_back(mid, grad_second, received, grad_rows, gain, out_w, att_first, att_last, chunk):
    pieces = 1 + len(received)
    total, width = mid.shape
    piece_rows = total // pieces
    split = att_first.shape[1]
    wide = split + att_last.shape[1]

    def body(*refs):
        mid_ref, gs_ref, refs = refs[0], refs[1], refs[2:]
        recv_refs, refs = refs[: pieces - 1], refs[pieces - 1 :]
        go_ref, gain_ref, wo_ref, att_ref, last_ref = refs[:5]
        gm_ref, do_ref, sums_ref, *dwo_refs, low_ref = refs[5:]
        sums_ref[...] = jnp.zeros_like(sums_ref)
        for h in range(pieces):

            @pl.loop(0, piece_rows // ROWS)
            def _(i, h=h):
                at = pl.multiple_of(i * ROWS, ROWS)
                rows = pl.ds(h * piece_rows + at, ROWS)
                normed, inv_std = norm_rows(mid_ref[rows, :])
                grad = gs_ref[rows, :].astype(F32)
                for n in range(1, pieces):
                    src = pl.ds(((h - n) % pieces) * piece_rows + at, ROWS)
                    grad = grad + recv_refs[n - 1][src, :].astype(F32)
                go = go_ref[rows, :].astype(F32)
                grad_mid = go + norm_back(grad * gain_ref[...], normed, inv_std)
                low = grad_mid.astype(BF16)
                low_ref[rows, :] = low
                do_ref[rows, :] = dot_nt(low, wo_ref[...]).astype(BF16)
                if h == 0:
                    gm_ref[rows, :] = grad_mid
                    for n, item in enumerate((grad * normed, grad, low.astype(F32), go)):
                        sums_ref[n : n + 1, :] += jnp.sum(item, axis=0, keepdims=True)

        grad_out_w = jnp.concatenate(
            [
                dot(ref[...].astype(F32).T.astype(BF16), low_ref[...]).astype(BF16)
                for ref in (att_ref, last_ref)
            ],
            axis=0,
        )
        if chunk == 0:
            dwo_refs[0][...] = grad_out_w
            return
        _, part, _ = place(pieces)
        for c in range(pieces):

            @pl.when(part == c)
            def _(c=c):
                for n in range(dwo_refs[0].shape[0]):
                    for e in range(pieces):
                        at = (n * pieces + (c + e) % pieces) * chunk
                        dwo_refs[e][n] = grad_out_w[at : at + chunk, :]

    if chunk == 0:
        grads = [sds((wide, width), BF16)]
    else:
        grads = [sds((width // (pieces * pieces * chunk), chunk, width), BF16)] * pieces
    return run(
        body,
        [mid, grad_second, *received, grad_rows, gain, out_w, att_first, att_last],
        out_shape=[
            sds((piece_rows, width), F32),
            sds((total, wide), BF16),
            sds((8, width), F32),
        ]
        + grads,
        scratch_shapes=[pltpu.VMEM((total, width), BF16)],
        vmem=20,
        cost_estimate=cost(4 * total * width * wide, 14 * 1024 * 1024),
        name="mid_back",
    )


def attend_backward(
    qkv, grad_att, att, att_tile, logs, lane_first, tile, heads, head_dim, after=(), part=1
):
    total = qkv.shape[0]
    per_tile = LANES // head_dim
    live = min(per_tile, heads - tile * per_tile)
    scale = head_dim ** (-0.5)
    exp_scale = scale * LOG2E

    def body(qkv_ref, do_ref, att_ref, lse_ref, out_ref, *scratch):
        km, vm, qm, dm, key_t, query_t, do_t, dq_t, lse_t, mean_t = scratch
        lane = lax.broadcasted_iota(jnp.int32, (1, LANES), 1)
        lse_t[...] = lse_ref[...].T
        query = qkv_ref[:, 0:LANES].astype(F32)
        key = qkv_ref[:, LANES : 2 * LANES].astype(F32)
        val = qkv_ref[:, 2 * LANES : 3 * LANES].astype(F32)
        upstream = do_ref[...].astype(F32)
        both_t = (upstream * att_ref[...].astype(F32)).T
        for j in range(live):
            mean_t[j : j + 1, :] = jnp.sum(
                both_t[j * head_dim : (j + 1) * head_dim, :], axis=0, keepdims=True
            )
        query_t[...] = query.T.astype(BF16)
        do_t[...] = upstream.T.astype(BF16)
        key_t[...] = key.T.astype(BF16)
        for j in range(live):
            mine = lane // head_dim == j
            km[j] = jnp.where(mine, key, 0.0).astype(BF16)
            vm[j] = jnp.where(mine, val, 0.0).astype(BF16)
            qm[j] = jnp.where(mine, query, 0.0).astype(BF16)
            dm[j] = jnp.where(mine, upstream, 0.0).astype(BF16)
        dq_t[...] = jnp.zeros_like(dq_t)

        @pl.loop(0, total // ROWS)
        def _(i):
            rows = pl.ds(pl.multiple_of(i * ROWS, ROWS), ROWS)
            grad_key = jnp.zeros((ROWS, LANES), F32)
            grad_val = jnp.zeros((ROWS, LANES), F32)

            def enter(j):
                return dot(km[j, rows, :], query_t[...]), dot(vm[j, rows, :], do_t[...])

            ready = enter(0)
            for j in range(live):
                ahead = enter(j + 1) if j + 1 < live else None
                scores, grad_prob = ready
                head = lane_first + j
                own = slice(j * head_dim, (j + 1) * head_dim)
                probs = jnp.exp2(scores * exp_scale - lse_t[head : head + 1, :])
                grad_scores = (probs * (grad_prob - mean_t[j : j + 1, :])).astype(BF16)
                grad_val = grad_val + dot(probs.astype(BF16), dm[j])
                grad_key = grad_key + dot(grad_scores, qm[j])
                dq_t[own, :] += dot(key_t[own, rows], grad_scores)
                ready = ahead
            out_ref[rows, LANES : 2 * LANES] = (grad_key * scale).astype(BF16)
            out_ref[rows, 2 * LANES : 3 * LANES] = grad_val.astype(BF16)

        out_ref[:, 0:LANES] = (dq_t[...].T * scale).astype(BF16)

    masked = pltpu.VMEM((live, total, LANES), BF16)
    turned = pltpu.VMEM((LANES, total), BF16)
    turned_f = pltpu.VMEM((LANES, total), F32)
    return run(
        body,
        [qkv, grad_att, att, logs],
        after,
        grid=(1,),
        in_specs=[
            pl.BlockSpec((total, 3 * LANES), lambda i: (0, tile)),
            pl.BlockSpec((total, LANES), lambda i: (0, tile)),
            pl.BlockSpec((total, LANES), lambda i: (0, att_tile)),
            pl.BlockSpec((total, LANES), lambda i: (0, 0)),
        ],
        out_specs=pl.BlockSpec((total, 3 * LANES), lambda i: (0, 0)),
        out_shape=sds((total, 3 * LANES), BF16),
        scratch_shapes=[masked] * 4
        + [turned] * 3
        + [turned_f] * 2
        + [pltpu.VMEM((8, total), F32)],
        vmem=22,
        cost_estimate=cost(
            2 * live * total * total * 256 * 5, 3 * 1024 * 1024, live * total * total, part
        ),
        name="attend_backward",
    )


def project_weights(rows_all, gain, shift, grad_tiles, pieces, quads, packed, after):
    total, width = rows_all.shape
    tiles = len(grad_tiles)
    tile_cols = grad_tiles[0].shape[1]
    cols_all = tiles * tile_cols
    chunk = width // (quads * pieces)

    def body(*refs):
        x_ref, gain_ref, shift_ref, refs = refs[0], refs[1], refs[2], refs[3:]
        dq_refs, (*dw_refs, low_t, part_ref) = refs[:tiles], refs[tiles:]
        _, part, quad = place(pieces)

        @pl.loop(0, total // ROWS)
        def _(i):
            rows = pl.ds(pl.multiple_of(i * ROWS, ROWS), ROWS)
            normed, _ = norm_rows(x_ref[rows, :].astype(F32))
            low_t[:, rows] = (normed * gain_ref[...] + shift_ref[...]).T.astype(BF16)

        for t in range(tiles):
            cols = slice(t * tile_cols, (t + 1) * tile_cols)
            part_ref[...] = dot(low_t[...], dq_refs[t][...]).astype(BF16)
            if not packed:
                dw_refs[0][:, cols] = part_ref[...]
                continue
            for c in range(pieces):

                @pl.when(part == c)
                def _(c=c, cols=cols):
                    for q in range(quads):
                        for e in range(pieces):
                            at = (q * pieces + (c + e) % pieces) * chunk
                            dw_refs[e][q ^ quad, :, cols] = part_ref[at : at + chunk, :]

    if packed:
        grads = [sds((quads, chunk, cols_all), BF16)] * pieces
    else:
        grads = [sds((width, cols_all), BF16)]
    return run(
        body,
        [rows_all, gain, shift, *grad_tiles],
        after,
        out_shape=grads,
        scratch_shapes=[pltpu.VMEM((width, total), BF16), pltpu.VMEM((width, tile_cols), BF16)],
        vmem=14,
        cost_estimate=cost(2 * total * width * cols_all, 6 * 1024 * 1024, 0, 64),
        name="project_weights",
    )


def project_rows(
    rows_all, weight, grad_tiles, sums_mid, up_sums, pieces, quads, packed, real, after
):
    total, width = rows_all.shape
    piece_rows = total // pieces
    cols_all = weight.shape[1]
    tiles = len(grad_tiles)
    tile_cols = cols_all // tiles

    def body(*refs):
        x_ref, w_ref, mid_ref, refs = *refs[:3], refs[3:]
        ups_refs, refs = refs[: len(up_sums)], refs[len(up_sums) :]
        dq_refs, refs = refs[:tiles], refs[tiles:]
        own_ref, refs = refs[0], refs[1:]
        send_refs, (sums_ref, bias_ref) = refs[: pieces - 1], refs[pieces - 1 :]
        _, part, _ = place(pieces)
        sums_ref[...] = jnp.zeros_like(sums_ref)
        bias_ref[...] = jnp.zeros_like(bias_ref)
        for h in range(pieces):

            @pl.loop(0, piece_rows // ROWS)
            def _(i, h=h):
                at = pl.multiple_of(i * ROWS, ROWS)
                src = pl.ds(at, ROWS)
                rows = pl.ds(h * piece_rows + at, ROWS)
                normed, _ = norm_rows(x_ref[rows, :].astype(F32))
                grad = jnp.zeros((ROWS, width), F32)
                for t in range(tiles):
                    grad_rows = dq_refs[t][rows, :]
                    cols = slice(t * tile_cols, (t + 1) * tile_cols)
                    grad = grad + dot_nt(grad_rows, w_ref[:, cols])
                    bias_ref[0:1, cols] += jnp.sum(grad_rows.astype(F32), axis=0, keepdims=True)
                if h == 0:
                    own_ref[src, :] = grad
                else:
                    send_refs[h - 1][src, :] = grad.astype(BF16)
                sums_ref[0:1, :] += jnp.sum(grad * normed, axis=0, keepdims=True)
                sums_ref[1:2, :] += jnp.sum(grad, axis=0, keepdims=True)

        if not packed:
            return
        for row, src in ((4, 2), (5, 0), (6, 1), (15, 3)):
            sums_ref[row : row + 1, :] = mid_ref[src : src + 1, :]
        for c in range(pieces):

            @pl.when(part == c)
            def _(c=c):
                for row, p in ((2, 0), (3, 2)):
                    mine = jnp.concatenate(
                        [
                            bias_ref[0:1, (3 * t + p) * LANES :][:, : min(LANES, real - t * LANES)]
                            for t in range(tiles)
                        ],
                        axis=1,
                    )
                    sums_ref[row : row + 1, c * real : (c + 1) * real] = mine
                for n in range(quads):
                    row = 7 + n * pieces + c
                    start = 0
                    for ref in ups_refs:
                        size = ref.shape[1] // quads
                        here = ref[0:1, n * size : (n + 1) * size]
                        sums_ref[row : row + 1, start : start + size] = here
                        start += size

    return run(
        body,
        [rows_all, weight, sums_mid, *up_sums, *grad_tiles],
        after,
        out_shape=[sds((piece_rows, width), F32)]
        + [sds((piece_rows, width), BF16)] * (pieces - 1)
        + [sds((16, width), F32), sds((8, cols_all), F32)],
        vmem=16,
        cost_estimate=cost(2 * total * width * cols_all, 8 * 1024 * 1024, 0, 64),
        name="project_rows",
    )


def finish_rows(rows_all, gain, grad_mid, grad_own, received, count, after):
    rows, width = grad_mid.shape
    others = len(received)
    piece = rows // count
    per_step = ROWS // piece

    def body(*refs):
        x_ref, gain_ref, gm_ref, own_ref, refs = refs[0], refs[1], refs[2], refs[3], refs[4:]
        recv_refs, out_refs = refs[:others], refs[others:]
        for n in range(rows // ROWS):
            at = slice(n * ROWS, (n + 1) * ROWS)
            normed, inv_std = norm_rows(x_ref[at, :].astype(F32))
            grad = own_ref[at, :]
            for ref in recv_refs:
                grad = grad + ref[at, :].astype(F32)
            done = gm_ref[at, :] + norm_back(grad * gain_ref[...], normed, inv_std)
            for e in range(per_step):
                d = n * per_step + e
                out_refs[d % 2][d // 2] = done[e * piece : (e + 1) * piece, :].astype(BF16)

    return run(
        body,
        [rows_all, gain, grad_mid, grad_own, *received],
        after,
        out_shape=[sds((count // 2, piece, width), BF16)] * 2,
        vmem=16,
        cost_estimate=cost(20 * rows * width, 6 * 1024 * 1024),
        name="finish_rows",
    )


def finish_result(own, received, count):
    rows, width = own.shape
    others = len(received)
    piece = rows // count

    def body(*refs):
        out_refs = refs[1 + others :]
        for n in range(count):
            at = slice(n * piece, (n + 1) * piece)
            total = refs[0][at, :]
            for ref in refs[1 : 1 + others]:
                total = total + ref[at, :].astype(F32)
            out_refs[n % 2][n // 2] = total.astype(BF16)

    return run(
        body,
        [own, *received],
        out_shape=[sds((count // 2, piece, width), BF16)] * 2,
        vmem=16,
        cost_estimate=cost(2 * rows * width, 3 * 1024 * 1024),
        name="finish_result",
    )


def pass_on(keep, received, after):
    def body(keep_ref, recv_ref, out_ref):
        out_ref[0] = keep_ref[1]
        out_ref[1] = recv_ref[1]

    return run(
        body,
        [keep, received],
        after,
        out_shape=sds(keep.shape, keep.dtype),
        vmem=16,
        cost_estimate=cost(0, 4 * keep.size),
        name="pass_on",
    )


def collect_halves(keep, near, far, group, after):
    _, rows, width = keep.shape

    def body(keep_ref, near_ref, far_ref, out_ref):
        _, _, quad = place(group)
        out_ref[quad] = keep_ref[0]
        out_ref[quad ^ 1] = near_ref[0]
        out_ref[quad ^ 2] = far_ref[0]
        out_ref[quad ^ 3] = far_ref[1]

    return run(
        body,
        [keep, near, far],
        after,
        out_shape=sds((4, rows, width), keep.dtype),
        vmem=16,
        cost_estimate=cost(0, 16 * rows * width),
        name="collect_halves",
    )


def two_parts(item):
    first = item.astype(BF16)
    return first, (item - first.astype(F32)).astype(BF16)


def pack_attention(
    qkv_keep, qkv_recv, out_keep, out_recv, small, small_recv, real, blocks, after
):
    quads, chunk, cols_all = qkv_keep.shape
    wide = cols_all // 3
    tiles = wide // LANES
    width = out_keep.shape[2]
    qkv_lanes = 6 * real // blocks
    out_lanes = width // blocks
    lanes = qkv_lanes + out_lanes
    halves = quads // 2
    slot = halves * chunk
    small_rows = small.shape[0]

    def body(qk_ref, qr_ref, ok_ref, or_ref, small_ref, srecv_ref, *out_refs):
        _, part, quad = place(2)
        mine = lax.axis_index("batch")
        slots = out_refs[4]

        def heads_of(rows, p):
            return [
                rows[:, (3 * t + p) * LANES : (3 * t + p) * LANES + min(LANES, real - t * LANES)]
                for t in range(tiles)
            ]

        for c in range(2):

            @pl.when(part == c)
            def _(c=c):
                for q in range(quads):
                    pair = (qk_ref[q], qr_ref[q])
                    if c == 1:
                        pair = pair[::-1]
                    parts = []
                    for p in range(3):
                        parts += heads_of(pair[0], p) + heads_of(pair[1], p)
                    row = jnp.concatenate(parts, axis=1)
                    for b in range(blocks):
                        slots[b ^ mine, q, :, 0:qkv_lanes] = row[
                            :, b * qkv_lanes : (b + 1) * qkv_lanes
                        ]
                for e, ref in enumerate((ok_ref, or_ref)):
                    for n in range(halves):
                        q = ((c + e) % 2) * halves + n
                        for b in range(blocks):
                            slots[b ^ mine, q ^ quad, :, qkv_lanes:lanes] = ref[
                                n, :, b * out_lanes : (b + 1) * out_lanes
                            ]

        for n, order in enumerate(((0, 2), (1, 3), (0, 1), (2, 3))):
            for e in range(2):
                for f in range(halves):
                    at = e * slot + f * chunk
                    src = f if n < 2 else halves + f
                    out_refs[n][at : at + chunk, :] = slots[order[e], src]
        parts = two_parts(small_ref[...] + srecv_ref[...])
        for n in range(2):
            for e in range(2):
                at = 2 * slot + e * small_rows
                out_refs[n][at : at + small_rows, :] = parts[e]

    first = sds((2 * slot + 2 * small_rows, lanes), BF16)
    other = sds((2 * slot, lanes), BF16)
    return run(
        body,
        [qkv_keep, qkv_recv, out_keep, out_recv, small, small_recv],
        after,
        out_shape=[first, first, other, other],
        scratch_shapes=[pltpu.VMEM((blocks, quads, chunk, lanes), BF16)],
        vmem=24,
        cost_estimate=cost(0, 4 * 1024 * 1024),
        name="pack_attention",
    )


def sum_first(keeps, received, after=()):
    count = len(keeps)
    shape = keeps[0].shape[1:]

    def body(*refs):
        for n in range(count):
            for e in range(2):
                total = refs[n][e].astype(F32) + refs[count + n][e].astype(F32)
                refs[2 * count + 2 * n + e][...] = total.astype(BF16)

    return run(
        body,
        [*keeps, *received],
        after,
        out_shape=[sds(shape, BF16)] * (2 * count),
        vmem=24,
        cost_estimate=cost(0, 6 * count * keeps[0].size),
        name="sum_first",
    )


def sum_second(keeps, received, after=()):
    quads, rows, width = keeps[0].shape

    def body(ka, kb, ra, rb, keep_ref, send_ref):
        for d in range(quads):
            ref = send_ref if d % 2 else keep_ref
            for e, (keep, recv) in enumerate(((ka, ra), (kb, rb))):
                total = keep[d].astype(F32) + recv[d].astype(F32)
                ref[d // 2, e] = total.astype(BF16)

    return run(
        body,
        [*keeps, *received],
        after,
        out_shape=[sds((quads // 2, 2, rows, width), BF16)] * 2,
        vmem=24,
        cost_estimate=cost(0, 12 * keeps[0].size),
        name="sum_second",
    )


def sum_third(keep, received, after=()):
    def body(keep_ref, recv_ref, stay_ref, pass_ref):
        for ref, e in ((stay_ref, 0), (pass_ref, 1)):
            ref[...] = (keep_ref[e].astype(F32) + recv_ref[e].astype(F32)).astype(BF16)

    return run(
        body,
        [keep, received],
        after,
        out_shape=[sds(keep.shape[1:], BF16)] * 2,
        vmem=16,
        cost_estimate=cost(0, 6 * keep.size),
        name="sum_third",
    )


def small_sum(refs, rows, count):
    total = None
    for ref in refs:
        for e in range(2):
            item = ref[rows + e * count : rows + (e + 1) * count, :].astype(F32)
            total = item if total is None else total + item
    return total


def sum_first_attention(keeps, received, slot, small_rows, after):
    lanes = keeps[0].shape[1]

    def body(ka, kb, ra, rb, stay_a, pass_a, stay_b, pass_b):
        parts = two_parts(small_sum((ka, ra), 2 * slot, small_rows))
        for keep, recv, stay, on in ((ka, ra, stay_a, pass_a), (kb, rb, stay_b, pass_b)):
            for e, ref in enumerate((stay, on)):
                at = slice(e * slot, (e + 1) * slot)
                ref[0:slot, :] = (keep[at, :].astype(F32) + recv[at, :].astype(F32)).astype(BF16)
        for ref in (stay_a, pass_a):
            for e in range(2):
                ref[slot + e * small_rows : slot + (e + 1) * small_rows, :] = parts[e]

    first = sds((slot + 2 * small_rows, lanes), BF16)
    other = sds((slot, lanes), BF16)
    return run(
        body,
        [*keeps, *received],
        after,
        out_shape=[first, first, other, other],
        vmem=16,
        cost_estimate=cost(0, 3 * 1024 * 1024),
        name="sum_first_attention",
    )


def sum_second_attention(keeps, received, chunk, quads, small_rows, after):
    lanes = keeps[0].shape[1]
    halves = quads // 2
    slot = halves * chunk

    def body(ka, kb, ra, rb, *out_refs):
        parts = two_parts(small_sum((ka, ra), slot, small_rows))
        for d in range(quads):
            keep, recv = ((ka, ra), (kb, rb))[d // halves]
            at = slice(d % halves * chunk, (d % halves + 1) * chunk)
            total = keep[at, :].astype(F32) + recv[at, :].astype(F32)
            out_refs[d][0:chunk, :] = total.astype(BF16)
            for e in range(2):
                at = chunk + e * small_rows
                out_refs[d][at : at + small_rows, :] = parts[e]

    return run(
        body,
        [*keeps, *received],
        after,
        out_shape=[sds((chunk + 2 * small_rows, lanes), BF16)] * quads,
        vmem=16,
        cost_estimate=cost(0, 2 * 1024 * 1024),
        name="sum_second_attention",
    )


def final_attention(pieces, chunk, qkv_lanes, small_rows):
    lanes = pieces[0].shape[1]
    count = len(pieces)

    def body(*refs):
        total = refs[0][0:chunk, :].astype(F32)
        for ref in refs[1:count]:
            total = total + ref[0:chunk, :].astype(F32)
        refs[count][...] = total[:, :qkv_lanes]
        refs[count + 1][...] = total[:, qkv_lanes:]
        refs[count + 2][...] = small_sum(refs[:count], chunk, small_rows)

    return run(
        body,
        pieces,
        out_shape=[
            sds((chunk, qkv_lanes), F32),
            sds((chunk, lanes - qkv_lanes), F32),
            sds((small_rows, lanes), F32),
        ],
        vmem=16,
        cost_estimate=cost(0, 1024 * 1024),
        name="final_attention",
    )


def final_units(first, second, after):
    high = first[0].shape[1]
    sizes = [first[0].shape[2], second[0].shape[2]]
    unit_block = sum(sizes)
    count = len(first)
    half = high // 2

    def body(*refs):
        _, part, _ = place(2)
        keep_ref, send_ref, down_ref = refs[2 * count :]
        for h in range(2):
            pieces = refs[h * count : (h + 1) * count]
            up, down = pieces[0][0].astype(F32), pieces[0][1].astype(F32)
            for ref in pieces[1:]:
                up = up + ref[0].astype(F32)
                down = down + ref[1].astype(F32)
            here = slice(h * sizes[0], h * sizes[0] + sizes[h])
            down_ref[here, :] = down.T
            for c in range(2):

                @pl.when(part == c)
                def _(up=up, here=here, c=c):
                    keep_ref[:, here] = up[c * half : (c + 1) * half, :]
                    send_ref[:, here] = up[(1 - c) * half : (2 - c) * half, :].astype(BF16)

    return run(
        body,
        [*first, *second],
        after,
        out_shape=[
            sds((half, unit_block), F32),
            sds((half, unit_block), BF16),
            sds((unit_block, high), F32),
        ],
        vmem=24,
        cost_estimate=cost(0, 4 * 1024 * 1024),
        name="final_units",
    )


def final_join(keep, recv):
    chunk, unit_block = keep.shape

    def body(keep_ref, recv_ref, out_ref):
        _, part, _ = place(2)
        for c in range(2):

            @pl.when(part == c)
            def _(c=c):
                out_ref[:, c * unit_block : (c + 1) * unit_block] = keep_ref[...]
                out_ref[:, (1 - c) * unit_block : (2 - c) * unit_block] = recv_ref[...].astype(F32)

    return run(
        body,
        [keep, recv],
        out_shape=sds((chunk, 2 * unit_block), F32),
        vmem=16,
        cost_estimate=cost(0, 1024 * 1024),
        name="final_join",
    )


def on_device(
    tokens,
    mask,
    cotangent,
    ln1_gain,
    ln1_bias,
    qkv_weight,
    q_bias,
    v_bias,
    out_weight,
    out_bias,
    ln2_gain,
    ln2_bias,
    up_weight,
    up_bias,
    down_weight,
    down_bias,
):
    seq_size = lax.axis_size("seq")
    batch_size = lax.axis_size("batch")
    micro_count, seq_count, local_len, width = tokens.shape
    sequences = micro_count * seq_count
    group = seq_size // sequences
    units = up_weight.shape[1]
    head_dim = width // HEADS
    heads = HEADS // group
    real = heads * head_dim
    wide = -(-real // LANES) * LANES
    full_len = local_len * seq_size
    block_len = local_len // group
    rows = seq_size * block_len
    own_units = units // group
    part = lax.axis_index("seq") % group
    aligned = (
        seq_size == batch_size * group
        and group == 2
        and batch_size == 4
        and wide == 3 * LANES
        and (seq_size // group) % group == 0
        and units % (batch_size * group * LANES) == 0
        and own_units // batch_size == width
    )

    def from_part(item, ahead):
        if ahead % group == 0:
            return item
        pairs = [
            (q * group + (c + ahead) % group, q * group + c)
            for q in range(sequences)
            for c in range(group)
        ]
        return lax.ppermute(item, "seq", pairs)

    def gather_parts(item):
        return [from_part(item, n) for n in range(group)]

    def row_of(item):
        return item.astype(F32)[None, :]

    def blocks_of(item):
        return item.reshape(sequences, local_len, width)

    x_own = over_quads(deal(blocks_of(tokens), group), group)
    x_pieces = [from_part(item, n) for n in range(group) for item in x_own]

    count_rows = jnp.sum(mask, axis=2).reshape(sequences).astype(BF16)
    cot_low = jnp.where(mask[..., None] != 0, cotangent, jnp.zeros_like(cotangent))
    cot_send = jnp.concatenate(
        [blocks_of(cot_low), jnp.broadcast_to(count_rows[:, None, None], (sequences, 16, width))],
        axis=1,
    )
    cot_own = over_quads(deal(cot_send, group, x_pieces[sequences:]), group)

    qkv_w, qkv_b, *out_w = pick_weights(
        qkv_weight,
        jnp.concatenate([q_bias, jnp.zeros_like(q_bias), v_bias])[None, :],
        out_weight,
        group,
        real,
        wide,
    )
    if aligned:
        up_own, up_b, down_own = up_weight, up_bias[None, :], down_weight
    else:

        def own_columns(matrix, blocks):
            split = matrix.reshape(matrix.shape[0], blocks, group, -1)
            return lax.dynamic_index_in_dim(split, part, 2, keepdims=False)

        up_own = own_columns(up_weight, batch_size).reshape(width, own_units)
        up_b = own_columns(up_bias[None, :], batch_size).reshape(1, own_units)
        down_own = lax.dynamic_index_in_dim(
            down_weight.reshape(batch_size, group, -1, width), part, 1, keepdims=False
        ).reshape(own_units, width)

    tiles = wide // LANES
    x_all, qkv, att_first, logs_first = attend_first(
        x_pieces, row_of(ln1_gain), row_of(ln1_bias), qkv_w, qkv_b, tiles - 1, heads, head_dim
    )
    cot_stack = stack(cot_own, [logs_first])
    att_last, logs_last = attend_last(qkv, tiles - 1, heads, head_dim, [cot_stack])
    cot_pieces = cot_own + [
        item[d]
        for item in gather_parts(cot_stack)[1:]
        for d in range(sequences)
    ]
    blocks = batch_size if aligned else 1
    unit_block = own_units // blocks
    size = unit_block * 2 // 5
    shape = (group, sequences if aligned else None, width // sequences)
    calls = [
        Units(unit_block, blocks, 0, size, *shape),
        Units(unit_block, blocks, size, unit_block - size, *shape),
    ]
    mid, second, second_t, grad_rows, grad_t, result_own, grad_second, *found = feed_first(
        x_all,
        gather_parts(att_first),
        gather_parts(att_last),
        cot_pieces,
        out_w,
        row_of(out_bias),
        row_of(ln2_gain),
        row_of(ln2_bias),
        up_own,
        up_b,
        down_own,
        row_of(down_bias),
        calls[0],
    )
    up_sums, ff_grads = [found[0]], [found[group:]]
    result_own, grad_second, *found = feed_second(
        second,
        second_t,
        grad_rows,
        grad_t,
        result_own,
        grad_second,
        found[1:group],
        up_own,
        up_b,
        down_own,
        calls[1],
    )
    up_sums.append(found[0])
    result_send = found[1:group]
    ff_grads.append(found[group:])

    def begin_sum(e, sends, after):
        moved = [swap(sends[0], "batch", batch_size, 1), swap(sends[1], "batch", batch_size, 2)]
        stay_a, pass_a, stay_b, pass_b = sum_first(
            [ff_grads[e][0], ff_grads[e][2]], moved, after
        )
        moved = [swap(pass_a, "batch", batch_size, 2), swap(pass_b, "batch", batch_size, 1)]
        return [stay_a, stay_b], moved

    if aligned:
        waiting = begin_sum(0, [ff_grads[0][1], ff_grads[0][3]], [])
        (grad_second,) = gate([grad_second], waiting[0][:1])
    second_send = grad_second
    second_recv = [from_part(second_send, n) for n in range(1, group)]
    result_recv = [from_part(result_send[group - n - 1], n) for n in range(1, group)]
    result_keep, result_pass = finish_result(result_own, result_recv, sequences)

    def quad_swap(item, distance):
        return swap(item, "seq", seq_size, distance * group)

    result_near = quad_swap(result_pass, 1)

    chunk = width // seq_size
    grad_mid, grad_att, sums_mid, *out_grad = mid_back(
        mid,
        grad_second,
        second_recv,
        grad_rows,
        row_of(ln2_gain),
        out_w[0],
        att_first,
        att_last,
        chunk if aligned else 0,
    )

    def tile_back(t, after, cost_part=1):
        last = t == tiles - 1
        return attend_backward(
            qkv,
            grad_att,
            att_last if last else att_first,
            0 if last else t,
            logs_last if last else logs_first,
            0 if last else t * (LANES // head_dim),
            t,
            heads,
            head_dim,
            after,
            cost_part,
        )

    grad_tiles = [None] * tiles
    after = [result_keep]
    if aligned:
        keep, send = sum_second(*waiting, [grad_mid])
        moved = quad_swap(send, 1)
        sends = gate([ff_grads[1][1], ff_grads[1][3]], [keep])
        after = [result_keep, keep]
    grad_tiles[0] = tile_back(0, after, 64)
    result_pass = pass_on(result_keep, result_near, grad_tiles[:1])
    result_far = quad_swap(result_pass, 2)
    after = [result_pass]
    if aligned:
        unit_first = list(sum_third(keep, moved, [grad_tiles[0]]))
        unit_first[1] = quad_swap(unit_first[1], 2)
        after = [result_pass, unit_first[0]]
    grad_tiles[-1] = tile_back(tiles - 1, after, 64)
    after = []
    if aligned:
        waiting = begin_sum(1, sends, [grad_tiles[-1]])
        after = waiting[0][:1]
    for t in range(1, tiles - 1):
        grad_tiles[t] = tile_back(t, after)
    after = [result_far]
    if aligned:
        out_recv = from_part(out_grad[1], 1)
        keep, send = sum_second(*waiting, [grad_tiles[-2]])
        moved = quad_swap(send, 1)
        after = [keep, unit_first[1], result_far, out_recv]
    qkv_grad = project_weights(
        x_all, row_of(ln1_gain), row_of(ln1_bias), grad_tiles, group, sequences, aligned, after
    )
    first_own, *found = project_rows(
        x_all,
        qkv_w,
        grad_tiles,
        sums_mid,
        up_sums,
        group,
        sequences,
        aligned,
        real,
        qkv_grad[:1],
    )
    first_send, (small, bias_sums) = found[: group - 1], found[group - 1 :]
    first_recv = [from_part(first_send[group - n - 1], n) for n in range(1, group)]
    row_keep, row_pass = finish_rows(
        x_all, row_of(ln1_gain), grad_mid, first_own, first_recv, sequences, []
    )
    row_near = quad_swap(row_pass, 1)

    after = []
    if aligned:
        small_rows = small.shape[0]
        packed = pack_attention(
            qkv_grad[0],
            from_part(qkv_grad[1], 1),
            out_grad[0],
            out_recv,
            small,
            from_part(small, 1),
            real,
            batch_size,
            [],
        )
        unit_second = list(sum_third(keep, moved, packed[:1]))
        unit_second[1] = quad_swap(unit_second[1], 2)
        stay_a, pass_a, stay_b, pass_b = sum_first_attention(
            [packed[0], packed[2]],
            [swap(packed[1], "batch", batch_size, 1), swap(packed[3], "batch", batch_size, 2)],
            sequences // 2 * chunk,
            small_rows,
            unit_second[:1],
        )
        after = [stay_a]
    row_far = quad_swap(pass_on(row_keep, row_near, after), 2)
    if aligned:
        summed = sum_second_attention(
            [stay_a, stay_b],
            [swap(pass_a, "batch", batch_size, 2), swap(pass_b, "batch", batch_size, 1)],
            chunk,
            sequences,
            small_rows,
            [],
        )
        after = summed[:1]
        up_keep, up_send, down_grad = final_units(unit_first, unit_second, after)
        up_grad = final_join(up_keep, from_part(up_send, 1))
        qkv_final, out_final, small = final_attention(
            over_quads(summed, group), chunk, qkv_weight.shape[1] // batch_size, small_rows
        )
        small = small.reshape(-1)
    result = collect_halves(result_keep, result_near, result_far, group, after)
    result = result.reshape(tokens.shape)
    grad_in = collect_halves(row_keep, row_near, row_far, group, after).reshape(tokens.shape)
    if not aligned:

        def spread(item, blocks):
            split = item.reshape(blocks, 1, -1)
            empty = jnp.zeros((blocks, group, split.shape[2]), F32)
            return lax.dynamic_update_slice(empty, split, (0, part, 0)).reshape(-1)

        bias_sums = bias_sums[0].reshape(tiles, 3, LANES).transpose(1, 0, 2)
        bias_sums = bias_sums.reshape(3, wide)[:, :real]
        small = jnp.concatenate(
            [
                small[0],
                small[1],
                spread(bias_sums[0], 1),
                spread(bias_sums[2], 1),
                sums_mid[2],
                sums_mid[0],
                sums_mid[1],
                spread(jnp.concatenate([item[0] for item in up_sums]), batch_size),
                sums_mid[3],
            ]
        )

        def scattered(item):
            item = lax.psum_scatter(item.astype(BF16), "seq", scatter_dimension=0, tiled=True)
            return lax.psum_scatter(item, "batch", scatter_dimension=1, tiled=True).astype(F32)

        def spread_columns(item, blocks):
            split = item.reshape(item.shape[0], blocks, 1, -1)
            empty = jnp.zeros((item.shape[0], blocks, group, split.shape[3]), item.dtype)
            filled = lax.dynamic_update_slice(empty, split, (0, 0, part, 0))
            return filled.reshape(item.shape[0], -1)

        up_full, down_full = [
            jnp.concatenate([item[e] for item in ff_grads], axis=1) for e in range(2)
        ]
        up_grad = scattered(spread_columns(up_full, batch_size))
        down_grad = scattered(spread_columns(down_full, batch_size).T)
        rows_full = qkv_grad[0].reshape(width, tiles, 3, LANES).transpose(0, 2, 1, 3)
        rows_full = rows_full.reshape(width, 3, wide)[..., :real]
        qkv_final = scattered(spread_columns(rows_full.reshape(width, -1), 3))
        out_final = scattered(spread_columns(out_grad[0][:real].T, 1).T)
        small = lax.psum(small, ("seq", "batch"))

    edges = [width] * 7 + [units, width]
    pieces, start = [], 0
    for size in edges:
        pieces.append(small[start : start + size])
        start += size
    return (
        result,
        grad_in,
        pieces[0],
        pieces[1],
        qkv_final,
        pieces[2],
        pieces[3],
        out_final,
        pieces[4],
        pieces[5],
        pieces[6],
        up_grad,
        pieces[7],
        down_grad,
        pieces[8],
    )


def solution(mesh):
    rows = P(None, "batch", "seq", None)
    split = P("seq", "batch")
    in_specs = (rows, P(None, "batch", "seq"), rows) + (P(),) * 13
    out_specs = (
        rows,
        rows,
        P(),
        P(),
        split,
        P(),
        P(),
        split,
        P(),
        P(),
        P(),
        split,
        P(),
        split,
        P(),
    )
    return jax.shard_map(
        on_device, mesh=mesh, in_specs=in_specs, out_specs=out_specs, check_vma=False
    )
```

```python
import jax
import jax.numpy as jnp
from jax import lax
from jax.experimental import pallas as pl
from jax.experimental.pallas import tpu as pltpu
from jax.sharding import PartitionSpec as P

HEADS = 20
EPS = 1e-05
LOG2E = 1.4426950408889634
ROWS = 256
F32 = jnp.float32
BF16 = jnp.bfloat16
LANES = 128


def dot(left, right):
    return jnp.dot(left, right, preferred_element_type=F32)


def dot_nt(left, right):
    return lax.dot_general(left, right, (((1,), (1,)), ((), ())), preferred_element_type=F32)


def norm_rows(rows_in):
    mean_val = jnp.mean(rows_in, axis=-1, keepdims=True)
    centered = rows_in - mean_val
    inv_std = lax.rsqrt(jnp.mean(centered * centered, axis=-1, keepdims=True) + EPS)
    return centered * inv_std, inv_std


def norm_back(scaled, normed, inv_std):
    inner = (
        scaled
        - jnp.mean(scaled, axis=-1, keepdims=True)
        - normed * jnp.mean(scaled * normed, axis=-1, keepdims=True)
    )
    return inner * inv_std


def params_of(mib):
    return pltpu.CompilerParams(vmem_limit_bytes=mib * 1024 * 1024)


def cost(flops, moved, trans=0, part=1):
    return pl.CostEstimate(
        flops=flops // part, bytes_accessed=moved // part, transcendentals=trans // part
    )


def sds(shape, dtype):
    return jax.ShapeDtypeStruct(shape, dtype)


VMEM = pl.BlockSpec(memory_space=pltpu.VMEM)
ANY = pl.BlockSpec(memory_space=pl.ANY)
HBM = pl.BlockSpec(memory_space=pltpu.HBM)


def run(body, operands, after=(), in_specs=None, out_specs=None, vmem=32, **more):
    count, extra = len(operands), len(after)

    def inner(*refs):
        body(*refs[:count], *refs[count + extra :])

    specs = [VMEM] * count if in_specs is None else list(in_specs)
    shapes = more["out_shape"]
    if out_specs is None:
        out_specs = [VMEM] * len(shapes) if isinstance(shapes, (list, tuple)) else VMEM
    return pl.pallas_call(
        inner,
        in_specs=specs + [ANY] * extra,
        out_specs=out_specs,
        compiler_params=params_of(vmem),
        **more,
    )(*operands, *after)


def gate(items, after):
    def body(*refs):
        del refs

    return pl.pallas_call(
        body,
        in_specs=[ANY] * (len(items) + len(after)),
        out_specs=[ANY] * len(items),
        out_shape=[sds(item.shape, item.dtype) for item in items],
        input_output_aliases={n: n for n in range(len(items))},
        cost_estimate=cost(0, 0),
        name="gate",
    )(*items, *after)


def place(group):
    spot = lax.axis_index("seq")
    return spot, lax.rem(spot, group), lax.div(spot, group)


def deal(item, group, after=()):
    count, rows, width = item.shape

    def body(in_ref, *out_refs):
        _, _, quad = place(group)
        for d in range(count):
            out_refs[d][...] = in_ref[quad ^ d]

    return run(
        body,
        [item],
        after,
        out_shape=[sds((rows, width), item.dtype)] * count,
        vmem=6,
        cost_estimate=cost(0, 4 * count * rows * width),
        name="deal",
    )


def collect(pieces, group, after):
    count = len(pieces)
    rows, width = pieces[0].shape

    def body(*refs):
        _, _, quad = place(group)
        for d in range(count):
            refs[count][quad ^ d] = refs[d][...]

    return run(
        body,
        pieces,
        after,
        out_shape=sds((count, rows, width), pieces[0].dtype),
        vmem=6,
        cost_estimate=cost(0, 4 * count * rows * width),
        name="collect",
    )


def stack(pieces, after):
    count = len(pieces)

    def body(*refs):
        for d in range(count):
            refs[count][d] = refs[d][...]

    return run(
        body,
        pieces,
        after,
        out_shape=sds((count,) + pieces[0].shape, pieces[0].dtype),
        vmem=12,
        cost_estimate=cost(0, 4 * count * pieces[0].size),
        name="stack",
    )


def swap(item, axis, size, distance):
    return lax.ppermute(item, axis, [(i, i ^ distance) for i in range(size)])


def over_quads(pieces, group):
    return [
        piece if d == 0 else swap(piece, "seq", len(pieces) * group, d * group)
        for d, piece in enumerate(pieces)
    ]


def pick_weights(qkv_weight, qkv_bias, out_weight, group, real, wide):
    width = qkv_weight.shape[0]
    tiles = wide // LANES

    def body(w_ref, b_ref, o_ref, wo_ref, bo_ref, *out_refs):
        _, part, _ = place(group)
        wo_ref[...] = jnp.zeros_like(wo_ref)
        bo_ref[...] = jnp.zeros_like(bo_ref)
        for ref in out_refs:
            ref[...] = jnp.zeros_like(ref)
        for c in range(group):

            @pl.when(part == c)
            def _(c=c):
                for p in range(3):
                    for t in range(tiles):
                        some = min(LANES, real - t * LANES)
                        src = p * width + c * real + t * LANES
                        dst = (3 * t + p) * LANES
                        wo_ref[:, dst : dst + some] = w_ref[:, src : src + some]
                        bo_ref[:, dst : dst + some] = b_ref[:, src : src + some]
                for n in range(group):
                    src = (c + n) % group * real
                    out_refs[n][0:real, :] = o_ref[src : src + real, :]

    return pl.pallas_call(
        body,
        out_shape=[sds((width, 3 * wide), BF16), sds((1, 3 * wide), F32)]
        + [sds((wide, width), BF16)] * group,
        compiler_params=params_of(24),
        cost_estimate=cost(0, 8 * 1024 * 1024),
        name="pick_weights",
    )(qkv_weight, qkv_bias, out_weight)


def by_pairs(live, visit):
    size = 2 if live % 2 == 0 else 1

    @pl.loop(0, live // size)
    def _(i):
        visit([i * size + e for e in range(size)])


def attend_tiles(query_at, keys_at, vals_at, att_ref, lse_ref, keys, vals, acc, tiles, heads, head_dim):
    per_tile = LANES // head_dim
    total = att_ref.shape[0]
    exp_scale = head_dim ** (-0.5) * LOG2E
    lane = lax.broadcasted_iota(jnp.int32, (1, LANES), 1)
    row = lax.broadcasted_iota(jnp.int32, (LANES, 1), 0)
    lse_ref[...] = jnp.zeros_like(lse_ref)
    vals[:, :, LANES:] = jnp.ones((per_tile, total, LANES), BF16)
    for n, t in enumerate(tiles):
        live = min(per_tile, heads - t * per_tile)
        key_t = keys_at(n).astype(F32).T
        val_f = vals_at(n).astype(F32)
        for j in range(live):
            keys[j] = jnp.where(row // head_dim == j, key_t, 0.0).astype(BF16)
            vals[j, :, :LANES] = jnp.where(lane // head_dim == j, val_f, 0.0).astype(BF16)
        acc[...] = jnp.zeros_like(acc)

        def visit(some, n=n):
            scores = [dot(query_at(n), keys[j]) for j in some]
            for item, j in zip(scores, some):
                row_max = jnp.max(item, axis=-1, keepdims=True) * exp_scale
                expd = jnp.exp2(item * exp_scale - row_max).astype(BF16)
                mixed = dot(expd, vals[j])
                den = mixed[:, LANES:]
                acc[...] += mixed[:, :LANES] / den
                lse_ref[...] = jnp.where(
                    lane == n * per_tile + j, row_max + jnp.log2(den), lse_ref[...]
                )

        by_pairs(live, visit)
        att_ref[:, n * LANES : (n + 1) * LANES] = acc[...].astype(BF16)


def attend_scratch(total, head_dim):
    per_tile = LANES // head_dim
    return [
        pltpu.VMEM((per_tile, LANES, total), BF16),
        pltpu.VMEM((per_tile, total, 2 * LANES), BF16),
        pltpu.VMEM((total, LANES), F32),
    ]


def attend_first(x_pieces, gain, shift, weight, bias, tiles, heads, head_dim):
    count = len(x_pieces)
    piece_rows, width = x_pieces[0].shape
    total = count * piece_rows
    cols_all = weight.shape[1]

    def body(*refs):
        x_refs = refs[:count]
        gain_ref, shift_ref, w_ref, bias_ref = refs[count : count + 4]
        x_ref, qkv_ref, att_ref, lse_ref, keys, vals, acc = refs[count + 4 :]
        for n in range(count):
            x_ref[n * piece_rows : (n + 1) * piece_rows, :] = x_refs[n][...]

        @pl.loop(0, total // ROWS)
        def _(i):
            rows = pl.ds(pl.multiple_of(i * ROWS, ROWS), ROWS)
            normed, _ = norm_rows(x_ref[rows, :].astype(F32))
            low = (normed * gain_ref[...] + shift_ref[...]).astype(BF16)
            qkv_ref[rows, :] = (dot(low, w_ref[...]) + bias_ref[...]).astype(BF16)

        def columns(at):
            return slice(at * LANES, (at + 1) * LANES)

        attend_tiles(
            lambda n: qkv_ref[:, columns(3 * n)],
            lambda n: qkv_ref[:, columns(3 * n + 1)],
            lambda n: qkv_ref[:, columns(3 * n + 2)],
            att_ref,
            lse_ref,
            keys,
            vals,
            acc,
            range(tiles),
            heads,
            head_dim,
        )

    return run(
        body,
        [*x_pieces, gain, shift, weight, bias],
        out_shape=[
            sds((total, width), BF16),
            sds((total, cols_all), BF16),
            sds((total, tiles * LANES), BF16),
            sds((total, LANES), F32),
        ],
        scratch_shapes=attend_scratch(total, head_dim),
        vmem=23,
        cost_estimate=cost(
            2 * total * width * cols_all + 4 * heads * total * total * 256,
            8 * 1024 * 1024,
            heads * total * total,
        ),
        name="attend_first",
    )


def attend_last(qkv, tile, heads, head_dim, after):
    total = qkv.shape[0]

    def body(qkv_ref, att_ref, lse_ref, keys, vals, acc):
        attend_tiles(
            lambda n: qkv_ref[:, 0:LANES],
            lambda n: qkv_ref[:, LANES : 2 * LANES],
            lambda n: qkv_ref[:, 2 * LANES : 3 * LANES],
            att_ref,
            lse_ref,
            keys,
            vals,
            acc,
            [tile],
            heads,
            head_dim,
        )

    live = heads - tile * (LANES // head_dim)
    return run(
        body,
        [qkv],
        after,
        grid=(1,),
        in_specs=[pl.BlockSpec((total, 3 * LANES), lambda i: (0, tile))],
        out_specs=[pl.BlockSpec((total, LANES), lambda i: (0, 0))] * 2,
        out_shape=[sds((total, LANES), BF16), sds((total, LANES), F32)],
        scratch_shapes=attend_scratch(total, head_dim),
        vmem=14,
        cost_estimate=cost(4 * live * total * total * 256, 2 * 1024 * 1024, live * total * total),
        name="attend_last",
    )


def gelu_parts(value):
    size = jnp.abs(value)
    near = pl.reciprocal(1.0 + (0.3275911 * 0.7071067811865476) * size, approx=True)
    bell = jnp.exp2(value * value * (-0.5 * LOG2E))
    poly = near * (
        0.5 * 0.254829592
        + near
        * (
            0.5 * -0.284496736
            + near * (0.5 * 1.421413741 + near * (0.5 * -1.453152027 + near * (0.5 * 1.061405429)))
        )
    )
    tail = poly * bell
    area = jnp.where(value < 0.0, tail, 1.0 - tail)
    return value * area, area + value * bell * 0.3989422804014327


class Units:
    def __init__(self, block, blocks, start, size, stride, quads, high):
        self.block, self.blocks, self.start, self.size = block, blocks, start, size
        self.stride, self.quads, self.high = stride, quads, high
        self.count = blocks * size
        self.chunk = 512 if self.count % 512 == 0 else 256
        self.packed = quads is not None

    def loads(self, part, hbm_up, hbm_down, hbm_bias, up_ref, down_ref, bias_ref, sem):
        copies = []
        for b in range(self.blocks):
            src = self.start
            if self.packed:
                src = pl.multiple_of((b * self.stride + part) * self.block, LANES) + self.start
            src = pl.ds(src, self.size)
            dst = pl.ds(b * self.size, self.size)
            copies.append(
                pltpu.make_async_copy(hbm_up.at[:, src], up_ref.at[:, dst], sem.at[2 * b])
            )
            copies.append(
                pltpu.make_async_copy(hbm_down.at[src, :], down_ref.at[dst, :], sem.at[2 * b + 1])
            )
            bias_ref[0:1, dst] = hbm_bias[:, src]
        return copies

    def grad_shapes(self, width):
        if self.packed:
            return [sds((2, self.quads, self.high, self.size), BF16)] * 4
        return [sds((width, self.count), BF16)] * 2

    def scratch(self, total, width):
        grads = (self.blocks, self.quads, self.high, self.size) if self.packed else (8, LANES)
        return [
            pltpu.VMEM(grads, BF16),
            pltpu.VMEM(grads, BF16),
            pltpu.SemaphoreType.DMA((8,)),
            pltpu.VMEM((total, self.count), BF16),
            pltpu.VMEM((total, self.count), BF16),
            pltpu.VMEM((width, self.count), BF16),
            pltpu.VMEM((self.count, width), BF16),
            pltpu.VMEM((8, self.count), F32),
            pltpu.SemaphoreType.DMA((2 * self.blocks,)),
        ]

    def compute(self, part, second, second_t, grad, grad_t, acc, gs, ubg, scratch, outs):
        up_slots, down_slots, out_sem, acts, grad_pres, up_ref, down_ref, bias_ref, _ = scratch
        if not self.packed:
            up_slots, down_slots = outs
        quad = lax.div(lax.axis_index("seq"), self.stride)
        mine = lax.axis_index("batch")

        def enter(i):
            rows = slice(i * ROWS, (i + 1) * ROWS)
            pre = dot(second[rows, :], up_ref[...]) + bias_ref[0:1, :]
            return pre, dot_nt(grad[rows, :], down_ref[...])

        def weights(n):
            first, last = n * self.chunk, (n + 1) * self.chunk
            up_grad = dot(second_t[...], grad_pres[:, first:last]).astype(BF16)
            down_grad = dot(grad_t[...], acts[:, first:last]).astype(BF16)
            if not self.packed:
                up_slots[:, first:last] = up_grad
                down_slots[:, first:last] = down_grad
                return
            at = first
            while at < last:
                block = at // self.size
                stop = min(last, (block + 1) * self.size)
                src = slice(at - first, stop - first)
                dst = slice(at - block * self.size, stop - block * self.size)
                for m in range(self.blocks):
                    rows = slice(m * self.high, (m + 1) * self.high)
                    up_slots[block ^ mine, m ^ quad, :, dst] = up_grad[rows, src]
                    down_slots[m ^ mine, block ^ quad, :, dst] = down_grad[rows, src]
                at = stop

        ready = enter(0)
        chunks = second.shape[0] // ROWS
        for i in range(chunks):
            ahead = enter(i + 1) if i + 1 < chunks else None
            rows = slice(i * ROWS, (i + 1) * ROWS)
            pre, grad_act = ready
            value, slope = gelu_parts(pre)
            act = value.astype(BF16)
            grad_pre = (grad_act * slope).astype(BF16)
            acts[rows, :] = act
            grad_pres[rows, :] = grad_pre
            ubg[0:1, :] += jnp.sum(grad_pre.astype(F32), axis=0, keepdims=True)
            acc[rows, :] += dot(act, down_ref[...])
            gs[rows, :] += dot_nt(grad_pre, up_ref[...])
            ready = ahead
        for n in range(self.count // self.chunk):
            weights(n)
        stores = []
        if self.packed:
            order = ((up_slots, (0, 2)), (up_slots, (1, 3)), (down_slots, (0, 1)), (down_slots, (2, 3)))
            for m, (source, slots) in enumerate(order):
                for n in range(2):
                    stores.append(
                        pltpu.make_async_copy(
                            source.at[slots[n]], outs[m].at[n], out_sem.at[2 * m + n]
                        )
                    )
        return stores


def feed_first(
    rows_all, att_first, att_last, cot_pieces, out_w, out_b, gain, shift, up, up_b, down, down_b, units
):
    pieces = len(att_first)
    total, width = rows_all.shape
    piece_rows = total // pieces
    count = len(cot_pieces)
    cot_rows = total // count
    split = att_first[0].shape[1]
    grads = units.grad_shapes(width)

    def body(*refs):
        x_ref, refs = refs[0], refs[1:]
        att_refs, refs = refs[: 2 * pieces], refs[2 * pieces :]
        cot_refs, refs = refs[:count], refs[count:]
        wo_refs, refs = refs[:pieces], refs[pieces:]
        ob_ref, gain_ref, shift_ref, up_hbm, ub_ref, down_hbm, db_ref = refs[:7]
        mid_ref, second, second_t, grad, grad_t, own_ref, low_ref, ubg, refs = *refs[7:15], refs[15:]
        send_refs, refs = refs[: pieces - 1], refs[pieces - 1 :]
        outs, (acc, gs), scratch = refs[: len(grads)], refs[len(grads) :][:2], refs[len(grads) + 2 :]
        _, part, _ = place(pieces)
        loads = units.loads(part, up_hbm, down_hbm, ub_ref, *scratch[5:])
        for load in loads:
            load.start()
        ubg[...] = jnp.zeros_like(ubg)
        masked = jnp.zeros((1, width), F32)
        for ref in cot_refs:
            masked = masked + ref[cot_rows : cot_rows + 1, :].astype(F32)
        factor = total / (4.0 * masked)
        for n in range(count):
            scaled = cot_refs[n][0:cot_rows, :].astype(F32) * factor
            dst = slice(n * cot_rows, (n + 1) * cot_rows)
            grad[dst, :] = scaled.astype(BF16)

        for h in range(pieces):

            @pl.loop(0, piece_rows // ROWS)
            def _(i, h=h):
                at = pl.multiple_of(i * ROWS, ROWS)
                dst = pl.ds(h * piece_rows + at, ROWS)
                mid = x_ref[dst, :].astype(F32) + ob_ref[...]
                for n in range(pieces):
                    src = pl.ds(((h - n) % pieces) * piece_rows + at, ROWS)
                    mid = mid + dot(att_refs[2 * n][src, :], wo_refs[n][0:split, :])
                    mid = mid + dot(att_refs[2 * n + 1][src, :], wo_refs[n][split:, :])
                mid_ref[dst, :] = mid
                normed, _ = norm_rows(mid)
                low = normed * gain_ref[...] + shift_ref[...]
                second[dst, :] = low.astype(BF16)
                second_t[:, dst] = low.T.astype(BF16)
                grad_t[:, dst] = grad[dst, :].astype(F32).T.astype(BF16)
                acc[dst, :] = mid + db_ref[...] if h == 0 else jnp.zeros((ROWS, width), F32)
                gs[dst, :] = jnp.zeros((ROWS, width), F32)

        for load in loads:
            load.wait()
        stores = units.compute(
            part, second, second_t, grad, grad_t, acc, gs, ubg, scratch, outs
        )
        for store in stores:
            store.start()
        own_ref[...] = acc[0:piece_rows, :]
        low_ref[...] = gs[...].astype(BF16)
        for h in range(1, pieces):
            send_refs[h - 1][...] = acc[h * piece_rows : (h + 1) * piece_rows, :].astype(BF16)
        for store in stores:
            store.wait()

    att_all = [item for pair in zip(att_first, att_last) for item in pair]
    turned = sds((width, total), BF16)
    flat = sds((total, width), BF16)
    wide = sds((total, width), F32)
    half = sds((piece_rows, width), F32)
    return run(
        body,
        [rows_all, *att_all, *cot_pieces, *out_w, out_b, gain, shift, up, up_b, down, down_b],
        in_specs=[VMEM] * (1 + 3 * pieces + count) + [VMEM, VMEM, VMEM, HBM, VMEM, HBM, VMEM],
        out_specs=[VMEM] * (7 + pieces) + [HBM if units.packed else VMEM] * len(grads),
        out_shape=[wide, flat, turned, flat, turned, half, flat, sds((8, units.count), F32)]
        + [sds((piece_rows, width), BF16)] * (pieces - 1)
        + grads,
        scratch_shapes=[pltpu.VMEM((total, width), F32)] * 2 + units.scratch(total, width),
        vmem=22,
        cost_estimate=cost(12 * total * width * units.count, 24 * 1024 * 1024, total * units.count),
        name="feed_first",
    )


def feed_second(second, second_t, grad, grad_t, own_first, low_first, sends, up, up_b, down, units):
    pieces = 1 + len(sends)
    total, width = second.shape
    piece_rows = total // pieces
    grads = units.grad_shapes(width)

    def body(*refs):
        second, second_t, grad, grad_t, own_in, low_in, up_hbm, ub_ref, down_hbm, refs = (
            *refs[:9],
            refs[9:],
        )
        send_ins, refs = refs[: pieces - 1], refs[pieces - 1 :]
        own_ref, low_ref, ubg, refs = refs[0], refs[1], refs[2], refs[3:]
        send_refs, refs = refs[: pieces - 1], refs[pieces - 1 :]
        outs, (acc, gs), scratch = refs[: len(grads)], refs[len(grads) :][:2], refs[len(grads) + 2 :]
        _, part, _ = place(pieces)
        loads = units.loads(part, up_hbm, down_hbm, ub_ref, *scratch[5:])
        for load in loads:
            load.start()
        ubg[...] = jnp.zeros_like(ubg)
        acc[...] = jnp.zeros_like(acc)
        gs[...] = jnp.zeros_like(gs)
        for load in loads:
            load.wait()
        stores = units.compute(
            part, second, second_t, grad, grad_t, acc, gs, ubg, scratch, outs
        )
        for store in stores:
            store.start()
        low_ref[...] = (gs[...] + low_in[...].astype(F32)).astype(BF16)
        own_ref[...] = acc[0:piece_rows, :] + own_in[...]
        for h in range(1, pieces):
            item = acc[h * piece_rows : (h + 1) * piece_rows, :] + send_ins[h - 1][...].astype(F32)
            send_refs[h - 1][...] = item.astype(BF16)
        for store in stores:
            store.wait()

    return run(
        body,
        [second, second_t, grad, grad_t, own_first, low_first, up, up_b, down, *sends],
        in_specs=[VMEM] * 6 + [HBM, VMEM, HBM] + [VMEM] * (pieces - 1),
        out_specs=[VMEM] * (2 + pieces) + [HBM if units.packed else VMEM] * len(grads),
        out_shape=[
            sds((piece_rows, width), F32),
            sds((total, width), BF16),
            sds((8, units.count), F32),
        ]
        + [sds((piece_rows, width), BF16)] * (pieces - 1)
        + grads,
        scratch_shapes=[pltpu.VMEM((total, width), F32)] * 2 + units.scratch(total, width),
        vmem=28,
        cost_estimate=cost(12 * total * width * units.count, 24 * 1024 * 1024, total * units.count),
        name="feed_second",
    )


def mid_back(mid, grad_second, received, grad_rows, gain, out_w, att_first, att_last, chunk):
    pieces = 1 + len(received)
    total, width = mid.shape
    piece_rows = total // pieces
    split = att_first.shape[1]
    wide = split + att_last.shape[1]

    def body(*refs):
        mid_ref, gs_ref, refs = refs[0], refs[1], refs[2:]
        recv_refs, refs = refs[: pieces - 1], refs[pieces - 1 :]
        go_ref, gain_ref, wo_ref, att_ref, last_ref = refs[:5]
        gm_ref, do_ref, sums_ref, *dwo_refs, low_ref = refs[5:]
        sums_ref[...] = jnp.zeros_like(sums_ref)
        for h in range(pieces):

            @pl.loop(0, piece_rows // ROWS)
            def _(i, h=h):
                at = pl.multiple_of(i * ROWS, ROWS)
                rows = pl.ds(h * piece_rows + at, ROWS)
                normed, inv_std = norm_rows(mid_ref[rows, :])
                grad = gs_ref[rows, :].astype(F32)
                for n in range(1, pieces):
                    src = pl.ds(((h - n) % pieces) * piece_rows + at, ROWS)
                    grad = grad + recv_refs[n - 1][src, :].astype(F32)
                go = go_ref[rows, :].astype(F32)
                grad_mid = go + norm_back(grad * gain_ref[...], normed, inv_std)
                low = grad_mid.astype(BF16)
                low_ref[rows, :] = low
                do_ref[rows, :] = dot_nt(low, wo_ref[...]).astype(BF16)
                if h == 0:
                    gm_ref[rows, :] = grad_mid
                    for n, item in enumerate((grad * normed, grad, low.astype(F32), go)):
                        sums_ref[n : n + 1, :] += jnp.sum(item, axis=0, keepdims=True)

        grad_out_w = jnp.concatenate(
            [
                dot(ref[...].astype(F32).T.astype(BF16), low_ref[...]).astype(BF16)
                for ref in (att_ref, last_ref)
            ],
            axis=0,
        )
        if chunk == 0:
            dwo_refs[0][...] = grad_out_w
            return
        _, part, _ = place(pieces)
        for c in range(pieces):

            @pl.when(part == c)
            def _(c=c):
                for n in range(dwo_refs[0].shape[0]):
                    for e in range(pieces):
                        at = (n * pieces + (c + e) % pieces) * chunk
                        dwo_refs[e][n] = grad_out_w[at : at + chunk, :]

    if chunk == 0:
        grads = [sds((wide, width), BF16)]
    else:
        grads = [sds((width // (pieces * pieces * chunk), chunk, width), BF16)] * pieces
    return run(
        body,
        [mid, grad_second, *received, grad_rows, gain, out_w, att_first, att_last],
        out_shape=[
            sds((piece_rows, width), F32),
            sds((total, wide), BF16),
            sds((8, width), F32),
        ]
        + grads,
        scratch_shapes=[pltpu.VMEM((total, width), BF16)],
        vmem=17,
        cost_estimate=cost(4 * total * width * wide, 14 * 1024 * 1024),
        name="mid_back",
    )


def attend_backward(
    qkv, grad_att, att, att_tile, logs, lane_first, tile, heads, head_dim, after=(), part=1
):
    total = qkv.shape[0]
    per_tile = LANES // head_dim
    live = min(per_tile, heads - tile * per_tile)
    scale = head_dim ** (-0.5)
    exp_scale = scale * LOG2E

    def body(qkv_ref, do_ref, att_ref, lse_ref, out_ref, *scratch):
        km, vm, qm, dm, key_t, query_t, do_t, dq_t, lse_t, mean_t = scratch
        lane = lax.broadcasted_iota(jnp.int32, (1, LANES), 1)
        lse_t[...] = lse_ref[...].T
        query = qkv_ref[:, 0:LANES].astype(F32)
        key = qkv_ref[:, LANES : 2 * LANES].astype(F32)
        val = qkv_ref[:, 2 * LANES : 3 * LANES].astype(F32)
        upstream = do_ref[...].astype(F32)
        both_t = (upstream * att_ref[...].astype(F32)).T
        for j in range(live):
            mean_t[j : j + 1, :] = jnp.sum(
                both_t[j * head_dim : (j + 1) * head_dim, :], axis=0, keepdims=True
            )
        query_t[...] = query.T.astype(BF16)
        do_t[...] = upstream.T.astype(BF16)
        key_t[...] = key.T.astype(BF16)
        for j in range(live):
            mine = lane // head_dim == j
            km[j] = jnp.where(mine, key, 0.0).astype(BF16)
            vm[j] = jnp.where(mine, val, 0.0).astype(BF16)
            qm[j] = jnp.where(mine, query, 0.0).astype(BF16)
            dm[j] = jnp.where(mine, upstream, 0.0).astype(BF16)
        dq_t[...] = jnp.zeros_like(dq_t)

        @pl.loop(0, total // ROWS)
        def _(i):
            rows = pl.ds(pl.multiple_of(i * ROWS, ROWS), ROWS)
            grad_key = jnp.zeros((ROWS, LANES), F32)
            grad_val = jnp.zeros((ROWS, LANES), F32)

            def enter(j):
                return dot(km[j, rows, :], query_t[...]), dot(vm[j, rows, :], do_t[...])

            ready = enter(0)
            for j in range(live):
                ahead = enter(j + 1) if j + 1 < live else None
                scores, grad_prob = ready
                head = lane_first + j
                own = slice(j * head_dim, (j + 1) * head_dim)
                probs = jnp.exp2(scores * exp_scale - lse_t[head : head + 1, :])
                grad_scores = (probs * (grad_prob - mean_t[j : j + 1, :])).astype(BF16)
                grad_val = grad_val + dot(probs.astype(BF16), dm[j])
                grad_key = grad_key + dot(grad_scores, qm[j])
                dq_t[own, :] += dot(key_t[own, rows], grad_scores)
                ready = ahead
            out_ref[rows, LANES : 2 * LANES] = (grad_key * scale).astype(BF16)
            out_ref[rows, 2 * LANES : 3 * LANES] = grad_val.astype(BF16)

        out_ref[:, 0:LANES] = (dq_t[...].T * scale).astype(BF16)

    masked = pltpu.VMEM((live, total, LANES), BF16)
    turned = pltpu.VMEM((LANES, total), BF16)
    turned_f = pltpu.VMEM((LANES, total), F32)
    return run(
        body,
        [qkv, grad_att, att, logs],
        after,
        grid=(1,),
        in_specs=[
            pl.BlockSpec((total, 3 * LANES), lambda i: (0, tile)),
            pl.BlockSpec((total, LANES), lambda i: (0, tile)),
            pl.BlockSpec((total, LANES), lambda i: (0, att_tile)),
            pl.BlockSpec((total, LANES), lambda i: (0, 0)),
        ],
        out_specs=pl.BlockSpec((total, 3 * LANES), lambda i: (0, 0)),
        out_shape=sds((total, 3 * LANES), BF16),
        scratch_shapes=[masked] * 4
        + [turned] * 3
        + [turned_f] * 2
        + [pltpu.VMEM((8, total), F32)],
        vmem=17,
        cost_estimate=cost(
            2 * live * total * total * 256 * 5, 3 * 1024 * 1024, live * total * total, part
        ),
        name="attend_backward",
    )


def project_weights(rows_all, gain, shift, grad_tiles, pieces, quads, packed, after):
    total, width = rows_all.shape
    tiles = len(grad_tiles)
    tile_cols = grad_tiles[0].shape[1]
    cols_all = tiles * tile_cols
    chunk = width // (quads * pieces)

    def body(*refs):
        x_ref, gain_ref, shift_ref, refs = refs[0], refs[1], refs[2], refs[3:]
        dq_refs, (*dw_refs, low_t, part_ref) = refs[:tiles], refs[tiles:]
        _, part, quad = place(pieces)

        @pl.loop(0, total // ROWS)
        def _(i):
            rows = pl.ds(pl.multiple_of(i * ROWS, ROWS), ROWS)
            normed, _ = norm_rows(x_ref[rows, :].astype(F32))
            low_t[:, rows] = (normed * gain_ref[...] + shift_ref[...]).T.astype(BF16)

        for t in range(tiles):
            cols = slice(t * tile_cols, (t + 1) * tile_cols)
            part_ref[...] = dot(low_t[...], dq_refs[t][...]).astype(BF16)
            if not packed:
                dw_refs[0][:, cols] = part_ref[...]
                continue
            for c in range(pieces):

                @pl.when(part == c)
                def _(c=c, cols=cols):
                    for q in range(quads):
                        for e in range(pieces):
                            at = (q * pieces + (c + e) % pieces) * chunk
                            dw_refs[e][q ^ quad, :, cols] = part_ref[at : at + chunk, :]

    if packed:
        grads = [sds((quads, chunk, cols_all), BF16)] * pieces
    else:
        grads = [sds((width, cols_all), BF16)]
    return run(
        body,
        [rows_all, gain, shift, *grad_tiles],
        after,
        out_shape=grads,
        scratch_shapes=[pltpu.VMEM((width, total), BF16), pltpu.VMEM((width, tile_cols), BF16)],
        vmem=12,
        cost_estimate=cost(2 * total * width * cols_all, 6 * 1024 * 1024, 0, 64),
        name="project_weights",
    )


def project_rows(
    rows_all, weight, grad_tiles, sums_mid, up_sums, pieces, quads, packed, real, after
):
    total, width = rows_all.shape
    piece_rows = total // pieces
    cols_all = weight.shape[1]
    tiles = len(grad_tiles)
    tile_cols = cols_all // tiles

    def body(*refs):
        x_ref, w_ref, mid_ref, refs = *refs[:3], refs[3:]
        ups_refs, refs = refs[: len(up_sums)], refs[len(up_sums) :]
        dq_refs, refs = refs[:tiles], refs[tiles:]
        own_ref, refs = refs[0], refs[1:]
        send_refs, (sums_ref, bias_ref) = refs[: pieces - 1], refs[pieces - 1 :]
        _, part, _ = place(pieces)
        sums_ref[...] = jnp.zeros_like(sums_ref)
        bias_ref[...] = jnp.zeros_like(bias_ref)
        for h in range(pieces):

            @pl.loop(0, piece_rows // ROWS)
            def _(i, h=h):
                at = pl.multiple_of(i * ROWS, ROWS)
                src = pl.ds(at, ROWS)
                rows = pl.ds(h * piece_rows + at, ROWS)
                normed, _ = norm_rows(x_ref[rows, :].astype(F32))
                grad = jnp.zeros((ROWS, width), F32)
                for t in range(tiles):
                    grad_rows = dq_refs[t][rows, :]
                    cols = slice(t * tile_cols, (t + 1) * tile_cols)
                    grad = grad + dot_nt(grad_rows, w_ref[:, cols])
                    bias_ref[0:1, cols] += jnp.sum(grad_rows.astype(F32), axis=0, keepdims=True)
                if h == 0:
                    own_ref[src, :] = grad
                else:
                    send_refs[h - 1][src, :] = grad.astype(BF16)
                sums_ref[0:1, :] += jnp.sum(grad * normed, axis=0, keepdims=True)
                sums_ref[1:2, :] += jnp.sum(grad, axis=0, keepdims=True)

        if not packed:
            return
        for row, src in ((4, 2), (5, 0), (6, 1), (15, 3)):
            sums_ref[row : row + 1, :] = mid_ref[src : src + 1, :]
        for c in range(pieces):

            @pl.when(part == c)
            def _(c=c):
                for row, p in ((2, 0), (3, 2)):
                    mine = jnp.concatenate(
                        [
                            bias_ref[0:1, (3 * t + p) * LANES :][:, : min(LANES, real - t * LANES)]
                            for t in range(tiles)
                        ],
                        axis=1,
                    )
                    sums_ref[row : row + 1, c * real : (c + 1) * real] = mine
                for n in range(quads):
                    row = 7 + n * pieces + c
                    start = 0
                    for ref in ups_refs:
                        size = ref.shape[1] // quads
                        here = ref[0:1, n * size : (n + 1) * size]
                        sums_ref[row : row + 1, start : start + size] = here
                        start += size

    return run(
        body,
        [rows_all, weight, sums_mid, *up_sums, *grad_tiles],
        after,
        out_shape=[sds((piece_rows, width), F32)]
        + [sds((piece_rows, width), BF16)] * (pieces - 1)
        + [sds((16, width), F32), sds((8, cols_all), F32)],
        vmem=12,
        cost_estimate=cost(2 * total * width * cols_all, 8 * 1024 * 1024, 0, 64),
        name="project_rows",
    )


def finish_rows(rows_all, gain, grad_mid, grad_own, received, count, after):
    rows, width = grad_mid.shape
    others = len(received)
    piece = rows // count
    per_step = ROWS // piece

    def body(*refs):
        x_ref, gain_ref, gm_ref, own_ref, refs = refs[0], refs[1], refs[2], refs[3], refs[4:]
        recv_refs, out_refs = refs[:others], refs[others:]
        for n in range(rows // ROWS):
            at = slice(n * ROWS, (n + 1) * ROWS)
            normed, inv_std = norm_rows(x_ref[at, :].astype(F32))
            grad = own_ref[at, :]
            for ref in recv_refs:
                grad = grad + ref[at, :].astype(F32)
            done = gm_ref[at, :] + norm_back(grad * gain_ref[...], normed, inv_std)
            for e in range(per_step):
                out_refs[n * per_step + e][...] = done[e * piece : (e + 1) * piece, :].astype(BF16)

    return run(
        body,
        [rows_all, gain, grad_mid, grad_own, *received],
        after,
        out_shape=[sds((piece, width), BF16)] * count,
        vmem=12,
        cost_estimate=cost(20 * rows * width, 6 * 1024 * 1024),
        name="finish_rows",
    )


def finish_result(own, received, count):
    rows, width = own.shape
    others = len(received)
    piece = rows // count

    def body(*refs):
        out_refs = refs[1 + others :]
        for n in range(count):
            at = slice(n * piece, (n + 1) * piece)
            total = refs[0][at, :]
            for ref in refs[1 : 1 + others]:
                total = total + ref[at, :].astype(F32)
            out_refs[n % 2][n // 2] = total.astype(BF16)

    return run(
        body,
        [own, *received],
        out_shape=[sds((count // 2, piece, width), BF16)] * 2,
        vmem=8,
        cost_estimate=cost(2 * rows * width, 3 * 1024 * 1024),
        name="finish_result",
    )


def pass_on(keep, received, after):
    def body(keep_ref, recv_ref, out_ref):
        out_ref[0] = keep_ref[1]
        out_ref[1] = recv_ref[1]

    return run(
        body,
        [keep, received],
        after,
        out_shape=sds(keep.shape, keep.dtype),
        vmem=6,
        cost_estimate=cost(0, 4 * keep.size),
        name="pass_on",
    )


def collect_halves(keep, near, far, group, after):
    _, rows, width = keep.shape

    def body(keep_ref, near_ref, far_ref, out_ref):
        _, _, quad = place(group)
        out_ref[quad] = keep_ref[0]
        out_ref[quad ^ 1] = near_ref[0]
        out_ref[quad ^ 2] = far_ref[0]
        out_ref[quad ^ 3] = far_ref[1]

    return run(
        body,
        [keep, near, far],
        after,
        out_shape=sds((4, rows, width), keep.dtype),
        vmem=6,
        cost_estimate=cost(0, 16 * rows * width),
        name="collect_halves",
    )


def two_parts(item):
    first = item.astype(BF16)
    return first, (item - first.astype(F32)).astype(BF16)


def pack_attention(
    qkv_keep, qkv_recv, out_keep, out_recv, small, small_recv, real, blocks, after
):
    quads, chunk, cols_all = qkv_keep.shape
    wide = cols_all // 3
    tiles = wide // LANES
    width = out_keep.shape[2]
    qkv_lanes = 6 * real // blocks
    out_lanes = width // blocks
    lanes = qkv_lanes + out_lanes
    halves = quads // 2
    slot = halves * chunk
    small_rows = small.shape[0]

    def body(qk_ref, qr_ref, ok_ref, or_ref, small_ref, srecv_ref, *out_refs):
        _, part, quad = place(2)
        mine = lax.axis_index("batch")
        slots = out_refs[4]

        def heads_of(rows, p):
            return [
                rows[:, (3 * t + p) * LANES : (3 * t + p) * LANES + min(LANES, real - t * LANES)]
                for t in range(tiles)
            ]

        for c in range(2):

            @pl.when(part == c)
            def _(c=c):
                for q in range(quads):
                    pair = (qk_ref[q], qr_ref[q])
                    if c == 1:
                        pair = pair[::-1]
                    parts = []
                    for p in range(3):
                        parts += heads_of(pair[0], p) + heads_of(pair[1], p)
                    row = jnp.concatenate(parts, axis=1)
                    for b in range(blocks):
                        slots[b ^ mine, q, :, 0:qkv_lanes] = row[
                            :, b * qkv_lanes : (b + 1) * qkv_lanes
                        ]
                for e, ref in enumerate((ok_ref, or_ref)):
                    for n in range(halves):
                        q = ((c + e) % 2) * halves + n
                        for b in range(blocks):
                            slots[b ^ mine, q ^ quad, :, qkv_lanes:lanes] = ref[
                                n, :, b * out_lanes : (b + 1) * out_lanes
                            ]

        for n, order in enumerate(((0, 2), (1, 3), (0, 1), (2, 3))):
            for e in range(2):
                for f in range(halves):
                    at = e * slot + f * chunk
                    src = f if n < 2 else halves + f
                    out_refs[n][at : at + chunk, :] = slots[order[e], src]
        parts = two_parts(small_ref[...] + srecv_ref[...])
        for n in range(2):
            for e in range(2):
                at = 2 * slot + e * small_rows
                out_refs[n][at : at + small_rows, :] = parts[e]

    first = sds((2 * slot + 2 * small_rows, lanes), BF16)
    other = sds((2 * slot, lanes), BF16)
    return run(
        body,
        [qkv_keep, qkv_recv, out_keep, out_recv, small, small_recv],
        after,
        out_shape=[first, first, other, other],
        scratch_shapes=[pltpu.VMEM((blocks, quads, chunk, lanes), BF16)],
        vmem=12,
        cost_estimate=cost(0, 4 * 1024 * 1024),
        name="pack_attention",
    )


def sum_first(keeps, received, after=()):
    count = len(keeps)
    shape = keeps[0].shape[1:]

    def body(*refs):
        for n in range(count):
            for e in range(2):
                total = refs[n][e].astype(F32) + refs[count + n][e].astype(F32)
                refs[2 * count + 2 * n + e][...] = total.astype(BF16)

    return run(
        body,
        [*keeps, *received],
        after,
        out_shape=[sds(shape, BF16)] * (2 * count),
        vmem=12,
        cost_estimate=cost(0, 6 * count * keeps[0].size),
        name="sum_first",
    )


def sum_second(keeps, received, after=()):
    quads, rows, width = keeps[0].shape

    def body(ka, kb, ra, rb, keep_ref, send_ref):
        for d in range(quads):
            ref = send_ref if d % 2 else keep_ref
            for e, (keep, recv) in enumerate(((ka, ra), (kb, rb))):
                total = keep[d].astype(F32) + recv[d].astype(F32)
                ref[d // 2, e] = total.astype(BF16)

    return run(
        body,
        [*keeps, *received],
        after,
        out_shape=[sds((quads // 2, 2, rows, width), BF16)] * 2,
        vmem=10,
        cost_estimate=cost(0, 12 * keeps[0].size),
        name="sum_second",
    )


def sum_third(keep, received, after=()):
    def body(keep_ref, recv_ref, stay_ref, pass_ref):
        for ref, e in ((stay_ref, 0), (pass_ref, 1)):
            ref[...] = (keep_ref[e].astype(F32) + recv_ref[e].astype(F32)).astype(BF16)

    return run(
        body,
        [keep, received],
        after,
        out_shape=[sds(keep.shape[1:], BF16)] * 2,
        vmem=6,
        cost_estimate=cost(0, 6 * keep.size),
        name="sum_third",
    )


def small_sum(refs, rows, count):
    total = None
    for ref in refs:
        for e in range(2):
            item = ref[rows + e * count : rows + (e + 1) * count, :].astype(F32)
            total = item if total is None else total + item
    return total


def sum_first_attention(keeps, received, slot, small_rows, after):
    lanes = keeps[0].shape[1]

    def body(ka, kb, ra, rb, stay_a, pass_a, stay_b, pass_b):
        parts = two_parts(small_sum((ka, ra), 2 * slot, small_rows))
        for keep, recv, stay, on in ((ka, ra, stay_a, pass_a), (kb, rb, stay_b, pass_b)):
            for e, ref in enumerate((stay, on)):
                at = slice(e * slot, (e + 1) * slot)
                ref[0:slot, :] = (keep[at, :].astype(F32) + recv[at, :].astype(F32)).astype(BF16)
        for ref in (stay_a, pass_a):
            for e in range(2):
                ref[slot + e * small_rows : slot + (e + 1) * small_rows, :] = parts[e]

    first = sds((slot + 2 * small_rows, lanes), BF16)
    other = sds((slot, lanes), BF16)
    return run(
        body,
        [*keeps, *received],
        after,
        out_shape=[first, first, other, other],
        vmem=8,
        cost_estimate=cost(0, 3 * 1024 * 1024),
        name="sum_first_attention",
    )


def sum_second_attention(keeps, received, chunk, quads, small_rows, after):
    lanes = keeps[0].shape[1]
    halves = quads // 2
    slot = halves * chunk

    def body(ka, kb, ra, rb, *out_refs):
        parts = two_parts(small_sum((ka, ra), slot, small_rows))
        for d in range(quads):
            keep, recv = ((ka, ra), (kb, rb))[d // halves]
            at = slice(d % halves * chunk, (d % halves + 1) * chunk)
            total = keep[at, :].astype(F32) + recv[at, :].astype(F32)
            out_refs[d][0:chunk, :] = total.astype(BF16)
            for e in range(2):
                at = chunk + e * small_rows
                out_refs[d][at : at + small_rows, :] = parts[e]

    return run(
        body,
        [*keeps, *received],
        after,
        out_shape=[sds((chunk + 2 * small_rows, lanes), BF16)] * quads,
        vmem=8,
        cost_estimate=cost(0, 2 * 1024 * 1024),
        name="sum_second_attention",
    )


def final_attention(pieces, chunk, qkv_lanes, small_rows):
    lanes = pieces[0].shape[1]
    count = len(pieces)

    def body(*refs):
        total = refs[0][0:chunk, :].astype(F32)
        for ref in refs[1:count]:
            total = total + ref[0:chunk, :].astype(F32)
        refs[count][...] = total[:, :qkv_lanes]
        refs[count + 1][...] = total[:, qkv_lanes:]
        refs[count + 2][...] = small_sum(refs[:count], chunk, small_rows)

    return run(
        body,
        pieces,
        out_shape=[
            sds((chunk, qkv_lanes), F32),
            sds((chunk, lanes - qkv_lanes), F32),
            sds((small_rows, lanes), F32),
        ],
        vmem=6,
        cost_estimate=cost(0, 1024 * 1024),
        name="final_attention",
    )


def final_units(first, second, after):
    high = first[0].shape[1]
    sizes = [first[0].shape[2], second[0].shape[2]]
    unit_block = sum(sizes)
    count = len(first)
    half = high // 2

    def body(*refs):
        _, part, _ = place(2)
        keep_ref, send_ref, down_ref = refs[2 * count :]
        for h in range(2):
            pieces = refs[h * count : (h + 1) * count]
            up, down = pieces[0][0].astype(F32), pieces[0][1].astype(F32)
            for ref in pieces[1:]:
                up = up + ref[0].astype(F32)
                down = down + ref[1].astype(F32)
            here = slice(h * sizes[0], h * sizes[0] + sizes[h])
            down_ref[here, :] = down.T
            for c in range(2):

                @pl.when(part == c)
                def _(up=up, here=here, c=c):
                    keep_ref[:, here] = up[c * half : (c + 1) * half, :]
                    send_ref[:, here] = up[(1 - c) * half : (2 - c) * half, :].astype(BF16)

    return run(
        body,
        [*first, *second],
        after,
        out_shape=[
            sds((half, unit_block), F32),
            sds((half, unit_block), BF16),
            sds((unit_block, high), F32),
        ],
        vmem=10,
        cost_estimate=cost(0, 4 * 1024 * 1024),
        name="final_units",
    )


def final_join(keep, recv):
    chunk, unit_block = keep.shape

    def body(keep_ref, recv_ref, out_ref):
        _, part, _ = place(2)
        for c in range(2):

            @pl.when(part == c)
            def _(c=c):
                out_ref[:, c * unit_block : (c + 1) * unit_block] = keep_ref[...]
                out_ref[:, (1 - c) * unit_block : (2 - c) * unit_block] = recv_ref[...].astype(F32)

    return run(
        body,
        [keep, recv],
        out_shape=sds((chunk, 2 * unit_block), F32),
        vmem=5,
        cost_estimate=cost(0, 1024 * 1024),
        name="final_join",
    )


def on_device(
    tokens,
    mask,
    cotangent,
    ln1_gain,
    ln1_bias,
    qkv_weight,
    q_bias,
    v_bias,
    out_weight,
    out_bias,
    ln2_gain,
    ln2_bias,
    up_weight,
    up_bias,
    down_weight,
    down_bias,
):
    seq_size = lax.axis_size("seq")
    batch_size = lax.axis_size("batch")
    micro_count, seq_count, local_len, width = tokens.shape
    sequences = micro_count * seq_count
    group = seq_size // sequences
    units = up_weight.shape[1]
    head_dim = width // HEADS
    heads = HEADS // group
    real = heads * head_dim
    wide = -(-real // LANES) * LANES
    full_len = local_len * seq_size
    block_len = local_len // group
    rows = seq_size * block_len
    own_units = units // group
    part = lax.axis_index("seq") % group
    aligned = (
        seq_size == batch_size * group
        and group == 2
        and batch_size == 4
        and wide == 3 * LANES
        and (seq_size // group) % group == 0
        and units % (batch_size * group * LANES) == 0
        and own_units // batch_size == width
    )

    def from_part(item, ahead):
        if ahead % group == 0:
            return item
        pairs = [
            (q * group + (c + ahead) % group, q * group + c)
            for q in range(sequences)
            for c in range(group)
        ]
        return lax.ppermute(item, "seq", pairs)

    def gather_parts(item):
        return [from_part(item, n) for n in range(group)]

    def row_of(item):
        return item.astype(F32)[None, :]

    def blocks_of(item):
        return item.reshape(sequences, local_len, width)

    x_own = over_quads(deal(blocks_of(tokens), group), group)
    x_pieces = [from_part(item, n) for n in range(group) for item in x_own]

    count_rows = jnp.sum(mask, axis=2).reshape(sequences).astype(BF16)
    cot_low = jnp.where(mask[..., None] != 0, cotangent, jnp.zeros_like(cotangent))
    cot_send = jnp.concatenate(
        [blocks_of(cot_low), jnp.broadcast_to(count_rows[:, None, None], (sequences, 16, width))],
        axis=1,
    )
    cot_own = over_quads(deal(cot_send, group, x_pieces[sequences:]), group)

    qkv_w, qkv_b, *out_w = pick_weights(
        qkv_weight,
        jnp.concatenate([q_bias, jnp.zeros_like(q_bias), v_bias])[None, :],
        out_weight,
        group,
        real,
        wide,
    )
    if aligned:
        up_own, up_b, down_own = up_weight, up_bias[None, :], down_weight
    else:

        def own_columns(matrix, blocks):
            split = matrix.reshape(matrix.shape[0], blocks, group, -1)
            return lax.dynamic_index_in_dim(split, part, 2, keepdims=False)

        up_own = own_columns(up_weight, batch_size).reshape(width, own_units)
        up_b = own_columns(up_bias[None, :], batch_size).reshape(1, own_units)
        down_own = lax.dynamic_index_in_dim(
            down_weight.reshape(batch_size, group, -1, width), part, 1, keepdims=False
        ).reshape(own_units, width)

    tiles = wide // LANES
    x_all, qkv, att_first, logs_first = attend_first(
        x_pieces, row_of(ln1_gain), row_of(ln1_bias), qkv_w, qkv_b, tiles - 1, heads, head_dim
    )
    cot_stack = stack(cot_own, [logs_first])
    att_last, logs_last = attend_last(qkv, tiles - 1, heads, head_dim, [cot_stack])
    cot_pieces = cot_own + [
        item[d]
        for item in gather_parts(cot_stack)[1:]
        for d in range(sequences)
    ]
    blocks = batch_size if aligned else 1
    unit_block = own_units // blocks
    size = unit_block * 2 // 5
    shape = (group, sequences if aligned else None, width // sequences)
    calls = [
        Units(unit_block, blocks, 0, size, *shape),
        Units(unit_block, blocks, size, unit_block - size, *shape),
    ]
    mid, second, second_t, grad_rows, grad_t, result_own, grad_second, *found = feed_first(
        x_all,
        gather_parts(att_first),
        gather_parts(att_last),
        cot_pieces,
        out_w,
        row_of(out_bias),
        row_of(ln2_gain),
        row_of(ln2_bias),
        up_own,
        up_b,
        down_own,
        row_of(down_bias),
        calls[0],
    )
    up_sums, ff_grads = [found[0]], [found[group:]]
    result_own, grad_second, *found = feed_second(
        second,
        second_t,
        grad_rows,
        grad_t,
        result_own,
        grad_second,
        found[1:group],
        up_own,
        up_b,
        down_own,
        calls[1],
    )
    up_sums.append(found[0])
    result_send = found[1:group]
    ff_grads.append(found[group:])

    def begin_sum(e, sends, after):
        moved = [swap(sends[0], "batch", batch_size, 1), swap(sends[1], "batch", batch_size, 2)]
        stay_a, pass_a, stay_b, pass_b = sum_first(
            [ff_grads[e][0], ff_grads[e][2]], moved, after
        )
        moved = [swap(pass_a, "batch", batch_size, 2), swap(pass_b, "batch", batch_size, 1)]
        return [stay_a, stay_b], moved

    if aligned:
        waiting = begin_sum(0, [ff_grads[0][1], ff_grads[0][3]], [])
        (grad_second,) = gate([grad_second], waiting[0][:1])
    second_send = grad_second
    second_recv = [from_part(second_send, n) for n in range(1, group)]
    result_recv = [from_part(result_send[group - n - 1], n) for n in range(1, group)]
    result_keep, result_pass = finish_result(result_own, result_recv, sequences)

    def quad_swap(item, distance):
        return swap(item, "seq", seq_size, distance * group)

    result_near = quad_swap(result_pass, 1)

    chunk = width // seq_size
    grad_mid, grad_att, sums_mid, *out_grad = mid_back(
        mid,
        grad_second,
        second_recv,
        grad_rows,
        row_of(ln2_gain),
        out_w[0],
        att_first,
        att_last,
        chunk if aligned else 0,
    )

    def tile_back(t, after, cost_part=1):
        last = t == tiles - 1
        return attend_backward(
            qkv,
            grad_att,
            att_last if last else att_first,
            0 if last else t,
            logs_last if last else logs_first,
            0 if last else t * (LANES // head_dim),
            t,
            heads,
            head_dim,
            after,
            cost_part,
        )

    grad_tiles = [None] * tiles
    after = [result_keep]
    if aligned:
        keep, send = sum_second(*waiting, [grad_mid])
        moved = quad_swap(send, 1)
        sends = gate([ff_grads[1][1], ff_grads[1][3]], [keep])
        after = [result_keep, keep]
    grad_tiles[0] = tile_back(0, after, 64)
    result_pass = pass_on(result_keep, result_near, grad_tiles[:1])
    result_far = quad_swap(result_pass, 2)
    after = [result_pass]
    if aligned:
        unit_first = list(sum_third(keep, moved, [grad_tiles[0]]))
        unit_first[1] = quad_swap(unit_first[1], 2)
        after = [result_pass, unit_first[0]]
    grad_tiles[-1] = tile_back(tiles - 1, after, 64)
    after = []
    if aligned:
        waiting = begin_sum(1, sends, [grad_tiles[-1]])
        after = waiting[0][:1]
    for t in range(1, tiles - 1):
        grad_tiles[t] = tile_back(t, after)
    after = [result_far]
    if aligned:
        out_recv = from_part(out_grad[1], 1)
        keep, send = sum_second(*waiting, [grad_tiles[-2]])
        moved = quad_swap(send, 1)
        after = [keep, unit_first[1], result_far, out_recv]
    qkv_grad = project_weights(
        x_all, row_of(ln1_gain), row_of(ln1_bias), grad_tiles, group, sequences, aligned, after
    )
    first_own, *found = project_rows(
        x_all,
        qkv_w,
        grad_tiles,
        sums_mid,
        up_sums,
        group,
        sequences,
        aligned,
        real,
        qkv_grad[:1],
    )
    first_send, (small, bias_sums) = found[: group - 1], found[group - 1 :]
    first_recv = [from_part(first_send[group - n - 1], n) for n in range(1, group)]
    after = []
    if aligned:
        unit_second = list(sum_third(keep, moved, [first_own]))
        unit_second[1] = quad_swap(unit_second[1], 2)
        small_rows = small.shape[0]
        packed = pack_attention(
            qkv_grad[0],
            from_part(qkv_grad[1], 1),
            out_grad[0],
            out_recv,
            small,
            from_part(small, 1),
            real,
            batch_size,
            unit_second[:1],
        )
        after = packed[:1]
    row_parts = finish_rows(
        x_all, row_of(ln1_gain), grad_mid, first_own, first_recv, sequences, after
    )
    row_moved = over_quads(row_parts, group)
    if aligned:
        stay_a, pass_a, stay_b, pass_b = sum_first_attention(
            [packed[0], packed[2]],
            [swap(packed[1], "batch", batch_size, 1), swap(packed[3], "batch", batch_size, 2)],
            sequences // 2 * chunk,
            small_rows,
            row_parts[:1],
        )
        summed = sum_second_attention(
            [stay_a, stay_b],
            [swap(pass_a, "batch", batch_size, 2), swap(pass_b, "batch", batch_size, 1)],
            chunk,
            sequences,
            small_rows,
            unit_second[1:] + row_moved[1:],
        )
        after = summed[:1]
        up_keep, up_send, down_grad = final_units(unit_first, unit_second, after)
        up_grad = final_join(up_keep, from_part(up_send, 1))
        qkv_final, out_final, small = final_attention(
            over_quads(summed, group), chunk, qkv_weight.shape[1] // batch_size, small_rows
        )
        small = small.reshape(-1)
    result = collect_halves(result_keep, result_near, result_far, group, after)
    result = result.reshape(tokens.shape)
    grad_in = collect(row_moved, group, after).reshape(tokens.shape)
    if not aligned:

        def spread(item, blocks):
            split = item.reshape(blocks, 1, -1)
            empty = jnp.zeros((blocks, group, split.shape[2]), F32)
            return lax.dynamic_update_slice(empty, split, (0, part, 0)).reshape(-1)

        bias_sums = bias_sums[0].reshape(tiles, 3, LANES).transpose(1, 0, 2)
        bias_sums = bias_sums.reshape(3, wide)[:, :real]
        small = jnp.concatenate(
            [
                small[0],
                small[1],
                spread(bias_sums[0], 1),
                spread(bias_sums[2], 1),
                sums_mid[2],
                sums_mid[0],
                sums_mid[1],
                spread(jnp.concatenate([item[0] for item in up_sums]), batch_size),
                sums_mid[3],
            ]
        )

        def scattered(item):
            item = lax.psum_scatter(item.astype(BF16), "seq", scatter_dimension=0, tiled=True)
            return lax.psum_scatter(item, "batch", scatter_dimension=1, tiled=True).astype(F32)

        def spread_columns(item, blocks):
            split = item.reshape(item.shape[0], blocks, 1, -1)
            empty = jnp.zeros((item.shape[0], blocks, group, split.shape[3]), item.dtype)
            filled = lax.dynamic_update_slice(empty, split, (0, 0, part, 0))
            return filled.reshape(item.shape[0], -1)

        up_full, down_full = [
            jnp.concatenate([item[e] for item in ff_grads], axis=1) for e in range(2)
        ]
        up_grad = scattered(spread_columns(up_full, batch_size))
        down_grad = scattered(spread_columns(down_full, batch_size).T)
        rows_full = qkv_grad[0].reshape(width, tiles, 3, LANES).transpose(0, 2, 1, 3)
        rows_full = rows_full.reshape(width, 3, wide)[..., :real]
        qkv_final = scattered(spread_columns(rows_full.reshape(width, -1), 3))
        out_final = scattered(spread_columns(out_grad[0][:real].T, 1).T)
        small = lax.psum(small, ("seq", "batch"))

    edges = [width] * 7 + [units, width]
    pieces, start = [], 0
    for size in edges:
        pieces.append(small[start : start + size])
        start += size
    return (
        result,
        grad_in,
        pieces[0],
        pieces[1],
        qkv_final,
        pieces[2],
        pieces[3],
        out_final,
        pieces[4],
        pieces[5],
        pieces[6],
        up_grad,
        pieces[7],
        down_grad,
        pieces[8],
    )


def solution(mesh):
    rows = P(None, "batch", "seq", None)
    split = P("seq", "batch")
    in_specs = (rows, P(None, "batch", "seq"), rows) + (P(),) * 13
    out_specs = (
        rows,
        rows,
        P(),
        P(),
        split,
        P(),
        P(),
        split,
        P(),
        P(),
        P(),
        split,
        P(),
        split,
        P(),
    )
    return jax.shard_map(
        on_device, mesh=mesh, in_specs=in_specs, out_specs=out_specs, check_vma=False
    )
```

```python
import jax
import jax.numpy as jnp
from jax import lax
from jax.experimental import pallas as pl
from jax.experimental.pallas import tpu as pltpu
from jax.sharding import PartitionSpec as P

HEADS = 20
EPS = 1e-05
LOG2E = 1.4426950408889634
ROWS = 256
F32 = jnp.float32
BF16 = jnp.bfloat16
LANES = 128


def dot(left, right):
    return jnp.dot(left, right, preferred_element_type=F32)


def dot_nt(left, right):
    return lax.dot_general(left, right, (((1,), (1,)), ((), ())), preferred_element_type=F32)


def norm_rows(rows_in):
    mean_val = jnp.mean(rows_in, axis=-1, keepdims=True)
    centered = rows_in - mean_val
    inv_std = lax.rsqrt(jnp.mean(centered * centered, axis=-1, keepdims=True) + EPS)
    return centered * inv_std, inv_std


def norm_back(scaled, normed, inv_std):
    inner = (
        scaled
        - jnp.mean(scaled, axis=-1, keepdims=True)
        - normed * jnp.mean(scaled * normed, axis=-1, keepdims=True)
    )
    return inner * inv_std


def params_of(mib):
    return pltpu.CompilerParams(vmem_limit_bytes=mib * 1024 * 1024)


def cost(flops, moved, trans=0, part=1):
    return pl.CostEstimate(
        flops=flops // part, bytes_accessed=moved // part, transcendentals=trans // part
    )


def sds(shape, dtype):
    return jax.ShapeDtypeStruct(shape, dtype)


VMEM = pl.BlockSpec(memory_space=pltpu.VMEM)
ANY = pl.BlockSpec(memory_space=pl.ANY)
HBM = pl.BlockSpec(memory_space=pltpu.HBM)


def run(body, operands, after=(), in_specs=None, out_specs=None, vmem=32, **more):
    count, extra = len(operands), len(after)

    def inner(*refs):
        body(*refs[:count], *refs[count + extra :])

    specs = [VMEM] * count if in_specs is None else list(in_specs)
    shapes = more["out_shape"]
    if out_specs is None:
        out_specs = [VMEM] * len(shapes) if isinstance(shapes, (list, tuple)) else VMEM
    return pl.pallas_call(
        inner,
        in_specs=specs + [ANY] * extra,
        out_specs=out_specs,
        compiler_params=params_of(vmem),
        **more,
    )(*operands, *after)


def far(item):
    return pltpu.with_memory_space_constraint(item, pltpu.HBM)


def gate(items, after):
    def body(*refs):
        del refs

    return pl.pallas_call(
        body,
        in_specs=[ANY] * (len(items) + len(after)),
        out_specs=[ANY] * len(items),
        out_shape=[sds(item.shape, item.dtype) for item in items],
        input_output_aliases={n: n for n in range(len(items))},
        cost_estimate=cost(0, 0),
        name="gate",
    )(*items, *after)


def place(group):
    spot = lax.axis_index("seq")
    return spot, lax.rem(spot, group), lax.div(spot, group)


def deal(item, group, after=()):
    count, rows, width = item.shape

    def body(in_ref, *out_refs):
        _, _, quad = place(group)
        for d in range(count):
            out_refs[d][...] = in_ref[quad ^ d]

    return run(
        body,
        [item],
        after,
        out_shape=[sds((rows, width), item.dtype)] * count,
        vmem=6,
        cost_estimate=cost(0, 4 * count * rows * width),
        name="deal",
    )


def collect(pieces, group, after):
    count = len(pieces)
    rows, width = pieces[0].shape

    def body(*refs):
        _, _, quad = place(group)
        for d in range(count):
            refs[count][quad ^ d] = refs[d][...]

    return run(
        body,
        pieces,
        after,
        out_shape=sds((count, rows, width), pieces[0].dtype),
        vmem=6,
        cost_estimate=cost(0, 4 * count * rows * width),
        name="collect",
    )


def stack(pieces, after):
    count = len(pieces)

    def body(*refs):
        for d in range(count):
            refs[count][d] = refs[d][...]

    return run(
        body,
        pieces,
        after,
        out_shape=sds((count,) + pieces[0].shape, pieces[0].dtype),
        vmem=12,
        cost_estimate=cost(0, 4 * count * pieces[0].size),
        name="stack",
    )


def swap(item, axis, size, distance):
    return lax.ppermute(item, axis, [(i, i ^ distance) for i in range(size)])


def over_quads(pieces, group):
    return [
        piece if d == 0 else swap(piece, "seq", len(pieces) * group, d * group)
        for d, piece in enumerate(pieces)
    ]


def pick_weights(qkv_weight, qkv_bias, out_weight, group, real, wide):
    width = qkv_weight.shape[0]
    tiles = wide // LANES

    def body(w_ref, b_ref, o_ref, wo_ref, bo_ref, *out_refs):
        _, part, _ = place(group)
        wo_ref[...] = jnp.zeros_like(wo_ref)
        bo_ref[...] = jnp.zeros_like(bo_ref)
        for ref in out_refs:
            ref[...] = jnp.zeros_like(ref)
        for c in range(group):

            @pl.when(part == c)
            def _(c=c):
                for p in range(3):
                    for t in range(tiles):
                        some = min(LANES, real - t * LANES)
                        src = p * width + c * real + t * LANES
                        dst = (3 * t + p) * LANES
                        wo_ref[:, dst : dst + some] = w_ref[:, src : src + some]
                        bo_ref[:, dst : dst + some] = b_ref[:, src : src + some]
                for n in range(group):
                    src = (c + n) % group * real
                    out_refs[n][0:real, :] = o_ref[src : src + real, :]

    return pl.pallas_call(
        body,
        out_shape=[sds((width, 3 * wide), BF16), sds((1, 3 * wide), F32)]
        + [sds((wide, width), BF16)] * group,
        compiler_params=params_of(24),
        cost_estimate=cost(0, 8 * 1024 * 1024),
        name="pick_weights",
    )(qkv_weight, qkv_bias, out_weight)


def by_pairs(live, visit):
    size = 2 if live % 2 == 0 else 1

    @pl.loop(0, live // size)
    def _(i):
        visit([i * size + e for e in range(size)])


def attend_tiles(query_at, keys_at, vals_at, att_ref, lse_ref, keys, vals, acc, tiles, heads, head_dim):
    per_tile = LANES // head_dim
    total = att_ref.shape[0]
    exp_scale = head_dim ** (-0.5) * LOG2E
    lane = lax.broadcasted_iota(jnp.int32, (1, LANES), 1)
    row = lax.broadcasted_iota(jnp.int32, (LANES, 1), 0)
    lse_ref[...] = jnp.zeros_like(lse_ref)
    vals[:, :, LANES:] = jnp.ones((per_tile, total, LANES), BF16)
    for n, t in enumerate(tiles):
        live = min(per_tile, heads - t * per_tile)
        key_t = keys_at(n).astype(F32).T
        val_f = vals_at(n).astype(F32)
        for j in range(live):
            keys[j] = jnp.where(row // head_dim == j, key_t, 0.0).astype(BF16)
            vals[j, :, :LANES] = jnp.where(lane // head_dim == j, val_f, 0.0).astype(BF16)
        acc[...] = jnp.zeros_like(acc)

        def visit(some, n=n):
            scores = [dot(query_at(n), keys[j]) for j in some]
            for item, j in zip(scores, some):
                row_max = jnp.max(item, axis=-1, keepdims=True) * exp_scale
                expd = jnp.exp2(item * exp_scale - row_max).astype(BF16)
                mixed = dot(expd, vals[j])
                den = mixed[:, LANES:]
                acc[...] += mixed[:, :LANES] / den
                lse_ref[...] = jnp.where(
                    lane == n * per_tile + j, row_max + jnp.log2(den), lse_ref[...]
                )

        by_pairs(live, visit)
        att_ref[:, n * LANES : (n + 1) * LANES] = acc[...].astype(BF16)


def attend_scratch(total, head_dim):
    per_tile = LANES // head_dim
    return [
        pltpu.VMEM((per_tile, LANES, total), BF16),
        pltpu.VMEM((per_tile, total, 2 * LANES), BF16),
        pltpu.VMEM((total, LANES), F32),
    ]


def attend_first(x_pieces, gain, shift, weight, bias, tiles, heads, head_dim):
    count = len(x_pieces)
    piece_rows, width = x_pieces[0].shape
    total = count * piece_rows
    cols_all = weight.shape[1]

    def body(*refs):
        x_refs = refs[:count]
        gain_ref, shift_ref, w_ref, bias_ref = refs[count : count + 4]
        x_ref, qkv_ref, att_ref, lse_ref, keys, vals, acc = refs[count + 4 :]
        for n in range(count):
            x_ref[n * piece_rows : (n + 1) * piece_rows, :] = x_refs[n][...]

        @pl.loop(0, total // ROWS)
        def _(i):
            rows = pl.ds(pl.multiple_of(i * ROWS, ROWS), ROWS)
            normed, _ = norm_rows(x_ref[rows, :].astype(F32))
            low = (normed * gain_ref[...] + shift_ref[...]).astype(BF16)
            qkv_ref[rows, :] = (dot(low, w_ref[...]) + bias_ref[...]).astype(BF16)

        def columns(at):
            return slice(at * LANES, (at + 1) * LANES)

        attend_tiles(
            lambda n: qkv_ref[:, columns(3 * n)],
            lambda n: qkv_ref[:, columns(3 * n + 1)],
            lambda n: qkv_ref[:, columns(3 * n + 2)],
            att_ref,
            lse_ref,
            keys,
            vals,
            acc,
            range(tiles),
            heads,
            head_dim,
        )

    return run(
        body,
        [*x_pieces, gain, shift, weight, bias],
        out_shape=[
            sds((total, width), BF16),
            sds((total, cols_all), BF16),
            sds((total, tiles * LANES), BF16),
            sds((total, LANES), F32),
        ],
        scratch_shapes=attend_scratch(total, head_dim),
        vmem=23,
        cost_estimate=cost(
            2 * total * width * cols_all + 4 * heads * total * total * 256,
            8 * 1024 * 1024,
            heads * total * total,
        ),
        name="attend_first",
    )


def attend_last(qkv, tile, heads, head_dim, after):
    total = qkv.shape[0]

    def body(qkv_ref, att_ref, lse_ref, keys, vals, acc):
        attend_tiles(
            lambda n: qkv_ref[:, 0:LANES],
            lambda n: qkv_ref[:, LANES : 2 * LANES],
            lambda n: qkv_ref[:, 2 * LANES : 3 * LANES],
            att_ref,
            lse_ref,
            keys,
            vals,
            acc,
            [tile],
            heads,
            head_dim,
        )

    live = heads - tile * (LANES // head_dim)
    return run(
        body,
        [qkv],
        after,
        grid=(1,),
        in_specs=[pl.BlockSpec((total, 3 * LANES), lambda i: (0, tile))],
        out_specs=[pl.BlockSpec((total, LANES), lambda i: (0, 0))] * 2,
        out_shape=[sds((total, LANES), BF16), sds((total, LANES), F32)],
        scratch_shapes=attend_scratch(total, head_dim),
        vmem=14,
        cost_estimate=cost(4 * live * total * total * 256, 2 * 1024 * 1024, live * total * total),
        name="attend_last",
    )


def gelu_parts(value):
    size = jnp.abs(value)
    near = pl.reciprocal(1.0 + (0.3275911 * 0.7071067811865476) * size, approx=True)
    bell = jnp.exp2(value * value * (-0.5 * LOG2E))
    poly = near * (
        0.5 * 0.254829592
        + near
        * (
            0.5 * -0.284496736
            + near * (0.5 * 1.421413741 + near * (0.5 * -1.453152027 + near * (0.5 * 1.061405429)))
        )
    )
    tail = poly * bell
    area = jnp.where(value < 0.0, tail, 1.0 - tail)
    return value * area, area + value * bell * 0.3989422804014327


class Units:
    def __init__(self, block, blocks, start, size, stride, quads, high):
        self.block, self.blocks, self.start, self.size = block, blocks, start, size
        self.stride, self.quads, self.high = stride, quads, high
        self.count = blocks * size
        self.chunk = 512 if self.count % 512 == 0 else 256
        self.packed = quads is not None

    def loads(self, part, hbm_up, hbm_down, hbm_bias, up_ref, down_ref, bias_ref, sem):
        copies = []
        for b in range(self.blocks):
            src = self.start
            if self.packed:
                src = pl.multiple_of((b * self.stride + part) * self.block, LANES) + self.start
            src = pl.ds(src, self.size)
            dst = pl.ds(b * self.size, self.size)
            copies.append(
                pltpu.make_async_copy(hbm_up.at[:, src], up_ref.at[:, dst], sem.at[2 * b])
            )
            copies.append(
                pltpu.make_async_copy(hbm_down.at[src, :], down_ref.at[dst, :], sem.at[2 * b + 1])
            )
            bias_ref[0:1, dst] = hbm_bias[:, src]
        return copies

    def grad_shapes(self, width):
        if self.packed:
            return [pltpu.HBM((2, self.quads, self.high, self.size), BF16)] * 4
        return [sds((width, self.count), BF16)] * 2

    def scratch(self, total, width):
        grads = (self.blocks, self.quads, self.high, self.size) if self.packed else (8, LANES)
        return [
            pltpu.VMEM(grads, BF16),
            pltpu.VMEM(grads, BF16),
            pltpu.SemaphoreType.DMA((8,)),
            pltpu.VMEM((total, self.count), BF16),
            pltpu.VMEM((total, self.count), BF16),
            pltpu.VMEM((width, self.count), BF16),
            pltpu.VMEM((self.count, width), BF16),
            pltpu.VMEM((8, self.count), F32),
            pltpu.SemaphoreType.DMA((2 * self.blocks,)),
        ]

    def compute(self, part, second, second_t, grad, grad_t, acc, gs, ubg, scratch, outs):
        up_slots, down_slots, out_sem, acts, grad_pres, up_ref, down_ref, bias_ref, _ = scratch
        if not self.packed:
            up_slots, down_slots = outs
        quad = lax.div(lax.axis_index("seq"), self.stride)
        mine = lax.axis_index("batch")

        def enter(i):
            rows = slice(i * ROWS, (i + 1) * ROWS)
            pre = dot(second[rows, :], up_ref[...]) + bias_ref[0:1, :]
            return pre, dot_nt(grad[rows, :], down_ref[...])

        def weights(n):
            first, last = n * self.chunk, (n + 1) * self.chunk
            up_grad = dot(second_t[...], grad_pres[:, first:last]).astype(BF16)
            down_grad = dot(grad_t[...], acts[:, first:last]).astype(BF16)
            if not self.packed:
                up_slots[:, first:last] = up_grad
                down_slots[:, first:last] = down_grad
                return
            at = first
            while at < last:
                block = at // self.size
                stop = min(last, (block + 1) * self.size)
                src = slice(at - first, stop - first)
                dst = slice(at - block * self.size, stop - block * self.size)
                for m in range(self.blocks):
                    rows = slice(m * self.high, (m + 1) * self.high)
                    up_slots[block ^ mine, m ^ quad, :, dst] = up_grad[rows, src]
                    down_slots[m ^ mine, block ^ quad, :, dst] = down_grad[rows, src]
                at = stop

        ready = enter(0)
        chunks = second.shape[0] // ROWS
        for i in range(chunks):
            ahead = enter(i + 1) if i + 1 < chunks else None
            rows = slice(i * ROWS, (i + 1) * ROWS)
            pre, grad_act = ready
            value, slope = gelu_parts(pre)
            act = value.astype(BF16)
            grad_pre = (grad_act * slope).astype(BF16)
            acts[rows, :] = act
            grad_pres[rows, :] = grad_pre
            ubg[0:1, :] += jnp.sum(grad_pre.astype(F32), axis=0, keepdims=True)
            acc[rows, :] += dot(act, down_ref[...])
            gs[rows, :] += dot_nt(grad_pre, up_ref[...])
            ready = ahead
        for n in range(self.count // self.chunk):
            weights(n)
        stores = []
        if self.packed:
            order = ((up_slots, (0, 2)), (up_slots, (1, 3)), (down_slots, (0, 1)), (down_slots, (2, 3)))
            for m, (source, slots) in enumerate(order):
                for n in range(2):
                    stores.append(
                        pltpu.make_async_copy(
                            source.at[slots[n]], outs[m].at[n], out_sem.at[2 * m + n]
                        )
                    )
        return stores


def feed_first(
    rows_all, att_first, att_last, cot_pieces, out_w, out_b, gain, shift, up, up_b, down, down_b, units
):
    pieces = len(att_first)
    total, width = rows_all.shape
    piece_rows = total // pieces
    count = len(cot_pieces)
    cot_rows = total // count
    split = att_first[0].shape[1]
    grads = units.grad_shapes(width)

    def body(*refs):
        x_ref, refs = refs[0], refs[1:]
        att_refs, refs = refs[: 2 * pieces], refs[2 * pieces :]
        cot_refs, refs = refs[:count], refs[count:]
        wo_refs, refs = refs[:pieces], refs[pieces:]
        ob_ref, gain_ref, shift_ref, up_hbm, ub_ref, down_hbm, db_ref = refs[:7]
        mid_ref, second, second_t, grad, grad_t, own_ref, low_ref, ubg, refs = *refs[7:15], refs[15:]
        send_refs, refs = refs[: pieces - 1], refs[pieces - 1 :]
        outs, refs = refs[: len(grads)], refs[len(grads) :]
        acc, gs, mid_rows, mid_sem, *scratch = refs
        _, part, _ = place(pieces)
        loads = units.loads(part, up_hbm, down_hbm, ub_ref, *scratch[5:])
        for load in loads:
            load.start()
        ubg[...] = jnp.zeros_like(ubg)
        masked = jnp.zeros((1, width), F32)
        for ref in cot_refs:
            masked = masked + ref[cot_rows : cot_rows + 1, :].astype(F32)
        factor = total / (4.0 * masked)
        for n in range(count):
            scaled = cot_refs[n][0:cot_rows, :].astype(F32) * factor
            dst = slice(n * cot_rows, (n + 1) * cot_rows)
            grad[dst, :] = scaled.astype(BF16)

        for h in range(pieces):

            @pl.loop(0, piece_rows // ROWS)
            def _(i, h=h):
                at = pl.multiple_of(i * ROWS, ROWS)
                dst = pl.ds(h * piece_rows + at, ROWS)
                mid = x_ref[dst, :].astype(F32) + ob_ref[...]
                for n in range(pieces):
                    src = pl.ds(((h - n) % pieces) * piece_rows + at, ROWS)
                    mid = mid + dot(att_refs[2 * n][src, :], wo_refs[n][0:split, :])
                    mid = mid + dot(att_refs[2 * n + 1][src, :], wo_refs[n][split:, :])
                mid_rows[dst, :] = mid
                normed, _ = norm_rows(mid)
                low = normed * gain_ref[...] + shift_ref[...]
                second[dst, :] = low.astype(BF16)
                second_t[:, dst] = low.T.astype(BF16)
                grad_t[:, dst] = grad[dst, :].astype(F32).T.astype(BF16)
                acc[dst, :] = mid + db_ref[...] if h == 0 else jnp.zeros((ROWS, width), F32)
                gs[dst, :] = jnp.zeros((ROWS, width), F32)

        keep_mid = pltpu.make_async_copy(mid_rows, mid_ref, mid_sem)
        keep_mid.start()
        for load in loads:
            load.wait()
        stores = units.compute(
            part, second, second_t, grad, grad_t, acc, gs, ubg, scratch, outs
        )
        for store in stores:
            store.start()
        keep_mid.wait()
        own_ref[...] = acc[0:piece_rows, :]
        low_ref[...] = gs[...].astype(BF16)
        for h in range(1, pieces):
            send_refs[h - 1][...] = acc[h * piece_rows : (h + 1) * piece_rows, :].astype(BF16)
        for store in stores:
            store.wait()

    att_all = [item for pair in zip(att_first, att_last) for item in pair]
    turned = sds((width, total), BF16)
    flat = sds((total, width), BF16)
    half = sds((piece_rows, width), F32)
    return run(
        body,
        [
            rows_all,
            *att_all,
            *cot_pieces,
            *out_w,
            out_b,
            gain,
            shift,
            far(up),
            up_b,
            far(down),
            down_b,
        ],
        in_specs=[VMEM] * (1 + 3 * pieces + count) + [VMEM, VMEM, VMEM, HBM, VMEM, HBM, VMEM],
        out_specs=[HBM] + [VMEM] * (6 + pieces) + [HBM if units.packed else VMEM] * len(grads),
        out_shape=[pltpu.HBM((total, width), F32), flat, turned, flat, turned, half, flat, sds((8, units.count), F32)]
        + [sds((piece_rows, width), BF16)] * (pieces - 1)
        + grads,
        scratch_shapes=[pltpu.VMEM((total, width), F32)] * 3
        + [pltpu.SemaphoreType.DMA]
        + units.scratch(total, width),
        vmem=31,
        cost_estimate=cost(12 * total * width * units.count, 24 * 1024 * 1024, total * units.count),
        name="feed_first",
    )


def feed_second(second, second_t, grad, grad_t, own_first, low_first, sends, up, up_b, down, units):
    pieces = 1 + len(sends)
    total, width = second.shape
    piece_rows = total // pieces
    grads = units.grad_shapes(width)

    def body(*refs):
        second, second_t, grad, grad_t, own_in, low_in, up_hbm, ub_ref, down_hbm, refs = (
            *refs[:9],
            refs[9:],
        )
        send_ins, refs = refs[: pieces - 1], refs[pieces - 1 :]
        own_ref, low_ref, ubg, refs = refs[0], refs[1], refs[2], refs[3:]
        send_refs, refs = refs[: pieces - 1], refs[pieces - 1 :]
        outs, (acc, gs), scratch = refs[: len(grads)], refs[len(grads) :][:2], refs[len(grads) + 2 :]
        _, part, _ = place(pieces)
        loads = units.loads(part, up_hbm, down_hbm, ub_ref, *scratch[5:])
        for load in loads:
            load.start()
        ubg[...] = jnp.zeros_like(ubg)
        acc[...] = jnp.zeros_like(acc)
        gs[...] = jnp.zeros_like(gs)
        for load in loads:
            load.wait()
        stores = units.compute(
            part, second, second_t, grad, grad_t, acc, gs, ubg, scratch, outs
        )
        for store in stores:
            store.start()
        low_ref[...] = (gs[...] + low_in[...].astype(F32)).astype(BF16)
        own_ref[...] = acc[0:piece_rows, :] + own_in[...]
        for h in range(1, pieces):
            item = acc[h * piece_rows : (h + 1) * piece_rows, :] + send_ins[h - 1][...].astype(F32)
            send_refs[h - 1][...] = item.astype(BF16)
        for store in stores:
            store.wait()

    return run(
        body,
        [
            second,
            second_t,
            grad,
            grad_t,
            own_first,
            low_first,
            far(up),
            up_b,
            far(down),
            *sends,
        ],
        in_specs=[VMEM] * 6 + [HBM, VMEM, HBM] + [VMEM] * (pieces - 1),
        out_specs=[VMEM] * (2 + pieces) + [HBM if units.packed else VMEM] * len(grads),
        out_shape=[
            sds((piece_rows, width), F32),
            sds((total, width), BF16),
            sds((8, units.count), F32),
        ]
        + [sds((piece_rows, width), BF16)] * (pieces - 1)
        + grads,
        scratch_shapes=[pltpu.VMEM((total, width), F32)] * 2 + units.scratch(total, width),
        vmem=24,
        cost_estimate=cost(12 * total * width * units.count, 24 * 1024 * 1024, total * units.count),
        name="feed_second",
    )


def mid_back(mid, grad_second, received, grad_rows, gain, out_w, att_first, att_last, chunk):
    pieces = 1 + len(received)
    total, width = mid.shape
    per_piece = total // pieces // ROWS
    split = att_first.shape[1]
    wide = split + att_last.shape[1]
    steps = total // ROWS

    def body(*refs):
        mid_ref, gs_ref, refs = refs[0], refs[1], refs[2:]
        recv_refs, refs = refs[: pieces - 1], refs[pieces - 1 :]
        go_ref, gain_ref, wo_ref, att_ref, last_ref = refs[:5]
        gm_ref, do_ref, sums_ref, *dwo_refs, acc = refs[5:]
        i = pl.program_id(0)

        @pl.when(i == 0)
        def _():
            sums_ref[...] = jnp.zeros_like(sums_ref)
            acc[...] = jnp.zeros_like(acc)

        normed, inv_std = norm_rows(mid_ref[...])
        grad = gs_ref[...].astype(F32)
        for ref in recv_refs:
            grad = grad + ref[...].astype(F32)
        go = go_ref[...].astype(F32)
        grad_mid = go + norm_back(grad * gain_ref[...], normed, inv_std)
        low = grad_mid.astype(BF16)
        do_ref[...] = dot_nt(low, wo_ref[...]).astype(BF16)
        acc[0:split, :] += dot(att_ref[...].astype(F32).T.astype(BF16), low)
        acc[split:, :] += dot(last_ref[...].astype(F32).T.astype(BF16), low)

        @pl.when(i < per_piece)
        def _():
            gm_ref[...] = grad_mid
            for n, item in enumerate((grad * normed, grad, low.astype(F32), go)):
                sums_ref[n : n + 1, :] += jnp.sum(item, axis=0, keepdims=True)

        @pl.when(i == steps - 1)
        def _():
            if chunk == 0:
                dwo_refs[0][...] = acc[...].astype(BF16)
                return
            _, part, _ = place(pieces)
            for c in range(pieces):

                @pl.when(part == c)
                def _(c=c):
                    for n in range(dwo_refs[0].shape[0]):
                        for e in range(pieces):
                            at = (n * pieces + (c + e) % pieces) * chunk
                            dwo_refs[e][n] = acc[at : at + chunk, :].astype(BF16)

    def rows_of(columns):
        return pl.BlockSpec((ROWS, columns), lambda i: (i, 0))

    def theirs(n):
        def index(i):
            piece = lax.rem(lax.div(i, per_piece) + pieces - n, pieces)
            return piece * per_piece + lax.rem(i, per_piece), 0

        return pl.BlockSpec((ROWS, width), index)

    def whole(*shape):
        return pl.BlockSpec(shape, lambda i: (0,) * len(shape))

    if chunk == 0:
        grads = [((wide, width), sds((wide, width), BF16))]
    else:
        shape = (width // (pieces * pieces * chunk), chunk, width)
        grads = [(shape, pltpu.HBM(shape, BF16))] * pieces
    return run(
        body,
        [far(mid), grad_second, *received, grad_rows, gain, out_w, far(att_first), far(att_last)],
        grid=(steps,),
        in_specs=[rows_of(width), rows_of(width)]
        + [theirs(n) for n in range(1, pieces)]
        + [rows_of(width), whole(1, width), whole(wide, width), rows_of(split), rows_of(wide - split)],
        out_specs=[
            pl.BlockSpec((ROWS, width), lambda i: (jnp.minimum(i, per_piece - 1), 0)),
            rows_of(wide),
            whole(8, width),
        ]
        + [whole(*shape) for shape, _ in grads],
        out_shape=[
            sds((per_piece * ROWS, width), F32),
            sds((total, wide), BF16),
            sds((8, width), F32),
        ]
        + [item for _, item in grads],
        scratch_shapes=[pltpu.VMEM((wide, width), F32)],
        vmem=16,
        cost_estimate=cost(4 * total * width * wide, 14 * 1024 * 1024),
        name="mid_back",
    )


def attend_backward(
    qkv, grad_att, att, att_tile, logs, lane_first, tile, heads, head_dim, after=(), part=1
):
    total = qkv.shape[0]
    per_tile = LANES // head_dim
    live = min(per_tile, heads - tile * per_tile)
    scale = head_dim ** (-0.5)
    exp_scale = scale * LOG2E

    def body(qkv_ref, do_ref, att_ref, lse_ref, out_ref, *scratch):
        km, vm, qm, dm, key_t, query_t, do_t, dq_t, lse_t, mean_t = scratch
        lane = lax.broadcasted_iota(jnp.int32, (1, LANES), 1)
        lse_t[...] = lse_ref[...].T
        query = qkv_ref[:, 0:LANES].astype(F32)
        key = qkv_ref[:, LANES : 2 * LANES].astype(F32)
        val = qkv_ref[:, 2 * LANES : 3 * LANES].astype(F32)
        upstream = do_ref[...].astype(F32)
        both_t = (upstream * att_ref[...].astype(F32)).T
        for j in range(live):
            mean_t[j : j + 1, :] = jnp.sum(
                both_t[j * head_dim : (j + 1) * head_dim, :], axis=0, keepdims=True
            )
        query_t[...] = query.T.astype(BF16)
        do_t[...] = upstream.T.astype(BF16)
        key_t[...] = key.T.astype(BF16)
        for j in range(live):
            mine = lane // head_dim == j
            km[j] = jnp.where(mine, key, 0.0).astype(BF16)
            vm[j] = jnp.where(mine, val, 0.0).astype(BF16)
            qm[j] = jnp.where(mine, query, 0.0).astype(BF16)
            dm[j] = jnp.where(mine, upstream, 0.0).astype(BF16)
        dq_t[...] = jnp.zeros_like(dq_t)

        @pl.loop(0, total // ROWS)
        def _(i):
            rows = pl.ds(pl.multiple_of(i * ROWS, ROWS), ROWS)
            grad_key = jnp.zeros((ROWS, LANES), F32)
            grad_val = jnp.zeros((ROWS, LANES), F32)

            def enter(j):
                return dot(km[j, rows, :], query_t[...]), dot(vm[j, rows, :], do_t[...])

            ready = enter(0)
            for j in range(live):
                ahead = enter(j + 1) if j + 1 < live else None
                scores, grad_prob = ready
                head = lane_first + j
                own = slice(j * head_dim, (j + 1) * head_dim)
                probs = jnp.exp2(scores * exp_scale - lse_t[head : head + 1, :])
                grad_scores = (probs * (grad_prob - mean_t[j : j + 1, :])).astype(BF16)
                grad_val = grad_val + dot(probs.astype(BF16), dm[j])
                grad_key = grad_key + dot(grad_scores, qm[j])
                dq_t[own, :] += dot(key_t[own, rows], grad_scores)
                ready = ahead
            out_ref[rows, LANES : 2 * LANES] = (grad_key * scale).astype(BF16)
            out_ref[rows, 2 * LANES : 3 * LANES] = grad_val.astype(BF16)

        out_ref[:, 0:LANES] = (dq_t[...].T * scale).astype(BF16)

    masked = pltpu.VMEM((live, total, LANES), BF16)
    turned = pltpu.VMEM((LANES, total), BF16)
    turned_f = pltpu.VMEM((LANES, total), F32)
    return run(
        body,
        [far(qkv), grad_att, att, logs],
        after,
        grid=(1,),
        in_specs=[
            pl.BlockSpec((total, 3 * LANES), lambda i: (0, tile)),
            pl.BlockSpec((total, LANES), lambda i: (0, tile)),
            pl.BlockSpec((total, LANES), lambda i: (0, att_tile)),
            pl.BlockSpec((total, LANES), lambda i: (0, 0)),
        ],
        out_specs=pl.BlockSpec((total, 3 * LANES), lambda i: (0, 0)),
        out_shape=sds((total, 3 * LANES), BF16),
        scratch_shapes=[masked] * 4
        + [turned] * 3
        + [turned_f] * 2
        + [pltpu.VMEM((8, total), F32)],
        vmem=17,
        cost_estimate=cost(
            2 * live * total * total * 256 * 5, 3 * 1024 * 1024, live * total * total, part
        ),
        name="attend_backward",
    )


def project_weights(rows_all, gain, shift, grad_tiles, pieces, quads, packed, after):
    total, width = rows_all.shape
    tiles = len(grad_tiles)
    tile_cols = grad_tiles[0].shape[1]
    cols_all = tiles * tile_cols
    chunk = width // (quads * pieces)

    def body(*refs):
        x_ref, gain_ref, shift_ref, refs = refs[0], refs[1], refs[2], refs[3:]
        dq_refs, (*dw_refs, low_t, part_ref) = refs[:tiles], refs[tiles:]
        _, part, quad = place(pieces)

        @pl.loop(0, total // ROWS)
        def _(i):
            rows = pl.ds(pl.multiple_of(i * ROWS, ROWS), ROWS)
            normed, _ = norm_rows(x_ref[rows, :].astype(F32))
            low_t[:, rows] = (normed * gain_ref[...] + shift_ref[...]).T.astype(BF16)

        for t in range(tiles):
            cols = slice(t * tile_cols, (t + 1) * tile_cols)
            part_ref[...] = dot(low_t[...], dq_refs[t][...]).astype(BF16)
            if not packed:
                dw_refs[0][:, cols] = part_ref[...]
                continue
            for c in range(pieces):

                @pl.when(part == c)
                def _(c=c, cols=cols):
                    for q in range(quads):
                        for e in range(pieces):
                            at = (q * pieces + (c + e) % pieces) * chunk
                            dw_refs[e][q ^ quad, :, cols] = part_ref[at : at + chunk, :]

    if packed:
        grads = [sds((quads, chunk, cols_all), BF16)] * pieces
    else:
        grads = [sds((width, cols_all), BF16)]
    return run(
        body,
        [rows_all, gain, shift, *grad_tiles],
        after,
        out_shape=grads,
        scratch_shapes=[pltpu.VMEM((width, total), BF16), pltpu.VMEM((width, tile_cols), BF16)],
        vmem=12,
        cost_estimate=cost(2 * total * width * cols_all, 6 * 1024 * 1024),
        name="project_weights",
    )


def project_rows(
    rows_all, weight, grad_tiles, sums_mid, up_sums, pieces, quads, packed, real, after
):
    total, width = rows_all.shape
    piece_rows = total // pieces
    cols_all = weight.shape[1]
    tiles = len(grad_tiles)
    tile_cols = cols_all // tiles

    def body(*refs):
        x_ref, w_ref, mid_ref, refs = *refs[:3], refs[3:]
        ups_refs, refs = refs[: len(up_sums)], refs[len(up_sums) :]
        dq_refs, refs = refs[:tiles], refs[tiles:]
        own_ref, refs = refs[0], refs[1:]
        send_refs, (sums_ref, bias_ref) = refs[: pieces - 1], refs[pieces - 1 :]
        _, part, _ = place(pieces)
        sums_ref[...] = jnp.zeros_like(sums_ref)
        bias_ref[...] = jnp.zeros_like(bias_ref)
        for h in range(pieces):

            @pl.loop(0, piece_rows // ROWS)
            def _(i, h=h):
                at = pl.multiple_of(i * ROWS, ROWS)
                src = pl.ds(at, ROWS)
                rows = pl.ds(h * piece_rows + at, ROWS)
                normed, _ = norm_rows(x_ref[rows, :].astype(F32))
                grad = jnp.zeros((ROWS, width), F32)
                for t in range(tiles):
                    grad_rows = dq_refs[t][rows, :]
                    cols = slice(t * tile_cols, (t + 1) * tile_cols)
                    grad = grad + dot_nt(grad_rows, w_ref[:, cols])
                    bias_ref[0:1, cols] += jnp.sum(grad_rows.astype(F32), axis=0, keepdims=True)
                if h == 0:
                    own_ref[src, :] = grad
                else:
                    send_refs[h - 1][src, :] = grad.astype(BF16)
                sums_ref[0:1, :] += jnp.sum(grad * normed, axis=0, keepdims=True)
                sums_ref[1:2, :] += jnp.sum(grad, axis=0, keepdims=True)

        if not packed:
            return
        for row, src in ((4, 2), (5, 0), (6, 1), (15, 3)):
            sums_ref[row : row + 1, :] = mid_ref[src : src + 1, :]
        for c in range(pieces):

            @pl.when(part == c)
            def _(c=c):
                for row, p in ((2, 0), (3, 2)):
                    mine = jnp.concatenate(
                        [
                            bias_ref[0:1, (3 * t + p) * LANES :][:, : min(LANES, real - t * LANES)]
                            for t in range(tiles)
                        ],
                        axis=1,
                    )
                    sums_ref[row : row + 1, c * real : (c + 1) * real] = mine
                for n in range(quads):
                    row = 7 + n * pieces + c
                    start = 0
                    for ref in ups_refs:
                        size = ref.shape[1] // quads
                        here = ref[0:1, n * size : (n + 1) * size]
                        sums_ref[row : row + 1, start : start + size] = here
                        start += size

    return run(
        body,
        [rows_all, weight, sums_mid, *up_sums, *grad_tiles],
        after,
        out_shape=[sds((piece_rows, width), F32)]
        + [sds((piece_rows, width), BF16)] * (pieces - 1)
        + [sds((16, width), F32), sds((8, cols_all), F32)],
        vmem=12,
        cost_estimate=cost(2 * total * width * cols_all, 8 * 1024 * 1024),
        name="project_rows",
    )


def finish_rows(rows_all, gain, grad_mid, grad_own, received, count, after):
    rows, width = grad_mid.shape
    others = len(received)
    piece = rows // count
    per_step = ROWS // piece

    def body(*refs):
        x_ref, gain_ref, gm_ref, own_ref, refs = refs[0], refs[1], refs[2], refs[3], refs[4:]
        recv_refs, out_refs = refs[:others], refs[others:]
        for n in range(rows // ROWS):
            at = slice(n * ROWS, (n + 1) * ROWS)
            normed, inv_std = norm_rows(x_ref[at, :].astype(F32))
            grad = own_ref[at, :]
            for ref in recv_refs:
                grad = grad + ref[at, :].astype(F32)
            done = gm_ref[at, :] + norm_back(grad * gain_ref[...], normed, inv_std)
            for e in range(per_step):
                out_refs[n * per_step + e][...] = done[e * piece : (e + 1) * piece, :].astype(BF16)

    return run(
        body,
        [rows_all, gain, grad_mid, grad_own, *received],
        after,
        out_shape=[sds((piece, width), BF16)] * count,
        vmem=12,
        cost_estimate=cost(20 * rows * width, 6 * 1024 * 1024),
        name="finish_rows",
    )


def finish_result(own, received, count):
    rows, width = own.shape
    others = len(received)
    piece = rows // count

    def body(*refs):
        out_refs = refs[1 + others :]
        for n in range(count):
            at = slice(n * piece, (n + 1) * piece)
            total = refs[0][at, :]
            for ref in refs[1 : 1 + others]:
                total = total + ref[at, :].astype(F32)
            out_refs[n % 2][n // 2] = total.astype(BF16)

    return run(
        body,
        [own, *received],
        out_shape=[sds((count // 2, piece, width), BF16)] * 2,
        vmem=8,
        cost_estimate=cost(2 * rows * width, 3 * 1024 * 1024),
        name="finish_result",
    )


def pass_on(keep, received, after):
    def body(keep_ref, recv_ref, out_ref):
        out_ref[0] = keep_ref[1]
        out_ref[1] = recv_ref[1]

    return run(
        body,
        [keep, received],
        after,
        out_shape=sds(keep.shape, keep.dtype),
        vmem=6,
        cost_estimate=cost(0, 4 * keep.size),
        name="pass_on",
    )


def collect_halves(keep, near, far, group, after):
    _, rows, width = keep.shape

    def body(keep_ref, near_ref, far_ref, out_ref):
        _, _, quad = place(group)
        out_ref[quad] = keep_ref[0]
        out_ref[quad ^ 1] = near_ref[0]
        out_ref[quad ^ 2] = far_ref[0]
        out_ref[quad ^ 3] = far_ref[1]

    return run(
        body,
        [keep, near, far],
        after,
        out_shape=sds((4, rows, width), keep.dtype),
        vmem=6,
        cost_estimate=cost(0, 16 * rows * width),
        name="collect_halves",
    )


def two_parts(item):
    first = item.astype(BF16)
    return first, (item - first.astype(F32)).astype(BF16)


def pack_attention(
    qkv_keep, qkv_recv, out_keep, out_recv, small, small_recv, real, blocks, after
):
    quads, chunk, cols_all = qkv_keep.shape
    wide = cols_all // 3
    tiles = wide // LANES
    width = out_keep.shape[2]
    qkv_lanes = 6 * real // blocks
    out_lanes = width // blocks
    lanes = qkv_lanes + out_lanes
    halves = quads // 2
    slot = halves * chunk
    small_rows = small.shape[0]

    def body(qk_ref, qr_ref, ok_ref, or_ref, small_ref, srecv_ref, *out_refs):
        _, part, quad = place(2)
        mine = lax.axis_index("batch")
        slots = out_refs[4]

        def heads_of(rows, p):
            return [
                rows[:, (3 * t + p) * LANES : (3 * t + p) * LANES + min(LANES, real - t * LANES)]
                for t in range(tiles)
            ]

        for c in range(2):

            @pl.when(part == c)
            def _(c=c):
                for q in range(quads):
                    pair = (qk_ref[q], qr_ref[q])
                    if c == 1:
                        pair = pair[::-1]
                    parts = []
                    for p in range(3):
                        parts += heads_of(pair[0], p) + heads_of(pair[1], p)
                    row = jnp.concatenate(parts, axis=1)
                    for b in range(blocks):
                        slots[b ^ mine, q, :, 0:qkv_lanes] = row[
                            :, b * qkv_lanes : (b + 1) * qkv_lanes
                        ]
                for e, ref in enumerate((ok_ref, or_ref)):
                    for n in range(halves):
                        q = ((c + e) % 2) * halves + n
                        for b in range(blocks):
                            slots[b ^ mine, q ^ quad, :, qkv_lanes:lanes] = ref[
                                n, :, b * out_lanes : (b + 1) * out_lanes
                            ]

        for n, order in enumerate(((0, 2), (1, 3), (0, 1), (2, 3))):
            for e in range(2):
                for f in range(halves):
                    at = e * slot + f * chunk
                    src = f if n < 2 else halves + f
                    out_refs[n][at : at + chunk, :] = slots[order[e], src]
        parts = two_parts(small_ref[...] + srecv_ref[...])
        for n in range(2):
            for e in range(2):
                at = 2 * slot + e * small_rows
                out_refs[n][at : at + small_rows, :] = parts[e]

    first = sds((2 * slot + 2 * small_rows, lanes), BF16)
    other = sds((2 * slot, lanes), BF16)
    return run(
        body,
        [qkv_keep, qkv_recv, out_keep, out_recv, small, small_recv],
        after,
        out_shape=[first, first, other, other],
        scratch_shapes=[pltpu.VMEM((blocks, quads, chunk, lanes), BF16)],
        vmem=12,
        cost_estimate=cost(0, 4 * 1024 * 1024),
        name="pack_attention",
    )


def sum_first(keeps, received, after=()):
    count = len(keeps)
    shape = keeps[0].shape[1:]

    def body(*refs):
        for n in range(count):
            for e in range(2):
                total = refs[n][e].astype(F32) + refs[count + n][e].astype(F32)
                refs[2 * count + 2 * n + e][...] = total.astype(BF16)

    return run(
        body,
        [*keeps, *received],
        after,
        out_shape=[pltpu.HBM(shape, BF16), sds(shape, BF16)] * count,
        vmem=12,
        cost_estimate=cost(0, 6 * count * keeps[0].size),
        name="sum_first",
    )


def sum_second(keeps, received, after=()):
    quads, rows, width = keeps[0].shape

    def body(ka, kb, ra, rb, keep_ref, send_ref):
        for d in range(quads):
            ref = send_ref if d % 2 else keep_ref
            for e, (keep, recv) in enumerate(((ka, ra), (kb, rb))):
                total = keep[d].astype(F32) + recv[d].astype(F32)
                ref[d // 2, e] = total.astype(BF16)

    return run(
        body,
        [*keeps, *received],
        after,
        out_shape=[sds((quads // 2, 2, rows, width), BF16)] * 2,
        vmem=10,
        cost_estimate=cost(0, 12 * keeps[0].size),
        name="sum_second",
    )


def sum_third(keep, received, after=()):
    def body(keep_ref, recv_ref, stay_ref, pass_ref):
        for ref, e in ((stay_ref, 0), (pass_ref, 1)):
            ref[...] = (keep_ref[e].astype(F32) + recv_ref[e].astype(F32)).astype(BF16)

    return run(
        body,
        [keep, received],
        after,
        out_shape=[sds(keep.shape[1:], BF16)] * 2,
        vmem=6,
        cost_estimate=cost(0, 6 * keep.size),
        name="sum_third",
    )


def small_sum(refs, rows, count):
    total = None
    for ref in refs:
        for e in range(2):
            item = ref[rows + e * count : rows + (e + 1) * count, :].astype(F32)
            total = item if total is None else total + item
    return total


def sum_first_attention(keeps, received, slot, small_rows, after):
    lanes = keeps[0].shape[1]

    def body(ka, kb, ra, rb, stay_a, pass_a, stay_b, pass_b):
        parts = two_parts(small_sum((ka, ra), 2 * slot, small_rows))
        for keep, recv, stay, on in ((ka, ra, stay_a, pass_a), (kb, rb, stay_b, pass_b)):
            for e, ref in enumerate((stay, on)):
                at = slice(e * slot, (e + 1) * slot)
                ref[0:slot, :] = (keep[at, :].astype(F32) + recv[at, :].astype(F32)).astype(BF16)
        for ref in (stay_a, pass_a):
            for e in range(2):
                ref[slot + e * small_rows : slot + (e + 1) * small_rows, :] = parts[e]

    first = sds((slot + 2 * small_rows, lanes), BF16)
    other = sds((slot, lanes), BF16)
    return run(
        body,
        [*keeps, *received],
        after,
        out_shape=[first, first, other, other],
        vmem=8,
        cost_estimate=cost(0, 3 * 1024 * 1024),
        name="sum_first_attention",
    )


def sum_second_attention(keeps, received, chunk, quads, small_rows, after):
    lanes = keeps[0].shape[1]
    halves = quads // 2
    slot = halves * chunk

    def body(ka, kb, ra, rb, *out_refs):
        parts = two_parts(small_sum((ka, ra), slot, small_rows))
        for d in range(quads):
            keep, recv = ((ka, ra), (kb, rb))[d // halves]
            at = slice(d % halves * chunk, (d % halves + 1) * chunk)
            total = keep[at, :].astype(F32) + recv[at, :].astype(F32)
            out_refs[d][0:chunk, :] = total.astype(BF16)
            for e in range(2):
                at = chunk + e * small_rows
                out_refs[d][at : at + small_rows, :] = parts[e]

    return run(
        body,
        [*keeps, *received],
        after,
        out_shape=[sds((chunk + 2 * small_rows, lanes), BF16)] * quads,
        vmem=8,
        cost_estimate=cost(0, 2 * 1024 * 1024),
        name="sum_second_attention",
    )


def final_attention(pieces, chunk, qkv_lanes, small_rows):
    lanes = pieces[0].shape[1]
    count = len(pieces)

    def body(*refs):
        total = refs[0][0:chunk, :].astype(F32)
        for ref in refs[1:count]:
            total = total + ref[0:chunk, :].astype(F32)
        refs[count][...] = total[:, :qkv_lanes]
        refs[count + 1][...] = total[:, qkv_lanes:]
        refs[count + 2][...] = small_sum(refs[:count], chunk, small_rows)

    return run(
        body,
        pieces,
        out_shape=[
            sds((chunk, qkv_lanes), F32),
            sds((chunk, lanes - qkv_lanes), F32),
            sds((small_rows, lanes), F32),
        ],
        vmem=6,
        cost_estimate=cost(0, 1024 * 1024),
        name="final_attention",
    )


def final_units(first, second, after):
    high = first[0].shape[1]
    sizes = [first[0].shape[2], second[0].shape[2]]
    unit_block = sum(sizes)
    count = len(first)
    half = high // 2

    def body(*refs):
        _, part, _ = place(2)
        keep_ref, send_ref, down_ref = refs[2 * count :]
        for h in range(2):
            pieces = refs[h * count : (h + 1) * count]
            up, down = pieces[0][0].astype(F32), pieces[0][1].astype(F32)
            for ref in pieces[1:]:
                up = up + ref[0].astype(F32)
                down = down + ref[1].astype(F32)
            here = slice(h * sizes[0], h * sizes[0] + sizes[h])
            down_ref[here, :] = down.T
            for c in range(2):

                @pl.when(part == c)
                def _(up=up, here=here, c=c):
                    keep_ref[:, here] = up[c * half : (c + 1) * half, :]
                    send_ref[:, here] = up[(1 - c) * half : (2 - c) * half, :].astype(BF16)

    return run(
        body,
        [*first, *second],
        after,
        out_shape=[
            sds((half, unit_block), F32),
            sds((half, unit_block), BF16),
            sds((unit_block, high), F32),
        ],
        vmem=10,
        cost_estimate=cost(0, 4 * 1024 * 1024),
        name="final_units",
    )


def final_join(keep, recv):
    chunk, unit_block = keep.shape

    def body(keep_ref, recv_ref, out_ref):
        _, part, _ = place(2)
        for c in range(2):

            @pl.when(part == c)
            def _(c=c):
                out_ref[:, c * unit_block : (c + 1) * unit_block] = keep_ref[...]
                out_ref[:, (1 - c) * unit_block : (2 - c) * unit_block] = recv_ref[...].astype(F32)

    return run(
        body,
        [keep, recv],
        out_shape=sds((chunk, 2 * unit_block), F32),
        vmem=5,
        cost_estimate=cost(0, 1024 * 1024),
        name="final_join",
    )


def on_device(
    tokens,
    mask,
    cotangent,
    ln1_gain,
    ln1_bias,
    qkv_weight,
    q_bias,
    v_bias,
    out_weight,
    out_bias,
    ln2_gain,
    ln2_bias,
    up_weight,
    up_bias,
    down_weight,
    down_bias,
):
    seq_size = lax.axis_size("seq")
    batch_size = lax.axis_size("batch")
    micro_count, seq_count, local_len, width = tokens.shape
    sequences = micro_count * seq_count
    group = seq_size // sequences
    units = up_weight.shape[1]
    head_dim = width // HEADS
    heads = HEADS // group
    real = heads * head_dim
    wide = -(-real // LANES) * LANES
    full_len = local_len * seq_size
    block_len = local_len // group
    rows = seq_size * block_len
    own_units = units // group
    part = lax.axis_index("seq") % group
    aligned = (
        seq_size == batch_size * group
        and group == 2
        and batch_size == 4
        and wide == 3 * LANES
        and (seq_size // group) % group == 0
        and units % (batch_size * group * LANES) == 0
        and own_units // batch_size == width
    )

    def from_part(item, ahead):
        if ahead % group == 0:
            return item
        pairs = [
            (q * group + (c + ahead) % group, q * group + c)
            for q in range(sequences)
            for c in range(group)
        ]
        return lax.ppermute(item, "seq", pairs)

    def gather_parts(item):
        return [from_part(item, n) for n in range(group)]

    def row_of(item):
        return item.astype(F32)[None, :]

    def blocks_of(item):
        return item.reshape(sequences, local_len, width)

    x_own = over_quads(deal(blocks_of(tokens), group), group)
    x_pieces = [from_part(item, n) for n in range(group) for item in x_own]

    count_rows = jnp.sum(mask, axis=2).reshape(sequences).astype(BF16)
    cot_low = jnp.where(mask[..., None] != 0, cotangent, jnp.zeros_like(cotangent))
    cot_send = jnp.concatenate(
        [blocks_of(cot_low), jnp.broadcast_to(count_rows[:, None, None], (sequences, 16, width))],
        axis=1,
    )
    cot_own = over_quads(deal(cot_send, group, x_pieces[sequences:]), group)

    qkv_w, qkv_b, *out_w = pick_weights(
        qkv_weight,
        jnp.concatenate([q_bias, jnp.zeros_like(q_bias), v_bias])[None, :],
        out_weight,
        group,
        real,
        wide,
    )
    if aligned:
        up_own, up_b, down_own = up_weight, up_bias[None, :], down_weight
    else:

        def own_columns(matrix, blocks):
            split = matrix.reshape(matrix.shape[0], blocks, group, -1)
            return lax.dynamic_index_in_dim(split, part, 2, keepdims=False)

        up_own = own_columns(up_weight, batch_size).reshape(width, own_units)
        up_b = own_columns(up_bias[None, :], batch_size).reshape(1, own_units)
        down_own = lax.dynamic_index_in_dim(
            down_weight.reshape(batch_size, group, -1, width), part, 1, keepdims=False
        ).reshape(own_units, width)

    tiles = wide // LANES
    x_all, qkv, att_first, logs_first = attend_first(
        x_pieces, row_of(ln1_gain), row_of(ln1_bias), qkv_w, qkv_b, tiles - 1, heads, head_dim
    )
    cot_stack = stack(cot_own, [logs_first])
    att_last, logs_last = attend_last(qkv, tiles - 1, heads, head_dim, [cot_stack])
    cot_pieces = cot_own + [
        item[d]
        for item in gather_parts(cot_stack)[1:]
        for d in range(sequences)
    ]
    blocks = batch_size if aligned else 1
    unit_block = own_units // blocks
    size = unit_block * 3 // 5
    shape = (group, sequences if aligned else None, width // sequences)
    calls = [
        Units(unit_block, blocks, 0, size, *shape),
        Units(unit_block, blocks, size, unit_block - size, *shape),
    ]
    mid, second, second_t, grad_rows, grad_t, result_own, grad_second, *found = feed_first(
        x_all,
        gather_parts(att_first),
        gather_parts(att_last),
        cot_pieces,
        out_w,
        row_of(out_bias),
        row_of(ln2_gain),
        row_of(ln2_bias),
        up_own,
        up_b,
        down_own,
        row_of(down_bias),
        calls[0],
    )
    up_sums, ff_grads = [found[0]], [found[group:]]
    result_own, grad_second, *found = feed_second(
        second,
        second_t,
        grad_rows,
        grad_t,
        result_own,
        grad_second,
        found[1:group],
        up_own,
        up_b,
        down_own,
        calls[1],
    )
    up_sums.append(found[0])
    result_send = found[1:group]
    ff_grads.append(found[group:])

    def begin_sum(e, sends, after):
        moved = [swap(sends[0], "batch", batch_size, 1), swap(sends[1], "batch", batch_size, 2)]
        stay_a, pass_a, stay_b, pass_b = sum_first(
            [ff_grads[e][0], ff_grads[e][2]], moved, after
        )
        moved = [swap(pass_a, "batch", batch_size, 2), swap(pass_b, "batch", batch_size, 1)]
        return [stay_a, stay_b], moved

    if aligned:
        waiting = begin_sum(0, [ff_grads[0][1], ff_grads[0][3]], [])
        (grad_second,) = gate([grad_second], waiting[0][:1])
    second_send = grad_second
    second_recv = [from_part(second_send, n) for n in range(1, group)]
    result_recv = [from_part(result_send[group - n - 1], n) for n in range(1, group)]
    result_keep, result_pass = finish_result(result_own, result_recv, sequences)

    def quad_swap(item, distance):
        return swap(item, "seq", seq_size, distance * group)

    result_near = quad_swap(result_pass, 1)

    chunk = width // seq_size
    grad_mid, grad_att, sums_mid, *out_grad = mid_back(
        mid,
        grad_second,
        second_recv,
        grad_rows,
        row_of(ln2_gain),
        out_w[0],
        att_first,
        att_last,
        chunk if aligned else 0,
    )

    def tile_back(t, after, cost_part=1):
        last = t == tiles - 1
        return attend_backward(
            qkv,
            grad_att,
            att_last if last else att_first,
            0 if last else t,
            logs_last if last else logs_first,
            0 if last else t * (LANES // head_dim),
            t,
            heads,
            head_dim,
            after,
            cost_part,
        )

    grad_tiles = [None] * tiles
    after = [result_keep]
    if aligned:
        keep, send = sum_second(*waiting, [grad_mid, result_keep])
        moved = quad_swap(send, 1)
        sends = gate([ff_grads[1][1], ff_grads[1][3]], [keep])
        after = [keep]
    grad_tiles[0] = tile_back(0, after, 64)
    result_pass = pass_on(result_keep, result_near, grad_tiles[:1])
    result_far = quad_swap(result_pass, 2)
    after = [result_pass]
    if aligned:
        unit_first = list(sum_third(keep, moved, [grad_tiles[0]]))
        unit_first[1] = quad_swap(unit_first[1], 2)
        waiting = begin_sum(1, sends, [grad_tiles[0]])
        after = [result_pass, unit_first[0], waiting[0][0]]
    for t in range(1, tiles - 1):
        grad_tiles[t] = tile_back(t, after)
    after = [grad_tiles[-2], result_far]
    if aligned:
        out_recv = from_part(out_grad[1], 1)
        keep, send = sum_second(*waiting, [grad_tiles[-2]])
        moved = quad_swap(send, 1)
        after = [keep, result_far, unit_first[1]]
    grad_tiles[-1] = tile_back(tiles - 1, after)
    after = []
    if aligned:
        after = [out_recv]
    qkv_grad = project_weights(
        x_all, row_of(ln1_gain), row_of(ln1_bias), grad_tiles, group, sequences, aligned, after
    )
    after = qkv_grad[:1]
    if aligned:
        unit_second = list(sum_third(keep, moved, qkv_grad[:1]))
        unit_second[1] = quad_swap(unit_second[1], 2)
        after = unit_second[:1]
    first_own, *found = project_rows(
        x_all,
        qkv_w,
        grad_tiles,
        sums_mid,
        up_sums,
        group,
        sequences,
        aligned,
        real,
        after,
    )
    first_send, (small, bias_sums) = found[: group - 1], found[group - 1 :]
    first_recv = [from_part(first_send[group - n - 1], n) for n in range(1, group)]
    after = []
    if aligned:
        small_rows = small.shape[0]
        packed = pack_attention(
            qkv_grad[0],
            from_part(qkv_grad[1], 1),
            out_grad[0],
            out_recv,
            small,
            from_part(small, 1),
            real,
            batch_size,
            [],
        )
        after = packed[:1]
    row_parts = finish_rows(
        x_all, row_of(ln1_gain), grad_mid, first_own, first_recv, sequences, after
    )
    row_moved = over_quads(row_parts, group)
    if aligned:
        stay_a, pass_a, stay_b, pass_b = sum_first_attention(
            [packed[0], packed[2]],
            [swap(packed[1], "batch", batch_size, 1), swap(packed[3], "batch", batch_size, 2)],
            sequences // 2 * chunk,
            small_rows,
            [*row_parts[:1], *row_moved[1::2], unit_second[1]],
        )
        summed = sum_second_attention(
            [stay_a, stay_b],
            [swap(pass_a, "batch", batch_size, 2), swap(pass_b, "batch", batch_size, 1)],
            chunk,
            sequences,
            small_rows,
            row_moved[2:3],
        )
        after = summed[:1]
        up_keep, up_send, down_grad = final_units(unit_first, unit_second, after)
        up_grad = final_join(up_keep, from_part(up_send, 1))
        qkv_final, out_final, small = final_attention(
            over_quads(summed, group), chunk, qkv_weight.shape[1] // batch_size, small_rows
        )
        small = small.reshape(-1)
    result = collect_halves(result_keep, result_near, result_far, group, after)
    result = result.reshape(tokens.shape)
    grad_in = collect(row_moved, group, after).reshape(tokens.shape)
    if not aligned:

        def spread(item, blocks):
            split = item.reshape(blocks, 1, -1)
            empty = jnp.zeros((blocks, group, split.shape[2]), F32)
            return lax.dynamic_update_slice(empty, split, (0, part, 0)).reshape(-1)

        bias_sums = bias_sums[0].reshape(tiles, 3, LANES).transpose(1, 0, 2)
        bias_sums = bias_sums.reshape(3, wide)[:, :real]
        small = jnp.concatenate(
            [
                small[0],
                small[1],
                spread(bias_sums[0], 1),
                spread(bias_sums[2], 1),
                sums_mid[2],
                sums_mid[0],
                sums_mid[1],
                spread(jnp.concatenate([item[0] for item in up_sums]), batch_size),
                sums_mid[3],
            ]
        )

        def scattered(item):
            item = lax.psum_scatter(item.astype(BF16), "seq", scatter_dimension=0, tiled=True)
            return lax.psum_scatter(item, "batch", scatter_dimension=1, tiled=True).astype(F32)

        def spread_columns(item, blocks):
            split = item.reshape(item.shape[0], blocks, 1, -1)
            empty = jnp.zeros((item.shape[0], blocks, group, split.shape[3]), item.dtype)
            filled = lax.dynamic_update_slice(empty, split, (0, 0, part, 0))
            return filled.reshape(item.shape[0], -1)

        up_full, down_full = [
            jnp.concatenate([item[e] for item in ff_grads], axis=1) for e in range(2)
        ]
        up_grad = scattered(spread_columns(up_full, batch_size))
        down_grad = scattered(spread_columns(down_full, batch_size).T)
        rows_full = qkv_grad[0].reshape(width, tiles, 3, LANES).transpose(0, 2, 1, 3)
        rows_full = rows_full.reshape(width, 3, wide)[..., :real]
        qkv_final = scattered(spread_columns(rows_full.reshape(width, -1), 3))
        out_final = scattered(spread_columns(out_grad[0][:real].T, 1).T)
        small = lax.psum(small, ("seq", "batch"))

    edges = [width] * 7 + [units, width]
    pieces, start = [], 0
    for size in edges:
        pieces.append(small[start : start + size])
        start += size
    return (
        result,
        grad_in,
        pieces[0],
        pieces[1],
        qkv_final,
        pieces[2],
        pieces[3],
        out_final,
        pieces[4],
        pieces[5],
        pieces[6],
        up_grad,
        pieces[7],
        down_grad,
        pieces[8],
    )


def solution(mesh):
    rows = P(None, "batch", "seq", None)
    split = P("seq", "batch")
    in_specs = (rows, P(None, "batch", "seq"), rows) + (P(),) * 13
    out_specs = (
        rows,
        rows,
        P(),
        P(),
        split,
        P(),
        P(),
        split,
        P(),
        P(),
        P(),
        split,
        P(),
        split,
        P(),
    )
    return jax.shard_map(
        on_device, mesh=mesh, in_specs=in_specs, out_specs=out_specs, check_vma=False
    )
```

```python
import jax
import jax.numpy as jnp
from jax import lax
from jax.experimental import pallas as pl
from jax.experimental.pallas import tpu as pltpu
from jax.sharding import PartitionSpec as P

HEADS = 20
EPS = 1e-05
LOG2E = 1.4426950408889634
ROWS = 256
F32 = jnp.float32
BF16 = jnp.bfloat16
LANES = 128


def dot(left, right):
    return jnp.dot(left, right, preferred_element_type=F32)


def dot_nt(left, right):
    return lax.dot_general(left, right, (((1,), (1,)), ((), ())), preferred_element_type=F32)


def norm_rows(rows_in):
    mean_val = jnp.mean(rows_in, axis=-1, keepdims=True)
    centered = rows_in - mean_val
    inv_std = lax.rsqrt(jnp.mean(centered * centered, axis=-1, keepdims=True) + EPS)
    return centered * inv_std, inv_std


def norm_back(scaled, normed, inv_std):
    inner = (
        scaled
        - jnp.mean(scaled, axis=-1, keepdims=True)
        - normed * jnp.mean(scaled * normed, axis=-1, keepdims=True)
    )
    return inner * inv_std


def params_of(mib):
    return pltpu.CompilerParams(vmem_limit_bytes=mib * 1024 * 1024)


def cost(flops, moved, trans=0, part=1):
    return pl.CostEstimate(
        flops=flops // part, bytes_accessed=moved // part, transcendentals=trans // part
    )


def sds(shape, dtype):
    return jax.ShapeDtypeStruct(shape, dtype)


VMEM = pl.BlockSpec(memory_space=pltpu.VMEM)
ANY = pl.BlockSpec(memory_space=pl.ANY)
HBM = pl.BlockSpec(memory_space=pltpu.HBM)


def run(body, operands, after=(), in_specs=None, out_specs=None, vmem=32, **more):
    count, extra = len(operands), len(after)

    def inner(*refs):
        body(*refs[:count], *refs[count + extra :])

    specs = [VMEM] * count if in_specs is None else list(in_specs)
    shapes = more["out_shape"]
    if out_specs is None:
        out_specs = [VMEM] * len(shapes) if isinstance(shapes, (list, tuple)) else VMEM
    return pl.pallas_call(
        inner,
        in_specs=specs + [ANY] * extra,
        out_specs=out_specs,
        compiler_params=params_of(vmem),
        **more,
    )(*operands, *after)


def far(item):
    return pltpu.with_memory_space_constraint(item, pltpu.HBM)


def gate(items, after):
    def body(*refs):
        del refs

    return pl.pallas_call(
        body,
        in_specs=[ANY] * (len(items) + len(after)),
        out_specs=[ANY] * len(items),
        out_shape=[sds(item.shape, item.dtype) for item in items],
        input_output_aliases={n: n for n in range(len(items))},
        cost_estimate=cost(0, 0),
        name="gate",
    )(*items, *after)


def place(group):
    spot = lax.axis_index("seq")
    return spot, lax.rem(spot, group), lax.div(spot, group)


def deal(item, group, after=()):
    count, rows, width = item.shape

    def body(in_ref, *out_refs):
        _, _, quad = place(group)
        for d in range(count):
            out_refs[d][...] = in_ref[quad ^ d]

    return run(
        body,
        [item],
        after,
        out_shape=[sds((rows, width), item.dtype)] * count,
        vmem=6,
        cost_estimate=cost(0, 4 * count * rows * width),
        name="deal",
    )


def collect(pieces, group, after):
    count = len(pieces)
    rows, width = pieces[0].shape

    def body(*refs):
        _, _, quad = place(group)
        for d in range(count):
            refs[count][quad ^ d] = refs[d][...]

    return run(
        body,
        pieces,
        after,
        out_shape=sds((count, rows, width), pieces[0].dtype),
        vmem=6,
        cost_estimate=cost(0, 4 * count * rows * width),
        name="collect",
    )


def stack(pieces, after):
    count = len(pieces)

    def body(*refs):
        for d in range(count):
            refs[count][d] = refs[d][...]

    return run(
        body,
        pieces,
        after,
        out_shape=sds((count,) + pieces[0].shape, pieces[0].dtype),
        vmem=12,
        cost_estimate=cost(0, 4 * count * pieces[0].size),
        name="stack",
    )


def swap(item, axis, size, distance):
    return lax.ppermute(item, axis, [(i, i ^ distance) for i in range(size)])


def over_quads(pieces, group):
    return [
        piece if d == 0 else swap(piece, "seq", len(pieces) * group, d * group)
        for d, piece in enumerate(pieces)
    ]


def pick_weights(qkv_weight, qkv_bias, out_weight, group, real, wide):
    width = qkv_weight.shape[0]
    tiles = wide // LANES

    def body(w_ref, b_ref, o_ref, wo_ref, bo_ref, *out_refs):
        _, part, _ = place(group)
        wo_ref[...] = jnp.zeros_like(wo_ref)
        bo_ref[...] = jnp.zeros_like(bo_ref)
        for ref in out_refs:
            ref[...] = jnp.zeros_like(ref)
        for c in range(group):

            @pl.when(part == c)
            def _(c=c):
                for p in range(3):
                    for t in range(tiles):
                        some = min(LANES, real - t * LANES)
                        src = p * width + c * real + t * LANES
                        dst = (3 * t + p) * LANES
                        wo_ref[:, dst : dst + some] = w_ref[:, src : src + some]
                        bo_ref[:, dst : dst + some] = b_ref[:, src : src + some]
                for n in range(group):
                    src = (c + n) % group * real
                    out_refs[n][0:real, :] = o_ref[src : src + real, :]

    return pl.pallas_call(
        body,
        out_shape=[sds((width, 3 * wide), BF16), sds((1, 3 * wide), F32)]
        + [sds((wide, width), BF16)] * group,
        compiler_params=params_of(24),
        cost_estimate=cost(0, 8 * 1024 * 1024),
        name="pick_weights",
    )(qkv_weight, qkv_bias, out_weight)


def by_pairs(live, visit):
    size = 2 if live % 2 == 0 else 1

    @pl.loop(0, live // size)
    def _(i):
        visit([i * size + e for e in range(size)])


def attend_tiles(query_at, keys_at, vals_at, att_ref, lse_ref, keys, vals, acc, tiles, heads, head_dim):
    per_tile = LANES // head_dim
    total = att_ref.shape[0]
    exp_scale = head_dim ** (-0.5) * LOG2E
    lane = lax.broadcasted_iota(jnp.int32, (1, LANES), 1)
    row = lax.broadcasted_iota(jnp.int32, (LANES, 1), 0)
    lse_ref[...] = jnp.zeros_like(lse_ref)
    vals[:, :, LANES:] = jnp.ones((per_tile, total, LANES), BF16)
    for n, t in enumerate(tiles):
        live = min(per_tile, heads - t * per_tile)
        key_t = keys_at(n).astype(F32).T
        val_f = vals_at(n).astype(F32)
        for j in range(live):
            keys[j] = jnp.where(row // head_dim == j, key_t, 0.0).astype(BF16)
            vals[j, :, :LANES] = jnp.where(lane // head_dim == j, val_f, 0.0).astype(BF16)
        acc[...] = jnp.zeros_like(acc)

        def visit(some, n=n):
            scores = [dot(query_at(n), keys[j]) for j in some]
            for item, j in zip(scores, some):
                row_max = jnp.max(item, axis=-1, keepdims=True) * exp_scale
                expd = jnp.exp2(item * exp_scale - row_max).astype(BF16)
                mixed = dot(expd, vals[j])
                den = mixed[:, LANES:]
                acc[...] += mixed[:, :LANES] / den
                lse_ref[...] = jnp.where(
                    lane == n * per_tile + j, row_max + jnp.log2(den), lse_ref[...]
                )

        by_pairs(live, visit)
        att_ref[:, n * LANES : (n + 1) * LANES] = acc[...].astype(BF16)


def attend_scratch(total, head_dim):
    per_tile = LANES // head_dim
    return [
        pltpu.VMEM((per_tile, LANES, total), BF16),
        pltpu.VMEM((per_tile, total, 2 * LANES), BF16),
        pltpu.VMEM((total, LANES), F32),
    ]


def attend_first(x_pieces, gain, shift, weight, bias, tiles, heads, head_dim):
    count = len(x_pieces)
    piece_rows, width = x_pieces[0].shape
    total = count * piece_rows
    cols_all = weight.shape[1]

    def body(*refs):
        x_refs = refs[:count]
        gain_ref, shift_ref, w_ref, bias_ref = refs[count : count + 4]
        x_ref, qkv_ref, att_ref, lse_ref, keys, vals, acc = refs[count + 4 :]
        for n in range(count):
            x_ref[n * piece_rows : (n + 1) * piece_rows, :] = x_refs[n][...]

        @pl.loop(0, total // ROWS)
        def _(i):
            rows = pl.ds(pl.multiple_of(i * ROWS, ROWS), ROWS)
            normed, _ = norm_rows(x_ref[rows, :].astype(F32))
            low = (normed * gain_ref[...] + shift_ref[...]).astype(BF16)
            qkv_ref[rows, :] = (dot(low, w_ref[...]) + bias_ref[...]).astype(BF16)

        def columns(at):
            return slice(at * LANES, (at + 1) * LANES)

        attend_tiles(
            lambda n: qkv_ref[:, columns(3 * n)],
            lambda n: qkv_ref[:, columns(3 * n + 1)],
            lambda n: qkv_ref[:, columns(3 * n + 2)],
            att_ref,
            lse_ref,
            keys,
            vals,
            acc,
            range(tiles),
            heads,
            head_dim,
        )

    return run(
        body,
        [*x_pieces, gain, shift, weight, bias],
        out_shape=[
            sds((total, width), BF16),
            sds((total, cols_all), BF16),
            sds((total, tiles * LANES), BF16),
            sds((total, LANES), F32),
        ],
        scratch_shapes=attend_scratch(total, head_dim),
        vmem=23,
        cost_estimate=cost(
            2 * total * width * cols_all + 4 * heads * total * total * 256,
            8 * 1024 * 1024,
            heads * total * total,
        ),
        name="attend_first",
    )


def attend_last(qkv, tile, heads, head_dim, after):
    total = qkv.shape[0]

    def body(qkv_ref, att_ref, lse_ref, keys, vals, acc):
        attend_tiles(
            lambda n: qkv_ref[:, 0:LANES],
            lambda n: qkv_ref[:, LANES : 2 * LANES],
            lambda n: qkv_ref[:, 2 * LANES : 3 * LANES],
            att_ref,
            lse_ref,
            keys,
            vals,
            acc,
            [tile],
            heads,
            head_dim,
        )

    live = heads - tile * (LANES // head_dim)
    return run(
        body,
        [qkv],
        after,
        grid=(1,),
        in_specs=[pl.BlockSpec((total, 3 * LANES), lambda i: (0, tile))],
        out_specs=[pl.BlockSpec((total, LANES), lambda i: (0, 0))] * 2,
        out_shape=[sds((total, LANES), BF16), sds((total, LANES), F32)],
        scratch_shapes=attend_scratch(total, head_dim),
        vmem=14,
        cost_estimate=cost(4 * live * total * total * 256, 2 * 1024 * 1024, live * total * total),
        name="attend_last",
    )


def gelu_parts(value):
    size = jnp.abs(value)
    near = pl.reciprocal(1.0 + (0.3275911 * 0.7071067811865476) * size, approx=True)
    bell = jnp.exp2(value * value * (-0.5 * LOG2E))
    poly = near * (
        0.5 * 0.254829592
        + near
        * (
            0.5 * -0.284496736
            + near * (0.5 * 1.421413741 + near * (0.5 * -1.453152027 + near * (0.5 * 1.061405429)))
        )
    )
    tail = poly * bell
    area = jnp.where(value < 0.0, tail, 1.0 - tail)
    return value * area, area + value * bell * 0.3989422804014327


class Units:
    def __init__(self, block, blocks, start, size, stride, quads, high):
        self.block, self.blocks, self.start, self.size = block, blocks, start, size
        self.stride, self.quads, self.high = stride, quads, high
        self.count = blocks * size
        self.chunk = 512 if self.count % 512 == 0 else 256
        self.packed = quads is not None

    def loads(self, part, hbm_up, hbm_down, hbm_bias, up_ref, down_ref, bias_ref, sem):
        copies = []
        for b in range(self.blocks):
            src = self.start
            if self.packed:
                src = pl.multiple_of((b * self.stride + part) * self.block, LANES) + self.start
            src = pl.ds(src, self.size)
            dst = pl.ds(b * self.size, self.size)
            copies.append(
                pltpu.make_async_copy(hbm_up.at[:, src], up_ref.at[:, dst], sem.at[2 * b])
            )
            copies.append(
                pltpu.make_async_copy(hbm_down.at[src, :], down_ref.at[dst, :], sem.at[2 * b + 1])
            )
            bias_ref[0:1, dst] = hbm_bias[:, src]
        return copies

    def grad_shapes(self, width):
        if self.packed:
            return [pltpu.HBM((2, self.quads, self.high, self.size), BF16)] * 4
        return [sds((width, self.count), BF16)] * 2

    def scratch(self, total, width):
        grads = (self.blocks, self.quads, self.high, self.size) if self.packed else (8, LANES)
        return [
            pltpu.VMEM(grads, BF16),
            pltpu.VMEM(grads, BF16),
            pltpu.SemaphoreType.DMA((8,)),
            pltpu.VMEM((total, self.count), BF16),
            pltpu.VMEM((total, self.count), BF16),
            pltpu.VMEM((width, self.count), BF16),
            pltpu.VMEM((self.count, width), BF16),
            pltpu.VMEM((8, self.count), F32),
            pltpu.SemaphoreType.DMA((2 * self.blocks,)),
        ]

    def compute(self, part, second, second_t, grad, grad_t, acc, gs, ubg, scratch, outs):
        up_slots, down_slots, out_sem, acts, grad_pres, up_ref, down_ref, bias_ref, _ = scratch
        if not self.packed:
            up_slots, down_slots = outs
        quad = lax.div(lax.axis_index("seq"), self.stride)
        mine = lax.axis_index("batch")

        def enter(i):
            rows = slice(i * ROWS, (i + 1) * ROWS)
            pre = dot(second[rows, :], up_ref[...]) + bias_ref[0:1, :]
            return pre, dot_nt(grad[rows, :], down_ref[...])

        def weights(n):
            first, last = n * self.chunk, (n + 1) * self.chunk
            up_grad = dot(second_t[...], grad_pres[:, first:last]).astype(BF16)
            down_grad = dot(grad_t[...], acts[:, first:last]).astype(BF16)
            if not self.packed:
                up_slots[:, first:last] = up_grad
                down_slots[:, first:last] = down_grad
                return
            at = first
            while at < last:
                block = at // self.size
                stop = min(last, (block + 1) * self.size)
                src = slice(at - first, stop - first)
                dst = slice(at - block * self.size, stop - block * self.size)
                for m in range(self.blocks):
                    rows = slice(m * self.high, (m + 1) * self.high)
                    up_slots[block ^ mine, m ^ quad, :, dst] = up_grad[rows, src]
                    down_slots[m ^ mine, block ^ quad, :, dst] = down_grad[rows, src]
                at = stop

        ready = enter(0)
        chunks = second.shape[0] // ROWS
        for i in range(chunks):
            ahead = enter(i + 1) if i + 1 < chunks else None
            rows = slice(i * ROWS, (i + 1) * ROWS)
            pre, grad_act = ready
            value, slope = gelu_parts(pre)
            act = value.astype(BF16)
            grad_pre = (grad_act * slope).astype(BF16)
            acts[rows, :] = act
            grad_pres[rows, :] = grad_pre
            ubg[0:1, :] += jnp.sum(grad_pre.astype(F32), axis=0, keepdims=True)
            acc[rows, :] += dot(act, down_ref[...])
            gs[rows, :] += dot_nt(grad_pre, up_ref[...])
            ready = ahead
        for n in range(self.count // self.chunk):
            weights(n)
        stores = []
        if self.packed:
            order = ((up_slots, (0, 2)), (up_slots, (1, 3)), (down_slots, (0, 1)), (down_slots, (2, 3)))
            for m, (source, slots) in enumerate(order):
                for n in range(2):
                    stores.append(
                        pltpu.make_async_copy(
                            source.at[slots[n]], outs[m].at[n], out_sem.at[2 * m + n]
                        )
                    )
        return stores


def feed_first(
    rows_all, att_first, att_last, cot_pieces, out_w, out_b, gain, shift, up, up_b, down, down_b, units
):
    pieces = len(att_first)
    total, width = rows_all.shape
    piece_rows = total // pieces
    count = len(cot_pieces)
    cot_rows = total // count
    split = att_first[0].shape[1]
    grads = units.grad_shapes(width)

    def body(*refs):
        x_ref, refs = refs[0], refs[1:]
        att_refs, refs = refs[: 2 * pieces], refs[2 * pieces :]
        cot_refs, refs = refs[:count], refs[count:]
        wo_refs, refs = refs[:pieces], refs[pieces:]
        ob_ref, gain_ref, shift_ref, up_hbm, ub_ref, down_hbm, db_ref = refs[:7]
        mid_ref, second, second_t, grad, grad_t, own_ref, low_ref, ubg, refs = *refs[7:15], refs[15:]
        send_refs, refs = refs[: pieces - 1], refs[pieces - 1 :]
        outs, refs = refs[: len(grads)], refs[len(grads) :]
        acc, gs, mid_rows, mid_sem, *scratch = refs
        _, part, _ = place(pieces)
        loads = units.loads(part, up_hbm, down_hbm, ub_ref, *scratch[5:])
        for load in loads:
            load.start()
        ubg[...] = jnp.zeros_like(ubg)
        masked = jnp.zeros((1, width), F32)
        for ref in cot_refs:
            masked = masked + ref[cot_rows : cot_rows + 1, :].astype(F32)
        factor = total / (4.0 * masked)
        for n in range(count):
            scaled = cot_refs[n][0:cot_rows, :].astype(F32) * factor
            dst = slice(n * cot_rows, (n + 1) * cot_rows)
            grad[dst, :] = scaled.astype(BF16)

        for h in range(pieces):

            @pl.loop(0, piece_rows // ROWS)
            def _(i, h=h):
                at = pl.multiple_of(i * ROWS, ROWS)
                dst = pl.ds(h * piece_rows + at, ROWS)
                mid = x_ref[dst, :].astype(F32) + ob_ref[...]
                for n in range(pieces):
                    src = pl.ds(((h - n) % pieces) * piece_rows + at, ROWS)
                    mid = mid + dot(att_refs[2 * n][src, :], wo_refs[n][0:split, :])
                    mid = mid + dot(att_refs[2 * n + 1][src, :], wo_refs[n][split:, :])
                mid_rows[dst, :] = mid
                normed, _ = norm_rows(mid)
                low = normed * gain_ref[...] + shift_ref[...]
                second[dst, :] = low.astype(BF16)
                second_t[:, dst] = low.T.astype(BF16)
                grad_t[:, dst] = grad[dst, :].astype(F32).T.astype(BF16)
                acc[dst, :] = mid + db_ref[...] if h == 0 else jnp.zeros((ROWS, width), F32)
                gs[dst, :] = jnp.zeros((ROWS, width), F32)

        keep_mid = pltpu.make_async_copy(mid_rows, mid_ref, mid_sem)
        keep_mid.start()
        for load in loads:
            load.wait()
        stores = units.compute(
            part, second, second_t, grad, grad_t, acc, gs, ubg, scratch, outs
        )
        for store in stores:
            store.start()
        keep_mid.wait()
        own_ref[...] = acc[0:piece_rows, :]
        low_ref[...] = gs[...].astype(BF16)
        for h in range(1, pieces):
            send_refs[h - 1][...] = acc[h * piece_rows : (h + 1) * piece_rows, :].astype(BF16)
        for store in stores:
            store.wait()

    att_all = [item for pair in zip(att_first, att_last) for item in pair]
    turned = sds((width, total), BF16)
    flat = sds((total, width), BF16)
    half = sds((piece_rows, width), F32)
    return run(
        body,
        [
            rows_all,
            *att_all,
            *cot_pieces,
            *out_w,
            out_b,
            gain,
            shift,
            far(up),
            up_b,
            far(down),
            down_b,
        ],
        in_specs=[VMEM] * (1 + 3 * pieces + count) + [VMEM, VMEM, VMEM, HBM, VMEM, HBM, VMEM],
        out_specs=[HBM] + [VMEM] * (6 + pieces) + [HBM if units.packed else VMEM] * len(grads),
        out_shape=[pltpu.HBM((total, width), F32), flat, turned, flat, turned, half, flat, sds((8, units.count), F32)]
        + [sds((piece_rows, width), BF16)] * (pieces - 1)
        + grads,
        scratch_shapes=[pltpu.VMEM((total, width), F32)] * 3
        + [pltpu.SemaphoreType.DMA]
        + units.scratch(total, width),
        vmem=26,
        cost_estimate=cost(12 * total * width * units.count, 24 * 1024 * 1024, total * units.count),
        name="feed_first",
    )


def feed_second(second, second_t, grad, grad_t, own_first, low_first, sends, up, up_b, down, units):
    pieces = 1 + len(sends)
    total, width = second.shape
    piece_rows = total // pieces
    grads = units.grad_shapes(width)

    def body(*refs):
        second, second_t, grad, grad_t, own_in, low_in, up_hbm, ub_ref, down_hbm, refs = (
            *refs[:9],
            refs[9:],
        )
        send_ins, refs = refs[: pieces - 1], refs[pieces - 1 :]
        own_ref, low_ref, ubg, refs = refs[0], refs[1], refs[2], refs[3:]
        send_refs, refs = refs[: pieces - 1], refs[pieces - 1 :]
        outs, (acc, gs), scratch = refs[: len(grads)], refs[len(grads) :][:2], refs[len(grads) + 2 :]
        _, part, _ = place(pieces)
        loads = units.loads(part, up_hbm, down_hbm, ub_ref, *scratch[5:])
        for load in loads:
            load.start()
        ubg[...] = jnp.zeros_like(ubg)
        acc[...] = jnp.zeros_like(acc)
        gs[...] = jnp.zeros_like(gs)
        for load in loads:
            load.wait()
        stores = units.compute(
            part, second, second_t, grad, grad_t, acc, gs, ubg, scratch, outs
        )
        for store in stores:
            store.start()
        low_ref[...] = (gs[...] + low_in[...].astype(F32)).astype(BF16)
        own_ref[...] = acc[0:piece_rows, :] + own_in[...]
        for h in range(1, pieces):
            item = acc[h * piece_rows : (h + 1) * piece_rows, :] + send_ins[h - 1][...].astype(F32)
            send_refs[h - 1][...] = item.astype(BF16)
        for store in stores:
            store.wait()

    return run(
        body,
        [
            second,
            second_t,
            grad,
            grad_t,
            own_first,
            low_first,
            far(up),
            up_b,
            far(down),
            *sends,
        ],
        in_specs=[VMEM] * 6 + [HBM, VMEM, HBM] + [VMEM] * (pieces - 1),
        out_specs=[VMEM] * (2 + pieces) + [HBM if units.packed else VMEM] * len(grads),
        out_shape=[
            sds((piece_rows, width), F32),
            sds((total, width), BF16),
            sds((8, units.count), F32),
        ]
        + [sds((piece_rows, width), BF16)] * (pieces - 1)
        + grads,
        scratch_shapes=[pltpu.VMEM((total, width), F32)] * 2 + units.scratch(total, width),
        vmem=30,
        cost_estimate=cost(12 * total * width * units.count, 24 * 1024 * 1024, total * units.count),
        name="feed_second",
    )


def mid_back(mid, grad_second, received, grad_rows, gain, out_w, att_first, att_last, chunk):
    pieces = 1 + len(received)
    total, width = mid.shape
    per_piece = total // pieces // ROWS
    split = att_first.shape[1]
    wide = split + att_last.shape[1]
    steps = total // ROWS

    def body(*refs):
        mid_ref, gs_ref, refs = refs[0], refs[1], refs[2:]
        recv_refs, refs = refs[: pieces - 1], refs[pieces - 1 :]
        go_ref, gain_ref, wo_ref, att_ref, last_ref = refs[:5]
        gm_ref, do_ref, sums_ref, *dwo_refs, acc = refs[5:]
        i = pl.program_id(0)

        @pl.when(i == 0)
        def _():
            sums_ref[...] = jnp.zeros_like(sums_ref)
            acc[...] = jnp.zeros_like(acc)

        normed, inv_std = norm_rows(mid_ref[...])
        grad = gs_ref[...].astype(F32)
        for ref in recv_refs:
            grad = grad + ref[...].astype(F32)
        go = go_ref[...].astype(F32)
        grad_mid = go + norm_back(grad * gain_ref[...], normed, inv_std)
        low = grad_mid.astype(BF16)
        do_ref[...] = dot_nt(low, wo_ref[...]).astype(BF16)
        acc[0:split, :] += dot(att_ref[...].astype(F32).T.astype(BF16), low)
        acc[split:, :] += dot(last_ref[...].astype(F32).T.astype(BF16), low)

        @pl.when(i < per_piece)
        def _():
            gm_ref[...] = grad_mid
            for n, item in enumerate((grad * normed, grad, low.astype(F32), go)):
                sums_ref[n : n + 1, :] += jnp.sum(item, axis=0, keepdims=True)

        @pl.when(i == steps - 1)
        def _():
            if chunk == 0:
                dwo_refs[0][...] = acc[...].astype(BF16)
                return
            _, part, _ = place(pieces)
            for c in range(pieces):

                @pl.when(part == c)
                def _(c=c):
                    for n in range(dwo_refs[0].shape[0]):
                        for e in range(pieces):
                            at = (n * pieces + (c + e) % pieces) * chunk
                            dwo_refs[e][n] = acc[at : at + chunk, :].astype(BF16)

    def rows_of(columns):
        return pl.BlockSpec((ROWS, columns), lambda i: (i, 0))

    def theirs(n):
        def index(i):
            piece = lax.rem(lax.div(i, per_piece) + pieces - n, pieces)
            return piece * per_piece + lax.rem(i, per_piece), 0

        return pl.BlockSpec((ROWS, width), index)

    def whole(*shape):
        return pl.BlockSpec(shape, lambda i: (0,) * len(shape))

    if chunk == 0:
        grads = [((wide, width), sds((wide, width), BF16))]
    else:
        shape = (width // (pieces * pieces * chunk), chunk, width)
        grads = [(shape, pltpu.HBM(shape, BF16))] * pieces
    return run(
        body,
        [far(mid), grad_second, *received, grad_rows, gain, out_w, far(att_first), far(att_last)],
        grid=(steps,),
        in_specs=[rows_of(width), rows_of(width)]
        + [theirs(n) for n in range(1, pieces)]
        + [rows_of(width), whole(1, width), whole(wide, width), rows_of(split), rows_of(wide - split)],
        out_specs=[
            pl.BlockSpec((ROWS, width), lambda i: (jnp.minimum(i, per_piece - 1), 0)),
            rows_of(wide),
            whole(8, width),
        ]
        + [whole(*shape) for shape, _ in grads],
        out_shape=[
            sds((per_piece * ROWS, width), F32),
            sds((total, wide), BF16),
            sds((8, width), F32),
        ]
        + [item for _, item in grads],
        scratch_shapes=[pltpu.VMEM((wide, width), F32)],
        vmem=16,
        cost_estimate=cost(4 * total * width * wide, 14 * 1024 * 1024),
        name="mid_back",
    )


def attend_backward(
    qkv, grad_att, att, att_tile, logs, lane_first, tile, heads, head_dim, after=(), part=1
):
    total = qkv.shape[0]
    per_tile = LANES // head_dim
    live = min(per_tile, heads - tile * per_tile)
    scale = head_dim ** (-0.5)
    exp_scale = scale * LOG2E

    def body(qkv_ref, do_ref, att_ref, lse_ref, out_ref, *scratch):
        km, vm, qm, dm, key_t, query_t, do_t, dq_t, lse_t, mean_t = scratch
        lane = lax.broadcasted_iota(jnp.int32, (1, LANES), 1)
        lse_t[...] = lse_ref[...].T
        query = qkv_ref[:, 0:LANES].astype(F32)
        key = qkv_ref[:, LANES : 2 * LANES].astype(F32)
        val = qkv_ref[:, 2 * LANES : 3 * LANES].astype(F32)
        upstream = do_ref[...].astype(F32)
        both_t = (upstream * att_ref[...].astype(F32)).T
        for j in range(live):
            mean_t[j : j + 1, :] = jnp.sum(
                both_t[j * head_dim : (j + 1) * head_dim, :], axis=0, keepdims=True
            )
        query_t[...] = query.T.astype(BF16)
        do_t[...] = upstream.T.astype(BF16)
        key_t[...] = key.T.astype(BF16)
        for j in range(live):
            mine = lane // head_dim == j
            km[j] = jnp.where(mine, key, 0.0).astype(BF16)
            vm[j] = jnp.where(mine, val, 0.0).astype(BF16)
            qm[j] = jnp.where(mine, query, 0.0).astype(BF16)
            dm[j] = jnp.where(mine, upstream, 0.0).astype(BF16)
        dq_t[...] = jnp.zeros_like(dq_t)

        @pl.loop(0, total // ROWS)
        def _(i):
            rows = pl.ds(pl.multiple_of(i * ROWS, ROWS), ROWS)
            grad_key = jnp.zeros((ROWS, LANES), F32)
            grad_val = jnp.zeros((ROWS, LANES), F32)

            def enter(j):
                return dot(km[j, rows, :], query_t[...]), dot(vm[j, rows, :], do_t[...])

            ready = enter(0)
            for j in range(live):
                ahead = enter(j + 1) if j + 1 < live else None
                scores, grad_prob = ready
                head = lane_first + j
                own = slice(j * head_dim, (j + 1) * head_dim)
                probs = jnp.exp2(scores * exp_scale - lse_t[head : head + 1, :])
                grad_scores = (probs * (grad_prob - mean_t[j : j + 1, :])).astype(BF16)
                grad_val = grad_val + dot(probs.astype(BF16), dm[j])
                grad_key = grad_key + dot(grad_scores, qm[j])
                dq_t[own, :] += dot(key_t[own, rows], grad_scores)
                ready = ahead
            out_ref[rows, LANES : 2 * LANES] = (grad_key * scale).astype(BF16)
            out_ref[rows, 2 * LANES : 3 * LANES] = grad_val.astype(BF16)

        out_ref[:, 0:LANES] = (dq_t[...].T * scale).astype(BF16)

    masked = pltpu.VMEM((live, total, LANES), BF16)
    turned = pltpu.VMEM((LANES, total), BF16)
    turned_f = pltpu.VMEM((LANES, total), F32)
    return run(
        body,
        [qkv, grad_att, att, logs],
        after,
        grid=(1,),
        in_specs=[
            pl.BlockSpec((total, 3 * LANES), lambda i: (0, tile)),
            pl.BlockSpec((total, LANES), lambda i: (0, tile)),
            pl.BlockSpec((total, LANES), lambda i: (0, att_tile)),
            pl.BlockSpec((total, LANES), lambda i: (0, 0)),
        ],
        out_specs=pl.BlockSpec((total, 3 * LANES), lambda i: (0, 0)),
        out_shape=sds((total, 3 * LANES), BF16),
        scratch_shapes=[masked] * 4
        + [turned] * 3
        + [turned_f] * 2
        + [pltpu.VMEM((8, total), F32)],
        vmem=17,
        cost_estimate=cost(
            2 * live * total * total * 256 * 5, 3 * 1024 * 1024, live * total * total, part
        ),
        name="attend_backward",
    )


def project_weights(rows_all, gain, shift, grad_tiles, pieces, quads, packed, after):
    total, width = rows_all.shape
    tiles = len(grad_tiles)
    tile_cols = grad_tiles[0].shape[1]
    cols_all = tiles * tile_cols
    chunk = width // (quads * pieces)

    def body(*refs):
        x_ref, gain_ref, shift_ref, refs = refs[0], refs[1], refs[2], refs[3:]
        dq_refs, (*dw_refs, low_t, part_ref) = refs[:tiles], refs[tiles:]
        _, part, quad = place(pieces)

        @pl.loop(0, total // ROWS)
        def _(i):
            rows = pl.ds(pl.multiple_of(i * ROWS, ROWS), ROWS)
            normed, _ = norm_rows(x_ref[rows, :].astype(F32))
            low_t[:, rows] = (normed * gain_ref[...] + shift_ref[...]).T.astype(BF16)

        for t in range(tiles):
            cols = slice(t * tile_cols, (t + 1) * tile_cols)
            part_ref[...] = dot(low_t[...], dq_refs[t][...]).astype(BF16)
            if not packed:
                dw_refs[0][:, cols] = part_ref[...]
                continue
            for c in range(pieces):

                @pl.when(part == c)
                def _(c=c, cols=cols):
                    for q in range(quads):
                        for e in range(pieces):
                            at = (q * pieces + (c + e) % pieces) * chunk
                            dw_refs[e][q ^ quad, :, cols] = part_ref[at : at + chunk, :]

    if packed:
        grads = [sds((quads, chunk, cols_all), BF16)] * pieces
    else:
        grads = [sds((width, cols_all), BF16)]
    return run(
        body,
        [rows_all, gain, shift, *grad_tiles],
        after,
        out_shape=grads,
        scratch_shapes=[pltpu.VMEM((width, total), BF16), pltpu.VMEM((width, tile_cols), BF16)],
        vmem=12,
        cost_estimate=cost(2 * total * width * cols_all, 6 * 1024 * 1024),
        name="project_weights",
    )


def project_rows(
    rows_all, weight, grad_tiles, sums_mid, up_sums, pieces, quads, packed, real, after
):
    total, width = rows_all.shape
    piece_rows = total // pieces
    cols_all = weight.shape[1]
    tiles = len(grad_tiles)
    tile_cols = cols_all // tiles

    def body(*refs):
        x_ref, w_ref, mid_ref, refs = *refs[:3], refs[3:]
        ups_refs, refs = refs[: len(up_sums)], refs[len(up_sums) :]
        dq_refs, refs = refs[:tiles], refs[tiles:]
        own_ref, refs = refs[0], refs[1:]
        send_refs, (sums_ref, bias_ref) = refs[: pieces - 1], refs[pieces - 1 :]
        _, part, _ = place(pieces)
        sums_ref[...] = jnp.zeros_like(sums_ref)
        bias_ref[...] = jnp.zeros_like(bias_ref)
        for h in range(pieces):

            @pl.loop(0, piece_rows // ROWS)
            def _(i, h=h):
                at = pl.multiple_of(i * ROWS, ROWS)
                src = pl.ds(at, ROWS)
                rows = pl.ds(h * piece_rows + at, ROWS)
                normed, _ = norm_rows(x_ref[rows, :].astype(F32))
                grad = jnp.zeros((ROWS, width), F32)
                for t in range(tiles):
                    grad_rows = dq_refs[t][rows, :]
                    cols = slice(t * tile_cols, (t + 1) * tile_cols)
                    grad = grad + dot_nt(grad_rows, w_ref[:, cols])
                    bias_ref[0:1, cols] += jnp.sum(grad_rows.astype(F32), axis=0, keepdims=True)
                if h == 0:
                    own_ref[src, :] = grad
                else:
                    send_refs[h - 1][src, :] = grad.astype(BF16)
                sums_ref[0:1, :] += jnp.sum(grad * normed, axis=0, keepdims=True)
                sums_ref[1:2, :] += jnp.sum(grad, axis=0, keepdims=True)

        if not packed:
            return
        for row, src in ((4, 2), (5, 0), (6, 1), (15, 3)):
            sums_ref[row : row + 1, :] = mid_ref[src : src + 1, :]
        for c in range(pieces):

            @pl.when(part == c)
            def _(c=c):
                for row, p in ((2, 0), (3, 2)):
                    mine = jnp.concatenate(
                        [
                            bias_ref[0:1, (3 * t + p) * LANES :][:, : min(LANES, real - t * LANES)]
                            for t in range(tiles)
                        ],
                        axis=1,
                    )
                    sums_ref[row : row + 1, c * real : (c + 1) * real] = mine
                for n in range(quads):
                    row = 7 + n * pieces + c
                    start = 0
                    for ref in ups_refs:
                        size = ref.shape[1] // quads
                        here = ref[0:1, n * size : (n + 1) * size]
                        sums_ref[row : row + 1, start : start + size] = here
                        start += size

    return run(
        body,
        [rows_all, weight, sums_mid, *up_sums, *grad_tiles],
        after,
        out_shape=[sds((piece_rows, width), F32)]
        + [sds((piece_rows, width), BF16)] * (pieces - 1)
        + [sds((16, width), F32), sds((8, cols_all), F32)],
        vmem=12,
        cost_estimate=cost(2 * total * width * cols_all, 8 * 1024 * 1024),
        name="project_rows",
    )


def finish_rows(rows_all, gain, grad_mid, grad_own, received, count, after):
    rows, width = grad_mid.shape
    others = len(received)
    piece = rows // count
    per_step = ROWS // piece

    def body(*refs):
        x_ref, gain_ref, gm_ref, own_ref, refs = refs[0], refs[1], refs[2], refs[3], refs[4:]
        recv_refs, out_refs = refs[:others], refs[others:]
        for n in range(rows // ROWS):
            at = slice(n * ROWS, (n + 1) * ROWS)
            normed, inv_std = norm_rows(x_ref[at, :].astype(F32))
            grad = own_ref[at, :]
            for ref in recv_refs:
                grad = grad + ref[at, :].astype(F32)
            done = gm_ref[at, :] + norm_back(grad * gain_ref[...], normed, inv_std)
            for e in range(per_step):
                out_refs[n * per_step + e][...] = done[e * piece : (e + 1) * piece, :].astype(BF16)

    return run(
        body,
        [rows_all, gain, grad_mid, grad_own, *received],
        after,
        out_shape=[sds((piece, width), BF16)] * count,
        vmem=12,
        cost_estimate=cost(20 * rows * width, 6 * 1024 * 1024),
        name="finish_rows",
    )


def finish_result(own, received, count):
    rows, width = own.shape
    others = len(received)
    piece = rows // count

    def body(*refs):
        out_refs = refs[1 + others :]
        for n in range(count):
            at = slice(n * piece, (n + 1) * piece)
            total = refs[0][at, :]
            for ref in refs[1 : 1 + others]:
                total = total + ref[at, :].astype(F32)
            out_refs[n % 2][n // 2] = total.astype(BF16)

    return run(
        body,
        [own, *received],
        out_shape=[sds((count // 2, piece, width), BF16)] * 2,
        vmem=8,
        cost_estimate=cost(2 * rows * width, 3 * 1024 * 1024),
        name="finish_result",
    )


def pass_on(keep, received, after):
    def body(keep_ref, recv_ref, out_ref):
        out_ref[0] = keep_ref[1]
        out_ref[1] = recv_ref[1]

    return run(
        body,
        [keep, received],
        after,
        out_shape=sds(keep.shape, keep.dtype),
        vmem=6,
        cost_estimate=cost(0, 4 * keep.size),
        name="pass_on",
    )


def collect_halves(keep, near, far, group, after):
    _, rows, width = keep.shape

    def body(keep_ref, near_ref, far_ref, out_ref):
        _, _, quad = place(group)
        out_ref[quad] = keep_ref[0]
        out_ref[quad ^ 1] = near_ref[0]
        out_ref[quad ^ 2] = far_ref[0]
        out_ref[quad ^ 3] = far_ref[1]

    return run(
        body,
        [keep, near, far],
        after,
        out_shape=sds((4, rows, width), keep.dtype),
        vmem=6,
        cost_estimate=cost(0, 16 * rows * width),
        name="collect_halves",
    )


def two_parts(item):
    first = item.astype(BF16)
    return first, (item - first.astype(F32)).astype(BF16)


def pack_attention(
    qkv_keep, qkv_recv, out_keep, out_recv, small, small_recv, real, blocks, after
):
    quads, chunk, cols_all = qkv_keep.shape
    wide = cols_all // 3
    tiles = wide // LANES
    width = out_keep.shape[2]
    qkv_lanes = 6 * real // blocks
    out_lanes = width // blocks
    lanes = qkv_lanes + out_lanes
    halves = quads // 2
    slot = halves * chunk
    small_rows = small.shape[0]

    def body(qk_ref, qr_ref, ok_ref, or_ref, small_ref, srecv_ref, *out_refs):
        _, part, quad = place(2)
        mine = lax.axis_index("batch")
        slots = out_refs[4]

        def heads_of(rows, p):
            return [
                rows[:, (3 * t + p) * LANES : (3 * t + p) * LANES + min(LANES, real - t * LANES)]
                for t in range(tiles)
            ]

        for c in range(2):

            @pl.when(part == c)
            def _(c=c):
                for q in range(quads):
                    pair = (qk_ref[q], qr_ref[q])
                    if c == 1:
                        pair = pair[::-1]
                    parts = []
                    for p in range(3):
                        parts += heads_of(pair[0], p) + heads_of(pair[1], p)
                    row = jnp.concatenate(parts, axis=1)
                    for b in range(blocks):
                        slots[b ^ mine, q, :, 0:qkv_lanes] = row[
                            :, b * qkv_lanes : (b + 1) * qkv_lanes
                        ]
                for e, ref in enumerate((ok_ref, or_ref)):
                    for n in range(halves):
                        q = ((c + e) % 2) * halves + n
                        for b in range(blocks):
                            slots[b ^ mine, q ^ quad, :, qkv_lanes:lanes] = ref[
                                n, :, b * out_lanes : (b + 1) * out_lanes
                            ]

        for n, order in enumerate(((0, 2), (1, 3), (0, 1), (2, 3))):
            for e in range(2):
                for f in range(halves):
                    at = e * slot + f * chunk
                    src = f if n < 2 else halves + f
                    out_refs[n][at : at + chunk, :] = slots[order[e], src]
        parts = two_parts(small_ref[...] + srecv_ref[...])
        for n in range(2):
            for e in range(2):
                at = 2 * slot + e * small_rows
                out_refs[n][at : at + small_rows, :] = parts[e]

    first = sds((2 * slot + 2 * small_rows, lanes), BF16)
    other = sds((2 * slot, lanes), BF16)
    return run(
        body,
        [qkv_keep, qkv_recv, out_keep, out_recv, small, small_recv],
        after,
        out_shape=[first, first, other, other],
        scratch_shapes=[pltpu.VMEM((blocks, quads, chunk, lanes), BF16)],
        vmem=12,
        cost_estimate=cost(0, 4 * 1024 * 1024),
        name="pack_attention",
    )


def sum_first(keeps, received, after=()):
    count = len(keeps)
    shape = keeps[0].shape[1:]

    def body(*refs):
        for n in range(count):
            for e in range(2):
                total = refs[n][e].astype(F32) + refs[count + n][e].astype(F32)
                refs[2 * count + 2 * n + e][...] = total.astype(BF16)

    return run(
        body,
        [*keeps, *received],
        after,
        out_shape=[pltpu.HBM(shape, BF16), sds(shape, BF16)] * count,
        vmem=12,
        cost_estimate=cost(0, 6 * count * keeps[0].size),
        name="sum_first",
    )


def sum_second(keeps, received, after=()):
    quads, rows, width = keeps[0].shape

    def body(ka, kb, ra, rb, keep_ref, send_ref):
        for d in range(quads):
            ref = send_ref if d % 2 else keep_ref
            for e, (keep, recv) in enumerate(((ka, ra), (kb, rb))):
                total = keep[d].astype(F32) + recv[d].astype(F32)
                ref[d // 2, e] = total.astype(BF16)

    return run(
        body,
        [*keeps, *received],
        after,
        out_shape=[sds((quads // 2, 2, rows, width), BF16)] * 2,
        vmem=10,
        cost_estimate=cost(0, 12 * keeps[0].size),
        name="sum_second",
    )


def sum_third(keep, received, after=()):
    def body(keep_ref, recv_ref, stay_ref, pass_ref):
        for ref, e in ((stay_ref, 0), (pass_ref, 1)):
            ref[...] = (keep_ref[e].astype(F32) + recv_ref[e].astype(F32)).astype(BF16)

    return run(
        body,
        [keep, received],
        after,
        out_shape=[sds(keep.shape[1:], BF16)] * 2,
        vmem=6,
        cost_estimate=cost(0, 6 * keep.size),
        name="sum_third",
    )


def small_sum(refs, rows, count):
    total = None
    for ref in refs:
        for e in range(2):
            item = ref[rows + e * count : rows + (e + 1) * count, :].astype(F32)
            total = item if total is None else total + item
    return total


def sum_first_attention(keeps, received, slot, small_rows, after):
    lanes = keeps[0].shape[1]

    def body(ka, kb, ra, rb, stay_a, pass_a, stay_b, pass_b):
        parts = two_parts(small_sum((ka, ra), 2 * slot, small_rows))
        for keep, recv, stay, on in ((ka, ra, stay_a, pass_a), (kb, rb, stay_b, pass_b)):
            for e, ref in enumerate((stay, on)):
                at = slice(e * slot, (e + 1) * slot)
                ref[0:slot, :] = (keep[at, :].astype(F32) + recv[at, :].astype(F32)).astype(BF16)
        for ref in (stay_a, pass_a):
            for e in range(2):
                ref[slot + e * small_rows : slot + (e + 1) * small_rows, :] = parts[e]

    first = sds((slot + 2 * small_rows, lanes), BF16)
    other = sds((slot, lanes), BF16)
    return run(
        body,
        [*keeps, *received],
        after,
        out_shape=[first, first, other, other],
        vmem=8,
        cost_estimate=cost(0, 3 * 1024 * 1024),
        name="sum_first_attention",
    )


def sum_second_attention(keeps, received, chunk, quads, small_rows, after):
    lanes = keeps[0].shape[1]
    halves = quads // 2
    slot = halves * chunk

    def body(ka, kb, ra, rb, *out_refs):
        parts = two_parts(small_sum((ka, ra), slot, small_rows))
        for d in range(quads):
            keep, recv = ((ka, ra), (kb, rb))[d // halves]
            at = slice(d % halves * chunk, (d % halves + 1) * chunk)
            total = keep[at, :].astype(F32) + recv[at, :].astype(F32)
            out_refs[d][0:chunk, :] = total.astype(BF16)
            for e in range(2):
                at = chunk + e * small_rows
                out_refs[d][at : at + small_rows, :] = parts[e]

    return run(
        body,
        [*keeps, *received],
        after,
        out_shape=[sds((chunk + 2 * small_rows, lanes), BF16)] * quads,
        vmem=8,
        cost_estimate=cost(0, 2 * 1024 * 1024),
        name="sum_second_attention",
    )


def final_attention(pieces, chunk, qkv_lanes, small_rows):
    lanes = pieces[0].shape[1]
    count = len(pieces)

    def body(*refs):
        total = refs[0][0:chunk, :].astype(F32)
        for ref in refs[1:count]:
            total = total + ref[0:chunk, :].astype(F32)
        refs[count][...] = total[:, :qkv_lanes]
        refs[count + 1][...] = total[:, qkv_lanes:]
        refs[count + 2][...] = small_sum(refs[:count], chunk, small_rows)

    return run(
        body,
        pieces,
        out_shape=[
            sds((chunk, qkv_lanes), F32),
            sds((chunk, lanes - qkv_lanes), F32),
            sds((small_rows, lanes), F32),
        ],
        vmem=6,
        cost_estimate=cost(0, 1024 * 1024),
        name="final_attention",
    )


def final_units(first, second, after):
    high = first[0].shape[1]
    sizes = [first[0].shape[2], second[0].shape[2]]
    unit_block = sum(sizes)
    count = len(first)
    half = high // 2

    def body(*refs):
        _, part, _ = place(2)
        keep_ref, send_ref, down_ref = refs[2 * count :]
        for h in range(2):
            pieces = refs[h * count : (h + 1) * count]
            up, down = pieces[0][0].astype(F32), pieces[0][1].astype(F32)
            for ref in pieces[1:]:
                up = up + ref[0].astype(F32)
                down = down + ref[1].astype(F32)
            here = slice(h * sizes[0], h * sizes[0] + sizes[h])
            down_ref[here, :] = down.T
            for c in range(2):

                @pl.when(part == c)
                def _(up=up, here=here, c=c):
                    keep_ref[:, here] = up[c * half : (c + 1) * half, :]
                    send_ref[:, here] = up[(1 - c) * half : (2 - c) * half, :].astype(BF16)

    return run(
        body,
        [*first, *second],
        after,
        out_shape=[
            sds((half, unit_block), F32),
            sds((half, unit_block), BF16),
            sds((unit_block, high), F32),
        ],
        vmem=10,
        cost_estimate=cost(0, 4 * 1024 * 1024),
        name="final_units",
    )


def final_join(keep, recv):
    chunk, unit_block = keep.shape

    def body(keep_ref, recv_ref, out_ref):
        _, part, _ = place(2)
        for c in range(2):

            @pl.when(part == c)
            def _(c=c):
                out_ref[:, c * unit_block : (c + 1) * unit_block] = keep_ref[...]
                out_ref[:, (1 - c) * unit_block : (2 - c) * unit_block] = recv_ref[...].astype(F32)

    return run(
        body,
        [keep, recv],
        out_shape=sds((chunk, 2 * unit_block), F32),
        vmem=5,
        cost_estimate=cost(0, 1024 * 1024),
        name="final_join",
    )


def on_device(
    tokens,
    mask,
    cotangent,
    ln1_gain,
    ln1_bias,
    qkv_weight,
    q_bias,
    v_bias,
    out_weight,
    out_bias,
    ln2_gain,
    ln2_bias,
    up_weight,
    up_bias,
    down_weight,
    down_bias,
):
    seq_size = lax.axis_size("seq")
    batch_size = lax.axis_size("batch")
    micro_count, seq_count, local_len, width = tokens.shape
    sequences = micro_count * seq_count
    group = seq_size // sequences
    units = up_weight.shape[1]
    head_dim = width // HEADS
    heads = HEADS // group
    real = heads * head_dim
    wide = -(-real // LANES) * LANES
    full_len = local_len * seq_size
    block_len = local_len // group
    rows = seq_size * block_len
    own_units = units // group
    part = lax.axis_index("seq") % group
    aligned = (
        seq_size == batch_size * group
        and group == 2
        and batch_size == 4
        and wide == 3 * LANES
        and (seq_size // group) % group == 0
        and units % (batch_size * group * LANES) == 0
        and own_units // batch_size == width
    )

    def from_part(item, ahead):
        if ahead % group == 0:
            return item
        pairs = [
            (q * group + (c + ahead) % group, q * group + c)
            for q in range(sequences)
            for c in range(group)
        ]
        return lax.ppermute(item, "seq", pairs)

    def gather_parts(item):
        return [from_part(item, n) for n in range(group)]

    def row_of(item):
        return item.astype(F32)[None, :]

    def blocks_of(item):
        return item.reshape(sequences, local_len, width)

    x_own = over_quads(deal(blocks_of(tokens), group), group)
    x_pieces = [from_part(item, n) for n in range(group) for item in x_own]

    count_rows = jnp.sum(mask, axis=2).reshape(sequences).astype(BF16)
    cot_low = jnp.where(mask[..., None] != 0, cotangent, jnp.zeros_like(cotangent))
    cot_send = jnp.concatenate(
        [blocks_of(cot_low), jnp.broadcast_to(count_rows[:, None, None], (sequences, 16, width))],
        axis=1,
    )
    cot_own = over_quads(deal(cot_send, group, x_pieces[sequences:]), group)

    qkv_w, qkv_b, *out_w = pick_weights(
        qkv_weight,
        jnp.concatenate([q_bias, jnp.zeros_like(q_bias), v_bias])[None, :],
        out_weight,
        group,
        real,
        wide,
    )
    if aligned:
        up_own, up_b, down_own = up_weight, up_bias[None, :], down_weight
    else:

        def own_columns(matrix, blocks):
            split = matrix.reshape(matrix.shape[0], blocks, group, -1)
            return lax.dynamic_index_in_dim(split, part, 2, keepdims=False)

        up_own = own_columns(up_weight, batch_size).reshape(width, own_units)
        up_b = own_columns(up_bias[None, :], batch_size).reshape(1, own_units)
        down_own = lax.dynamic_index_in_dim(
            down_weight.reshape(batch_size, group, -1, width), part, 1, keepdims=False
        ).reshape(own_units, width)

    tiles = wide // LANES
    x_all, qkv, att_first, logs_first = attend_first(
        x_pieces, row_of(ln1_gain), row_of(ln1_bias), qkv_w, qkv_b, tiles - 1, heads, head_dim
    )
    cot_stack = stack(cot_own, [logs_first])
    att_last, logs_last = attend_last(qkv, tiles - 1, heads, head_dim, [cot_stack])
    cot_pieces = cot_own + [
        item[d]
        for item in gather_parts(cot_stack)[1:]
        for d in range(sequences)
    ]
    blocks = batch_size if aligned else 1
    unit_block = own_units // blocks
    size = unit_block * 2 // 5
    shape = (group, sequences if aligned else None, width // sequences)
    calls = [
        Units(unit_block, blocks, 0, size, *shape),
        Units(unit_block, blocks, size, unit_block - size, *shape),
    ]
    mid, second, second_t, grad_rows, grad_t, result_own, grad_second, *found = feed_first(
        x_all,
        gather_parts(att_first),
        gather_parts(att_last),
        cot_pieces,
        out_w,
        row_of(out_bias),
        row_of(ln2_gain),
        row_of(ln2_bias),
        up_own,
        up_b,
        down_own,
        row_of(down_bias),
        calls[0],
    )
    up_sums, ff_grads = [found[0]], [found[group:]]
    result_own, grad_second, *found = feed_second(
        second,
        second_t,
        grad_rows,
        grad_t,
        result_own,
        grad_second,
        found[1:group],
        up_own,
        up_b,
        down_own,
        calls[1],
    )
    up_sums.append(found[0])
    result_send = found[1:group]
    ff_grads.append(found[group:])

    def begin_sum(e, sends, after):
        moved = [swap(sends[0], "batch", batch_size, 1), swap(sends[1], "batch", batch_size, 2)]
        stay_a, pass_a, stay_b, pass_b = sum_first(
            [ff_grads[e][0], ff_grads[e][2]], moved, after
        )
        moved = [swap(pass_a, "batch", batch_size, 2), swap(pass_b, "batch", batch_size, 1)]
        return [stay_a, stay_b], moved

    if aligned:
        waiting = begin_sum(0, [ff_grads[0][1], ff_grads[0][3]], [])
        (grad_second,) = gate([grad_second], waiting[0][:1])
    second_send = grad_second
    second_recv = [from_part(second_send, n) for n in range(1, group)]
    result_recv = [from_part(result_send[group - n - 1], n) for n in range(1, group)]
    result_keep, result_pass = finish_result(result_own, result_recv, sequences)

    def quad_swap(item, distance):
        return swap(item, "seq", seq_size, distance * group)

    result_near = quad_swap(result_pass, 1)

    chunk = width // seq_size
    grad_mid, grad_att, sums_mid, *out_grad = mid_back(
        mid,
        grad_second,
        second_recv,
        grad_rows,
        row_of(ln2_gain),
        out_w[0],
        att_first,
        att_last,
        chunk if aligned else 0,
    )

    def tile_back(t, after, cost_part=1):
        last = t == tiles - 1
        return attend_backward(
            qkv,
            grad_att,
            att_last if last else att_first,
            0 if last else t,
            logs_last if last else logs_first,
            0 if last else t * (LANES // head_dim),
            t,
            heads,
            head_dim,
            after,
            cost_part,
        )

    grad_tiles = [None] * tiles
    after = [result_keep]
    if aligned:
        keep, send = sum_second(*waiting, [grad_mid])
        moved = quad_swap(send, 1)
        sends = gate([ff_grads[1][1], ff_grads[1][3]], [keep])
        after = [result_keep, keep]
    grad_tiles[0] = tile_back(0, after, 64)
    result_pass = pass_on(result_keep, result_near, grad_tiles[:1])
    result_far = quad_swap(result_pass, 2)
    after = [result_pass]
    if aligned:
        unit_first = list(sum_third(keep, moved, [grad_tiles[0]]))
        unit_first[1] = quad_swap(unit_first[1], 2)
        after = [result_pass, unit_first[0]]
    grad_tiles[-1] = tile_back(tiles - 1, after, 64)
    after = []
    if aligned:
        waiting = begin_sum(1, sends, [grad_tiles[-1]])
        after = waiting[0][:1]
    for t in range(1, tiles - 1):
        grad_tiles[t] = tile_back(t, after)
    after = [result_far]
    if aligned:
        out_recv = from_part(out_grad[1], 1)
        keep, send = sum_second(*waiting, [grad_tiles[-2]])
        moved = quad_swap(send, 1)
        after = [keep, unit_first[1], result_far, out_recv]
    qkv_grad = project_weights(
        x_all,
        row_of(ln1_gain),
        row_of(ln1_bias),
        grad_tiles,
        group,
        sequences,
        aligned,
        after,
    )
    first_own, *found = project_rows(
        x_all,
        qkv_w,
        grad_tiles,
        sums_mid,
        up_sums,
        group,
        sequences,
        aligned,
        real,
        qkv_grad[:1],
    )
    first_send, (small, bias_sums) = found[: group - 1], found[group - 1 :]
    first_recv = [from_part(first_send[group - n - 1], n) for n in range(1, group)]
    after = []
    if aligned:
        small_rows = small.shape[0]
        packed = pack_attention(
            qkv_grad[0],
            from_part(qkv_grad[1], 1),
            out_grad[0],
            out_recv,
            small,
            from_part(small, 1),
            real,
            batch_size,
            [],
        )
        unit_second = list(sum_third(keep, moved, packed[:1]))
        unit_second[1] = quad_swap(unit_second[1], 2)
        after = packed[:1]
    row_parts = finish_rows(
        x_all, row_of(ln1_gain), grad_mid, first_own, first_recv, sequences, after
    )
    row_moved = over_quads(row_parts, group)
    if aligned:
        stay_a, pass_a, stay_b, pass_b = sum_first_attention(
            [packed[0], packed[2]],
            [swap(packed[1], "batch", batch_size, 1), swap(packed[3], "batch", batch_size, 2)],
            sequences // 2 * chunk,
            small_rows,
            [row_parts[0], row_moved[1]],
        )
        summed = sum_second_attention(
            [stay_a, stay_b],
            [swap(pass_a, "batch", batch_size, 2), swap(pass_b, "batch", batch_size, 1)],
            chunk,
            sequences,
            small_rows,
            [*row_moved[2:], unit_second[1]],
        )
        after = summed[:1]
        up_keep, up_send, down_grad = final_units(unit_first, unit_second, after)
        up_grad = final_join(up_keep, from_part(up_send, 1))
        qkv_final, out_final, small = final_attention(
            over_quads(summed, group), chunk, qkv_weight.shape[1] // batch_size, small_rows
        )
        small = small.reshape(-1)
    result = collect_halves(result_keep, result_near, result_far, group, after)
    result = result.reshape(tokens.shape)
    grad_in = collect(row_moved, group, after).reshape(tokens.shape)
    if not aligned:

        def spread(item, blocks):
            split = item.reshape(blocks, 1, -1)
            empty = jnp.zeros((blocks, group, split.shape[2]), F32)
            return lax.dynamic_update_slice(empty, split, (0, part, 0)).reshape(-1)

        bias_sums = bias_sums[0].reshape(tiles, 3, LANES).transpose(1, 0, 2)
        bias_sums = bias_sums.reshape(3, wide)[:, :real]
        small = jnp.concatenate(
            [
                small[0],
                small[1],
                spread(bias_sums[0], 1),
                spread(bias_sums[2], 1),
                sums_mid[2],
                sums_mid[0],
                sums_mid[1],
                spread(jnp.concatenate([item[0] for item in up_sums]), batch_size),
                sums_mid[3],
            ]
        )

        def scattered(item):
            item = lax.psum_scatter(item.astype(BF16), "seq", scatter_dimension=0, tiled=True)
            return lax.psum_scatter(item, "batch", scatter_dimension=1, tiled=True).astype(F32)

        def spread_columns(item, blocks):
            split = item.reshape(item.shape[0], blocks, 1, -1)
            empty = jnp.zeros((item.shape[0], blocks, group, split.shape[3]), item.dtype)
            filled = lax.dynamic_update_slice(empty, split, (0, 0, part, 0))
            return filled.reshape(item.shape[0], -1)

        up_full, down_full = [
            jnp.concatenate([item[e] for item in ff_grads], axis=1) for e in range(2)
        ]
        up_grad = scattered(spread_columns(up_full, batch_size))
        down_grad = scattered(spread_columns(down_full, batch_size).T)
        rows_full = qkv_grad[0].reshape(width, tiles, 3, LANES).transpose(0, 2, 1, 3)
        rows_full = rows_full.reshape(width, 3, wide)[..., :real]
        qkv_final = scattered(spread_columns(rows_full.reshape(width, -1), 3))
        out_final = scattered(spread_columns(out_grad[0][:real].T, 1).T)
        small = lax.psum(small, ("seq", "batch"))

    edges = [width] * 7 + [units, width]
    pieces, start = [], 0
    for size in edges:
        pieces.append(small[start : start + size])
        start += size
    return (
        result,
        grad_in,
        pieces[0],
        pieces[1],
        qkv_final,
        pieces[2],
        pieces[3],
        out_final,
        pieces[4],
        pieces[5],
        pieces[6],
        up_grad,
        pieces[7],
        down_grad,
        pieces[8],
    )


def solution(mesh):
    rows = P(None, "batch", "seq", None)
    split = P("seq", "batch")
    in_specs = (rows, P(None, "batch", "seq"), rows) + (P(),) * 13
    out_specs = (
        rows,
        rows,
        P(),
        P(),
        split,
        P(),
        P(),
        split,
        P(),
        P(),
        P(),
        split,
        P(),
        split,
        P(),
    )
    return jax.shard_map(
        on_device, mesh=mesh, in_specs=in_specs, out_specs=out_specs, check_vma=False
    )
```

```python
import jax
import jax.numpy as jnp
from jax import lax
from jax.experimental import pallas as pl
from jax.experimental.pallas import tpu as pltpu
from jax.sharding import PartitionSpec as P

HEADS = 20
EPS = 1e-05
LOG2E = 1.4426950408889634
ROWS = 256
F32 = jnp.float32
BF16 = jnp.bfloat16
LANES = 128


def dot(left, right):
    return jnp.dot(left, right, preferred_element_type=F32)


def dot_nt(left, right):
    return lax.dot_general(left, right, (((1,), (1,)), ((), ())), preferred_element_type=F32)


def norm_rows(rows_in):
    mean_val = jnp.mean(rows_in, axis=-1, keepdims=True)
    centered = rows_in - mean_val
    inv_std = lax.rsqrt(jnp.mean(centered * centered, axis=-1, keepdims=True) + EPS)
    return centered * inv_std, inv_std


def norm_back(scaled, normed, inv_std):
    inner = (
        scaled
        - jnp.mean(scaled, axis=-1, keepdims=True)
        - normed * jnp.mean(scaled * normed, axis=-1, keepdims=True)
    )
    return inner * inv_std


def params_of(mib):
    return pltpu.CompilerParams(vmem_limit_bytes=mib * 1024 * 1024)


def cost(flops, moved, trans=0, part=1):
    return pl.CostEstimate(
        flops=flops // part, bytes_accessed=moved // part, transcendentals=trans // part
    )


def sds(shape, dtype):
    return jax.ShapeDtypeStruct(shape, dtype)


VMEM = pl.BlockSpec(memory_space=pltpu.VMEM)
ANY = pl.BlockSpec(memory_space=pl.ANY)
HBM = pl.BlockSpec(memory_space=pltpu.HBM)


def run(body, operands, after=(), in_specs=None, out_specs=None, vmem=32, **more):
    count, extra = len(operands), len(after)

    def inner(*refs):
        body(*refs[:count], *refs[count + extra :])

    specs = [VMEM] * count if in_specs is None else list(in_specs)
    shapes = more["out_shape"]
    if out_specs is None:
        out_specs = [VMEM] * len(shapes) if isinstance(shapes, (list, tuple)) else VMEM
    return pl.pallas_call(
        inner,
        in_specs=specs + [ANY] * extra,
        out_specs=out_specs,
        compiler_params=params_of(vmem),
        **more,
    )(*operands, *after)


def far(item):
    return pltpu.with_memory_space_constraint(item, pltpu.HBM)


def gate(items, after):
    def body(*refs):
        del refs

    return pl.pallas_call(
        body,
        in_specs=[ANY] * (len(items) + len(after)),
        out_specs=[ANY] * len(items),
        out_shape=[sds(item.shape, item.dtype) for item in items],
        input_output_aliases={n: n for n in range(len(items))},
        cost_estimate=cost(0, 0),
        name="gate",
    )(*items, *after)


def place(group):
    spot = lax.axis_index("seq")
    return spot, lax.rem(spot, group), lax.div(spot, group)


def deal(item, group, after=()):
    count, rows, width = item.shape

    def body(in_ref, *out_refs):
        _, _, quad = place(group)
        for d in range(count):
            out_refs[d][...] = in_ref[quad ^ d]

    return run(
        body,
        [item],
        after,
        out_shape=[sds((rows, width), item.dtype)] * count,
        vmem=6,
        cost_estimate=cost(0, 4 * count * rows * width),
        name="deal",
    )


def collect(pieces, group, after):
    count = len(pieces)
    rows, width = pieces[0].shape

    def body(*refs):
        _, _, quad = place(group)
        for d in range(count):
            refs[count][quad ^ d] = refs[d][...]

    return run(
        body,
        pieces,
        after,
        out_shape=sds((count, rows, width), pieces[0].dtype),
        vmem=6,
        cost_estimate=cost(0, 4 * count * rows * width),
        name="collect",
    )


def stack(pieces, after):
    count = len(pieces)

    def body(*refs):
        for d in range(count):
            refs[count][d] = refs[d][...]

    return run(
        body,
        pieces,
        after,
        out_shape=sds((count,) + pieces[0].shape, pieces[0].dtype),
        vmem=12,
        cost_estimate=cost(0, 4 * count * pieces[0].size),
        name="stack",
    )


def swap(item, axis, size, distance):
    return lax.ppermute(item, axis, [(i, i ^ distance) for i in range(size)])


def over_quads(pieces, group):
    return [
        piece if d == 0 else swap(piece, "seq", len(pieces) * group, d * group)
        for d, piece in enumerate(pieces)
    ]


def pick_weights(qkv_weight, qkv_bias, out_weight, group, real, wide):
    width = qkv_weight.shape[0]
    tiles = wide // LANES

    def body(w_ref, b_ref, o_ref, wo_ref, bo_ref, *out_refs):
        _, part, _ = place(group)
        wo_ref[...] = jnp.zeros_like(wo_ref)
        bo_ref[...] = jnp.zeros_like(bo_ref)
        for ref in out_refs:
            ref[...] = jnp.zeros_like(ref)
        for c in range(group):

            @pl.when(part == c)
            def _(c=c):
                for p in range(3):
                    for t in range(tiles):
                        some = min(LANES, real - t * LANES)
                        src = p * width + c * real + t * LANES
                        dst = (3 * t + p) * LANES
                        wo_ref[:, dst : dst + some] = w_ref[:, src : src + some]
                        bo_ref[:, dst : dst + some] = b_ref[:, src : src + some]
                for n in range(group):
                    src = (c + n) % group * real
                    out_refs[n][0:real, :] = o_ref[src : src + real, :]

    return pl.pallas_call(
        body,
        out_shape=[sds((width, 3 * wide), BF16), sds((1, 3 * wide), F32)]
        + [sds((wide, width), BF16)] * group,
        compiler_params=params_of(24),
        cost_estimate=cost(0, 8 * 1024 * 1024),
        name="pick_weights",
    )(qkv_weight, qkv_bias, out_weight)


def by_pairs(live, visit):
    size = 2 if live % 2 == 0 else 1

    @pl.loop(0, live // size)
    def _(i):
        visit([i * size + e for e in range(size)])


def attend_tiles(query_at, keys_at, vals_at, att_ref, lse_ref, keys, vals, acc, tiles, heads, head_dim):
    per_tile = LANES // head_dim
    total = att_ref.shape[0]
    exp_scale = head_dim ** (-0.5) * LOG2E
    lane = lax.broadcasted_iota(jnp.int32, (1, LANES), 1)
    row = lax.broadcasted_iota(jnp.int32, (LANES, 1), 0)
    lse_ref[...] = jnp.zeros_like(lse_ref)
    vals[:, :, LANES:] = jnp.ones((per_tile, total, LANES), BF16)
    for n, t in enumerate(tiles):
        live = min(per_tile, heads - t * per_tile)
        key_t = keys_at(n).astype(F32).T
        val_f = vals_at(n).astype(F32)
        for j in range(live):
            keys[j] = jnp.where(row // head_dim == j, key_t, 0.0).astype(BF16)
            vals[j, :, :LANES] = jnp.where(lane // head_dim == j, val_f, 0.0).astype(BF16)
        acc[...] = jnp.zeros_like(acc)

        def visit(some, n=n):
            scores = [dot(query_at(n), keys[j]) for j in some]
            for item, j in zip(scores, some):
                row_max = jnp.max(item, axis=-1, keepdims=True) * exp_scale
                expd = jnp.exp2(item * exp_scale - row_max).astype(BF16)
                mixed = dot(expd, vals[j])
                den = mixed[:, LANES:]
                acc[...] += mixed[:, :LANES] / den
                lse_ref[...] = jnp.where(
                    lane == n * per_tile + j, row_max + jnp.log2(den), lse_ref[...]
                )

        by_pairs(live, visit)
        att_ref[:, n * LANES : (n + 1) * LANES] = acc[...].astype(BF16)


def attend_scratch(total, head_dim):
    per_tile = LANES // head_dim
    return [
        pltpu.VMEM((per_tile, LANES, total), BF16),
        pltpu.VMEM((per_tile, total, 2 * LANES), BF16),
        pltpu.VMEM((total, LANES), F32),
    ]


def attend_first(x_pieces, gain, shift, weight, bias, tiles, heads, head_dim):
    count = len(x_pieces)
    piece_rows, width = x_pieces[0].shape
    total = count * piece_rows
    cols_all = weight.shape[1]

    def body(*refs):
        x_refs = refs[:count]
        gain_ref, shift_ref, w_ref, bias_ref = refs[count : count + 4]
        x_ref, qkv_ref, att_ref, lse_ref, keys, vals, acc = refs[count + 4 :]
        for n in range(count):
            x_ref[n * piece_rows : (n + 1) * piece_rows, :] = x_refs[n][...]

        @pl.loop(0, total // ROWS)
        def _(i):
            rows = pl.ds(pl.multiple_of(i * ROWS, ROWS), ROWS)
            normed, _ = norm_rows(x_ref[rows, :].astype(F32))
            low = (normed * gain_ref[...] + shift_ref[...]).astype(BF16)
            qkv_ref[rows, :] = (dot(low, w_ref[...]) + bias_ref[...]).astype(BF16)

        def columns(at):
            return slice(at * LANES, (at + 1) * LANES)

        attend_tiles(
            lambda n: qkv_ref[:, columns(3 * n)],
            lambda n: qkv_ref[:, columns(3 * n + 1)],
            lambda n: qkv_ref[:, columns(3 * n + 2)],
            att_ref,
            lse_ref,
            keys,
            vals,
            acc,
            range(tiles),
            heads,
            head_dim,
        )

    return run(
        body,
        [*x_pieces, gain, shift, weight, bias],
        out_shape=[
            sds((total, width), BF16),
            sds((total, cols_all), BF16),
            sds((total, tiles * LANES), BF16),
            sds((total, LANES), F32),
        ],
        scratch_shapes=attend_scratch(total, head_dim),
        vmem=23,
        cost_estimate=cost(
            2 * total * width * cols_all + 4 * heads * total * total * 256,
            8 * 1024 * 1024,
            heads * total * total,
        ),
        name="attend_first",
    )


def attend_last(qkv, tile, heads, head_dim, after):
    total = qkv.shape[0]

    def body(qkv_ref, att_ref, lse_ref, keys, vals, acc):
        attend_tiles(
            lambda n: qkv_ref[:, 0:LANES],
            lambda n: qkv_ref[:, LANES : 2 * LANES],
            lambda n: qkv_ref[:, 2 * LANES : 3 * LANES],
            att_ref,
            lse_ref,
            keys,
            vals,
            acc,
            [tile],
            heads,
            head_dim,
        )

    live = heads - tile * (LANES // head_dim)
    return run(
        body,
        [qkv],
        after,
        grid=(1,),
        in_specs=[pl.BlockSpec((total, 3 * LANES), lambda i: (0, tile))],
        out_specs=[pl.BlockSpec((total, LANES), lambda i: (0, 0))] * 2,
        out_shape=[sds((total, LANES), BF16), sds((total, LANES), F32)],
        scratch_shapes=attend_scratch(total, head_dim),
        vmem=14,
        cost_estimate=cost(4 * live * total * total * 256, 2 * 1024 * 1024, live * total * total),
        name="attend_last",
    )


def gelu_parts(value):
    size = jnp.abs(value)
    near = pl.reciprocal(1.0 + (0.3275911 * 0.7071067811865476) * size, approx=True)
    bell = jnp.exp2(value * value * (-0.5 * LOG2E))
    poly = near * (
        0.5 * 0.254829592
        + near
        * (
            0.5 * -0.284496736
            + near * (0.5 * 1.421413741 + near * (0.5 * -1.453152027 + near * (0.5 * 1.061405429)))
        )
    )
    tail = poly * bell
    area = jnp.where(value < 0.0, tail, 1.0 - tail)
    return value * area, area + value * bell * 0.3989422804014327


class Units:
    def __init__(self, block, blocks, start, size, stride, quads, high):
        self.block, self.blocks, self.start, self.size = block, blocks, start, size
        self.stride, self.quads, self.high = stride, quads, high
        self.count = blocks * size
        self.chunk = 512 if self.count % 512 == 0 else 256
        self.packed = quads is not None

    def loads(self, part, hbm_up, hbm_down, hbm_bias, up_ref, down_ref, bias_ref, sem):
        copies = []
        for b in range(self.blocks):
            src = self.start
            if self.packed:
                src = pl.multiple_of((b * self.stride + part) * self.block, LANES) + self.start
            src = pl.ds(src, self.size)
            dst = pl.ds(b * self.size, self.size)
            copies.append(
                pltpu.make_async_copy(hbm_up.at[:, src], up_ref.at[:, dst], sem.at[2 * b])
            )
            copies.append(
                pltpu.make_async_copy(hbm_down.at[src, :], down_ref.at[dst, :], sem.at[2 * b + 1])
            )
            bias_ref[0:1, dst] = hbm_bias[:, src]
        return copies

    def grad_shapes(self, width):
        if self.packed:
            return [pltpu.HBM((2, self.quads, self.high, self.size), BF16)] * 4
        return [sds((width, self.count), BF16)] * 2

    def scratch(self, total, width):
        grads = (self.blocks, self.quads, self.high, self.size) if self.packed else (8, LANES)
        return [
            pltpu.VMEM(grads, BF16),
            pltpu.VMEM(grads, BF16),
            pltpu.SemaphoreType.DMA((8,)),
            pltpu.VMEM((total, self.count), BF16),
            pltpu.VMEM((total, self.count), BF16),
            pltpu.VMEM((width, self.count), BF16),
            pltpu.VMEM((self.count, width), BF16),
            pltpu.VMEM((8, self.count), F32),
            pltpu.SemaphoreType.DMA((2 * self.blocks,)),
        ]

    def compute(self, part, second, second_t, grad, grad_t, acc, gs, ubg, scratch, outs):
        up_slots, down_slots, out_sem, acts, grad_pres, up_ref, down_ref, bias_ref, _ = scratch
        if not self.packed:
            up_slots, down_slots = outs
        quad = lax.div(lax.axis_index("seq"), self.stride)
        mine = lax.axis_index("batch")

        def enter(i):
            rows = slice(i * ROWS, (i + 1) * ROWS)
            pre = dot(second[rows, :], up_ref[...]) + bias_ref[0:1, :]
            return pre, dot_nt(grad[rows, :], down_ref[...])

        def weights(n):
            first, last = n * self.chunk, (n + 1) * self.chunk
            up_grad = dot(second_t[...], grad_pres[:, first:last]).astype(BF16)
            down_grad = dot(grad_t[...], acts[:, first:last]).astype(BF16)
            if not self.packed:
                up_slots[:, first:last] = up_grad
                down_slots[:, first:last] = down_grad
                return
            at = first
            while at < last:
                block = at // self.size
                stop = min(last, (block + 1) * self.size)
                src = slice(at - first, stop - first)
                dst = slice(at - block * self.size, stop - block * self.size)
                for m in range(self.blocks):
                    rows = slice(m * self.high, (m + 1) * self.high)
                    up_slots[block ^ mine, m ^ quad, :, dst] = up_grad[rows, src]
                    down_slots[m ^ mine, block ^ quad, :, dst] = down_grad[rows, src]
                at = stop

        ready = enter(0)
        chunks = second.shape[0] // ROWS
        for i in range(chunks):
            ahead = enter(i + 1) if i + 1 < chunks else None
            rows = slice(i * ROWS, (i + 1) * ROWS)
            pre, grad_act = ready
            value, slope = gelu_parts(pre)
            act = value.astype(BF16)
            grad_pre = (grad_act * slope).astype(BF16)
            acts[rows, :] = act
            grad_pres[rows, :] = grad_pre
            ubg[0:1, :] += jnp.sum(grad_pre.astype(F32), axis=0, keepdims=True)
            acc[rows, :] += dot(act, down_ref[...])
            gs[rows, :] += dot_nt(grad_pre, up_ref[...])
            ready = ahead
        for n in range(self.count // self.chunk):
            weights(n)
        stores = []
        if self.packed:
            order = ((up_slots, (0, 2)), (up_slots, (1, 3)), (down_slots, (0, 1)), (down_slots, (2, 3)))
            for m, (source, slots) in enumerate(order):
                for n in range(2):
                    stores.append(
                        pltpu.make_async_copy(
                            source.at[slots[n]], outs[m].at[n], out_sem.at[2 * m + n]
                        )
                    )
        return stores


def feed_first(
    rows_all, att_first, att_last, cot_pieces, out_w, out_b, gain, shift, up, up_b, down, down_b, units
):
    pieces = len(att_first)
    total, width = rows_all.shape
    piece_rows = total // pieces
    count = len(cot_pieces)
    cot_rows = total // count
    split = att_first[0].shape[1]
    grads = units.grad_shapes(width)

    def body(*refs):
        x_ref, refs = refs[0], refs[1:]
        att_refs, refs = refs[: 2 * pieces], refs[2 * pieces :]
        cot_refs, refs = refs[:count], refs[count:]
        wo_refs, refs = refs[:pieces], refs[pieces:]
        ob_ref, gain_ref, shift_ref, up_hbm, ub_ref, down_hbm, db_ref = refs[:7]
        mid_ref, second, second_t, grad, grad_t, own_ref, low_ref, ubg, refs = *refs[7:15], refs[15:]
        send_refs, refs = refs[: pieces - 1], refs[pieces - 1 :]
        outs, refs = refs[: len(grads)], refs[len(grads) :]
        acc, gs, mid_rows, mid_sem, *scratch = refs
        _, part, _ = place(pieces)
        loads = units.loads(part, up_hbm, down_hbm, ub_ref, *scratch[5:])
        for load in loads:
            load.start()
        ubg[...] = jnp.zeros_like(ubg)
        masked = jnp.zeros((1, width), F32)
        for ref in cot_refs:
            masked = masked + ref[cot_rows : cot_rows + 1, :].astype(F32)
        factor = total / (4.0 * masked)
        for n in range(count):
            scaled = cot_refs[n][0:cot_rows, :].astype(F32) * factor
            dst = slice(n * cot_rows, (n + 1) * cot_rows)
            grad[dst, :] = scaled.astype(BF16)

        for h in range(pieces):

            @pl.loop(0, piece_rows // ROWS)
            def _(i, h=h):
                at = pl.multiple_of(i * ROWS, ROWS)
                dst = pl.ds(h * piece_rows + at, ROWS)
                mid = x_ref[dst, :].astype(F32) + ob_ref[...]
                for n in range(pieces):
                    src = pl.ds(((h - n) % pieces) * piece_rows + at, ROWS)
                    mid = mid + dot(att_refs[2 * n][src, :], wo_refs[n][0:split, :])
                    mid = mid + dot(att_refs[2 * n + 1][src, :], wo_refs[n][split:, :])
                mid_rows[dst, :] = mid
                normed, _ = norm_rows(mid)
                low = normed * gain_ref[...] + shift_ref[...]
                second[dst, :] = low.astype(BF16)
                second_t[:, dst] = low.T.astype(BF16)
                grad_t[:, dst] = grad[dst, :].astype(F32).T.astype(BF16)
                acc[dst, :] = mid + db_ref[...] if h == 0 else jnp.zeros((ROWS, width), F32)
                gs[dst, :] = jnp.zeros((ROWS, width), F32)

        keep_mid = pltpu.make_async_copy(mid_rows, mid_ref, mid_sem)
        keep_mid.start()
        for load in loads:
            load.wait()
        stores = units.compute(
            part, second, second_t, grad, grad_t, acc, gs, ubg, scratch, outs
        )
        for store in stores:
            store.start()
        keep_mid.wait()
        own_ref[...] = acc[0:piece_rows, :]
        low_ref[...] = gs[...].astype(BF16)
        for h in range(1, pieces):
            send_refs[h - 1][...] = acc[h * piece_rows : (h + 1) * piece_rows, :].astype(BF16)
        for store in stores:
            store.wait()

    att_all = [item for pair in zip(att_first, att_last) for item in pair]
    turned = sds((width, total), BF16)
    flat = sds((total, width), BF16)
    half = sds((piece_rows, width), F32)
    return run(
        body,
        [
            rows_all,
            *att_all,
            *cot_pieces,
            *out_w,
            out_b,
            gain,
            shift,
            far(up),
            up_b,
            far(down),
            down_b,
        ],
        in_specs=[VMEM] * (1 + 3 * pieces + count) + [VMEM, VMEM, VMEM, HBM, VMEM, HBM, VMEM],
        out_specs=[HBM] + [VMEM] * (6 + pieces) + [HBM if units.packed else VMEM] * len(grads),
        out_shape=[pltpu.HBM((total, width), F32), flat, turned, flat, turned, half, flat, sds((8, units.count), F32)]
        + [sds((piece_rows, width), BF16)] * (pieces - 1)
        + grads,
        scratch_shapes=[pltpu.VMEM((total, width), F32)] * 3
        + [pltpu.SemaphoreType.DMA]
        + units.scratch(total, width),
        vmem=26,
        cost_estimate=cost(12 * total * width * units.count, 24 * 1024 * 1024, total * units.count),
        name="feed_first",
    )


def feed_second(second, second_t, grad, grad_t, own_first, low_first, sends, up, up_b, down, units):
    pieces = 1 + len(sends)
    total, width = second.shape
    piece_rows = total // pieces
    grads = units.grad_shapes(width)

    def body(*refs):
        second, second_t, grad, grad_t, own_in, low_in, up_hbm, ub_ref, down_hbm, refs = (
            *refs[:9],
            refs[9:],
        )
        send_ins, refs = refs[: pieces - 1], refs[pieces - 1 :]
        own_ref, low_ref, ubg, refs = refs[0], refs[1], refs[2], refs[3:]
        send_refs, refs = refs[: pieces - 1], refs[pieces - 1 :]
        outs, (acc, gs), scratch = refs[: len(grads)], refs[len(grads) :][:2], refs[len(grads) + 2 :]
        _, part, _ = place(pieces)
        loads = units.loads(part, up_hbm, down_hbm, ub_ref, *scratch[5:])
        for load in loads:
            load.start()
        ubg[...] = jnp.zeros_like(ubg)
        acc[...] = jnp.zeros_like(acc)
        gs[...] = jnp.zeros_like(gs)
        for load in loads:
            load.wait()
        stores = units.compute(
            part, second, second_t, grad, grad_t, acc, gs, ubg, scratch, outs
        )
        for store in stores:
            store.start()
        low_ref[...] = (gs[...] + low_in[...].astype(F32)).astype(BF16)
        own_ref[...] = acc[0:piece_rows, :] + own_in[...]
        for h in range(1, pieces):
            item = acc[h * piece_rows : (h + 1) * piece_rows, :] + send_ins[h - 1][...].astype(F32)
            send_refs[h - 1][...] = item.astype(BF16)
        for store in stores:
            store.wait()

    return run(
        body,
        [
            second,
            second_t,
            grad,
            grad_t,
            own_first,
            low_first,
            far(up),
            up_b,
            far(down),
            *sends,
        ],
        in_specs=[VMEM] * 6 + [HBM, VMEM, HBM] + [VMEM] * (pieces - 1),
        out_specs=[VMEM] * (2 + pieces) + [HBM if units.packed else VMEM] * len(grads),
        out_shape=[
            sds((piece_rows, width), F32),
            sds((total, width), BF16),
            sds((8, units.count), F32),
        ]
        + [sds((piece_rows, width), BF16)] * (pieces - 1)
        + grads,
        scratch_shapes=[pltpu.VMEM((total, width), F32)] * 2 + units.scratch(total, width),
        vmem=30,
        cost_estimate=cost(12 * total * width * units.count, 24 * 1024 * 1024, total * units.count),
        name="feed_second",
    )


def mid_back(mid, grad_second, received, grad_rows, gain, out_w, att_first, att_last, chunk):
    pieces = 1 + len(received)
    total, width = mid.shape
    per_piece = total // pieces // ROWS
    split = att_first.shape[1]
    wide = split + att_last.shape[1]
    steps = total // ROWS

    def body(*refs):
        mid_ref, gs_ref, refs = refs[0], refs[1], refs[2:]
        recv_refs, refs = refs[: pieces - 1], refs[pieces - 1 :]
        go_ref, gain_ref, wo_ref, att_ref, last_ref = refs[:5]
        gm_ref, do_ref, sums_ref, *dwo_refs, acc = refs[5:]
        i = pl.program_id(0)

        @pl.when(i == 0)
        def _():
            sums_ref[...] = jnp.zeros_like(sums_ref)
            acc[...] = jnp.zeros_like(acc)

        normed, inv_std = norm_rows(mid_ref[...])
        grad = gs_ref[...].astype(F32)
        for ref in recv_refs:
            grad = grad + ref[...].astype(F32)
        go = go_ref[...].astype(F32)
        grad_mid = go + norm_back(grad * gain_ref[...], normed, inv_std)
        low = grad_mid.astype(BF16)
        do_ref[...] = dot_nt(low, wo_ref[...]).astype(BF16)
        acc[0:split, :] += dot(att_ref[...].astype(F32).T.astype(BF16), low)
        acc[split:, :] += dot(last_ref[...].astype(F32).T.astype(BF16), low)

        @pl.when(i < per_piece)
        def _():
            gm_ref[...] = grad_mid
            for n, item in enumerate((grad * normed, grad, low.astype(F32), go)):
                sums_ref[n : n + 1, :] += jnp.sum(item, axis=0, keepdims=True)

        @pl.when(i == steps - 1)
        def _():
            if chunk == 0:
                dwo_refs[0][...] = acc[...].astype(BF16)
                return
            _, part, _ = place(pieces)
            for c in range(pieces):

                @pl.when(part == c)
                def _(c=c):
                    for n in range(dwo_refs[0].shape[0]):
                        for e in range(pieces):
                            at = (n * pieces + (c + e) % pieces) * chunk
                            dwo_refs[e][n] = acc[at : at + chunk, :].astype(BF16)

    def rows_of(columns):
        return pl.BlockSpec((ROWS, columns), lambda i: (i, 0))

    def theirs(n):
        def index(i):
            piece = lax.rem(lax.div(i, per_piece) + pieces - n, pieces)
            return piece * per_piece + lax.rem(i, per_piece), 0

        return pl.BlockSpec((ROWS, width), index)

    def whole(*shape):
        return pl.BlockSpec(shape, lambda i: (0,) * len(shape))

    if chunk == 0:
        grads = [((wide, width), sds((wide, width), BF16))]
    else:
        shape = (width // (pieces * pieces * chunk), chunk, width)
        grads = [(shape, pltpu.HBM(shape, BF16))] * pieces
    return run(
        body,
        [
            far(mid),
            far(grad_second),
            *received,
            far(grad_rows),
            gain,
            out_w,
            far(att_first),
            far(att_last),
        ],
        grid=(steps,),
        in_specs=[rows_of(width), rows_of(width)]
        + [theirs(n) for n in range(1, pieces)]
        + [rows_of(width), whole(1, width), whole(wide, width), rows_of(split), rows_of(wide - split)],
        out_specs=[
            pl.BlockSpec((ROWS, width), lambda i: (jnp.minimum(i, per_piece - 1), 0)),
            rows_of(wide),
            whole(8, width),
        ]
        + [whole(*shape) for shape, _ in grads],
        out_shape=[
            sds((per_piece * ROWS, width), F32),
            sds((total, wide), BF16),
            sds((8, width), F32),
        ]
        + [item for _, item in grads],
        scratch_shapes=[pltpu.VMEM((wide, width), F32)],
        vmem=16,
        cost_estimate=cost(4 * total * width * wide, 14 * 1024 * 1024),
        name="mid_back",
    )


def attend_backward(
    qkv, grad_att, att, att_tile, logs, lane_first, tile, heads, head_dim, after=(), part=1
):
    total = qkv.shape[0]
    per_tile = LANES // head_dim
    live = min(per_tile, heads - tile * per_tile)
    scale = head_dim ** (-0.5)
    exp_scale = scale * LOG2E

    def body(qkv_ref, do_ref, att_ref, lse_ref, out_ref, *scratch):
        km, vm, qm, dm, key_t, query_t, do_t, dq_t, lse_t, mean_t = scratch
        lane = lax.broadcasted_iota(jnp.int32, (1, LANES), 1)
        lse_t[...] = lse_ref[...].T
        query = qkv_ref[:, 0:LANES].astype(F32)
        key = qkv_ref[:, LANES : 2 * LANES].astype(F32)
        val = qkv_ref[:, 2 * LANES : 3 * LANES].astype(F32)
        upstream = do_ref[...].astype(F32)
        both_t = (upstream * att_ref[...].astype(F32)).T
        for j in range(live):
            mean_t[j : j + 1, :] = jnp.sum(
                both_t[j * head_dim : (j + 1) * head_dim, :], axis=0, keepdims=True
            )
        query_t[...] = query.T.astype(BF16)
        do_t[...] = upstream.T.astype(BF16)
        key_t[...] = key.T.astype(BF16)
        for j in range(live):
            mine = lane // head_dim == j
            km[j] = jnp.where(mine, key, 0.0).astype(BF16)
            vm[j] = jnp.where(mine, val, 0.0).astype(BF16)
            qm[j] = jnp.where(mine, query, 0.0).astype(BF16)
            dm[j] = jnp.where(mine, upstream, 0.0).astype(BF16)
        dq_t[...] = jnp.zeros_like(dq_t)

        @pl.loop(0, total // ROWS)
        def _(i):
            rows = pl.ds(pl.multiple_of(i * ROWS, ROWS), ROWS)
            grad_key = jnp.zeros((ROWS, LANES), F32)
            grad_val = jnp.zeros((ROWS, LANES), F32)

            def enter(j):
                return dot(km[j, rows, :], query_t[...]), dot(vm[j, rows, :], do_t[...])

            ready = enter(0)
            for j in range(live):
                ahead = enter(j + 1) if j + 1 < live else None
                scores, grad_prob = ready
                head = lane_first + j
                own = slice(j * head_dim, (j + 1) * head_dim)
                probs = jnp.exp2(scores * exp_scale - lse_t[head : head + 1, :])
                grad_scores = (probs * (grad_prob - mean_t[j : j + 1, :])).astype(BF16)
                grad_val = grad_val + dot(probs.astype(BF16), dm[j])
                grad_key = grad_key + dot(grad_scores, qm[j])
                dq_t[own, :] += dot(key_t[own, rows], grad_scores)
                ready = ahead
            out_ref[rows, LANES : 2 * LANES] = (grad_key * scale).astype(BF16)
            out_ref[rows, 2 * LANES : 3 * LANES] = grad_val.astype(BF16)

        out_ref[:, 0:LANES] = (dq_t[...].T * scale).astype(BF16)

    masked = pltpu.VMEM((live, total, LANES), BF16)
    turned = pltpu.VMEM((LANES, total), BF16)
    turned_f = pltpu.VMEM((LANES, total), F32)
    return run(
        body,
        [qkv, grad_att, att, logs],
        after,
        grid=(1,),
        in_specs=[
            pl.BlockSpec((total, 3 * LANES), lambda i: (0, tile)),
            pl.BlockSpec((total, LANES), lambda i: (0, tile)),
            pl.BlockSpec((total, LANES), lambda i: (0, att_tile)),
            pl.BlockSpec((total, LANES), lambda i: (0, 0)),
        ],
        out_specs=pl.BlockSpec((total, 3 * LANES), lambda i: (0, 0)),
        out_shape=sds((total, 3 * LANES), BF16),
        scratch_shapes=[masked] * 4
        + [turned] * 3
        + [turned_f] * 2
        + [pltpu.VMEM((8, total), F32)],
        vmem=17,
        cost_estimate=cost(
            2 * live * total * total * 256 * 5, 3 * 1024 * 1024, live * total * total, part
        ),
        name="attend_backward",
    )


def project_weights(rows_all, gain, shift, grad_tiles, pieces, quads, packed, after):
    total, width = rows_all.shape
    tiles = len(grad_tiles)
    tile_cols = grad_tiles[0].shape[1]
    cols_all = tiles * tile_cols
    chunk = width // (quads * pieces)

    def body(*refs):
        x_ref, gain_ref, shift_ref, refs = refs[0], refs[1], refs[2], refs[3:]
        dq_refs, (*dw_refs, low_t, part_ref) = refs[:tiles], refs[tiles:]
        _, part, quad = place(pieces)

        @pl.loop(0, total // ROWS)
        def _(i):
            rows = pl.ds(pl.multiple_of(i * ROWS, ROWS), ROWS)
            normed, _ = norm_rows(x_ref[rows, :].astype(F32))
            low_t[:, rows] = (normed * gain_ref[...] + shift_ref[...]).T.astype(BF16)

        for t in range(tiles):
            cols = slice(t * tile_cols, (t + 1) * tile_cols)
            part_ref[...] = dot(low_t[...], dq_refs[t][...]).astype(BF16)
            if not packed:
                dw_refs[0][:, cols] = part_ref[...]
                continue
            for c in range(pieces):

                @pl.when(part == c)
                def _(c=c, cols=cols):
                    for q in range(quads):
                        for e in range(pieces):
                            at = (q * pieces + (c + e) % pieces) * chunk
                            dw_refs[e][q ^ quad, :, cols] = part_ref[at : at + chunk, :]

    if packed:
        grads = [sds((quads, chunk, cols_all), BF16)] * pieces
    else:
        grads = [sds((width, cols_all), BF16)]
    return run(
        body,
        [rows_all, gain, shift, *grad_tiles],
        after,
        out_shape=grads,
        scratch_shapes=[pltpu.VMEM((width, total), BF16), pltpu.VMEM((width, tile_cols), BF16)],
        vmem=12,
        cost_estimate=cost(2 * total * width * cols_all, 6 * 1024 * 1024),
        name="project_weights",
    )


def project_rows(
    rows_all, weight, grad_tiles, sums_mid, up_sums, pieces, quads, packed, real, after
):
    total, width = rows_all.shape
    piece_rows = total // pieces
    cols_all = weight.shape[1]
    tiles = len(grad_tiles)
    tile_cols = cols_all // tiles

    def body(*refs):
        x_ref, w_ref, mid_ref, refs = *refs[:3], refs[3:]
        ups_refs, refs = refs[: len(up_sums)], refs[len(up_sums) :]
        dq_refs, refs = refs[:tiles], refs[tiles:]
        own_ref, refs = refs[0], refs[1:]
        send_refs, (sums_ref, bias_ref) = refs[: pieces - 1], refs[pieces - 1 :]
        _, part, _ = place(pieces)
        sums_ref[...] = jnp.zeros_like(sums_ref)
        bias_ref[...] = jnp.zeros_like(bias_ref)
        for h in range(pieces):

            @pl.loop(0, piece_rows // ROWS)
            def _(i, h=h):
                at = pl.multiple_of(i * ROWS, ROWS)
                src = pl.ds(at, ROWS)
                rows = pl.ds(h * piece_rows + at, ROWS)
                normed, _ = norm_rows(x_ref[rows, :].astype(F32))
                grad = jnp.zeros((ROWS, width), F32)
                for t in range(tiles):
                    grad_rows = dq_refs[t][rows, :]
                    cols = slice(t * tile_cols, (t + 1) * tile_cols)
                    grad = grad + dot_nt(grad_rows, w_ref[:, cols])
                    bias_ref[0:1, cols] += jnp.sum(grad_rows.astype(F32), axis=0, keepdims=True)
                if h == 0:
                    own_ref[src, :] = grad
                else:
                    send_refs[h - 1][src, :] = grad.astype(BF16)
                sums_ref[0:1, :] += jnp.sum(grad * normed, axis=0, keepdims=True)
                sums_ref[1:2, :] += jnp.sum(grad, axis=0, keepdims=True)

        if not packed:
            return
        for row, src in ((4, 2), (5, 0), (6, 1), (15, 3)):
            sums_ref[row : row + 1, :] = mid_ref[src : src + 1, :]
        for c in range(pieces):

            @pl.when(part == c)
            def _(c=c):
                for row, p in ((2, 0), (3, 2)):
                    mine = jnp.concatenate(
                        [
                            bias_ref[0:1, (3 * t + p) * LANES :][:, : min(LANES, real - t * LANES)]
                            for t in range(tiles)
                        ],
                        axis=1,
                    )
                    sums_ref[row : row + 1, c * real : (c + 1) * real] = mine
                for n in range(quads):
                    row = 7 + n * pieces + c
                    start = 0
                    for ref in ups_refs:
                        size = ref.shape[1] // quads
                        here = ref[0:1, n * size : (n + 1) * size]
                        sums_ref[row : row + 1, start : start + size] = here
                        start += size

    return run(
        body,
        [rows_all, weight, sums_mid, *up_sums, *grad_tiles],
        after,
        out_shape=[sds((piece_rows, width), F32)]
        + [sds((piece_rows, width), BF16)] * (pieces - 1)
        + [sds((16, width), F32), sds((8, cols_all), F32)],
        vmem=12,
        cost_estimate=cost(2 * total * width * cols_all, 8 * 1024 * 1024),
        name="project_rows",
    )


def finish_rows(rows_all, gain, grad_mid, grad_own, received, count, after):
    rows, width = grad_mid.shape
    others = len(received)
    piece = rows // count
    per_step = ROWS // piece

    def body(*refs):
        x_ref, gain_ref, gm_ref, own_ref, refs = refs[0], refs[1], refs[2], refs[3], refs[4:]
        recv_refs, out_refs = refs[:others], refs[others:]
        for n in range(rows // ROWS):
            at = slice(n * ROWS, (n + 1) * ROWS)
            normed, inv_std = norm_rows(x_ref[at, :].astype(F32))
            grad = own_ref[at, :]
            for ref in recv_refs:
                grad = grad + ref[at, :].astype(F32)
            done = gm_ref[at, :] + norm_back(grad * gain_ref[...], normed, inv_std)
            for e in range(per_step):
                out_refs[n * per_step + e][...] = done[e * piece : (e + 1) * piece, :].astype(BF16)

    return run(
        body,
        [rows_all, gain, grad_mid, grad_own, *received],
        after,
        out_shape=[sds((piece, width), BF16)] * count,
        vmem=12,
        cost_estimate=cost(20 * rows * width, 6 * 1024 * 1024),
        name="finish_rows",
    )


def finish_result(own, received, count):
    rows, width = own.shape
    others = len(received)
    piece = rows // count

    def body(*refs):
        out_refs = refs[1 + others :]
        for n in range(count):
            at = slice(n * piece, (n + 1) * piece)
            total = refs[0][at, :]
            for ref in refs[1 : 1 + others]:
                total = total + ref[at, :].astype(F32)
            out_refs[n % 2][n // 2] = total.astype(BF16)

    return run(
        body,
        [far(own), *received],
        out_shape=[sds((count // 2, piece, width), BF16)] * 2,
        vmem=8,
        cost_estimate=cost(2 * rows * width, 3 * 1024 * 1024),
        name="finish_result",
    )


def pass_on(keep, received, after):
    def body(keep_ref, recv_ref, out_ref):
        out_ref[0] = keep_ref[1]
        out_ref[1] = recv_ref[1]

    return run(
        body,
        [keep, received],
        after,
        out_shape=sds(keep.shape, keep.dtype),
        vmem=6,
        cost_estimate=cost(0, 4 * keep.size),
        name="pass_on",
    )


def collect_halves(keep, near, far, group, after):
    _, rows, width = keep.shape

    def body(keep_ref, near_ref, far_ref, out_ref):
        _, _, quad = place(group)
        out_ref[quad] = keep_ref[0]
        out_ref[quad ^ 1] = near_ref[0]
        out_ref[quad ^ 2] = far_ref[0]
        out_ref[quad ^ 3] = far_ref[1]

    return run(
        body,
        [keep, near, far],
        after,
        out_shape=sds((4, rows, width), keep.dtype),
        vmem=6,
        cost_estimate=cost(0, 16 * rows * width),
        name="collect_halves",
    )


def two_parts(item):
    first = item.astype(BF16)
    return first, (item - first.astype(F32)).astype(BF16)


def pack_attention(
    qkv_keep, qkv_recv, out_keep, out_recv, small, small_recv, real, blocks, after
):
    quads, chunk, cols_all = qkv_keep.shape
    wide = cols_all // 3
    tiles = wide // LANES
    width = out_keep.shape[2]
    qkv_lanes = 6 * real // blocks
    out_lanes = width // blocks
    lanes = qkv_lanes + out_lanes
    halves = quads // 2
    slot = halves * chunk
    small_rows = small.shape[0]

    def body(qk_ref, qr_ref, ok_ref, or_ref, small_ref, srecv_ref, *out_refs):
        _, part, quad = place(2)
        mine = lax.axis_index("batch")
        slots = out_refs[4]

        def heads_of(rows, p):
            return [
                rows[:, (3 * t + p) * LANES : (3 * t + p) * LANES + min(LANES, real - t * LANES)]
                for t in range(tiles)
            ]

        for c in range(2):

            @pl.when(part == c)
            def _(c=c):
                for q in range(quads):
                    pair = (qk_ref[q], qr_ref[q])
                    if c == 1:
                        pair = pair[::-1]
                    parts = []
                    for p in range(3):
                        parts += heads_of(pair[0], p) + heads_of(pair[1], p)
                    row = jnp.concatenate(parts, axis=1)
                    for b in range(blocks):
                        slots[b ^ mine, q, :, 0:qkv_lanes] = row[
                            :, b * qkv_lanes : (b + 1) * qkv_lanes
                        ]
                for e, ref in enumerate((ok_ref, or_ref)):
                    for n in range(halves):
                        q = ((c + e) % 2) * halves + n
                        for b in range(blocks):
                            slots[b ^ mine, q ^ quad, :, qkv_lanes:lanes] = ref[
                                n, :, b * out_lanes : (b + 1) * out_lanes
                            ]

        for n, order in enumerate(((0, 2), (1, 3), (0, 1), (2, 3))):
            for e in range(2):
                for f in range(halves):
                    at = e * slot + f * chunk
                    src = f if n < 2 else halves + f
                    out_refs[n][at : at + chunk, :] = slots[order[e], src]
        parts = two_parts(small_ref[...] + srecv_ref[...])
        for n in range(2):
            for e in range(2):
                at = 2 * slot + e * small_rows
                out_refs[n][at : at + small_rows, :] = parts[e]

    first = sds((2 * slot + 2 * small_rows, lanes), BF16)
    other = sds((2 * slot, lanes), BF16)
    return run(
        body,
        [qkv_keep, qkv_recv, out_keep, out_recv, small, small_recv],
        after,
        out_shape=[first, first, other, other],
        scratch_shapes=[pltpu.VMEM((blocks, quads, chunk, lanes), BF16)],
        vmem=12,
        cost_estimate=cost(0, 4 * 1024 * 1024),
        name="pack_attention",
    )


def sum_first(keeps, received, after=()):
    count = len(keeps)
    shape = keeps[0].shape[1:]

    def body(*refs):
        for n in range(count):
            for e in range(2):
                total = refs[n][e].astype(F32) + refs[count + n][e].astype(F32)
                refs[2 * count + 2 * n + e][...] = total.astype(BF16)

    return run(
        body,
        [*keeps, *received],
        after,
        out_shape=[pltpu.HBM(shape, BF16), sds(shape, BF16)] * count,
        vmem=12,
        cost_estimate=cost(0, 6 * count * keeps[0].size),
        name="sum_first",
    )


def sum_second(keeps, received, after=()):
    quads, rows, width = keeps[0].shape

    def body(ka, kb, ra, rb, keep_ref, send_ref):
        for d in range(quads):
            ref = send_ref if d % 2 else keep_ref
            for e, (keep, recv) in enumerate(((ka, ra), (kb, rb))):
                total = keep[d].astype(F32) + recv[d].astype(F32)
                ref[d // 2, e] = total.astype(BF16)

    return run(
        body,
        [*keeps, *received],
        after,
        out_shape=[pltpu.HBM((quads // 2, 2, rows, width), BF16)] * 2,
        vmem=10,
        cost_estimate=cost(0, 12 * keeps[0].size),
        name="sum_second",
    )


def sum_third(keep, received, after=()):
    def body(keep_ref, recv_ref, stay_ref, pass_ref):
        for ref, e in ((stay_ref, 0), (pass_ref, 1)):
            ref[...] = (keep_ref[e].astype(F32) + recv_ref[e].astype(F32)).astype(BF16)

    return run(
        body,
        [keep, received],
        after,
        out_shape=[sds(keep.shape[1:], BF16)] * 2,
        vmem=6,
        cost_estimate=cost(0, 6 * keep.size),
        name="sum_third",
    )


def small_sum(refs, rows, count):
    total = None
    for ref in refs:
        for e in range(2):
            item = ref[rows + e * count : rows + (e + 1) * count, :].astype(F32)
            total = item if total is None else total + item
    return total


def sum_first_attention(keeps, received, slot, small_rows, after):
    lanes = keeps[0].shape[1]

    def body(ka, kb, ra, rb, stay_a, pass_a, stay_b, pass_b):
        parts = two_parts(small_sum((ka, ra), 2 * slot, small_rows))
        for keep, recv, stay, on in ((ka, ra, stay_a, pass_a), (kb, rb, stay_b, pass_b)):
            for e, ref in enumerate((stay, on)):
                at = slice(e * slot, (e + 1) * slot)
                ref[0:slot, :] = (keep[at, :].astype(F32) + recv[at, :].astype(F32)).astype(BF16)
        for ref in (stay_a, pass_a):
            for e in range(2):
                ref[slot + e * small_rows : slot + (e + 1) * small_rows, :] = parts[e]

    first = sds((slot + 2 * small_rows, lanes), BF16)
    other = sds((slot, lanes), BF16)
    return run(
        body,
        [*keeps, *received],
        after,
        out_shape=[first, first, other, other],
        vmem=8,
        cost_estimate=cost(0, 3 * 1024 * 1024),
        name="sum_first_attention",
    )


def sum_second_attention(keeps, received, chunk, quads, small_rows, after):
    lanes = keeps[0].shape[1]
    halves = quads // 2
    slot = halves * chunk

    def body(ka, kb, ra, rb, *out_refs):
        parts = two_parts(small_sum((ka, ra), slot, small_rows))
        for d in range(quads):
            keep, recv = ((ka, ra), (kb, rb))[d // halves]
            at = slice(d % halves * chunk, (d % halves + 1) * chunk)
            total = keep[at, :].astype(F32) + recv[at, :].astype(F32)
            out_refs[d][0:chunk, :] = total.astype(BF16)
            for e in range(2):
                at = chunk + e * small_rows
                out_refs[d][at : at + small_rows, :] = parts[e]

    return run(
        body,
        [*keeps, *received],
        after,
        out_shape=[sds((chunk + 2 * small_rows, lanes), BF16)] * quads,
        vmem=8,
        cost_estimate=cost(0, 2 * 1024 * 1024),
        name="sum_second_attention",
    )


def final_attention(pieces, chunk, qkv_lanes, small_rows):
    lanes = pieces[0].shape[1]
    count = len(pieces)

    def body(*refs):
        total = refs[0][0:chunk, :].astype(F32)
        for ref in refs[1:count]:
            total = total + ref[0:chunk, :].astype(F32)
        refs[count][...] = total[:, :qkv_lanes]
        refs[count + 1][...] = total[:, qkv_lanes:]
        refs[count + 2][...] = small_sum(refs[:count], chunk, small_rows)

    return run(
        body,
        pieces,
        out_shape=[
            sds((chunk, qkv_lanes), F32),
            sds((chunk, lanes - qkv_lanes), F32),
            sds((small_rows, lanes), F32),
        ],
        vmem=6,
        cost_estimate=cost(0, 1024 * 1024),
        name="final_attention",
    )


def final_units(first, second, after):
    high = first[0].shape[1]
    sizes = [first[0].shape[2], second[0].shape[2]]
    unit_block = sum(sizes)
    count = len(first)
    half = high // 2

    def body(*refs):
        _, part, _ = place(2)
        keep_ref, send_ref, down_ref = refs[2 * count :]
        for h in range(2):
            pieces = refs[h * count : (h + 1) * count]
            up, down = pieces[0][0].astype(F32), pieces[0][1].astype(F32)
            for ref in pieces[1:]:
                up = up + ref[0].astype(F32)
                down = down + ref[1].astype(F32)
            here = slice(h * sizes[0], h * sizes[0] + sizes[h])
            down_ref[here, :] = down.T
            for c in range(2):

                @pl.when(part == c)
                def _(up=up, here=here, c=c):
                    keep_ref[:, here] = up[c * half : (c + 1) * half, :]
                    send_ref[:, here] = up[(1 - c) * half : (2 - c) * half, :].astype(BF16)

    return run(
        body,
        [*first, *second],
        after,
        out_shape=[
            sds((half, unit_block), F32),
            sds((half, unit_block), BF16),
            sds((unit_block, high), F32),
        ],
        vmem=10,
        cost_estimate=cost(0, 4 * 1024 * 1024),
        name="final_units",
    )


def final_join(keep, recv):
    chunk, unit_block = keep.shape

    def body(keep_ref, recv_ref, out_ref):
        _, part, _ = place(2)
        for c in range(2):

            @pl.when(part == c)
            def _(c=c):
                out_ref[:, c * unit_block : (c + 1) * unit_block] = keep_ref[...]
                out_ref[:, (1 - c) * unit_block : (2 - c) * unit_block] = recv_ref[...].astype(F32)

    return run(
        body,
        [keep, recv],
        out_shape=sds((chunk, 2 * unit_block), F32),
        vmem=5,
        cost_estimate=cost(0, 1024 * 1024),
        name="final_join",
    )


def on_device(
    tokens,
    mask,
    cotangent,
    ln1_gain,
    ln1_bias,
    qkv_weight,
    q_bias,
    v_bias,
    out_weight,
    out_bias,
    ln2_gain,
    ln2_bias,
    up_weight,
    up_bias,
    down_weight,
    down_bias,
):
    seq_size = lax.axis_size("seq")
    batch_size = lax.axis_size("batch")
    micro_count, seq_count, local_len, width = tokens.shape
    sequences = micro_count * seq_count
    group = seq_size // sequences
    units = up_weight.shape[1]
    head_dim = width // HEADS
    heads = HEADS // group
    real = heads * head_dim
    wide = -(-real // LANES) * LANES
    full_len = local_len * seq_size
    block_len = local_len // group
    rows = seq_size * block_len
    own_units = units // group
    part = lax.axis_index("seq") % group
    aligned = (
        seq_size == batch_size * group
        and group == 2
        and batch_size == 4
        and wide == 3 * LANES
        and (seq_size // group) % group == 0
        and units % (batch_size * group * LANES) == 0
        and own_units // batch_size == width
    )

    def from_part(item, ahead):
        if ahead % group == 0:
            return item
        pairs = [
            (q * group + (c + ahead) % group, q * group + c)
            for q in range(sequences)
            for c in range(group)
        ]
        return lax.ppermute(item, "seq", pairs)

    def gather_parts(item):
        return [from_part(item, n) for n in range(group)]

    def row_of(item):
        return item.astype(F32)[None, :]

    def blocks_of(item):
        return item.reshape(sequences, local_len, width)

    x_own = over_quads(deal(blocks_of(tokens), group), group)
    x_pieces = [from_part(item, n) for n in range(group) for item in x_own]

    count_rows = jnp.sum(mask, axis=2).reshape(sequences).astype(BF16)
    cot_low = jnp.where(mask[..., None] != 0, cotangent, jnp.zeros_like(cotangent))
    cot_send = jnp.concatenate(
        [blocks_of(cot_low), jnp.broadcast_to(count_rows[:, None, None], (sequences, 16, width))],
        axis=1,
    )
    cot_own = over_quads(deal(cot_send, group, x_pieces[sequences:]), group)

    qkv_w, qkv_b, *out_w = pick_weights(
        qkv_weight,
        jnp.concatenate([q_bias, jnp.zeros_like(q_bias), v_bias])[None, :],
        out_weight,
        group,
        real,
        wide,
    )
    if aligned:
        up_own, up_b, down_own = up_weight, up_bias[None, :], down_weight
    else:

        def own_columns(matrix, blocks):
            split = matrix.reshape(matrix.shape[0], blocks, group, -1)
            return lax.dynamic_index_in_dim(split, part, 2, keepdims=False)

        up_own = own_columns(up_weight, batch_size).reshape(width, own_units)
        up_b = own_columns(up_bias[None, :], batch_size).reshape(1, own_units)
        down_own = lax.dynamic_index_in_dim(
            down_weight.reshape(batch_size, group, -1, width), part, 1, keepdims=False
        ).reshape(own_units, width)

    tiles = wide // LANES
    x_all, qkv, att_first, logs_first = attend_first(
        x_pieces, row_of(ln1_gain), row_of(ln1_bias), qkv_w, qkv_b, tiles - 1, heads, head_dim
    )
    cot_stack = stack(cot_own, [logs_first])
    att_last, logs_last = attend_last(qkv, tiles - 1, heads, head_dim, [cot_stack])
    cot_pieces = cot_own + [
        item[d]
        for item in gather_parts(cot_stack)[1:]
        for d in range(sequences)
    ]
    blocks = batch_size if aligned else 1
    unit_block = own_units // blocks
    size = unit_block * 2 // 5
    shape = (group, sequences if aligned else None, width // sequences)
    calls = [
        Units(unit_block, blocks, 0, size, *shape),
        Units(unit_block, blocks, size, unit_block - size, *shape),
    ]
    mid, second, second_t, grad_rows, grad_t, result_own, grad_second, *found = feed_first(
        x_all,
        gather_parts(att_first),
        gather_parts(att_last),
        cot_pieces,
        out_w,
        row_of(out_bias),
        row_of(ln2_gain),
        row_of(ln2_bias),
        up_own,
        up_b,
        down_own,
        row_of(down_bias),
        calls[0],
    )
    up_sums, ff_grads = [found[0]], [found[group:]]
    result_own, grad_second, *found = feed_second(
        second,
        second_t,
        grad_rows,
        grad_t,
        result_own,
        grad_second,
        found[1:group],
        up_own,
        up_b,
        down_own,
        calls[1],
    )
    up_sums.append(found[0])
    result_send = found[1:group]
    ff_grads.append(found[group:])

    def begin_sum(e, sends, after):
        moved = [swap(sends[0], "batch", batch_size, 1), swap(sends[1], "batch", batch_size, 2)]
        stay_a, pass_a, stay_b, pass_b = sum_first(
            [ff_grads[e][0], ff_grads[e][2]], moved, after
        )
        moved = [swap(pass_a, "batch", batch_size, 2), swap(pass_b, "batch", batch_size, 1)]
        return [stay_a, stay_b], moved

    if aligned:
        waiting = begin_sum(0, [ff_grads[0][1], ff_grads[0][3]], [])
        (grad_second,) = gate([grad_second], waiting[0][:1])
    second_send = grad_second
    second_recv = [from_part(second_send, n) for n in range(1, group)]
    result_recv = [from_part(result_send[group - n - 1], n) for n in range(1, group)]
    result_keep, result_pass = finish_result(result_own, result_recv, sequences)

    def quad_swap(item, distance):
        return swap(item, "seq", seq_size, distance * group)

    result_near = quad_swap(result_pass, 1)

    chunk = width // seq_size
    grad_mid, grad_att, sums_mid, *out_grad = mid_back(
        mid,
        grad_second,
        second_recv,
        grad_rows,
        row_of(ln2_gain),
        out_w[0],
        att_first,
        att_last,
        chunk if aligned else 0,
    )

    def tile_back(t, after, cost_part=1):
        last = t == tiles - 1
        return attend_backward(
            qkv,
            grad_att,
            att_last if last else att_first,
            0 if last else t,
            logs_last if last else logs_first,
            0 if last else t * (LANES // head_dim),
            t,
            heads,
            head_dim,
            after,
            cost_part,
        )

    grad_tiles = [None] * tiles
    after = [result_keep]
    if aligned:
        keep, send = sum_second(*waiting, [grad_mid])
        moved = quad_swap(send, 1)
        sends = gate([ff_grads[1][1], ff_grads[1][3]], [keep])
        after = [result_keep, keep]
    grad_tiles[0] = tile_back(0, after, 64)
    result_pass = pass_on(result_keep, result_near, grad_tiles[:1])
    result_far = quad_swap(result_pass, 2)
    after = [result_pass]
    if aligned:
        unit_first = list(sum_third(keep, moved, [grad_tiles[0]]))
        unit_first[1] = quad_swap(unit_first[1], 2)
        waiting = begin_sum(1, sends, [grad_tiles[0]])
        after = [result_pass, unit_first[0], waiting[0][0]]
    for t in range(1, tiles - 1):
        grad_tiles[t] = tile_back(t, after)
    after = [grad_tiles[-2], result_far]
    if aligned:
        out_recv = from_part(out_grad[1], 1)
        keep, send = sum_second(*waiting, [grad_tiles[-2]])
        moved = quad_swap(send, 1)
        after = [keep, result_far, unit_first[1]]
    grad_tiles[-1] = tile_back(tiles - 1, after)
    after = []
    if aligned:
        after = [out_recv]
    qkv_grad = project_weights(
        x_all,
        row_of(ln1_gain),
        row_of(ln1_bias),
        grad_tiles,
        group,
        sequences,
        aligned,
        after,
    )
    after = qkv_grad[:1]
    if aligned:
        unit_second = list(sum_third(keep, moved, qkv_grad[:1]))
        unit_second[1] = quad_swap(unit_second[1], 2)
        after = unit_second[:1]
    first_own, *found = project_rows(
        x_all,
        qkv_w,
        grad_tiles,
        sums_mid,
        up_sums,
        group,
        sequences,
        aligned,
        real,
        after,
    )
    first_send, (small, bias_sums) = found[: group - 1], found[group - 1 :]
    first_recv = [from_part(first_send[group - n - 1], n) for n in range(1, group)]
    after = []
    if aligned:
        small_rows = small.shape[0]
        packed = pack_attention(
            qkv_grad[0],
            from_part(qkv_grad[1], 1),
            out_grad[0],
            out_recv,
            small,
            from_part(small, 1),
            real,
            batch_size,
            [],
        )
        after = packed[:1]
    row_parts = finish_rows(
        x_all, row_of(ln1_gain), grad_mid, first_own, first_recv, sequences, after
    )
    row_moved = over_quads(row_parts, group)
    if aligned:
        stay_a, pass_a, stay_b, pass_b = sum_first_attention(
            [packed[0], packed[2]],
            [swap(packed[1], "batch", batch_size, 1), swap(packed[3], "batch", batch_size, 2)],
            sequences // 2 * chunk,
            small_rows,
            [row_parts[0], *row_moved[1::2]],
        )
        summed = sum_second_attention(
            [stay_a, stay_b],
            [swap(pass_a, "batch", batch_size, 2), swap(pass_b, "batch", batch_size, 1)],
            chunk,
            sequences,
            small_rows,
            [],
        )
        after = summed[:1]
        up_keep, up_send, down_grad = final_units(unit_first, unit_second, after)
        up_grad = final_join(up_keep, from_part(up_send, 1))
        qkv_final, out_final, small = final_attention(
            over_quads(summed, group), chunk, qkv_weight.shape[1] // batch_size, small_rows
        )
        small = small.reshape(-1)
    result = collect_halves(result_keep, result_near, result_far, group, after)
    result = result.reshape(tokens.shape)
    grad_in = collect(row_moved, group, after).reshape(tokens.shape)
    if not aligned:

        def spread(item, blocks):
            split = item.reshape(blocks, 1, -1)
            empty = jnp.zeros((blocks, group, split.shape[2]), F32)
            return lax.dynamic_update_slice(empty, split, (0, part, 0)).reshape(-1)

        bias_sums = bias_sums[0].reshape(tiles, 3, LANES).transpose(1, 0, 2)
        bias_sums = bias_sums.reshape(3, wide)[:, :real]
        small = jnp.concatenate(
            [
                small[0],
                small[1],
                spread(bias_sums[0], 1),
                spread(bias_sums[2], 1),
                sums_mid[2],
                sums_mid[0],
                sums_mid[1],
                spread(jnp.concatenate([item[0] for item in up_sums]), batch_size),
                sums_mid[3],
            ]
        )

        def scattered(item):
            item = lax.psum_scatter(item.astype(BF16), "seq", scatter_dimension=0, tiled=True)
            return lax.psum_scatter(item, "batch", scatter_dimension=1, tiled=True).astype(F32)

        def spread_columns(item, blocks):
            split = item.reshape(item.shape[0], blocks, 1, -1)
            empty = jnp.zeros((item.shape[0], blocks, group, split.shape[3]), item.dtype)
            filled = lax.dynamic_update_slice(empty, split, (0, 0, part, 0))
            return filled.reshape(item.shape[0], -1)

        up_full, down_full = [
            jnp.concatenate([item[e] for item in ff_grads], axis=1) for e in range(2)
        ]
        up_grad = scattered(spread_columns(up_full, batch_size))
        down_grad = scattered(spread_columns(down_full, batch_size).T)
        rows_full = qkv_grad[0].reshape(width, tiles, 3, LANES).transpose(0, 2, 1, 3)
        rows_full = rows_full.reshape(width, 3, wide)[..., :real]
        qkv_final = scattered(spread_columns(rows_full.reshape(width, -1), 3))
        out_final = scattered(spread_columns(out_grad[0][:real].T, 1).T)
        small = lax.psum(small, ("seq", "batch"))

    edges = [width] * 7 + [units, width]
    pieces, start = [], 0
    for size in edges:
        pieces.append(small[start : start + size])
        start += size
    return (
        result,
        grad_in,
        pieces[0],
        pieces[1],
        qkv_final,
        pieces[2],
        pieces[3],
        out_final,
        pieces[4],
        pieces[5],
        pieces[6],
        up_grad,
        pieces[7],
        down_grad,
        pieces[8],
    )


def solution(mesh):
    rows = P(None, "batch", "seq", None)
    split = P("seq", "batch")
    in_specs = (rows, P(None, "batch", "seq"), rows) + (P(),) * 13
    out_specs = (
        rows,
        rows,
        P(),
        P(),
        split,
        P(),
        P(),
        split,
        P(),
        P(),
        P(),
        split,
        P(),
        split,
        P(),
    )
    return jax.shard_map(
        on_device, mesh=mesh, in_specs=in_specs, out_specs=out_specs, check_vma=False
    )
```

```python
import jax
import jax.numpy as jnp
from jax import lax
from jax.experimental import pallas as pl
from jax.experimental.pallas import tpu as pltpu
from jax.sharding import PartitionSpec as P

HEADS = 20
EPS = 1e-05
LOG2E = 1.4426950408889634
ROWS = 256
F32 = jnp.float32
BF16 = jnp.bfloat16
LANES = 128


def dot(left, right):
    return jnp.dot(left, right, preferred_element_type=F32)


def dot_nt(left, right):
    return lax.dot_general(left, right, (((1,), (1,)), ((), ())), preferred_element_type=F32)


def norm_rows(rows_in):
    mean_val = jnp.mean(rows_in, axis=-1, keepdims=True)
    centered = rows_in - mean_val
    inv_std = lax.rsqrt(jnp.mean(centered * centered, axis=-1, keepdims=True) + EPS)
    return centered * inv_std, inv_std


def norm_back(scaled, normed, inv_std):
    inner = (
        scaled
        - jnp.mean(scaled, axis=-1, keepdims=True)
        - normed * jnp.mean(scaled * normed, axis=-1, keepdims=True)
    )
    return inner * inv_std


def params_of(mib):
    return pltpu.CompilerParams(vmem_limit_bytes=mib * 1024 * 1024)


def cost(flops, moved, trans=0, part=1):
    return pl.CostEstimate(
        flops=flops // part, bytes_accessed=moved // part, transcendentals=trans // part
    )


def sds(shape, dtype):
    return jax.ShapeDtypeStruct(shape, dtype)


VMEM = pl.BlockSpec(memory_space=pltpu.VMEM)
ANY = pl.BlockSpec(memory_space=pl.ANY)
HBM = pl.BlockSpec(memory_space=pltpu.HBM)


def run(body, operands, after=(), in_specs=None, out_specs=None, vmem=32, **more):
    count, extra = len(operands), len(after)

    def inner(*refs):
        body(*refs[:count], *refs[count + extra :])

    specs = [VMEM] * count if in_specs is None else list(in_specs)
    shapes = more["out_shape"]
    if out_specs is None:
        out_specs = [VMEM] * len(shapes) if isinstance(shapes, (list, tuple)) else VMEM
    return pl.pallas_call(
        inner,
        in_specs=specs + [ANY] * extra,
        out_specs=out_specs,
        compiler_params=params_of(vmem),
        **more,
    )(*operands, *after)


def far(item):
    return pltpu.with_memory_space_constraint(item, pltpu.HBM)


def gate(items, after):
    def body(*refs):
        del refs

    return pl.pallas_call(
        body,
        in_specs=[ANY] * (len(items) + len(after)),
        out_specs=[ANY] * len(items),
        out_shape=[sds(item.shape, item.dtype) for item in items],
        input_output_aliases={n: n for n in range(len(items))},
        cost_estimate=cost(0, 0),
        name="gate",
    )(*items, *after)


def place(group):
    spot = lax.axis_index("seq")
    return spot, lax.rem(spot, group), lax.div(spot, group)


def deal(item, group, after=()):
    count, rows, width = item.shape

    def body(in_ref, *out_refs):
        _, _, quad = place(group)
        for d in range(count):
            out_refs[d][...] = in_ref[quad ^ d]

    return run(
        body,
        [item],
        after,
        out_shape=[sds((rows, width), item.dtype)] * count,
        vmem=6,
        cost_estimate=cost(0, 4 * count * rows * width),
        name="deal",
    )


def collect(pieces, group, after):
    count = len(pieces)
    rows, width = pieces[0].shape

    def body(*refs):
        _, _, quad = place(group)
        for d in range(count):
            refs[count][quad ^ d] = refs[d][...]

    return run(
        body,
        pieces,
        after,
        out_shape=sds((count, rows, width), pieces[0].dtype),
        vmem=6,
        cost_estimate=cost(0, 4 * count * rows * width),
        name="collect",
    )


def stack(pieces, after):
    count = len(pieces)

    def body(*refs):
        for d in range(count):
            refs[count][d] = refs[d][...]

    return run(
        body,
        pieces,
        after,
        out_shape=sds((count,) + pieces[0].shape, pieces[0].dtype),
        vmem=12,
        cost_estimate=cost(0, 4 * count * pieces[0].size),
        name="stack",
    )


def swap(item, axis, size, distance):
    return lax.ppermute(item, axis, [(i, i ^ distance) for i in range(size)])


def over_quads(pieces, group):
    return [
        piece if d == 0 else swap(piece, "seq", len(pieces) * group, d * group)
        for d, piece in enumerate(pieces)
    ]


def pick_weights(qkv_weight, qkv_bias, out_weight, group, real, wide):
    width = qkv_weight.shape[0]
    tiles = wide // LANES

    def body(w_ref, b_ref, o_ref, wo_ref, bo_ref, *out_refs):
        _, part, _ = place(group)
        wo_ref[...] = jnp.zeros_like(wo_ref)
        bo_ref[...] = jnp.zeros_like(bo_ref)
        for ref in out_refs:
            ref[...] = jnp.zeros_like(ref)
        for c in range(group):

            @pl.when(part == c)
            def _(c=c):
                for p in range(3):
                    for t in range(tiles):
                        some = min(LANES, real - t * LANES)
                        src = p * width + c * real + t * LANES
                        dst = (3 * t + p) * LANES
                        wo_ref[:, dst : dst + some] = w_ref[:, src : src + some]
                        bo_ref[:, dst : dst + some] = b_ref[:, src : src + some]
                for n in range(group):
                    src = (c + n) % group * real
                    out_refs[n][0:real, :] = o_ref[src : src + real, :]

    return pl.pallas_call(
        body,
        out_shape=[sds((width, 3 * wide), BF16), sds((1, 3 * wide), F32)]
        + [sds((wide, width), BF16)] * group,
        compiler_params=params_of(24),
        cost_estimate=cost(0, 8 * 1024 * 1024),
        name="pick_weights",
    )(qkv_weight, qkv_bias, out_weight)


def by_pairs(live, visit):
    size = 2 if live % 2 == 0 else 1

    @pl.loop(0, live // size)
    def _(i):
        visit([i * size + e for e in range(size)])


def attend_tiles(query_at, keys_at, vals_at, att_ref, lse_ref, keys, vals, acc, tiles, heads, head_dim):
    per_tile = LANES // head_dim
    total = att_ref.shape[0]
    exp_scale = head_dim ** (-0.5) * LOG2E
    lane = lax.broadcasted_iota(jnp.int32, (1, LANES), 1)
    row = lax.broadcasted_iota(jnp.int32, (LANES, 1), 0)
    lse_ref[...] = jnp.zeros_like(lse_ref)
    vals[:, :, LANES:] = jnp.ones((per_tile, total, LANES), BF16)
    for n, t in enumerate(tiles):
        live = min(per_tile, heads - t * per_tile)
        key_t = keys_at(n).astype(F32).T
        val_f = vals_at(n).astype(F32)
        for j in range(live):
            keys[j] = jnp.where(row // head_dim == j, key_t, 0.0).astype(BF16)
            vals[j, :, :LANES] = jnp.where(lane // head_dim == j, val_f, 0.0).astype(BF16)
        acc[...] = jnp.zeros_like(acc)

        def visit(some, n=n):
            scores = [dot(query_at(n), keys[j]) for j in some]
            for item, j in zip(scores, some):
                row_max = jnp.max(item, axis=-1, keepdims=True) * exp_scale
                expd = jnp.exp2(item * exp_scale - row_max).astype(BF16)
                mixed = dot(expd, vals[j])
                den = mixed[:, LANES:]
                acc[...] += mixed[:, :LANES] / den
                lse_ref[...] = jnp.where(
                    lane == n * per_tile + j, row_max + jnp.log2(den), lse_ref[...]
                )

        by_pairs(live, visit)
        att_ref[:, n * LANES : (n + 1) * LANES] = acc[...].astype(BF16)


def attend_scratch(total, head_dim):
    per_tile = LANES // head_dim
    return [
        pltpu.VMEM((per_tile, LANES, total), BF16),
        pltpu.VMEM((per_tile, total, 2 * LANES), BF16),
        pltpu.VMEM((total, LANES), F32),
    ]


def attend_first(x_pieces, gain, shift, weight, bias, tiles, heads, head_dim):
    count = len(x_pieces)
    piece_rows, width = x_pieces[0].shape
    total = count * piece_rows
    cols_all = weight.shape[1]

    def body(*refs):
        x_refs = refs[:count]
        gain_ref, shift_ref, w_ref, bias_ref = refs[count : count + 4]
        x_ref, qkv_ref, att_ref, lse_ref, keys, vals, acc = refs[count + 4 :]
        for n in range(count):
            x_ref[n * piece_rows : (n + 1) * piece_rows, :] = x_refs[n][...]

        @pl.loop(0, total // ROWS)
        def _(i):
            rows = pl.ds(pl.multiple_of(i * ROWS, ROWS), ROWS)
            normed, _ = norm_rows(x_ref[rows, :].astype(F32))
            low = (normed * gain_ref[...] + shift_ref[...]).astype(BF16)
            qkv_ref[rows, :] = (dot(low, w_ref[...]) + bias_ref[...]).astype(BF16)

        def columns(at):
            return slice(at * LANES, (at + 1) * LANES)

        attend_tiles(
            lambda n: qkv_ref[:, columns(3 * n)],
            lambda n: qkv_ref[:, columns(3 * n + 1)],
            lambda n: qkv_ref[:, columns(3 * n + 2)],
            att_ref,
            lse_ref,
            keys,
            vals,
            acc,
            range(tiles),
            heads,
            head_dim,
        )

    return run(
        body,
        [*x_pieces, gain, shift, weight, bias],
        out_shape=[
            sds((total, width), BF16),
            sds((total, cols_all), BF16),
            sds((total, tiles * LANES), BF16),
            sds((total, LANES), F32),
        ],
        scratch_shapes=attend_scratch(total, head_dim),
        vmem=23,
        cost_estimate=cost(
            2 * total * width * cols_all + 4 * heads * total * total * 256,
            8 * 1024 * 1024,
            heads * total * total,
        ),
        name="attend_first",
    )


def attend_last(qkv, tile, heads, head_dim, after):
    total = qkv.shape[0]

    def body(qkv_ref, att_ref, lse_ref, keys, vals, acc):
        attend_tiles(
            lambda n: qkv_ref[:, 0:LANES],
            lambda n: qkv_ref[:, LANES : 2 * LANES],
            lambda n: qkv_ref[:, 2 * LANES : 3 * LANES],
            att_ref,
            lse_ref,
            keys,
            vals,
            acc,
            [tile],
            heads,
            head_dim,
        )

    live = heads - tile * (LANES // head_dim)
    return run(
        body,
        [qkv],
        after,
        grid=(1,),
        in_specs=[pl.BlockSpec((total, 3 * LANES), lambda i: (0, tile))],
        out_specs=[pl.BlockSpec((total, LANES), lambda i: (0, 0))] * 2,
        out_shape=[sds((total, LANES), BF16), sds((total, LANES), F32)],
        scratch_shapes=attend_scratch(total, head_dim),
        vmem=14,
        cost_estimate=cost(4 * live * total * total * 256, 2 * 1024 * 1024, live * total * total),
        name="attend_last",
    )


def gelu_parts(value):
    size = jnp.abs(value)
    near = pl.reciprocal(1.0 + (0.3275911 * 0.7071067811865476) * size, approx=True)
    bell = jnp.exp2(value * value * (-0.5 * LOG2E))
    poly = near * (
        0.5 * 0.254829592
        + near
        * (
            0.5 * -0.284496736
            + near * (0.5 * 1.421413741 + near * (0.5 * -1.453152027 + near * (0.5 * 1.061405429)))
        )
    )
    tail = poly * bell
    area = jnp.where(value < 0.0, tail, 1.0 - tail)
    return value * area, area + value * bell * 0.3989422804014327


class Units:
    def __init__(self, block, blocks, start, size, stride, quads, high):
        self.block, self.blocks, self.start, self.size = block, blocks, start, size
        self.stride, self.quads, self.high = stride, quads, high
        self.count = blocks * size
        self.chunk = 512 if self.count % 512 == 0 else 256
        self.packed = quads is not None

    def loads(self, part, hbm_up, hbm_down, hbm_bias, up_ref, down_ref, bias_ref, sem):
        copies = []
        for b in range(self.blocks):
            src = self.start
            if self.packed:
                src = pl.multiple_of((b * self.stride + part) * self.block, LANES) + self.start
            src = pl.ds(src, self.size)
            dst = pl.ds(b * self.size, self.size)
            copies.append(
                pltpu.make_async_copy(hbm_up.at[:, src], up_ref.at[:, dst], sem.at[2 * b])
            )
            copies.append(
                pltpu.make_async_copy(hbm_down.at[src, :], down_ref.at[dst, :], sem.at[2 * b + 1])
            )
            bias_ref[0:1, dst] = hbm_bias[:, src]
        return copies

    def grad_shapes(self, width):
        if self.packed:
            return [pltpu.HBM((2, self.quads, self.high, self.size), BF16)] * 4
        return [sds((width, self.count), BF16)] * 2

    def scratch(self, total, width):
        grads = (self.blocks, self.quads, self.high, self.size) if self.packed else (8, LANES)
        return [
            pltpu.VMEM(grads, BF16),
            pltpu.VMEM(grads, BF16),
            pltpu.SemaphoreType.DMA((8,)),
            pltpu.VMEM((total, self.count), BF16),
            pltpu.VMEM((total, self.count), BF16),
            pltpu.VMEM((width, self.count), BF16),
            pltpu.VMEM((self.count, width), BF16),
            pltpu.VMEM((8, self.count), F32),
            pltpu.SemaphoreType.DMA((2 * self.blocks,)),
        ]

    def compute(self, second, second_t, grad, grad_t, ubg, scratch, outs, give):
        up_slots, down_slots, out_sem, acts, grad_pres, up_ref, down_ref, bias_ref, _ = scratch
        if not self.packed:
            up_slots, down_slots = outs
        quad = lax.div(lax.axis_index("seq"), self.stride)
        mine = lax.axis_index("batch")

        def enter(i):
            rows = slice(i * ROWS, (i + 1) * ROWS)
            pre = dot(second[rows, :], up_ref[...]) + bias_ref[0:1, :]
            return pre, dot_nt(grad[rows, :], down_ref[...])

        def weights(n):
            first, last = n * self.chunk, (n + 1) * self.chunk
            up_grad = dot(second_t[...], grad_pres[:, first:last]).astype(BF16)
            down_grad = dot(grad_t[...], acts[:, first:last]).astype(BF16)
            if not self.packed:
                up_slots[:, first:last] = up_grad
                down_slots[:, first:last] = down_grad
                return
            at = first
            while at < last:
                block = at // self.size
                stop = min(last, (block + 1) * self.size)
                src = slice(at - first, stop - first)
                dst = slice(at - block * self.size, stop - block * self.size)
                for m in range(self.blocks):
                    rows = slice(m * self.high, (m + 1) * self.high)
                    up_slots[block ^ mine, m ^ quad, :, dst] = up_grad[rows, src]
                    down_slots[m ^ mine, block ^ quad, :, dst] = down_grad[rows, src]
                at = stop

        ready = enter(0)
        chunks = second.shape[0] // ROWS
        for i in range(chunks):
            ahead = enter(i + 1) if i + 1 < chunks else None
            rows = slice(i * ROWS, (i + 1) * ROWS)
            pre, grad_act = ready
            value, slope = gelu_parts(pre)
            act = value.astype(BF16)
            grad_pre = (grad_act * slope).astype(BF16)
            acts[rows, :] = act
            grad_pres[rows, :] = grad_pre
            ubg[0:1, :] += jnp.sum(grad_pre.astype(F32), axis=0, keepdims=True)
            give(i, rows, dot(act, down_ref[...]), dot_nt(grad_pre, up_ref[...]))
            ready = ahead
        for n in range(self.count // self.chunk):
            weights(n)
        stores = []
        if self.packed:
            order = ((up_slots, (0, 2)), (up_slots, (1, 3)), (down_slots, (0, 1)), (down_slots, (2, 3)))
            for m, (source, slots) in enumerate(order):
                for n in range(2):
                    stores.append(
                        pltpu.make_async_copy(
                            source.at[slots[n]], outs[m].at[n], out_sem.at[2 * m + n]
                        )
                    )
        return stores


def feed_first(
    rows_all, att_first, att_last, cot_pieces, out_w, out_b, gain, shift, up, up_b, down, down_b, units
):
    pieces = len(att_first)
    total, width = rows_all.shape
    piece_rows = total // pieces
    count = len(cot_pieces)
    cot_rows = total // count
    split = att_first[0].shape[1]
    grads = units.grad_shapes(width)

    def body(*refs):
        x_ref, refs = refs[0], refs[1:]
        att_refs, refs = refs[: 2 * pieces], refs[2 * pieces :]
        cot_refs, refs = refs[:count], refs[count:]
        wo_refs, refs = refs[:pieces], refs[pieces:]
        ob_ref, gain_ref, shift_ref, up_hbm, ub_ref, down_hbm, db_ref = refs[:7]
        mid_ref, second, second_t, grad, grad_t, own_ref, low_ref, ubg, refs = *refs[7:15], refs[15:]
        send_refs, refs = refs[: pieces - 1], refs[pieces - 1 :]
        outs, refs = refs[: len(grads)], refs[len(grads) :]
        mid_rows, mid_sem, *scratch = refs
        _, part, _ = place(pieces)
        loads = units.loads(part, up_hbm, down_hbm, ub_ref, *scratch[5:])
        for load in loads:
            load.start()
        ubg[...] = jnp.zeros_like(ubg)
        masked = jnp.zeros((1, width), F32)
        for ref in cot_refs:
            masked = masked + ref[cot_rows : cot_rows + 1, :].astype(F32)
        factor = total / (4.0 * masked)
        for n in range(count):
            scaled = cot_refs[n][0:cot_rows, :].astype(F32) * factor
            dst = slice(n * cot_rows, (n + 1) * cot_rows)
            grad[dst, :] = scaled.astype(BF16)

        for h in range(pieces):

            @pl.loop(0, piece_rows // ROWS)
            def _(i, h=h):
                at = pl.multiple_of(i * ROWS, ROWS)
                dst = pl.ds(h * piece_rows + at, ROWS)
                mid = x_ref[dst, :].astype(F32) + ob_ref[...]
                for n in range(pieces):
                    src = pl.ds(((h - n) % pieces) * piece_rows + at, ROWS)
                    mid = mid + dot(att_refs[2 * n][src, :], wo_refs[n][0:split, :])
                    mid = mid + dot(att_refs[2 * n + 1][src, :], wo_refs[n][split:, :])
                mid_rows[dst, :] = mid
                normed, _ = norm_rows(mid)
                low = normed * gain_ref[...] + shift_ref[...]
                second[dst, :] = low.astype(BF16)
                second_t[:, dst] = low.astype(BF16).T
                grad_t[:, dst] = grad[dst, :].T

        keep_mid = pltpu.make_async_copy(mid_rows, mid_ref, mid_sem)
        keep_mid.start()
        for load in loads:
            load.wait()

        def give(i, rows, result, grad_second):
            low_ref[rows, :] = grad_second.astype(BF16)
            h = i * ROWS // piece_rows
            at = slice(rows.start - h * piece_rows, rows.stop - h * piece_rows)
            if h == 0:
                own_ref[at, :] = mid_rows[rows, :] + db_ref[...] + result
            else:
                send_refs[h - 1][at, :] = result.astype(BF16)

        stores = units.compute(second, second_t, grad, grad_t, ubg, scratch, outs, give)
        for store in stores:
            store.start()
        keep_mid.wait()
        for store in stores:
            store.wait()

    att_all = [item for pair in zip(att_first, att_last) for item in pair]
    turned = sds((width, total), BF16)
    flat = sds((total, width), BF16)
    half = sds((piece_rows, width), F32)
    return run(
        body,
        [
            rows_all,
            *att_all,
            *cot_pieces,
            *out_w,
            out_b,
            gain,
            shift,
            far(up),
            up_b,
            far(down),
            down_b,
        ],
        in_specs=[VMEM] * (1 + 3 * pieces + count) + [VMEM, VMEM, VMEM, HBM, VMEM, HBM, VMEM],
        out_specs=[HBM] + [VMEM] * (6 + pieces) + [HBM if units.packed else VMEM] * len(grads),
        out_shape=[pltpu.HBM((total, width), F32), flat, turned, flat, turned, half, flat, sds((8, units.count), F32)]
        + [sds((piece_rows, width), BF16)] * (pieces - 1)
        + grads,
        scratch_shapes=[pltpu.VMEM((total, width), F32)]
        + [pltpu.SemaphoreType.DMA]
        + units.scratch(total, width),
        vmem=22,
        cost_estimate=cost(12 * total * width * units.count, 24 * 1024 * 1024, total * units.count),
        name="feed_first",
    )


def feed_second(second, second_t, grad, grad_t, own_first, low_first, sends, up, up_b, down, units):
    pieces = 1 + len(sends)
    total, width = second.shape
    piece_rows = total // pieces
    grads = units.grad_shapes(width)

    def body(*refs):
        second, second_t, grad, grad_t, own_in, low_in, up_hbm, ub_ref, down_hbm, refs = (
            *refs[:9],
            refs[9:],
        )
        send_ins, refs = refs[: pieces - 1], refs[pieces - 1 :]
        own_ref, low_ref, ubg, refs = refs[0], refs[1], refs[2], refs[3:]
        send_refs, refs = refs[: pieces - 1], refs[pieces - 1 :]
        outs, scratch = refs[: len(grads)], refs[len(grads) :]
        _, part, _ = place(pieces)
        loads = units.loads(part, up_hbm, down_hbm, ub_ref, *scratch[5:])
        for load in loads:
            load.start()
        ubg[...] = jnp.zeros_like(ubg)
        for load in loads:
            load.wait()

        def give(i, rows, result, grad_second):
            low_ref[rows, :] = (grad_second + low_in[rows, :].astype(F32)).astype(BF16)
            h = i * ROWS // piece_rows
            at = slice(rows.start - h * piece_rows, rows.stop - h * piece_rows)
            if h == 0:
                own_ref[at, :] = own_in[at, :] + result
            else:
                send_refs[h - 1][at, :] = (result + send_ins[h - 1][at, :].astype(F32)).astype(BF16)

        stores = units.compute(second, second_t, grad, grad_t, ubg, scratch, outs, give)
        for store in stores:
            store.start()
        for store in stores:
            store.wait()

    return run(
        body,
        [
            second,
            second_t,
            grad,
            grad_t,
            own_first,
            low_first,
            far(up),
            up_b,
            far(down),
            *sends,
        ],
        in_specs=[VMEM] * 6 + [HBM, VMEM, HBM] + [VMEM] * (pieces - 1),
        out_specs=[VMEM] * (2 + pieces) + [HBM if units.packed else VMEM] * len(grads),
        out_shape=[
            sds((piece_rows, width), F32),
            sds((total, width), BF16),
            sds((8, units.count), F32),
        ]
        + [sds((piece_rows, width), BF16)] * (pieces - 1)
        + grads,
        scratch_shapes=units.scratch(total, width),
        vmem=26,
        cost_estimate=cost(12 * total * width * units.count, 24 * 1024 * 1024, total * units.count),
        name="feed_second",
    )


def mid_back(mid, grad_second, received, grad_rows, gain, out_w, att_first, att_last, chunk):
    pieces = 1 + len(received)
    total, width = mid.shape
    per_piece = total // pieces // ROWS
    split = att_first.shape[1]
    wide = split + att_last.shape[1]
    steps = total // ROWS

    def body(*refs):
        mid_ref, gs_ref, refs = refs[0], refs[1], refs[2:]
        recv_refs, refs = refs[: pieces - 1], refs[pieces - 1 :]
        go_ref, gain_ref, wo_ref, att_ref, last_ref = refs[:5]
        gm_ref, do_ref, sums_ref, *dwo_refs, acc = refs[5:]
        i = pl.program_id(0)

        @pl.when(i == 0)
        def _():
            sums_ref[...] = jnp.zeros_like(sums_ref)
            acc[...] = jnp.zeros_like(acc)

        normed, inv_std = norm_rows(mid_ref[...])
        grad = gs_ref[...].astype(F32)
        for ref in recv_refs:
            grad = grad + ref[...].astype(F32)
        go = go_ref[...].astype(F32)
        grad_mid = go + norm_back(grad * gain_ref[...], normed, inv_std)
        low = grad_mid.astype(BF16)
        do_ref[...] = dot_nt(low, wo_ref[...]).astype(BF16)
        acc[0:split, :] += dot(att_ref[...].astype(F32).T.astype(BF16), low)
        acc[split:, :] += dot(last_ref[...].astype(F32).T.astype(BF16), low)

        @pl.when(i < per_piece)
        def _():
            gm_ref[...] = grad_mid
            for n, item in enumerate((grad * normed, grad, low.astype(F32), go)):
                sums_ref[n : n + 1, :] += jnp.sum(item, axis=0, keepdims=True)

        @pl.when(i == steps - 1)
        def _():
            if chunk == 0:
                dwo_refs[0][...] = acc[...].astype(BF16)
                return
            _, part, _ = place(pieces)
            for c in range(pieces):

                @pl.when(part == c)
                def _(c=c):
                    for n in range(dwo_refs[0].shape[0]):
                        for e in range(pieces):
                            at = (n * pieces + (c + e) % pieces) * chunk
                            dwo_refs[e][n] = acc[at : at + chunk, :].astype(BF16)

    def rows_of(columns):
        return pl.BlockSpec((ROWS, columns), lambda i: (i, 0))

    def theirs(n):
        def index(i):
            piece = lax.rem(lax.div(i, per_piece) + pieces - n, pieces)
            return piece * per_piece + lax.rem(i, per_piece), 0

        return pl.BlockSpec((ROWS, width), index)

    def whole(*shape):
        return pl.BlockSpec(shape, lambda i: (0,) * len(shape))

    if chunk == 0:
        grads = [((wide, width), sds((wide, width), BF16))]
    else:
        shape = (width // (pieces * pieces * chunk), chunk, width)
        grads = [(shape, pltpu.HBM(shape, BF16))] * pieces
    return run(
        body,
        [
            far(mid),
            far(grad_second),
            *received,
            far(grad_rows),
            gain,
            out_w,
            far(att_first),
            far(att_last),
        ],
        grid=(steps,),
        in_specs=[rows_of(width), rows_of(width)]
        + [theirs(n) for n in range(1, pieces)]
        + [rows_of(width), whole(1, width), whole(wide, width), rows_of(split), rows_of(wide - split)],
        out_specs=[
            pl.BlockSpec((ROWS, width), lambda i: (jnp.minimum(i, per_piece - 1), 0)),
            rows_of(wide),
            whole(8, width),
        ]
        + [whole(*shape) for shape, _ in grads],
        out_shape=[
            sds((per_piece * ROWS, width), F32),
            sds((total, wide), BF16),
            sds((8, width), F32),
        ]
        + [item for _, item in grads],
        scratch_shapes=[pltpu.VMEM((wide, width), F32)],
        vmem=16,
        cost_estimate=cost(4 * total * width * wide, 14 * 1024 * 1024),
        name="mid_back",
    )


def attend_backward(
    qkv, grad_att, att, att_tile, logs, lane_first, tile, heads, head_dim, after=(), part=1
):
    total = qkv.shape[0]
    per_tile = LANES // head_dim
    live = min(per_tile, heads - tile * per_tile)
    scale = head_dim ** (-0.5)
    exp_scale = scale * LOG2E

    def body(qkv_ref, do_ref, att_ref, lse_ref, out_ref, *scratch):
        km, vm, qm, dm, key_t, query_t, do_t, dq_t, lse_t, mean_t = scratch
        lane = lax.broadcasted_iota(jnp.int32, (1, LANES), 1)
        lse_t[...] = lse_ref[...].T
        query = qkv_ref[:, 0:LANES].astype(F32)
        key = qkv_ref[:, LANES : 2 * LANES].astype(F32)
        val = qkv_ref[:, 2 * LANES : 3 * LANES].astype(F32)
        upstream = do_ref[...].astype(F32)
        both_t = (upstream * att_ref[...].astype(F32)).T
        for j in range(live):
            mean_t[j : j + 1, :] = jnp.sum(
                both_t[j * head_dim : (j + 1) * head_dim, :], axis=0, keepdims=True
            )
        query_t[...] = query.T.astype(BF16)
        do_t[...] = upstream.T.astype(BF16)
        key_t[...] = key.T.astype(BF16)
        for j in range(live):
            mine = lane // head_dim == j
            km[j] = jnp.where(mine, key, 0.0).astype(BF16)
            vm[j] = jnp.where(mine, val, 0.0).astype(BF16)
            qm[j] = jnp.where(mine, query, 0.0).astype(BF16)
            dm[j] = jnp.where(mine, upstream, 0.0).astype(BF16)
        dq_t[...] = jnp.zeros_like(dq_t)

        @pl.loop(0, total // ROWS)
        def _(i):
            rows = pl.ds(pl.multiple_of(i * ROWS, ROWS), ROWS)
            grad_key = jnp.zeros((ROWS, LANES), F32)
            grad_val = jnp.zeros((ROWS, LANES), F32)

            def enter(j):
                return dot(km[j, rows, :], query_t[...]), dot(vm[j, rows, :], do_t[...])

            ready = enter(0)
            for j in range(live):
                ahead = enter(j + 1) if j + 1 < live else None
                scores, grad_prob = ready
                head = lane_first + j
                own = slice(j * head_dim, (j + 1) * head_dim)
                probs = jnp.exp2(scores * exp_scale - lse_t[head : head + 1, :])
                grad_scores = (probs * (grad_prob - mean_t[j : j + 1, :])).astype(BF16)
                grad_val = grad_val + dot(probs.astype(BF16), dm[j])
                grad_key = grad_key + dot(grad_scores, qm[j])
                dq_t[own, :] += dot(key_t[own, rows], grad_scores)
                ready = ahead
            out_ref[rows, LANES : 2 * LANES] = (grad_key * scale).astype(BF16)
            out_ref[rows, 2 * LANES : 3 * LANES] = grad_val.astype(BF16)

        out_ref[:, 0:LANES] = (dq_t[...].T * scale).astype(BF16)

    masked = pltpu.VMEM((live, total, LANES), BF16)
    turned = pltpu.VMEM((LANES, total), BF16)
    turned_f = pltpu.VMEM((LANES, total), F32)
    return run(
        body,
        [qkv, grad_att, att, logs],
        after,
        grid=(1,),
        in_specs=[
            pl.BlockSpec((total, 3 * LANES), lambda i: (0, tile)),
            pl.BlockSpec((total, LANES), lambda i: (0, tile)),
            pl.BlockSpec((total, LANES), lambda i: (0, att_tile)),
            pl.BlockSpec((total, LANES), lambda i: (0, 0)),
        ],
        out_specs=pl.BlockSpec((total, 3 * LANES), lambda i: (0, 0)),
        out_shape=sds((total, 3 * LANES), BF16),
        scratch_shapes=[masked] * 4
        + [turned] * 3
        + [turned_f] * 2
        + [pltpu.VMEM((8, total), F32)],
        vmem=17,
        cost_estimate=cost(
            2 * live * total * total * 256 * 5, 3 * 1024 * 1024, live * total * total, part
        ),
        name="attend_backward",
    )


def project_weights(rows_all, gain, shift, grad_tiles, pieces, quads, packed, after):
    total, width = rows_all.shape
    tiles = len(grad_tiles)
    tile_cols = grad_tiles[0].shape[1]
    cols_all = tiles * tile_cols
    chunk = width // (quads * pieces)

    def body(*refs):
        x_ref, gain_ref, shift_ref, refs = refs[0], refs[1], refs[2], refs[3:]
        dq_refs, (*dw_refs, low_t, part_ref) = refs[:tiles], refs[tiles:]
        _, part, quad = place(pieces)

        @pl.loop(0, total // ROWS)
        def _(i):
            rows = pl.ds(pl.multiple_of(i * ROWS, ROWS), ROWS)
            normed, _ = norm_rows(x_ref[rows, :].astype(F32))
            low_t[:, rows] = (normed * gain_ref[...] + shift_ref[...]).T.astype(BF16)

        for t in range(tiles):
            cols = slice(t * tile_cols, (t + 1) * tile_cols)
            part_ref[...] = dot(low_t[...], dq_refs[t][...]).astype(BF16)
            if not packed:
                dw_refs[0][:, cols] = part_ref[...]
                continue
            for c in range(pieces):

                @pl.when(part == c)
                def _(c=c, cols=cols):
                    for q in range(quads):
                        for e in range(pieces):
                            at = (q * pieces + (c + e) % pieces) * chunk
                            dw_refs[e][q ^ quad, :, cols] = part_ref[at : at + chunk, :]

    if packed:
        grads = [sds((quads, chunk, cols_all), BF16)] * pieces
    else:
        grads = [sds((width, cols_all), BF16)]
    return run(
        body,
        [rows_all, gain, shift, *grad_tiles],
        after,
        out_shape=grads,
        scratch_shapes=[pltpu.VMEM((width, total), BF16), pltpu.VMEM((width, tile_cols), BF16)],
        vmem=12,
        cost_estimate=cost(2 * total * width * cols_all, 6 * 1024 * 1024),
        name="project_weights",
    )


def project_rows(
    rows_all, weight, grad_tiles, sums_mid, up_sums, pieces, quads, packed, real, after
):
    total, width = rows_all.shape
    piece_rows = total // pieces
    cols_all = weight.shape[1]
    tiles = len(grad_tiles)
    tile_cols = cols_all // tiles

    def body(*refs):
        x_ref, w_ref, mid_ref, refs = *refs[:3], refs[3:]
        ups_refs, refs = refs[: len(up_sums)], refs[len(up_sums) :]
        dq_refs, refs = refs[:tiles], refs[tiles:]
        own_ref, refs = refs[0], refs[1:]
        send_refs, (sums_ref, bias_ref) = refs[: pieces - 1], refs[pieces - 1 :]
        _, part, _ = place(pieces)
        sums_ref[...] = jnp.zeros_like(sums_ref)
        bias_ref[...] = jnp.zeros_like(bias_ref)
        for h in range(pieces):

            @pl.loop(0, piece_rows // ROWS)
            def _(i, h=h):
                at = pl.multiple_of(i * ROWS, ROWS)
                src = pl.ds(at, ROWS)
                rows = pl.ds(h * piece_rows + at, ROWS)
                normed, _ = norm_rows(x_ref[rows, :].astype(F32))
                grad = jnp.zeros((ROWS, width), F32)
                for t in range(tiles):
                    grad_rows = dq_refs[t][rows, :]
                    cols = slice(t * tile_cols, (t + 1) * tile_cols)
                    grad = grad + dot_nt(grad_rows, w_ref[:, cols])
                    bias_ref[0:1, cols] += jnp.sum(grad_rows.astype(F32), axis=0, keepdims=True)
                if h == 0:
                    own_ref[src, :] = grad
                else:
                    send_refs[h - 1][src, :] = grad.astype(BF16)
                sums_ref[0:1, :] += jnp.sum(grad * normed, axis=0, keepdims=True)
                sums_ref[1:2, :] += jnp.sum(grad, axis=0, keepdims=True)

        if not packed:
            return
        for row, src in ((4, 2), (5, 0), (6, 1), (15, 3)):
            sums_ref[row : row + 1, :] = mid_ref[src : src + 1, :]
        for c in range(pieces):

            @pl.when(part == c)
            def _(c=c):
                for row, p in ((2, 0), (3, 2)):
                    mine = jnp.concatenate(
                        [
                            bias_ref[0:1, (3 * t + p) * LANES :][:, : min(LANES, real - t * LANES)]
                            for t in range(tiles)
                        ],
                        axis=1,
                    )
                    sums_ref[row : row + 1, c * real : (c + 1) * real] = mine
                for n in range(quads):
                    row = 7 + n * pieces + c
                    start = 0
                    for ref in ups_refs:
                        size = ref.shape[1] // quads
                        here = ref[0:1, n * size : (n + 1) * size]
                        sums_ref[row : row + 1, start : start + size] = here
                        start += size

    return run(
        body,
        [rows_all, weight, sums_mid, *up_sums, *grad_tiles],
        after,
        out_shape=[sds((piece_rows, width), F32)]
        + [sds((piece_rows, width), BF16)] * (pieces - 1)
        + [sds((16, width), F32), sds((8, cols_all), F32)],
        vmem=12,
        cost_estimate=cost(2 * total * width * cols_all, 8 * 1024 * 1024),
        name="project_rows",
    )


def finish_rows(rows_all, gain, grad_mid, grad_own, received, count, after):
    rows, width = grad_mid.shape
    others = len(received)
    piece = rows // count
    per_step = ROWS // piece

    def body(*refs):
        x_ref, gain_ref, gm_ref, own_ref, refs = refs[0], refs[1], refs[2], refs[3], refs[4:]
        recv_refs, out_refs = refs[:others], refs[others:]
        for n in range(rows // ROWS):
            at = slice(n * ROWS, (n + 1) * ROWS)
            normed, inv_std = norm_rows(x_ref[at, :].astype(F32))
            grad = own_ref[at, :]
            for ref in recv_refs:
                grad = grad + ref[at, :].astype(F32)
            done = gm_ref[at, :] + norm_back(grad * gain_ref[...], normed, inv_std)
            for e in range(per_step):
                out_refs[n * per_step + e][...] = done[e * piece : (e + 1) * piece, :].astype(BF16)

    return run(
        body,
        [rows_all, gain, grad_mid, grad_own, *received],
        after,
        out_shape=[sds((piece, width), BF16)] * count,
        vmem=12,
        cost_estimate=cost(20 * rows * width, 6 * 1024 * 1024),
        name="finish_rows",
    )


def finish_result(own, received, count):
    rows, width = own.shape
    others = len(received)
    piece = rows // count

    def body(*refs):
        out_refs = refs[1 + others :]
        for n in range(count):
            at = slice(n * piece, (n + 1) * piece)
            total = refs[0][at, :]
            for ref in refs[1 : 1 + others]:
                total = total + ref[at, :].astype(F32)
            out_refs[n % 2][n // 2] = total.astype(BF16)

    return run(
        body,
        [far(own), *received],
        out_shape=[sds((count // 2, piece, width), BF16)] * 2,
        vmem=8,
        cost_estimate=cost(2 * rows * width, 3 * 1024 * 1024),
        name="finish_result",
    )


def pass_on(keep, received, after):
    def body(keep_ref, recv_ref, out_ref):
        out_ref[0] = keep_ref[1]
        out_ref[1] = recv_ref[1]

    return run(
        body,
        [keep, received],
        after,
        out_shape=sds(keep.shape, keep.dtype),
        vmem=6,
        cost_estimate=cost(0, 4 * keep.size),
        name="pass_on",
    )


def collect_halves(keep, near, far, group, after):
    _, rows, width = keep.shape

    def body(keep_ref, near_ref, far_ref, out_ref):
        _, _, quad = place(group)
        out_ref[quad] = keep_ref[0]
        out_ref[quad ^ 1] = near_ref[0]
        out_ref[quad ^ 2] = far_ref[0]
        out_ref[quad ^ 3] = far_ref[1]

    return run(
        body,
        [keep, near, far],
        after,
        out_shape=sds((4, rows, width), keep.dtype),
        vmem=6,
        cost_estimate=cost(0, 16 * rows * width),
        name="collect_halves",
    )


def two_parts(item):
    first = item.astype(BF16)
    return first, (item - first.astype(F32)).astype(BF16)


def pack_attention(
    qkv_keep, qkv_recv, out_keep, out_recv, small, small_recv, real, blocks, after
):
    quads, chunk, cols_all = qkv_keep.shape
    wide = cols_all // 3
    tiles = wide // LANES
    width = out_keep.shape[2]
    qkv_lanes = 6 * real // blocks
    out_lanes = width // blocks
    lanes = qkv_lanes + out_lanes
    halves = quads // 2
    slot = halves * chunk
    small_rows = small.shape[0]

    def body(qk_ref, qr_ref, ok_ref, or_ref, small_ref, srecv_ref, *out_refs):
        _, part, quad = place(2)
        mine = lax.axis_index("batch")
        slots = out_refs[4]

        def heads_of(rows, p):
            return [
                rows[:, (3 * t + p) * LANES : (3 * t + p) * LANES + min(LANES, real - t * LANES)]
                for t in range(tiles)
            ]

        for c in range(2):

            @pl.when(part == c)
            def _(c=c):
                for q in range(quads):
                    pair = (qk_ref[q], qr_ref[q])
                    if c == 1:
                        pair = pair[::-1]
                    parts = []
                    for p in range(3):
                        parts += heads_of(pair[0], p) + heads_of(pair[1], p)
                    row = jnp.concatenate(parts, axis=1)
                    for b in range(blocks):
                        slots[b ^ mine, q, :, 0:qkv_lanes] = row[
                            :, b * qkv_lanes : (b + 1) * qkv_lanes
                        ]
                for e, ref in enumerate((ok_ref, or_ref)):
                    for n in range(halves):
                        q = ((c + e) % 2) * halves + n
                        for b in range(blocks):
                            slots[b ^ mine, q ^ quad, :, qkv_lanes:lanes] = ref[
                                n, :, b * out_lanes : (b + 1) * out_lanes
                            ]

        for n, order in enumerate(((0, 2), (1, 3), (0, 1), (2, 3))):
            for e in range(2):
                for f in range(halves):
                    at = e * slot + f * chunk
                    src = f if n < 2 else halves + f
                    out_refs[n][at : at + chunk, :] = slots[order[e], src]
        parts = two_parts(small_ref[...] + srecv_ref[...])
        for n in range(2):
            for e in range(2):
                at = 2 * slot + e * small_rows
                out_refs[n][at : at + small_rows, :] = parts[e]

    first = sds((2 * slot + 2 * small_rows, lanes), BF16)
    other = sds((2 * slot, lanes), BF16)
    return run(
        body,
        [qkv_keep, qkv_recv, out_keep, out_recv, small, small_recv],
        after,
        out_shape=[first, first, other, other],
        scratch_shapes=[pltpu.VMEM((blocks, quads, chunk, lanes), BF16)],
        vmem=12,
        cost_estimate=cost(0, 4 * 1024 * 1024),
        name="pack_attention",
    )


def sum_first(keeps, received, after=()):
    count = len(keeps)
    shape = keeps[0].shape[1:]

    def body(*refs):
        for n in range(count):
            for e in range(2):
                total = refs[n][e].astype(F32) + refs[count + n][e].astype(F32)
                refs[2 * count + 2 * n + e][...] = total.astype(BF16)

    return run(
        body,
        [*keeps, *received],
        after,
        out_shape=[pltpu.HBM(shape, BF16), sds(shape, BF16)] * count,
        vmem=12,
        cost_estimate=cost(0, 6 * count * keeps[0].size),
        name="sum_first",
    )


def sum_second(keeps, received, after=()):
    quads, rows, width = keeps[0].shape

    def body(ka, kb, ra, rb, keep_ref, send_ref):
        for d in range(quads):
            ref = send_ref if d % 2 else keep_ref
            for e, (keep, recv) in enumerate(((ka, ra), (kb, rb))):
                total = keep[d].astype(F32) + recv[d].astype(F32)
                ref[d // 2, e] = total.astype(BF16)

    return run(
        body,
        [*keeps, *received],
        after,
        out_shape=[pltpu.HBM((quads // 2, 2, rows, width), BF16)] * 2,
        vmem=10,
        cost_estimate=cost(0, 12 * keeps[0].size),
        name="sum_second",
    )


def sum_third(keep, received, after=()):
    def body(keep_ref, recv_ref, stay_ref, pass_ref):
        for ref, e in ((stay_ref, 0), (pass_ref, 1)):
            ref[...] = (keep_ref[e].astype(F32) + recv_ref[e].astype(F32)).astype(BF16)

    return run(
        body,
        [keep, received],
        after,
        out_shape=[sds(keep.shape[1:], BF16)] * 2,
        vmem=6,
        cost_estimate=cost(0, 6 * keep.size),
        name="sum_third",
    )


def small_sum(refs, rows, count):
    total = None
    for ref in refs:
        for e in range(2):
            item = ref[rows + e * count : rows + (e + 1) * count, :].astype(F32)
            total = item if total is None else total + item
    return total


def sum_first_attention(keeps, received, slot, small_rows, after):
    lanes = keeps[0].shape[1]

    def body(ka, kb, ra, rb, stay_a, pass_a, stay_b, pass_b):
        parts = two_parts(small_sum((ka, ra), 2 * slot, small_rows))
        for keep, recv, stay, on in ((ka, ra, stay_a, pass_a), (kb, rb, stay_b, pass_b)):
            for e, ref in enumerate((stay, on)):
                at = slice(e * slot, (e + 1) * slot)
                ref[0:slot, :] = (keep[at, :].astype(F32) + recv[at, :].astype(F32)).astype(BF16)
        for ref in (stay_a, pass_a):
            for e in range(2):
                ref[slot + e * small_rows : slot + (e + 1) * small_rows, :] = parts[e]

    first = sds((slot + 2 * small_rows, lanes), BF16)
    other = sds((slot, lanes), BF16)
    return run(
        body,
        [*keeps, *received],
        after,
        out_shape=[first, first, other, other],
        vmem=8,
        cost_estimate=cost(0, 3 * 1024 * 1024),
        name="sum_first_attention",
    )


def sum_second_attention(keeps, received, chunk, quads, small_rows, after):
    lanes = keeps[0].shape[1]
    halves = quads // 2
    slot = halves * chunk

    def body(ka, kb, ra, rb, *out_refs):
        parts = two_parts(small_sum((ka, ra), slot, small_rows))
        for d in range(quads):
            keep, recv = ((ka, ra), (kb, rb))[d // halves]
            at = slice(d % halves * chunk, (d % halves + 1) * chunk)
            total = keep[at, :].astype(F32) + recv[at, :].astype(F32)
            out_refs[d][0:chunk, :] = total.astype(BF16)
            for e in range(2):
                at = chunk + e * small_rows
                out_refs[d][at : at + small_rows, :] = parts[e]

    return run(
        body,
        [*keeps, *received],
        after,
        out_shape=[sds((chunk + 2 * small_rows, lanes), BF16)] * quads,
        vmem=8,
        cost_estimate=cost(0, 2 * 1024 * 1024),
        name="sum_second_attention",
    )


def final_attention(pieces, chunk, qkv_lanes, small_rows):
    lanes = pieces[0].shape[1]
    count = len(pieces)

    def body(*refs):
        total = refs[0][0:chunk, :].astype(F32)
        for ref in refs[1:count]:
            total = total + ref[0:chunk, :].astype(F32)
        refs[count][...] = total[:, :qkv_lanes]
        refs[count + 1][...] = total[:, qkv_lanes:]
        refs[count + 2][...] = small_sum(refs[:count], chunk, small_rows)

    return run(
        body,
        pieces,
        out_shape=[
            sds((chunk, qkv_lanes), F32),
            sds((chunk, lanes - qkv_lanes), F32),
            sds((small_rows, lanes), F32),
        ],
        vmem=6,
        cost_estimate=cost(0, 1024 * 1024),
        name="final_attention",
    )


def final_units(first, second, after):
    high = first[0].shape[1]
    sizes = [first[0].shape[2], second[0].shape[2]]
    unit_block = sum(sizes)
    count = len(first)
    half = high // 2

    def body(*refs):
        _, part, _ = place(2)
        keep_ref, send_ref, down_ref = refs[2 * count :]
        for h in range(2):
            pieces = refs[h * count : (h + 1) * count]
            up, down = pieces[0][0].astype(F32), pieces[0][1].astype(F32)
            for ref in pieces[1:]:
                up = up + ref[0].astype(F32)
                down = down + ref[1].astype(F32)
            here = slice(h * sizes[0], h * sizes[0] + sizes[h])
            down_ref[here, :] = down.T
            for c in range(2):

                @pl.when(part == c)
                def _(up=up, here=here, c=c):
                    keep_ref[:, here] = up[c * half : (c + 1) * half, :]
                    send_ref[:, here] = up[(1 - c) * half : (2 - c) * half, :].astype(BF16)

    return run(
        body,
        [*first, *second],
        after,
        out_shape=[
            sds((half, unit_block), F32),
            sds((half, unit_block), BF16),
            sds((unit_block, high), F32),
        ],
        vmem=10,
        cost_estimate=cost(0, 4 * 1024 * 1024),
        name="final_units",
    )


def final_join(keep, recv):
    chunk, unit_block = keep.shape

    def body(keep_ref, recv_ref, out_ref):
        _, part, _ = place(2)
        for c in range(2):

            @pl.when(part == c)
            def _(c=c):
                out_ref[:, c * unit_block : (c + 1) * unit_block] = keep_ref[...]
                out_ref[:, (1 - c) * unit_block : (2 - c) * unit_block] = recv_ref[...].astype(F32)

    return run(
        body,
        [keep, recv],
        out_shape=sds((chunk, 2 * unit_block), F32),
        vmem=5,
        cost_estimate=cost(0, 1024 * 1024),
        name="final_join",
    )


def on_device(
    tokens,
    mask,
    cotangent,
    ln1_gain,
    ln1_bias,
    qkv_weight,
    q_bias,
    v_bias,
    out_weight,
    out_bias,
    ln2_gain,
    ln2_bias,
    up_weight,
    up_bias,
    down_weight,
    down_bias,
):
    seq_size = lax.axis_size("seq")
    batch_size = lax.axis_size("batch")
    micro_count, seq_count, local_len, width = tokens.shape
    sequences = micro_count * seq_count
    group = seq_size // sequences
    units = up_weight.shape[1]
    head_dim = width // HEADS
    heads = HEADS // group
    real = heads * head_dim
    wide = -(-real // LANES) * LANES
    full_len = local_len * seq_size
    block_len = local_len // group
    rows = seq_size * block_len
    own_units = units // group
    part = lax.axis_index("seq") % group
    aligned = (
        seq_size == batch_size * group
        and group == 2
        and batch_size == 4
        and wide == 3 * LANES
        and (seq_size // group) % group == 0
        and units % (batch_size * group * LANES) == 0
        and own_units // batch_size == width
    )

    def from_part(item, ahead):
        if ahead % group == 0:
            return item
        pairs = [
            (q * group + (c + ahead) % group, q * group + c)
            for q in range(sequences)
            for c in range(group)
        ]
        return lax.ppermute(item, "seq", pairs)

    def gather_parts(item):
        return [from_part(item, n) for n in range(group)]

    def row_of(item):
        return item.astype(F32)[None, :]

    def blocks_of(item):
        return item.reshape(sequences, local_len, width)

    x_own = over_quads(deal(blocks_of(tokens), group), group)
    x_pieces = [from_part(item, n) for n in range(group) for item in x_own]

    count_rows = jnp.sum(mask, axis=2).reshape(sequences).astype(BF16)
    cot_low = jnp.where(mask[..., None] != 0, cotangent, jnp.zeros_like(cotangent))
    cot_send = jnp.concatenate(
        [blocks_of(cot_low), jnp.broadcast_to(count_rows[:, None, None], (sequences, 16, width))],
        axis=1,
    )
    cot_own = over_quads(deal(cot_send, group, x_pieces[sequences:]), group)

    qkv_w, qkv_b, *out_w = pick_weights(
        qkv_weight,
        jnp.concatenate([q_bias, jnp.zeros_like(q_bias), v_bias])[None, :],
        out_weight,
        group,
        real,
        wide,
    )
    if aligned:
        up_own, up_b, down_own = up_weight, up_bias[None, :], down_weight
    else:

        def own_columns(matrix, blocks):
            split = matrix.reshape(matrix.shape[0], blocks, group, -1)
            return lax.dynamic_index_in_dim(split, part, 2, keepdims=False)

        up_own = own_columns(up_weight, batch_size).reshape(width, own_units)
        up_b = own_columns(up_bias[None, :], batch_size).reshape(1, own_units)
        down_own = lax.dynamic_index_in_dim(
            down_weight.reshape(batch_size, group, -1, width), part, 1, keepdims=False
        ).reshape(own_units, width)

    tiles = wide // LANES
    x_all, qkv, att_first, logs_first = attend_first(
        x_pieces, row_of(ln1_gain), row_of(ln1_bias), qkv_w, qkv_b, tiles - 1, heads, head_dim
    )
    cot_stack = stack(cot_own, [logs_first])
    att_last, logs_last = attend_last(qkv, tiles - 1, heads, head_dim, [cot_stack])
    cot_pieces = cot_own + [
        item[d]
        for item in gather_parts(cot_stack)[1:]
        for d in range(sequences)
    ]
    blocks = batch_size if aligned else 1
    unit_block = own_units // blocks
    size = unit_block * 2 // 5
    shape = (group, sequences if aligned else None, width // sequences)
    calls = [
        Units(unit_block, blocks, 0, size, *shape),
        Units(unit_block, blocks, size, unit_block - size, *shape),
    ]
    mid, second, second_t, grad_rows, grad_t, result_own, grad_second, *found = feed_first(
        x_all,
        gather_parts(att_first),
        gather_parts(att_last),
        cot_pieces,
        out_w,
        row_of(out_bias),
        row_of(ln2_gain),
        row_of(ln2_bias),
        up_own,
        up_b,
        down_own,
        row_of(down_bias),
        calls[0],
    )
    up_sums, ff_grads = [found[0]], [found[group:]]
    result_own, grad_second, *found = feed_second(
        second,
        second_t,
        grad_rows,
        grad_t,
        result_own,
        grad_second,
        found[1:group],
        up_own,
        up_b,
        down_own,
        calls[1],
    )
    up_sums.append(found[0])
    result_send = found[1:group]
    ff_grads.append(found[group:])

    def begin_sum(e, sends, after):
        moved = [swap(sends[0], "batch", batch_size, 1), swap(sends[1], "batch", batch_size, 2)]
        stay_a, pass_a, stay_b, pass_b = sum_first(
            [ff_grads[e][0], ff_grads[e][2]], moved, after
        )
        moved = [swap(pass_a, "batch", batch_size, 2), swap(pass_b, "batch", batch_size, 1)]
        return [stay_a, stay_b], moved

    if aligned:
        waiting = begin_sum(0, [ff_grads[0][1], ff_grads[0][3]], [])
        (grad_second,) = gate([grad_second], waiting[0][:1])
    second_send = grad_second
    second_recv = [from_part(second_send, n) for n in range(1, group)]
    result_recv = [from_part(result_send[group - n - 1], n) for n in range(1, group)]
    result_keep, result_pass = finish_result(result_own, result_recv, sequences)

    def quad_swap(item, distance):
        return swap(item, "seq", seq_size, distance * group)

    result_near = quad_swap(result_pass, 1)

    chunk = width // seq_size
    grad_mid, grad_att, sums_mid, *out_grad = mid_back(
        mid,
        grad_second,
        second_recv,
        grad_rows,
        row_of(ln2_gain),
        out_w[0],
        att_first,
        att_last,
        chunk if aligned else 0,
    )

    def tile_back(t, after, cost_part=1):
        last = t == tiles - 1
        return attend_backward(
            qkv,
            grad_att,
            att_last if last else att_first,
            0 if last else t,
            logs_last if last else logs_first,
            0 if last else t * (LANES // head_dim),
            t,
            heads,
            head_dim,
            after,
            cost_part,
        )

    grad_tiles = [None] * tiles
    after = [result_keep]
    if aligned:
        keep, send = sum_second(*waiting, [grad_mid])
        moved = quad_swap(send, 1)
        sends = gate([ff_grads[1][1], ff_grads[1][3]], [keep])
        after = [result_keep, keep]
    grad_tiles[0] = tile_back(0, after, 64)
    result_pass = pass_on(result_keep, result_near, grad_tiles[:1])
    result_far = quad_swap(result_pass, 2)
    after = [result_pass]
    if aligned:
        unit_first = list(sum_third(keep, moved, [grad_tiles[0]]))
        unit_first[1] = quad_swap(unit_first[1], 2)
        waiting = begin_sum(1, sends, [grad_tiles[0]])
        after = [result_pass, unit_first[0], waiting[0][0]]
    for t in range(1, tiles - 1):
        grad_tiles[t] = tile_back(t, after)
    after = [grad_tiles[-2], result_far]
    if aligned:
        out_recv = from_part(out_grad[1], 1)
        keep, send = sum_second(*waiting, [grad_tiles[-2]])
        moved = quad_swap(send, 1)
        after = [keep, result_far, unit_first[1]]
    grad_tiles[-1] = tile_back(tiles - 1, after)
    after = []
    if aligned:
        after = [out_recv]
    qkv_grad = project_weights(
        x_all,
        row_of(ln1_gain),
        row_of(ln1_bias),
        grad_tiles,
        group,
        sequences,
        aligned,
        after,
    )
    after = qkv_grad[:1]
    if aligned:
        unit_second = list(sum_third(keep, moved, qkv_grad[:1]))
        unit_second[1] = quad_swap(unit_second[1], 2)
        after = unit_second[:1]
    first_own, *found = project_rows(
        x_all,
        qkv_w,
        grad_tiles,
        sums_mid,
        up_sums,
        group,
        sequences,
        aligned,
        real,
        after,
    )
    first_send, (small, bias_sums) = found[: group - 1], found[group - 1 :]
    first_recv = [from_part(first_send[group - n - 1], n) for n in range(1, group)]
    after = []
    if aligned:
        small_rows = small.shape[0]
        packed = pack_attention(
            qkv_grad[0],
            from_part(qkv_grad[1], 1),
            out_grad[0],
            out_recv,
            small,
            from_part(small, 1),
            real,
            batch_size,
            [],
        )
        after = packed[:1]
    row_parts = finish_rows(
        x_all, row_of(ln1_gain), grad_mid, first_own, first_recv, sequences, after
    )
    row_moved = over_quads(row_parts, group)
    if aligned:
        stay_a, pass_a, stay_b, pass_b = sum_first_attention(
            [packed[0], packed[2]],
            [swap(packed[1], "batch", batch_size, 1), swap(packed[3], "batch", batch_size, 2)],
            sequences // 2 * chunk,
            small_rows,
            [row_parts[0], row_moved[1], unit_second[1]],
        )
        summed = sum_second_attention(
            [stay_a, stay_b],
            [swap(pass_a, "batch", batch_size, 2), swap(pass_b, "batch", batch_size, 1)],
            chunk,
            sequences,
            small_rows,
            row_moved[3:],
        )
        after = summed[:1]
        up_keep, up_send, down_grad = final_units(unit_first, unit_second, after)
        up_grad = final_join(up_keep, from_part(up_send, 1))
        qkv_final, out_final, small = final_attention(
            over_quads(summed, group), chunk, qkv_weight.shape[1] // batch_size, small_rows
        )
        small = small.reshape(-1)
    result = collect_halves(result_keep, result_near, result_far, group, after)
    result = result.reshape(tokens.shape)
    grad_in = collect(row_moved, group, after).reshape(tokens.shape)
    if not aligned:

        def spread(item, blocks):
            split = item.reshape(blocks, 1, -1)
            empty = jnp.zeros((blocks, group, split.shape[2]), F32)
            return lax.dynamic_update_slice(empty, split, (0, part, 0)).reshape(-1)

        bias_sums = bias_sums[0].reshape(tiles, 3, LANES).transpose(1, 0, 2)
        bias_sums = bias_sums.reshape(3, wide)[:, :real]
        small = jnp.concatenate(
            [
                small[0],
                small[1],
                spread(bias_sums[0], 1),
                spread(bias_sums[2], 1),
                sums_mid[2],
                sums_mid[0],
                sums_mid[1],
                spread(jnp.concatenate([item[0] for item in up_sums]), batch_size),
                sums_mid[3],
            ]
        )

        def scattered(item):
            item = lax.psum_scatter(item.astype(BF16), "seq", scatter_dimension=0, tiled=True)
            return lax.psum_scatter(item, "batch", scatter_dimension=1, tiled=True).astype(F32)

        def spread_columns(item, blocks):
            split = item.reshape(item.shape[0], blocks, 1, -1)
            empty = jnp.zeros((item.shape[0], blocks, group, split.shape[3]), item.dtype)
            filled = lax.dynamic_update_slice(empty, split, (0, 0, part, 0))
            return filled.reshape(item.shape[0], -1)

        up_full, down_full = [
            jnp.concatenate([item[e] for item in ff_grads], axis=1) for e in range(2)
        ]
        up_grad = scattered(spread_columns(up_full, batch_size))
        down_grad = scattered(spread_columns(down_full, batch_size).T)
        rows_full = qkv_grad[0].reshape(width, tiles, 3, LANES).transpose(0, 2, 1, 3)
        rows_full = rows_full.reshape(width, 3, wide)[..., :real]
        qkv_final = scattered(spread_columns(rows_full.reshape(width, -1), 3))
        out_final = scattered(spread_columns(out_grad[0][:real].T, 1).T)
        small = lax.psum(small, ("seq", "batch"))

    edges = [width] * 7 + [units, width]
    pieces, start = [], 0
    for size in edges:
        pieces.append(small[start : start + size])
        start += size
    return (
        result,
        grad_in,
        pieces[0],
        pieces[1],
        qkv_final,
        pieces[2],
        pieces[3],
        out_final,
        pieces[4],
        pieces[5],
        pieces[6],
        up_grad,
        pieces[7],
        down_grad,
        pieces[8],
    )


def solution(mesh):
    rows = P(None, "batch", "seq", None)
    split = P("seq", "batch")
    in_specs = (rows, P(None, "batch", "seq"), rows) + (P(),) * 13
    out_specs = (
        rows,
        rows,
        P(),
        P(),
        split,
        P(),
        P(),
        split,
        P(),
        P(),
        P(),
        split,
        P(),
        split,
        P(),
    )
    return jax.shard_map(
        on_device, mesh=mesh, in_specs=in_specs, out_specs=out_specs, check_vma=False
    )
```

```python
import jax
import jax.numpy as jnp
from jax import lax
from jax.experimental import pallas as pl
from jax.experimental.pallas import tpu as pltpu
from jax.sharding import PartitionSpec as P

HEADS = 20
EPS = 1e-05
LOG2E = 1.4426950408889634
ROWS = 256
F32 = jnp.float32
BF16 = jnp.bfloat16
LANES = 128


def dot(left, right):
    return jnp.dot(left, right, preferred_element_type=F32)


def dot_nt(left, right):
    return lax.dot_general(left, right, (((1,), (1,)), ((), ())), preferred_element_type=F32)


def norm_rows(rows_in):
    mean_val = jnp.mean(rows_in, axis=-1, keepdims=True)
    centered = rows_in - mean_val
    inv_std = lax.rsqrt(jnp.mean(centered * centered, axis=-1, keepdims=True) + EPS)
    return centered * inv_std, inv_std


def norm_back(scaled, normed, inv_std):
    inner = (
        scaled
        - jnp.mean(scaled, axis=-1, keepdims=True)
        - normed * jnp.mean(scaled * normed, axis=-1, keepdims=True)
    )
    return inner * inv_std


def params_of(mib):
    return pltpu.CompilerParams(vmem_limit_bytes=mib * 1024 * 1024)


def cost(flops, moved, trans=0, part=1):
    return pl.CostEstimate(
        flops=flops // part, bytes_accessed=moved // part, transcendentals=trans // part
    )


def sds(shape, dtype):
    return jax.ShapeDtypeStruct(shape, dtype)


VMEM = pl.BlockSpec(memory_space=pltpu.VMEM)
ANY = pl.BlockSpec(memory_space=pl.ANY)
HBM = pl.BlockSpec(memory_space=pltpu.HBM)


def run(body, operands, after=(), in_specs=None, out_specs=None, vmem=32, **more):
    count, extra = len(operands), len(after)

    def inner(*refs):
        body(*refs[:count], *refs[count + extra :])

    specs = [VMEM] * count if in_specs is None else list(in_specs)
    shapes = more["out_shape"]
    if out_specs is None:
        out_specs = [VMEM] * len(shapes) if isinstance(shapes, (list, tuple)) else VMEM
    return pl.pallas_call(
        inner,
        in_specs=specs + [ANY] * extra,
        out_specs=out_specs,
        compiler_params=params_of(vmem),
        **more,
    )(*operands, *after)


def far(item):
    return pltpu.with_memory_space_constraint(item, pltpu.HBM)


def gate(items, after):
    def body(*refs):
        del refs

    return pl.pallas_call(
        body,
        in_specs=[ANY] * (len(items) + len(after)),
        out_specs=[ANY] * len(items),
        out_shape=[sds(item.shape, item.dtype) for item in items],
        input_output_aliases={n: n for n in range(len(items))},
        cost_estimate=cost(0, 0),
        name="gate",
    )(*items, *after)


def place(group):
    spot = lax.axis_index("seq")
    return spot, lax.rem(spot, group), lax.div(spot, group)


def deal(item, group, after=()):
    count, rows, width = item.shape

    def body(in_ref, *out_refs):
        _, _, quad = place(group)
        for d in range(count):
            out_refs[d][...] = in_ref[quad ^ d]

    return run(
        body,
        [item],
        after,
        out_shape=[sds((rows, width), item.dtype)] * count,
        vmem=6,
        cost_estimate=cost(0, 4 * count * rows * width),
        name="deal",
    )


def collect(pieces, group, after):
    count = len(pieces)
    rows, width = pieces[0].shape

    def body(*refs):
        _, _, quad = place(group)
        for d in range(count):
            refs[count][quad ^ d] = refs[d][...]

    return run(
        body,
        pieces,
        after,
        out_shape=sds((count, rows, width), pieces[0].dtype),
        vmem=6,
        cost_estimate=cost(0, 4 * count * rows * width),
        name="collect",
    )


def stack(pieces, after):
    count = len(pieces)

    def body(*refs):
        for d in range(count):
            refs[count][d] = refs[d][...]

    return run(
        body,
        pieces,
        after,
        out_shape=sds((count,) + pieces[0].shape, pieces[0].dtype),
        vmem=12,
        cost_estimate=cost(0, 4 * count * pieces[0].size),
        name="stack",
    )


def swap(item, axis, size, distance):
    return lax.ppermute(item, axis, [(i, i ^ distance) for i in range(size)])


def over_quads(pieces, group):
    return [
        piece if d == 0 else swap(piece, "seq", len(pieces) * group, d * group)
        for d, piece in enumerate(pieces)
    ]


def pick_weights(qkv_weight, qkv_bias, out_weight, group, real, wide):
    width = qkv_weight.shape[0]
    tiles = wide // LANES

    def body(w_ref, b_ref, o_ref, wo_ref, bo_ref, *out_refs):
        _, part, _ = place(group)
        wo_ref[...] = jnp.zeros_like(wo_ref)
        bo_ref[...] = jnp.zeros_like(bo_ref)
        for ref in out_refs:
            ref[...] = jnp.zeros_like(ref)
        for c in range(group):

            @pl.when(part == c)
            def _(c=c):
                for p in range(3):
                    for t in range(tiles):
                        some = min(LANES, real - t * LANES)
                        src = p * width + c * real + t * LANES
                        dst = (3 * t + p) * LANES
                        wo_ref[:, dst : dst + some] = w_ref[:, src : src + some]
                        bo_ref[:, dst : dst + some] = b_ref[:, src : src + some]
                for n in range(group):
                    src = (c + n) % group * real
                    out_refs[n][0:real, :] = o_ref[src : src + real, :]

    return pl.pallas_call(
        body,
        out_shape=[sds((width, 3 * wide), BF16), sds((1, 3 * wide), F32)]
        + [sds((wide, width), BF16)] * group,
        compiler_params=params_of(24),
        cost_estimate=cost(0, 8 * 1024 * 1024),
        name="pick_weights",
    )(qkv_weight, qkv_bias, out_weight)


def by_pairs(live, visit):
    size = 2 if live % 2 == 0 else 1

    @pl.loop(0, live // size)
    def _(i):
        visit([i * size + e for e in range(size)])


def attend_tiles(query_at, keys_at, vals_at, att_ref, lse_ref, keys, vals, acc, tiles, heads, head_dim):
    per_tile = LANES // head_dim
    total = att_ref.shape[0]
    exp_scale = head_dim ** (-0.5) * LOG2E
    lane = lax.broadcasted_iota(jnp.int32, (1, LANES), 1)
    row = lax.broadcasted_iota(jnp.int32, (LANES, 1), 0)
    lse_ref[...] = jnp.zeros_like(lse_ref)
    vals[:, :, LANES:] = jnp.ones((per_tile, total, LANES), BF16)
    for n, t in enumerate(tiles):
        live = min(per_tile, heads - t * per_tile)
        key_t = keys_at(n).astype(F32).T
        val_f = vals_at(n).astype(F32)
        for j in range(live):
            keys[j] = jnp.where(row // head_dim == j, key_t, 0.0).astype(BF16)
            vals[j, :, :LANES] = jnp.where(lane // head_dim == j, val_f, 0.0).astype(BF16)
        acc[...] = jnp.zeros_like(acc)

        def visit(some, n=n):
            scores = [dot(query_at(n), keys[j]) for j in some]
            for item, j in zip(scores, some):
                row_max = jnp.max(item, axis=-1, keepdims=True) * exp_scale
                expd = jnp.exp2(item * exp_scale - row_max).astype(BF16)
                mixed = dot(expd, vals[j])
                den = mixed[:, LANES:]
                acc[...] += mixed[:, :LANES] / den
                lse_ref[...] = jnp.where(
                    lane == n * per_tile + j, row_max + jnp.log2(den), lse_ref[...]
                )

        by_pairs(live, visit)
        att_ref[:, n * LANES : (n + 1) * LANES] = acc[...].astype(BF16)


def attend_scratch(total, head_dim):
    per_tile = LANES // head_dim
    return [
        pltpu.VMEM((per_tile, LANES, total), BF16),
        pltpu.VMEM((per_tile, total, 2 * LANES), BF16),
        pltpu.VMEM((total, LANES), F32),
    ]


def attend_first(x_pieces, gain, shift, weight, bias, tiles, heads, head_dim):
    count = len(x_pieces)
    piece_rows, width = x_pieces[0].shape
    total = count * piece_rows
    cols_all = weight.shape[1]

    def body(*refs):
        x_refs = refs[:count]
        gain_ref, shift_ref, w_ref, bias_ref = refs[count : count + 4]
        x_ref, qkv_ref, att_ref, lse_ref, keys, vals, acc = refs[count + 4 :]
        for n in range(count):
            x_ref[n * piece_rows : (n + 1) * piece_rows, :] = x_refs[n][...]

        @pl.loop(0, total // ROWS)
        def _(i):
            rows = pl.ds(pl.multiple_of(i * ROWS, ROWS), ROWS)
            normed, _ = norm_rows(x_ref[rows, :].astype(F32))
            low = (normed * gain_ref[...] + shift_ref[...]).astype(BF16)
            qkv_ref[rows, :] = (dot(low, w_ref[...]) + bias_ref[...]).astype(BF16)

        def columns(at):
            return slice(at * LANES, (at + 1) * LANES)

        attend_tiles(
            lambda n: qkv_ref[:, columns(3 * n)],
            lambda n: qkv_ref[:, columns(3 * n + 1)],
            lambda n: qkv_ref[:, columns(3 * n + 2)],
            att_ref,
            lse_ref,
            keys,
            vals,
            acc,
            range(tiles),
            heads,
            head_dim,
        )

    return run(
        body,
        [*x_pieces, gain, shift, weight, bias],
        out_shape=[
            sds((total, width), BF16),
            sds((total, cols_all), BF16),
            sds((total, tiles * LANES), BF16),
            sds((total, LANES), F32),
        ],
        scratch_shapes=attend_scratch(total, head_dim),
        vmem=23,
        cost_estimate=cost(
            2 * total * width * cols_all + 4 * heads * total * total * 256,
            8 * 1024 * 1024,
            heads * total * total,
        ),
        name="attend_first",
    )


def attend_last(qkv, tile, heads, head_dim, after):
    total = qkv.shape[0]

    def body(qkv_ref, att_ref, lse_ref, keys, vals, acc):
        attend_tiles(
            lambda n: qkv_ref[:, 0:LANES],
            lambda n: qkv_ref[:, LANES : 2 * LANES],
            lambda n: qkv_ref[:, 2 * LANES : 3 * LANES],
            att_ref,
            lse_ref,
            keys,
            vals,
            acc,
            [tile],
            heads,
            head_dim,
        )

    live = heads - tile * (LANES // head_dim)
    return run(
        body,
        [qkv],
        after,
        grid=(1,),
        in_specs=[pl.BlockSpec((total, 3 * LANES), lambda i: (0, tile))],
        out_specs=[pl.BlockSpec((total, LANES), lambda i: (0, 0))] * 2,
        out_shape=[sds((total, LANES), BF16), sds((total, LANES), F32)],
        scratch_shapes=attend_scratch(total, head_dim),
        vmem=14,
        cost_estimate=cost(4 * live * total * total * 256, 2 * 1024 * 1024, live * total * total),
        name="attend_last",
    )


def gelu_parts(value):
    size = jnp.abs(value)
    near = pl.reciprocal(1.0 + (0.3275911 * 0.7071067811865476) * size, approx=True)
    bell = jnp.exp2(value * value * (-0.5 * LOG2E))
    poly = near * (
        0.5 * 0.254829592
        + near
        * (
            0.5 * -0.284496736
            + near * (0.5 * 1.421413741 + near * (0.5 * -1.453152027 + near * (0.5 * 1.061405429)))
        )
    )
    tail = poly * bell
    area = jnp.where(value < 0.0, tail, 1.0 - tail)
    return value * area, area + value * bell * 0.3989422804014327


class Units:
    def __init__(self, block, blocks, start, size, stride, quads, high):
        self.block, self.blocks, self.start, self.size = block, blocks, start, size
        self.stride, self.quads, self.high = stride, quads, high
        self.count = blocks * size
        self.chunk = 512 if self.count % 512 == 0 else 256
        self.packed = quads is not None

    def loads(self, part, hbm_up, hbm_down, hbm_bias, up_ref, down_ref, bias_ref, sem):
        copies = []
        for b in range(self.blocks):
            src = self.start
            if self.packed:
                src = pl.multiple_of((b * self.stride + part) * self.block, LANES) + self.start
            src = pl.ds(src, self.size)
            dst = pl.ds(b * self.size, self.size)
            copies.append(
                pltpu.make_async_copy(hbm_up.at[:, src], up_ref.at[:, dst], sem.at[2 * b])
            )
            copies.append(
                pltpu.make_async_copy(hbm_down.at[src, :], down_ref.at[dst, :], sem.at[2 * b + 1])
            )
            bias_ref[0:1, dst] = hbm_bias[:, src]
        return copies

    def grad_shapes(self, width):
        if self.packed:
            return [pltpu.HBM((2, self.quads, self.high, self.size), BF16)] * 4
        return [sds((width, self.count), BF16)] * 2

    def scratch(self, total, width):
        grads = (self.blocks, self.quads, self.high, self.size) if self.packed else (8, LANES)
        return [
            pltpu.VMEM(grads, BF16),
            pltpu.VMEM(grads, BF16),
            pltpu.SemaphoreType.DMA((8,)),
            pltpu.VMEM((total, self.count), BF16),
            pltpu.VMEM((total, self.count), BF16),
            pltpu.VMEM((width, self.count), BF16),
            pltpu.VMEM((self.count, width), BF16),
            pltpu.VMEM((8, self.count), F32),
            pltpu.SemaphoreType.DMA((2 * self.blocks,)),
        ]

    def compute(self, second, second_t, grad, grad_t, ubg, scratch, outs, give):
        up_slots, down_slots, out_sem, acts, grad_pres, up_ref, down_ref, bias_ref, _ = scratch
        if not self.packed:
            up_slots, down_slots = outs
        quad = lax.div(lax.axis_index("seq"), self.stride)
        mine = lax.axis_index("batch")

        def enter(i):
            rows = slice(i * ROWS, (i + 1) * ROWS)
            pre = dot(second[rows, :], up_ref[...]) + bias_ref[0:1, :]
            return pre, dot_nt(grad[rows, :], down_ref[...])

        def weights(n):
            first, last = n * self.chunk, (n + 1) * self.chunk
            up_grad = dot(second_t[...], grad_pres[:, first:last]).astype(BF16)
            down_grad = dot(grad_t[...], acts[:, first:last]).astype(BF16)
            if not self.packed:
                up_slots[:, first:last] = up_grad
                down_slots[:, first:last] = down_grad
                return
            at = first
            while at < last:
                block = at // self.size
                stop = min(last, (block + 1) * self.size)
                src = slice(at - first, stop - first)
                dst = slice(at - block * self.size, stop - block * self.size)
                for m in range(self.blocks):
                    rows = slice(m * self.high, (m + 1) * self.high)
                    up_slots[block ^ mine, m ^ quad, :, dst] = up_grad[rows, src]
                    down_slots[m ^ mine, block ^ quad, :, dst] = down_grad[rows, src]
                at = stop

        ready = enter(0)
        chunks = second.shape[0] // ROWS
        for i in range(chunks):
            ahead = enter(i + 1) if i + 1 < chunks else None
            rows = slice(i * ROWS, (i + 1) * ROWS)
            pre, grad_act = ready
            value, slope = gelu_parts(pre)
            act = value.astype(BF16)
            grad_pre = (grad_act * slope).astype(BF16)
            acts[rows, :] = act
            grad_pres[rows, :] = grad_pre
            ubg[0:1, :] += jnp.sum(grad_pre.astype(F32), axis=0, keepdims=True)
            give(i, rows, dot(act, down_ref[...]), dot_nt(grad_pre, up_ref[...]))
            ready = ahead
        for n in range(self.count // self.chunk):
            weights(n)
        stores = []
        if self.packed:
            order = ((up_slots, (0, 2)), (up_slots, (1, 3)), (down_slots, (0, 1)), (down_slots, (2, 3)))
            for m, (source, slots) in enumerate(order):
                for n in range(2):
                    stores.append(
                        pltpu.make_async_copy(
                            source.at[slots[n]], outs[m].at[n], out_sem.at[2 * m + n]
                        )
                    )
        return stores


def feed_first(
    rows_all, att_first, att_last, cot_pieces, out_w, out_b, gain, shift, up, up_b, down, down_b, units
):
    pieces = len(att_first)
    total, width = rows_all.shape
    piece_rows = total // pieces
    count = len(cot_pieces)
    cot_rows = total // count
    split = att_first[0].shape[1]
    grads = units.grad_shapes(width)

    def body(*refs):
        x_ref, refs = refs[0], refs[1:]
        att_refs, refs = refs[: 2 * pieces], refs[2 * pieces :]
        cot_refs, refs = refs[:count], refs[count:]
        wo_refs, refs = refs[:pieces], refs[pieces:]
        ob_ref, gain_ref, shift_ref, up_hbm, ub_ref, down_hbm, db_ref = refs[:7]
        mid_ref, second, second_t, grad, grad_t, own_ref, low_ref, ubg, refs = *refs[7:15], refs[15:]
        send_refs, refs = refs[: pieces - 1], refs[pieces - 1 :]
        outs, refs = refs[: len(grads)], refs[len(grads) :]
        mid_rows, mid_sem, *scratch = refs
        _, part, _ = place(pieces)
        loads = units.loads(part, up_hbm, down_hbm, ub_ref, *scratch[5:])
        for load in loads:
            load.start()
        ubg[...] = jnp.zeros_like(ubg)
        masked = jnp.zeros((1, width), F32)
        for ref in cot_refs:
            masked = masked + ref[cot_rows : cot_rows + 1, :].astype(F32)
        factor = total / (4.0 * masked)
        for n in range(count):
            scaled = cot_refs[n][0:cot_rows, :].astype(F32) * factor
            dst = slice(n * cot_rows, (n + 1) * cot_rows)
            grad[dst, :] = scaled.astype(BF16)

        for h in range(pieces):

            @pl.loop(0, piece_rows // ROWS)
            def _(i, h=h):
                at = pl.multiple_of(i * ROWS, ROWS)
                dst = pl.ds(h * piece_rows + at, ROWS)
                mid = x_ref[dst, :].astype(F32) + ob_ref[...]
                for n in range(pieces):
                    src = pl.ds(((h - n) % pieces) * piece_rows + at, ROWS)
                    mid = mid + dot(att_refs[2 * n][src, :], wo_refs[n][0:split, :])
                    mid = mid + dot(att_refs[2 * n + 1][src, :], wo_refs[n][split:, :])
                mid_rows[dst, :] = mid
                normed, _ = norm_rows(mid)
                low = normed * gain_ref[...] + shift_ref[...]
                second[dst, :] = low.astype(BF16)
                second_t[:, dst] = low.astype(BF16).T
                grad_t[:, dst] = grad[dst, :].T

        keep_mid = pltpu.make_async_copy(mid_rows, mid_ref, mid_sem)
        keep_mid.start()
        for load in loads:
            load.wait()

        def give(i, rows, result, grad_second):
            low_ref[rows, :] = grad_second.astype(BF16)
            h = i * ROWS // piece_rows
            at = slice(rows.start - h * piece_rows, rows.stop - h * piece_rows)
            if h == 0:
                own_ref[at, :] = mid_rows[rows, :] + db_ref[...] + result
            else:
                send_refs[h - 1][at, :] = result.astype(BF16)

        stores = units.compute(second, second_t, grad, grad_t, ubg, scratch, outs, give)
        for store in stores:
            store.start()
        keep_mid.wait()
        for store in stores:
            store.wait()

    att_all = [item for pair in zip(att_first, att_last) for item in pair]
    turned = sds((width, total), BF16)
    flat = sds((total, width), BF16)
    half = sds((piece_rows, width), F32)
    return run(
        body,
        [
            rows_all,
            *att_all,
            *cot_pieces,
            *out_w,
            out_b,
            gain,
            shift,
            far(up),
            up_b,
            far(down),
            down_b,
        ],
        in_specs=[VMEM] * (1 + 3 * pieces + count) + [VMEM, VMEM, VMEM, HBM, VMEM, HBM, VMEM],
        out_specs=[HBM] + [VMEM] * (6 + pieces) + [HBM if units.packed else VMEM] * len(grads),
        out_shape=[pltpu.HBM((total, width), F32), flat, turned, flat, turned, half, flat, sds((8, units.count), F32)]
        + [sds((piece_rows, width), BF16)] * (pieces - 1)
        + grads,
        scratch_shapes=[pltpu.VMEM((total, width), F32)]
        + [pltpu.SemaphoreType.DMA]
        + units.scratch(total, width),
        vmem=22,
        cost_estimate=cost(12 * total * width * units.count, 24 * 1024 * 1024, total * units.count),
        name="feed_first",
    )


def feed_second(second, second_t, grad, grad_t, own_first, low_first, sends, up, up_b, down, units):
    pieces = 1 + len(sends)
    total, width = second.shape
    piece_rows = total // pieces
    grads = units.grad_shapes(width)

    def body(*refs):
        second, second_t, grad, grad_t, own_in, low_in, up_hbm, ub_ref, down_hbm, refs = (
            *refs[:9],
            refs[9:],
        )
        send_ins, refs = refs[: pieces - 1], refs[pieces - 1 :]
        own_ref, low_ref, ubg, refs = refs[0], refs[1], refs[2], refs[3:]
        send_refs, refs = refs[: pieces - 1], refs[pieces - 1 :]
        outs, scratch = refs[: len(grads)], refs[len(grads) :]
        _, part, _ = place(pieces)
        loads = units.loads(part, up_hbm, down_hbm, ub_ref, *scratch[5:])
        for load in loads:
            load.start()
        ubg[...] = jnp.zeros_like(ubg)
        for load in loads:
            load.wait()

        def give(i, rows, result, grad_second):
            low_ref[rows, :] = (grad_second + low_in[rows, :].astype(F32)).astype(BF16)
            h = i * ROWS // piece_rows
            at = slice(rows.start - h * piece_rows, rows.stop - h * piece_rows)
            if h == 0:
                own_ref[at, :] = own_in[at, :] + result
            else:
                send_refs[h - 1][at, :] = (result + send_ins[h - 1][at, :].astype(F32)).astype(BF16)

        stores = units.compute(second, second_t, grad, grad_t, ubg, scratch, outs, give)
        for store in stores:
            store.start()
        for store in stores:
            store.wait()

    return run(
        body,
        [
            second,
            second_t,
            grad,
            grad_t,
            own_first,
            low_first,
            far(up),
            up_b,
            far(down),
            *sends,
        ],
        in_specs=[VMEM] * 6 + [HBM, VMEM, HBM] + [VMEM] * (pieces - 1),
        out_specs=[VMEM] * (2 + pieces) + [HBM if units.packed else VMEM] * len(grads),
        out_shape=[
            sds((piece_rows, width), F32),
            sds((total, width), BF16),
            sds((8, units.count), F32),
        ]
        + [sds((piece_rows, width), BF16)] * (pieces - 1)
        + grads,
        scratch_shapes=units.scratch(total, width),
        vmem=26,
        cost_estimate=cost(12 * total * width * units.count, 24 * 1024 * 1024, total * units.count),
        name="feed_second",
    )


def mid_back(mid, grad_second, received, grad_rows, gain, out_w, att_first, att_last, chunk):
    pieces = 1 + len(received)
    total, width = mid.shape
    per_piece = total // pieces // ROWS
    split = att_first.shape[1]
    wide = split + att_last.shape[1]
    steps = total // ROWS

    def body(*refs):
        mid_ref, gs_ref, refs = refs[0], refs[1], refs[2:]
        recv_refs, refs = refs[: pieces - 1], refs[pieces - 1 :]
        go_ref, gain_ref, wo_ref, att_ref, last_ref = refs[:5]
        gm_ref, do_ref, sums_ref, *dwo_refs, acc = refs[5:]
        i = pl.program_id(0)

        @pl.when(i == 0)
        def _():
            sums_ref[...] = jnp.zeros_like(sums_ref)
            acc[...] = jnp.zeros_like(acc)

        normed, inv_std = norm_rows(mid_ref[...])
        grad = gs_ref[...].astype(F32)
        for ref in recv_refs:
            grad = grad + ref[...].astype(F32)
        go = go_ref[...].astype(F32)
        grad_mid = go + norm_back(grad * gain_ref[...], normed, inv_std)
        low = grad_mid.astype(BF16)
        do_ref[...] = dot_nt(low, wo_ref[...]).astype(BF16)
        acc[0:split, :] += dot(att_ref[...].T, low)
        acc[split:, :] += dot(last_ref[...].T, low)

        @pl.when(i < per_piece)
        def _():
            gm_ref[...] = grad_mid
            for n, item in enumerate((grad * normed, grad, low.astype(F32), go)):
                sums_ref[n : n + 1, :] += jnp.sum(item, axis=0, keepdims=True)

        @pl.when(i == steps - 1)
        def _():
            if chunk == 0:
                dwo_refs[0][...] = acc[...].astype(BF16)
                return
            _, part, _ = place(pieces)
            for c in range(pieces):

                @pl.when(part == c)
                def _(c=c):
                    for n in range(dwo_refs[0].shape[0]):
                        for e in range(pieces):
                            at = (n * pieces + (c + e) % pieces) * chunk
                            dwo_refs[e][n] = acc[at : at + chunk, :].astype(BF16)

    def rows_of(columns):
        return pl.BlockSpec((ROWS, columns), lambda i: (i, 0))

    def theirs(n):
        def index(i):
            piece = lax.rem(lax.div(i, per_piece) + pieces - n, pieces)
            return piece * per_piece + lax.rem(i, per_piece), 0

        return pl.BlockSpec((ROWS, width), index)

    def whole(*shape):
        return pl.BlockSpec(shape, lambda i: (0,) * len(shape))

    if chunk == 0:
        grads = [((wide, width), sds((wide, width), BF16))]
    else:
        shape = (width // (pieces * pieces * chunk), chunk, width)
        grads = [(shape, pltpu.HBM(shape, BF16))] * pieces
    return run(
        body,
        [
            far(mid),
            far(grad_second),
            *received,
            far(grad_rows),
            gain,
            out_w,
            far(att_first),
            far(att_last),
        ],
        grid=(steps,),
        in_specs=[rows_of(width), rows_of(width)]
        + [theirs(n) for n in range(1, pieces)]
        + [rows_of(width), whole(1, width), whole(wide, width), rows_of(split), rows_of(wide - split)],
        out_specs=[
            pl.BlockSpec((ROWS, width), lambda i: (jnp.minimum(i, per_piece - 1), 0)),
            rows_of(wide),
            whole(8, width),
        ]
        + [whole(*shape) for shape, _ in grads],
        out_shape=[
            sds((per_piece * ROWS, width), F32),
            sds((total, wide), BF16),
            sds((8, width), F32),
        ]
        + [item for _, item in grads],
        scratch_shapes=[pltpu.VMEM((wide, width), F32)],
        vmem=16,
        cost_estimate=cost(4 * total * width * wide, 14 * 1024 * 1024),
        name="mid_back",
    )


def attend_backward(
    qkv, grad_att, att, att_tile, logs, lane_first, tile, heads, head_dim, after=(), part=1
):
    total = qkv.shape[0]
    per_tile = LANES // head_dim
    live = min(per_tile, heads - tile * per_tile)
    scale = head_dim ** (-0.5)
    exp_scale = scale * LOG2E

    def body(qkv_ref, do_ref, att_ref, lse_ref, out_ref, *scratch):
        km, vm, qm, dm, key_t, query_t, do_t, dq_t, lse_t, mean_t = scratch
        lane = lax.broadcasted_iota(jnp.int32, (1, LANES), 1)
        lse_t[...] = lse_ref[...].T
        query = qkv_ref[:, 0:LANES].astype(F32)
        key = qkv_ref[:, LANES : 2 * LANES].astype(F32)
        val = qkv_ref[:, 2 * LANES : 3 * LANES].astype(F32)
        upstream = do_ref[...].astype(F32)
        both_t = (upstream * att_ref[...].astype(F32)).T
        for j in range(live):
            mean_t[j : j + 1, :] = jnp.sum(
                both_t[j * head_dim : (j + 1) * head_dim, :], axis=0, keepdims=True
            )
        query_t[...] = qkv_ref[:, 0:LANES].T
        do_t[...] = do_ref[...].T
        key_t[...] = qkv_ref[:, LANES : 2 * LANES].T
        for j in range(live):
            mine = lane // head_dim == j
            km[j] = jnp.where(mine, key, 0.0).astype(BF16)
            vm[j] = jnp.where(mine, val, 0.0).astype(BF16)
            qm[j] = jnp.where(mine, query, 0.0).astype(BF16)
            dm[j] = jnp.where(mine, upstream, 0.0).astype(BF16)
        dq_t[...] = jnp.zeros_like(dq_t)

        @pl.loop(0, total // ROWS)
        def _(i):
            rows = pl.ds(pl.multiple_of(i * ROWS, ROWS), ROWS)
            grad_key = jnp.zeros((ROWS, LANES), F32)
            grad_val = jnp.zeros((ROWS, LANES), F32)

            def enter(j):
                return dot(km[j, rows, :], query_t[...]), dot(vm[j, rows, :], do_t[...])

            ready = enter(0)
            for j in range(live):
                ahead = enter(j + 1) if j + 1 < live else None
                scores, grad_prob = ready
                head = lane_first + j
                own = slice(j * head_dim, (j + 1) * head_dim)
                probs = jnp.exp2(scores * exp_scale - lse_t[head : head + 1, :])
                grad_scores = (probs * (grad_prob - mean_t[j : j + 1, :])).astype(BF16)
                grad_val = grad_val + dot(probs.astype(BF16), dm[j])
                grad_key = grad_key + dot(grad_scores, qm[j])
                dq_t[own, :] += dot(key_t[own, rows], grad_scores)
                ready = ahead
            out_ref[rows, LANES : 2 * LANES] = (grad_key * scale).astype(BF16)
            out_ref[rows, 2 * LANES : 3 * LANES] = grad_val.astype(BF16)

        out_ref[:, 0:LANES] = (dq_t[...].T * scale).astype(BF16)

    masked = pltpu.VMEM((live, total, LANES), BF16)
    turned = pltpu.VMEM((LANES, total), BF16)
    turned_f = pltpu.VMEM((LANES, total), F32)
    return run(
        body,
        [qkv, grad_att, att, logs],
        after,
        grid=(1,),
        in_specs=[
            pl.BlockSpec((total, 3 * LANES), lambda i: (0, tile)),
            pl.BlockSpec((total, LANES), lambda i: (0, tile)),
            pl.BlockSpec((total, LANES), lambda i: (0, att_tile)),
            pl.BlockSpec((total, LANES), lambda i: (0, 0)),
        ],
        out_specs=pl.BlockSpec((total, 3 * LANES), lambda i: (0, 0)),
        out_shape=sds((total, 3 * LANES), BF16),
        scratch_shapes=[masked] * 4
        + [turned] * 3
        + [turned_f] * 2
        + [pltpu.VMEM((8, total), F32)],
        vmem=17,
        cost_estimate=cost(
            2 * live * total * total * 256 * 5, 3 * 1024 * 1024, live * total * total, part
        ),
        name="attend_backward",
    )


def project_weights(rows_all, gain, shift, grad_tiles, pieces, quads, packed, after):
    total, width = rows_all.shape
    tiles = len(grad_tiles)
    tile_cols = grad_tiles[0].shape[1]
    cols_all = tiles * tile_cols
    chunk = width // (quads * pieces)

    def body(*refs):
        x_ref, gain_ref, shift_ref, refs = refs[0], refs[1], refs[2], refs[3:]
        dq_refs, (*dw_refs, low_t, part_ref) = refs[:tiles], refs[tiles:]
        _, part, quad = place(pieces)

        @pl.loop(0, total // ROWS)
        def _(i):
            rows = pl.ds(pl.multiple_of(i * ROWS, ROWS), ROWS)
            normed, _ = norm_rows(x_ref[rows, :].astype(F32))
            low_t[:, rows] = (normed * gain_ref[...] + shift_ref[...]).astype(BF16).T

        for t in range(tiles):
            cols = slice(t * tile_cols, (t + 1) * tile_cols)
            part_ref[...] = dot(low_t[...], dq_refs[t][...]).astype(BF16)
            if not packed:
                dw_refs[0][:, cols] = part_ref[...]
                continue
            for c in range(pieces):

                @pl.when(part == c)
                def _(c=c, cols=cols):
                    for q in range(quads):
                        for e in range(pieces):
                            at = (q * pieces + (c + e) % pieces) * chunk
                            dw_refs[e][q ^ quad, :, cols] = part_ref[at : at + chunk, :]

    if packed:
        grads = [sds((quads, chunk, cols_all), BF16)] * pieces
    else:
        grads = [sds((width, cols_all), BF16)]
    return run(
        body,
        [rows_all, gain, shift, *grad_tiles],
        after,
        out_shape=grads,
        scratch_shapes=[pltpu.VMEM((width, total), BF16), pltpu.VMEM((width, tile_cols), BF16)],
        vmem=12,
        cost_estimate=cost(2 * total * width * cols_all, 6 * 1024 * 1024),
        name="project_weights",
    )


def project_rows(
    rows_all, weight, grad_tiles, sums_mid, up_sums, pieces, quads, packed, real, after
):
    total, width = rows_all.shape
    piece_rows = total // pieces
    cols_all = weight.shape[1]
    tiles = len(grad_tiles)
    tile_cols = cols_all // tiles

    def body(*refs):
        x_ref, w_ref, mid_ref, refs = *refs[:3], refs[3:]
        ups_refs, refs = refs[: len(up_sums)], refs[len(up_sums) :]
        dq_refs, refs = refs[:tiles], refs[tiles:]
        own_ref, refs = refs[0], refs[1:]
        send_refs, (sums_ref, bias_ref) = refs[: pieces - 1], refs[pieces - 1 :]
        _, part, _ = place(pieces)
        sums_ref[...] = jnp.zeros_like(sums_ref)
        bias_ref[...] = jnp.zeros_like(bias_ref)
        for h in range(pieces):

            @pl.loop(0, piece_rows // ROWS)
            def _(i, h=h):
                at = pl.multiple_of(i * ROWS, ROWS)
                src = pl.ds(at, ROWS)
                rows = pl.ds(h * piece_rows + at, ROWS)
                normed, _ = norm_rows(x_ref[rows, :].astype(F32))
                grad = jnp.zeros((ROWS, width), F32)
                for t in range(tiles):
                    grad_rows = dq_refs[t][rows, :]
                    cols = slice(t * tile_cols, (t + 1) * tile_cols)
                    grad = grad + dot_nt(grad_rows, w_ref[:, cols])
                    bias_ref[0:1, cols] += jnp.sum(grad_rows.astype(F32), axis=0, keepdims=True)
                if h == 0:
                    own_ref[src, :] = grad
                else:
                    send_refs[h - 1][src, :] = grad.astype(BF16)
                sums_ref[0:1, :] += jnp.sum(grad * normed, axis=0, keepdims=True)
                sums_ref[1:2, :] += jnp.sum(grad, axis=0, keepdims=True)

        if not packed:
            return
        for row, src in ((4, 2), (5, 0), (6, 1), (15, 3)):
            sums_ref[row : row + 1, :] = mid_ref[src : src + 1, :]
        for c in range(pieces):

            @pl.when(part == c)
            def _(c=c):
                for row, p in ((2, 0), (3, 2)):
                    mine = jnp.concatenate(
                        [
                            bias_ref[0:1, (3 * t + p) * LANES :][:, : min(LANES, real - t * LANES)]
                            for t in range(tiles)
                        ],
                        axis=1,
                    )
                    sums_ref[row : row + 1, c * real : (c + 1) * real] = mine
                for n in range(quads):
                    row = 7 + n * pieces + c
                    start = 0
                    for ref in ups_refs:
                        size = ref.shape[1] // quads
                        here = ref[0:1, n * size : (n + 1) * size]
                        sums_ref[row : row + 1, start : start + size] = here
                        start += size

    return run(
        body,
        [rows_all, weight, sums_mid, *up_sums, *grad_tiles],
        after,
        out_shape=[sds((piece_rows, width), F32)]
        + [sds((piece_rows, width), BF16)] * (pieces - 1)
        + [sds((16, width), F32), sds((8, cols_all), F32)],
        vmem=12,
        cost_estimate=cost(2 * total * width * cols_all, 8 * 1024 * 1024),
        name="project_rows",
    )


def finish_rows(rows_all, gain, grad_mid, grad_own, received, count, after):
    rows, width = grad_mid.shape
    others = len(received)
    piece = rows // count
    per_step = ROWS // piece

    def body(*refs):
        x_ref, gain_ref, gm_ref, own_ref, refs = refs[0], refs[1], refs[2], refs[3], refs[4:]
        recv_refs, out_refs = refs[:others], refs[others:]
        for n in range(rows // ROWS):
            at = slice(n * ROWS, (n + 1) * ROWS)
            normed, inv_std = norm_rows(x_ref[at, :].astype(F32))
            grad = own_ref[at, :]
            for ref in recv_refs:
                grad = grad + ref[at, :].astype(F32)
            done = gm_ref[at, :] + norm_back(grad * gain_ref[...], normed, inv_std)
            for e in range(per_step):
                out_refs[n * per_step + e][...] = done[e * piece : (e + 1) * piece, :].astype(BF16)

    return run(
        body,
        [rows_all, gain, grad_mid, grad_own, *received],
        after,
        out_shape=[sds((piece, width), BF16)] * count,
        vmem=12,
        cost_estimate=cost(20 * rows * width, 6 * 1024 * 1024),
        name="finish_rows",
    )


def finish_result(own, received, count):
    rows, width = own.shape
    others = len(received)
    piece = rows // count

    def body(*refs):
        out_refs = refs[1 + others :]
        for n in range(count):
            at = slice(n * piece, (n + 1) * piece)
            total = refs[0][at, :]
            for ref in refs[1 : 1 + others]:
                total = total + ref[at, :].astype(F32)
            out_refs[n % 2][n // 2] = total.astype(BF16)

    return run(
        body,
        [far(own), *received],
        out_shape=[sds((count // 2, piece, width), BF16)] * 2,
        vmem=8,
        cost_estimate=cost(2 * rows * width, 3 * 1024 * 1024),
        name="finish_result",
    )


def pass_on(keep, received, after):
    def body(keep_ref, recv_ref, out_ref):
        out_ref[0] = keep_ref[1]
        out_ref[1] = recv_ref[1]

    return run(
        body,
        [keep, received],
        after,
        out_shape=sds(keep.shape, keep.dtype),
        vmem=6,
        cost_estimate=cost(0, 4 * keep.size),
        name="pass_on",
    )


def collect_halves(keep, near, far, group, after):
    _, rows, width = keep.shape

    def body(keep_ref, near_ref, far_ref, out_ref):
        _, _, quad = place(group)
        out_ref[quad] = keep_ref[0]
        out_ref[quad ^ 1] = near_ref[0]
        out_ref[quad ^ 2] = far_ref[0]
        out_ref[quad ^ 3] = far_ref[1]

    return run(
        body,
        [keep, near, far],
        after,
        out_shape=sds((4, rows, width), keep.dtype),
        vmem=6,
        cost_estimate=cost(0, 16 * rows * width),
        name="collect_halves",
    )


def two_parts(item):
    first = item.astype(BF16)
    return first, (item - first.astype(F32)).astype(BF16)


def pack_attention(
    qkv_keep, qkv_recv, out_keep, out_recv, small, small_recv, real, blocks, after
):
    quads, chunk, cols_all = qkv_keep.shape
    wide = cols_all // 3
    tiles = wide // LANES
    width = out_keep.shape[2]
    qkv_lanes = 6 * real // blocks
    out_lanes = width // blocks
    lanes = qkv_lanes + out_lanes
    halves = quads // 2
    slot = halves * chunk
    small_rows = small.shape[0]

    def body(qk_ref, qr_ref, ok_ref, or_ref, small_ref, srecv_ref, *out_refs):
        _, part, quad = place(2)
        mine = lax.axis_index("batch")
        slots = out_refs[4]

        def heads_of(rows, p):
            return [
                rows[:, (3 * t + p) * LANES : (3 * t + p) * LANES + min(LANES, real - t * LANES)]
                for t in range(tiles)
            ]

        for c in range(2):

            @pl.when(part == c)
            def _(c=c):
                for q in range(quads):
                    pair = (qk_ref[q], qr_ref[q])
                    if c == 1:
                        pair = pair[::-1]
                    parts = []
                    for p in range(3):
                        parts += heads_of(pair[0], p) + heads_of(pair[1], p)
                    row = jnp.concatenate(parts, axis=1)
                    for b in range(blocks):
                        slots[b ^ mine, q, :, 0:qkv_lanes] = row[
                            :, b * qkv_lanes : (b + 1) * qkv_lanes
                        ]
                for e, ref in enumerate((ok_ref, or_ref)):
                    for n in range(halves):
                        q = ((c + e) % 2) * halves + n
                        for b in range(blocks):
                            slots[b ^ mine, q ^ quad, :, qkv_lanes:lanes] = ref[
                                n, :, b * out_lanes : (b + 1) * out_lanes
                            ]

        for n, order in enumerate(((0, 2), (1, 3), (0, 1), (2, 3))):
            for e in range(2):
                for f in range(halves):
                    at = e * slot + f * chunk
                    src = f if n < 2 else halves + f
                    out_refs[n][at : at + chunk, :] = slots[order[e], src]
        parts = two_parts(small_ref[...] + srecv_ref[...])
        for n in range(2):
            for e in range(2):
                at = 2 * slot + e * small_rows
                out_refs[n][at : at + small_rows, :] = parts[e]

    first = sds((2 * slot + 2 * small_rows, lanes), BF16)
    other = sds((2 * slot, lanes), BF16)
    return run(
        body,
        [qkv_keep, qkv_recv, out_keep, out_recv, small, small_recv],
        after,
        out_shape=[first, first, other, other],
        scratch_shapes=[pltpu.VMEM((blocks, quads, chunk, lanes), BF16)],
        vmem=12,
        cost_estimate=cost(0, 4 * 1024 * 1024),
        name="pack_attention",
    )


def sum_first(keeps, received, after=()):
    count = len(keeps)
    shape = keeps[0].shape[1:]

    def body(*refs):
        for n in range(count):
            for e in range(2):
                total = refs[n][e].astype(F32) + refs[count + n][e].astype(F32)
                refs[2 * count + 2 * n + e][...] = total.astype(BF16)

    return run(
        body,
        [*keeps, *received],
        after,
        out_shape=[pltpu.HBM(shape, BF16), sds(shape, BF16)] * count,
        vmem=12,
        cost_estimate=cost(0, 6 * count * keeps[0].size),
        name="sum_first",
    )


def sum_second(keeps, received, after=()):
    quads, rows, width = keeps[0].shape

    def body(ka, kb, ra, rb, keep_ref, send_ref):
        for d in range(quads):
            ref = send_ref if d % 2 else keep_ref
            for e, (keep, recv) in enumerate(((ka, ra), (kb, rb))):
                total = keep[d].astype(F32) + recv[d].astype(F32)
                ref[d // 2, e] = total.astype(BF16)

    return run(
        body,
        [*keeps, *received],
        after,
        out_shape=[pltpu.HBM((quads // 2, 2, rows, width), BF16)] * 2,
        vmem=10,
        cost_estimate=cost(0, 12 * keeps[0].size),
        name="sum_second",
    )


def sum_third(keep, received, after=()):
    def body(keep_ref, recv_ref, stay_ref, pass_ref):
        for ref, e in ((stay_ref, 0), (pass_ref, 1)):
            ref[...] = (keep_ref[e].astype(F32) + recv_ref[e].astype(F32)).astype(BF16)

    return run(
        body,
        [keep, received],
        after,
        out_shape=[sds(keep.shape[1:], BF16)] * 2,
        vmem=6,
        cost_estimate=cost(0, 6 * keep.size),
        name="sum_third",
    )


def small_sum(refs, rows, count):
    total = None
    for ref in refs:
        for e in range(2):
            item = ref[rows + e * count : rows + (e + 1) * count, :].astype(F32)
            total = item if total is None else total + item
    return total


def sum_first_attention(keeps, received, slot, small_rows, after):
    lanes = keeps[0].shape[1]

    def body(ka, kb, ra, rb, stay_a, pass_a, stay_b, pass_b):
        parts = two_parts(small_sum((ka, ra), 2 * slot, small_rows))
        for keep, recv, stay, on in ((ka, ra, stay_a, pass_a), (kb, rb, stay_b, pass_b)):
            for e, ref in enumerate((stay, on)):
                at = slice(e * slot, (e + 1) * slot)
                ref[0:slot, :] = (keep[at, :].astype(F32) + recv[at, :].astype(F32)).astype(BF16)
        for ref in (stay_a, pass_a):
            for e in range(2):
                ref[slot + e * small_rows : slot + (e + 1) * small_rows, :] = parts[e]

    first = sds((slot + 2 * small_rows, lanes), BF16)
    other = sds((slot, lanes), BF16)
    return run(
        body,
        [*keeps, *received],
        after,
        out_shape=[first, first, other, other],
        vmem=8,
        cost_estimate=cost(0, 3 * 1024 * 1024),
        name="sum_first_attention",
    )


def sum_second_attention(keeps, received, chunk, quads, small_rows, after):
    lanes = keeps[0].shape[1]
    halves = quads // 2
    slot = halves * chunk

    def body(ka, kb, ra, rb, *out_refs):
        parts = two_parts(small_sum((ka, ra), slot, small_rows))
        for d in range(quads):
            keep, recv = ((ka, ra), (kb, rb))[d // halves]
            at = slice(d % halves * chunk, (d % halves + 1) * chunk)
            total = keep[at, :].astype(F32) + recv[at, :].astype(F32)
            out_refs[d][0:chunk, :] = total.astype(BF16)
            for e in range(2):
                at = chunk + e * small_rows
                out_refs[d][at : at + small_rows, :] = parts[e]

    return run(
        body,
        [*keeps, *received],
        after,
        out_shape=[sds((chunk + 2 * small_rows, lanes), BF16)] * quads,
        vmem=8,
        cost_estimate=cost(0, 2 * 1024 * 1024),
        name="sum_second_attention",
    )


def final_attention(pieces, chunk, qkv_lanes, small_rows):
    lanes = pieces[0].shape[1]
    count = len(pieces)

    def body(*refs):
        total = refs[0][0:chunk, :].astype(F32)
        for ref in refs[1:count]:
            total = total + ref[0:chunk, :].astype(F32)
        refs[count][...] = total[:, :qkv_lanes]
        refs[count + 1][...] = total[:, qkv_lanes:]
        refs[count + 2][...] = small_sum(refs[:count], chunk, small_rows)

    return run(
        body,
        pieces,
        out_shape=[
            sds((chunk, qkv_lanes), F32),
            sds((chunk, lanes - qkv_lanes), F32),
            sds((small_rows, lanes), F32),
        ],
        vmem=6,
        cost_estimate=cost(0, 1024 * 1024),
        name="final_attention",
    )


def final_units(first, second, after):
    high = first[0].shape[1]
    sizes = [first[0].shape[2], second[0].shape[2]]
    unit_block = sum(sizes)
    count = len(first)
    half = high // 2

    def body(*refs):
        _, part, _ = place(2)
        keep_ref, send_ref, down_ref = refs[2 * count :]
        for h in range(2):
            pieces = refs[h * count : (h + 1) * count]
            up, down = pieces[0][0].astype(F32), pieces[0][1].astype(F32)
            for ref in pieces[1:]:
                up = up + ref[0].astype(F32)
                down = down + ref[1].astype(F32)
            here = slice(h * sizes[0], h * sizes[0] + sizes[h])
            down_ref[here, :] = down.T
            for c in range(2):

                @pl.when(part == c)
                def _(up=up, here=here, c=c):
                    keep_ref[:, here] = up[c * half : (c + 1) * half, :]
                    send_ref[:, here] = up[(1 - c) * half : (2 - c) * half, :].astype(BF16)

    return run(
        body,
        [*first, *second],
        after,
        out_shape=[
            sds((half, unit_block), F32),
            sds((half, unit_block), BF16),
            sds((unit_block, high), F32),
        ],
        vmem=10,
        cost_estimate=cost(0, 4 * 1024 * 1024),
        name="final_units",
    )


def final_join(keep, recv):
    chunk, unit_block = keep.shape

    def body(keep_ref, recv_ref, out_ref):
        _, part, _ = place(2)
        for c in range(2):

            @pl.when(part == c)
            def _(c=c):
                out_ref[:, c * unit_block : (c + 1) * unit_block] = keep_ref[...]
                out_ref[:, (1 - c) * unit_block : (2 - c) * unit_block] = recv_ref[...].astype(F32)

    return run(
        body,
        [keep, recv],
        out_shape=sds((chunk, 2 * unit_block), F32),
        vmem=5,
        cost_estimate=cost(0, 1024 * 1024),
        name="final_join",
    )


def on_device(
    tokens,
    mask,
    cotangent,
    ln1_gain,
    ln1_bias,
    qkv_weight,
    q_bias,
    v_bias,
    out_weight,
    out_bias,
    ln2_gain,
    ln2_bias,
    up_weight,
    up_bias,
    down_weight,
    down_bias,
):
    seq_size = lax.axis_size("seq")
    batch_size = lax.axis_size("batch")
    micro_count, seq_count, local_len, width = tokens.shape
    sequences = micro_count * seq_count
    group = seq_size // sequences
    units = up_weight.shape[1]
    head_dim = width // HEADS
    heads = HEADS // group
    real = heads * head_dim
    wide = -(-real // LANES) * LANES
    full_len = local_len * seq_size
    block_len = local_len // group
    rows = seq_size * block_len
    own_units = units // group
    part = lax.axis_index("seq") % group
    aligned = (
        seq_size == batch_size * group
        and group == 2
        and batch_size == 4
        and wide == 3 * LANES
        and (seq_size // group) % group == 0
        and units % (batch_size * group * LANES) == 0
        and own_units // batch_size == width
    )

    def from_part(item, ahead):
        if ahead % group == 0:
            return item
        pairs = [
            (q * group + (c + ahead) % group, q * group + c)
            for q in range(sequences)
            for c in range(group)
        ]
        return lax.ppermute(item, "seq", pairs)

    def gather_parts(item):
        return [from_part(item, n) for n in range(group)]

    def row_of(item):
        return item.astype(F32)[None, :]

    def blocks_of(item):
        return item.reshape(sequences, local_len, width)

    x_own = over_quads(deal(blocks_of(tokens), group), group)
    x_pieces = [from_part(item, n) for n in range(group) for item in x_own]

    count_rows = jnp.sum(mask, axis=2).reshape(sequences).astype(BF16)
    cot_low = jnp.where(mask[..., None] != 0, cotangent, jnp.zeros_like(cotangent))
    cot_send = jnp.concatenate(
        [blocks_of(cot_low), jnp.broadcast_to(count_rows[:, None, None], (sequences, 16, width))],
        axis=1,
    )
    cot_own = over_quads(deal(cot_send, group, x_pieces[sequences:]), group)

    qkv_w, qkv_b, *out_w = pick_weights(
        qkv_weight,
        jnp.concatenate([q_bias, jnp.zeros_like(q_bias), v_bias])[None, :],
        out_weight,
        group,
        real,
        wide,
    )
    if aligned:
        up_own, up_b, down_own = up_weight, up_bias[None, :], down_weight
    else:

        def own_columns(matrix, blocks):
            split = matrix.reshape(matrix.shape[0], blocks, group, -1)
            return lax.dynamic_index_in_dim(split, part, 2, keepdims=False)

        up_own = own_columns(up_weight, batch_size).reshape(width, own_units)
        up_b = own_columns(up_bias[None, :], batch_size).reshape(1, own_units)
        down_own = lax.dynamic_index_in_dim(
            down_weight.reshape(batch_size, group, -1, width), part, 1, keepdims=False
        ).reshape(own_units, width)

    tiles = wide // LANES
    x_all, qkv, att_first, logs_first = attend_first(
        x_pieces, row_of(ln1_gain), row_of(ln1_bias), qkv_w, qkv_b, tiles - 1, heads, head_dim
    )
    cot_stack = stack(cot_own, [logs_first])
    att_last, logs_last = attend_last(qkv, tiles - 1, heads, head_dim, [cot_stack])
    cot_pieces = cot_own + [
        item[d]
        for item in gather_parts(cot_stack)[1:]
        for d in range(sequences)
    ]
    blocks = batch_size if aligned else 1
    unit_block = own_units // blocks
    size = unit_block * 2 // 5
    shape = (group, sequences if aligned else None, width // sequences)
    calls = [
        Units(unit_block, blocks, 0, size, *shape),
        Units(unit_block, blocks, size, unit_block - size, *shape),
    ]
    mid, second, second_t, grad_rows, grad_t, result_own, grad_second, *found = feed_first(
        x_all,
        gather_parts(att_first),
        gather_parts(att_last),
        cot_pieces,
        out_w,
        row_of(out_bias),
        row_of(ln2_gain),
        row_of(ln2_bias),
        up_own,
        up_b,
        down_own,
        row_of(down_bias),
        calls[0],
    )
    up_sums, ff_grads = [found[0]], [found[group:]]
    result_own, grad_second, *found = feed_second(
        second,
        second_t,
        grad_rows,
        grad_t,
        result_own,
        grad_second,
        found[1:group],
        up_own,
        up_b,
        down_own,
        calls[1],
    )
    up_sums.append(found[0])
    result_send = found[1:group]
    ff_grads.append(found[group:])

    def begin_sum(e, sends, after):
        moved = [swap(sends[0], "batch", batch_size, 1), swap(sends[1], "batch", batch_size, 2)]
        stay_a, pass_a, stay_b, pass_b = sum_first(
            [ff_grads[e][0], ff_grads[e][2]], moved, after
        )
        moved = [swap(pass_a, "batch", batch_size, 2), swap(pass_b, "batch", batch_size, 1)]
        return [stay_a, stay_b], moved

    if aligned:
        waiting = begin_sum(0, [ff_grads[0][1], ff_grads[0][3]], [])
        (grad_second,) = gate([grad_second], waiting[0][:1])
    second_send = grad_second
    second_recv = [from_part(second_send, n) for n in range(1, group)]
    result_recv = [from_part(result_send[group - n - 1], n) for n in range(1, group)]
    result_keep, result_pass = finish_result(result_own, result_recv, sequences)

    def quad_swap(item, distance):
        return swap(item, "seq", seq_size, distance * group)

    result_near = quad_swap(result_pass, 1)

    chunk = width // seq_size
    grad_mid, grad_att, sums_mid, *out_grad = mid_back(
        mid,
        grad_second,
        second_recv,
        grad_rows,
        row_of(ln2_gain),
        out_w[0],
        att_first,
        att_last,
        chunk if aligned else 0,
    )

    def tile_back(t, after, cost_part=1):
        last = t == tiles - 1
        return attend_backward(
            qkv,
            grad_att,
            att_last if last else att_first,
            0 if last else t,
            logs_last if last else logs_first,
            0 if last else t * (LANES // head_dim),
            t,
            heads,
            head_dim,
            after,
            cost_part,
        )

    grad_tiles = [None] * tiles
    after = [result_keep]
    if aligned:
        keep, send = sum_second(*waiting, [grad_mid])
        moved = quad_swap(send, 1)
        sends = gate([ff_grads[1][1], ff_grads[1][3]], [keep])
        after = [result_keep, keep]
    grad_tiles[0] = tile_back(0, after, 64)
    result_pass = pass_on(result_keep, result_near, grad_tiles[:1])
    result_far = quad_swap(result_pass, 2)
    after = [result_pass]
    if aligned:
        unit_first = list(sum_third(keep, moved, [grad_tiles[0]]))
        unit_first[1] = quad_swap(unit_first[1], 2)
        waiting = begin_sum(1, sends, [grad_tiles[0]])
        after = [result_pass, unit_first[0], waiting[0][0]]
    for t in range(1, tiles - 1):
        grad_tiles[t] = tile_back(t, after)
    after = [grad_tiles[-2], result_far]
    if aligned:
        out_recv = from_part(out_grad[1], 1)
        keep, send = sum_second(*waiting, [grad_tiles[-2]])
        moved = quad_swap(send, 1)
        after = [keep, result_far, unit_first[1]]
    grad_tiles[-1] = tile_back(tiles - 1, after)
    after = []
    if aligned:
        after = [out_recv]
    qkv_grad = project_weights(
        x_all,
        row_of(ln1_gain),
        row_of(ln1_bias),
        grad_tiles,
        group,
        sequences,
        aligned,
        after,
    )
    after = qkv_grad[:1]
    if aligned:
        unit_second = list(sum_third(keep, moved, qkv_grad[:1]))
        unit_second[1] = quad_swap(unit_second[1], 2)
        after = unit_second[:1]
    first_own, *found = project_rows(
        x_all,
        qkv_w,
        grad_tiles,
        sums_mid,
        up_sums,
        group,
        sequences,
        aligned,
        real,
        after,
    )
    first_send, (small, bias_sums) = found[: group - 1], found[group - 1 :]
    first_recv = [from_part(first_send[group - n - 1], n) for n in range(1, group)]
    after = []
    if aligned:
        small_rows = small.shape[0]
        packed = pack_attention(
            qkv_grad[0],
            from_part(qkv_grad[1], 1),
            out_grad[0],
            out_recv,
            small,
            from_part(small, 1),
            real,
            batch_size,
            [],
        )
        after = packed[:1]
    row_parts = finish_rows(
        x_all, row_of(ln1_gain), grad_mid, first_own, first_recv, sequences, after
    )
    row_moved = over_quads(row_parts, group)
    if aligned:
        stay_a, pass_a, stay_b, pass_b = sum_first_attention(
            [packed[0], packed[2]],
            [swap(packed[1], "batch", batch_size, 1), swap(packed[3], "batch", batch_size, 2)],
            sequences // 2 * chunk,
            small_rows,
            [row_parts[0], row_moved[1], unit_second[1]],
        )
        summed = sum_second_attention(
            [stay_a, stay_b],
            [swap(pass_a, "batch", batch_size, 2), swap(pass_b, "batch", batch_size, 1)],
            chunk,
            sequences,
            small_rows,
            row_moved[3:],
        )
        after = summed[:1]
        up_keep, up_send, down_grad = final_units(unit_first, unit_second, after)
        up_grad = final_join(up_keep, from_part(up_send, 1))
        qkv_final, out_final, small = final_attention(
            over_quads(summed, group), chunk, qkv_weight.shape[1] // batch_size, small_rows
        )
        small = small.reshape(-1)
    result = collect_halves(result_keep, result_near, result_far, group, after)
    result = result.reshape(tokens.shape)
    grad_in = collect(row_moved, group, after).reshape(tokens.shape)
    if not aligned:

        def spread(item, blocks):
            split = item.reshape(blocks, 1, -1)
            empty = jnp.zeros((blocks, group, split.shape[2]), F32)
            return lax.dynamic_update_slice(empty, split, (0, part, 0)).reshape(-1)

        bias_sums = bias_sums[0].reshape(tiles, 3, LANES).transpose(1, 0, 2)
        bias_sums = bias_sums.reshape(3, wide)[:, :real]
        small = jnp.concatenate(
            [
                small[0],
                small[1],
                spread(bias_sums[0], 1),
                spread(bias_sums[2], 1),
                sums_mid[2],
                sums_mid[0],
                sums_mid[1],
                spread(jnp.concatenate([item[0] for item in up_sums]), batch_size),
                sums_mid[3],
            ]
        )

        def scattered(item):
            item = lax.psum_scatter(item.astype(BF16), "seq", scatter_dimension=0, tiled=True)
            return lax.psum_scatter(item, "batch", scatter_dimension=1, tiled=True).astype(F32)

        def spread_columns(item, blocks):
            split = item.reshape(item.shape[0], blocks, 1, -1)
            empty = jnp.zeros((item.shape[0], blocks, group, split.shape[3]), item.dtype)
            filled = lax.dynamic_update_slice(empty, split, (0, 0, part, 0))
            return filled.reshape(item.shape[0], -1)

        up_full, down_full = [
            jnp.concatenate([item[e] for item in ff_grads], axis=1) for e in range(2)
        ]
        up_grad = scattered(spread_columns(up_full, batch_size))
        down_grad = scattered(spread_columns(down_full, batch_size).T)
        rows_full = qkv_grad[0].reshape(width, tiles, 3, LANES).transpose(0, 2, 1, 3)
        rows_full = rows_full.reshape(width, 3, wide)[..., :real]
        qkv_final = scattered(spread_columns(rows_full.reshape(width, -1), 3))
        out_final = scattered(spread_columns(out_grad[0][:real].T, 1).T)
        small = lax.psum(small, ("seq", "batch"))

    edges = [width] * 7 + [units, width]
    pieces, start = [], 0
    for size in edges:
        pieces.append(small[start : start + size])
        start += size
    return (
        result,
        grad_in,
        pieces[0],
        pieces[1],
        qkv_final,
        pieces[2],
        pieces[3],
        out_final,
        pieces[4],
        pieces[5],
        pieces[6],
        up_grad,
        pieces[7],
        down_grad,
        pieces[8],
    )


def solution(mesh):
    rows = P(None, "batch", "seq", None)
    split = P("seq", "batch")
    in_specs = (rows, P(None, "batch", "seq"), rows) + (P(),) * 13
    out_specs = (
        rows,
        rows,
        P(),
        P(),
        split,
        P(),
        P(),
        split,
        P(),
        P(),
        P(),
        split,
        P(),
        split,
        P(),
    )
    return jax.shard_map(
        on_device, mesh=mesh, in_specs=in_specs, out_specs=out_specs, check_vma=False
    )
```
